32 devices in a mesh: seq: 2 (over y), shard: 4 (over x, core), replica: 4 (over z).
Axes of the slice: x: 2, y: 2, z: 4, core: 2. Of those that a mesh axis runs over, the one named last changes fastest.
Arguments:
- tokens: bfloat16 [16, 256, 2048], P(('shard', 'replica'), 'seq'), may hold values from -6 to 6
- segments: int32 [16, 256], P(('shard', 'replica'), 'seq'), may hold values from 0 to 5, never falling along the last dimension, each value on 1 to 96 neighbouring positions
- cotangent: bfloat16 [16, 256, 2048], P(('shard', 'replica'), 'seq'), may hold values from -6 to 6
- norm_gain: float32 [2048], P(('seq', 'shard')), may hold values from 0.5 to 1.5
- branch_weight: float32 [2048, 2560], P(('seq', 'shard')), may hold values from -0.125 to 0.125
- input_weight: float32 [2048, 2560], P(('seq', 'shard')), may hold values from -0.125 to 0.125
- conv_weight: float32 [4, 2560], P(None, ('seq', 'shard')), may hold values from -3 to 3
- conv_bias: float32 [2560], P(('seq', 'shard')), may hold values from -3 to 3
- recur_gate_weight: float32 [16, 160, 160], P(('seq', 'shard')), may hold values from -0.5 to 0.5
- recur_gate_bias: float32 [2560], P(('seq', 'shard')), may hold values from -4 to 4
- input_gate_weight: float32 [16, 160, 160], P(('seq', 'shard')), may hold values from -0.5 to 0.5
- input_gate_bias: float32 [2560], P(('seq', 'shard')), may hold values from -4 to 4
- decay_param: float32 [2560], P(('seq', 'shard'))
- output_weight: float32 [2560, 2048], P(('seq', 'shard')), may hold values from -0.3125 to 0.3125
- mlp_norm_gain: float32 [2048], P(('seq', 'shard')), may hold values from 0.5 to 1.5
- gate_weight: float32 [2048, 6144], P(('seq', 'shard')), may hold values from -0.125 to 0.125
- up_weight: float32 [2048, 6144], P(('seq', 'shard')), may hold values from -0.125 to 0.125
- down_weight: float32 [6144, 2048], P(('seq', 'shard')), may hold values from -0.109375 to 0.109375
Outputs:
- block_out: bfloat16 [16, 256, 2048], P(('shard', 'replica'), 'seq')
- tokens_grad: bfloat16 [16, 256, 2048], P(('shard', 'replica'), 'seq')
- norm_gain_grad: float32 [2048], P(('seq', 'shard'))
- branch_weight_grad: float32 [2048, 2560], P(('seq', 'shard'))
- input_weight_grad: float32 [2048, 2560], P(('seq', 'shard'))
- conv_weight_grad: float32 [4, 2560], P(None, ('seq', 'shard'))
- conv_bias_grad: float32 [2560], P(('seq', 'shard'))
- recur_gate_weight_grad: float32 [16, 160, 160], P(('seq', 'shard'))
- recur_gate_bias_grad: float32 [2560], P(('seq', 'shard'))
- input_gate_weight_grad: float32 [16, 160, 160], P(('seq', 'shard'))
- input_gate_bias_grad: float32 [2560], P(('seq', 'shard'))
- decay_param_grad: float32 [2560], P(('seq', 'shard'))
- output_weight_grad: float32 [2560, 2048], P(('seq', 'shard'))
- mlp_norm_gain_grad: float32 [2048], P(('seq', 'shard'))
- gate_weight_grad: float32 [2048, 6144], P(('seq', 'shard'))
- up_weight_grad: float32 [2048, 6144], P(('seq', 'shard'))
- down_weight_grad: float32 [6144, 2048], P(('seq', 'shard'))
The draws below stay inside these ranges and needn't reach their ends.
Inputs may be any that keep to these rules, and one draw needn't show every extreme that they name: `segments`: segment numbers never fall along a sequence; each document has 1 to 96 tokens and one has exactly 96.
All inputs are finite; a program needn't handle non-finite values.
Results may differ from the reference program's by a relative error of at most 0.02.
Values may be sent and summed in bfloat16 or wider, within the bound.
A program may use at most 576 MiB of HBM per device.

```python
import math
import jax
import jax.numpy as jnp
import numpy as np
from jax import lax

D = 2048
LRU_WIDTH = 2560
FF = 6144
BLOCKS = 16
CONV = 4
DOCS = 6
BLOCK_WIDTH = 160
LENGTH = 256
SEQS = 16
DOC_MOST = 96


def draw_decay_param(key, part):
    slow_key = jax.random.fold_in(key, 11)
    logs = jax.random.uniform(slow_key, (LRU_WIDTH,), jnp.float32, math.log(0.1 / LENGTH), math.log(0.03))
    rate = jnp.exp(logs)
    return -jnp.log(jnp.expm1(rate))


def block_scale(key, extent, cuts, least, high):
    def one(dim, parts):
        heights = jax.random.uniform(jax.random.fold_in(jax.random.fold_in(key, 6), dim), (parts,), jnp.float32, least / len(cuts), high / len(cuts))
        return jnp.repeat(jnp.exp(heights), extent[dim] // parts).reshape((-1,) + (1,) * (len(extent) - dim - 1))

    level = one(*cuts[0])
    for cut in cuts[1:]:
        level = level * one(*cut)
    return level


def split_up(number_of, total, reach, skew):
    weights = [(1 << 20) // math.isqrt(grade ** skew) + 1 for grade in range(2, number_of + 1)]
    rest, holding = total - reach - (number_of - 1), [1] * (number_of - 1)
    while rest > 0:
        movable = [i for i in range(number_of - 1) if holding[i] < reach]
        whole, remaining = sum([weights[i] for i in movable]), rest
        for i in movable:
            more = min(reach - holding[i], max(1, remaining * weights[i] // whole), rest)
            holding[i] = holding[i] + more
            rest = rest - more
    return np.array([reach] + holding)


def uneven(own_key, amount, total, bound, skew):
    if amount == 2:
        one = jax.random.randint(own_key, (), max(1, total - bound), min(bound, total - 1) + 1)
        return jnp.stack([one, total - one])
    lengths = jnp.asarray(split_up(amount, total, bound, skew), jnp.int32)
    pairs = (amount - 1) // 2
    giver, taker = lengths[1:1 + 2 * pairs:2], lengths[2:2 + 2 * pairs:2]
    margin = jnp.minimum(giver - 1, bound - taker)
    passed = jax.random.randint(jax.random.fold_in(own_key, 1), (pairs,), 0, 1 << 20) % (margin + 1)
    lengths = lengths.at[1:1 + 2 * pairs:2].set(giver - passed).at[2:2 + 2 * pairs:2].set(taker + passed)
    return lengths[jax.random.permutation(jax.random.fold_in(own_key, 2), amount)]


def scatter_about(own_key, dims, spread, limit, pieces=(), dtype=jnp.bfloat16):
    entries = spread * jax.random.normal(own_key, dims, jnp.float32)
    if pieces:
        entries = entries * block_scale(own_key, dims, pieces, -0.22, 0.18)
    return jnp.clip(entries, -limit, limit).astype(dtype)


def setup_inputs(seed: int = 0) -> dict:
    keys = jax.random.split(jax.random.key(seed), 19)
    return {
        "tokens": scatter_about(keys[0], (SEQS, LENGTH, D), 1.0, 6.0, ((0, 16), (1, 2))),
        "segments": jax.vmap(lambda own: jnp.searchsorted(jnp.cumsum(uneven(own, DOCS, LENGTH, DOC_MOST, 1)), jnp.arange(LENGTH), side="right"))(jax.random.split(keys[1], SEQS)).reshape((SEQS, LENGTH)).astype(jnp.int32),
        "cotangent": scatter_about(keys[2], (SEQS, LENGTH, D), 1.0, 6.0, ((0, 16), (1, 2))),
        "norm_gain": jnp.clip(1.0 + 0.1 * jax.random.normal(keys[3], (D,), jnp.float32), 0.5, 1.5),
        "branch_weight": scatter_about(keys[4], (D, LRU_WIDTH), D ** -0.5, 0.125, ((0, 8),), jnp.float32),
        "input_weight": scatter_about(keys[5], (D, LRU_WIDTH), D ** -0.5, 0.125, ((0, 8),), jnp.float32),
        "conv_weight": scatter_about(keys[6], (CONV, LRU_WIDTH), CONV ** -0.5, 3.0, ((1, 8),), jnp.float32),
        "conv_bias": scatter_about(keys[7], (LRU_WIDTH,), 0.5, 3.0, ((0, 8),), jnp.float32),
        "recur_gate_weight": scatter_about(keys[8], (BLOCKS, BLOCK_WIDTH, BLOCK_WIDTH), BLOCK_WIDTH ** -0.5, 0.5, ((0, 8),), jnp.float32),
        "recur_gate_bias": scatter_about(keys[9], (LRU_WIDTH,), 1.0, 4.0, ((0, 8),), jnp.float32),
        "input_gate_weight": scatter_about(keys[10], (BLOCKS, BLOCK_WIDTH, BLOCK_WIDTH), BLOCK_WIDTH ** -0.5, 0.5, ((0, 8),), jnp.float32),
        "input_gate_bias": scatter_about(keys[11], (LRU_WIDTH,), 1.0, 4.0, ((0, 8),), jnp.float32),
        "decay_param": draw_decay_param(jax.random.fold_in(keys[18], 71), 0),
        "output_weight": scatter_about(keys[13], (LRU_WIDTH, D), (LRU_WIDTH // 8) ** -0.5, 0.3125, ((0, 8),), jnp.float32),
        "mlp_norm_gain": jnp.clip(1.0 + 0.1 * jax.random.normal(keys[14], (D,), jnp.float32), 0.5, 1.5),
        "gate_weight": scatter_about(keys[15], (D, FF), D ** -0.5, 0.125, ((0, 8),), jnp.float32),
        "up_weight": scatter_about(keys[16], (D, FF), D ** -0.5, 0.125, ((0, 8),), jnp.float32),
        "down_weight": scatter_about(keys[17], (FF, D), (FF // 2) ** -0.5, 0.109375, ((0, 8),), jnp.float32),
    }


@jax.custom_vjp
def low(v):
    return lax.optimization_barrier(v.astype(jnp.bfloat16)).astype(jnp.float32)

@jax.custom_vjp
def low_back(v):
    return v

def low_keep(v):
    return (low(v), None)

def low_pass(kept, grad):
    return (grad,)

def back_keep(v):
    return (v, None)

def back_low(kept, grad):
    return (low(grad),)
low.defvjp(low_keep, low_pass)
low_back.defvjp(back_keep, back_low)
epsilon = 1e-06
decay_scale = 8.0

def matmul(left, right):
    return jnp.dot(left, right, preferred_element_type=jnp.float32, precision=lax.Precision.HIGHEST)

def normalize(rows):
    return rows * lax.rsqrt(lax.optimization_barrier(jnp.mean(rows * rows, axis=-1, keepdims=True)) + epsilon)

def recurrence(decay, driven):

    def advance(state, inputs):
        step_decay, step_drive = inputs
        state = step_decay * state + step_drive
        return (state, state)
    first = jnp.zeros((decay.shape[0], decay.shape[2]), jnp.float32)
    _, states = lax.scan(jax.checkpoint(advance), first, (jnp.swapaxes(decay, 0, 1), jnp.swapaxes(driven, 0, 1)))
    return jnp.swapaxes(states, 0, 1)

def block_product(values, weights, group, length):
    blocks = values.reshape(group, length, BLOCKS, -1)
    mixed = jnp.einsum('gthi,hij->gthj', blocks, weights, precision=lax.Precision.HIGHEST)
    return mixed.reshape(group, length, -1)

def forward(params, tokens, segments):
    norm_gain, branch_weight, input_weight, conv_weight, conv_bias, recur_weight, recur_bias, inject_weight, inject_bias, decay_param, output_weight, mlp_gain, gate_weight, up_weight, down_weight = [low(item) for item in params]
    group, length = segments.shape
    rows = tokens.reshape(group * length, -1)
    normed = low(normalize(rows) * norm_gain)
    branch = jax.nn.gelu(low_back(matmul(normed, branch_weight)))
    conv_in = low(low_back(matmul(normed, input_weight))).reshape(group, length, -1)
    labels = segments + 1
    lead = CONV - 1
    padded = jnp.pad(conv_in, ((0, 0), (lead, 0), (0, 0)))
    labels_pad = jnp.pad(labels, ((0, 0), (lead, 0)))
    conv_out = jnp.zeros_like(conv_in) + conv_bias
    for offset in range(CONV):
        same = (labels_pad[:, lead - offset:lead - offset + length] == labels).astype(jnp.float32)[..., None]
        conv_out = conv_out + conv_weight[offset] * padded[:, lead - offset:lead - offset + length] * same
    values = low(conv_out)
    recur_gate = jax.nn.sigmoid(low_back(block_product(values, recur_weight, group, length) + recur_bias))
    inject_gate = jax.nn.sigmoid(low_back(block_product(values, inject_weight, group, length) + inject_bias))
    starts = (labels != labels_pad[:, lead - 1:lead - 1 + length])[..., None]
    log_decay = -decay_scale * jax.nn.softplus(-decay_param) * recur_gate
    decay = jnp.where(starts, 0.0, jnp.exp(log_decay))
    scale = jnp.where(starts, 1.0, jnp.sqrt(-jnp.expm1(2.0 * log_decay)))
    states = recurrence(decay, scale * inject_gate * values)
    product = low(branch * states.reshape(group * length, -1))
    middle = rows + low_back(matmul(product, output_weight))
    normed_two = low(normalize(middle) * mlp_gain)
    gate_pre = low_back(matmul(normed_two, gate_weight))
    up_pre = low_back(matmul(normed_two, up_weight))
    hidden = low(jax.nn.gelu(gate_pre) * up_pre)
    block_out = middle + low_back(matmul(hidden, down_weight))
    return block_out.reshape(group, length, -1)

def reference(tokens, segments, cotangent, norm_gain, branch_weight, input_weight, conv_weight, conv_bias, recur_gate_weight, recur_gate_bias, input_gate_weight, input_gate_bias, decay_param, output_weight, mlp_norm_gain, gate_weight, up_weight, down_weight):
    params = (norm_gain, branch_weight, input_weight, conv_weight, conv_bias, recur_gate_weight, recur_gate_bias, input_gate_weight, input_gate_bias, decay_param, output_weight, mlp_norm_gain, gate_weight, up_weight, down_weight)
    group = math.gcd(SEQS, max(1, 4096 // LENGTH))
    rounds = SEQS // group
    tok_groups = tokens.astype(jnp.float32).reshape(rounds, group, LENGTH, D)
    seg_groups = segments.reshape(rounds, group, LENGTH)
    cot_groups = cotangent.astype(jnp.float32).reshape(rounds, group, LENGTH, D)

    def one_group(totals, inputs):
        tok_group, seg_group, cot_group = inputs

        def apply(weights, inputs_now):
            return forward(weights, inputs_now, seg_group)
        outputs, pullback = jax.vjp(apply, params, tok_group)
        weight_grads, input_grads = pullback(cot_group)
        totals = jax.tree.map(lambda first, second: first + second, totals, weight_grads)
        return (totals, (outputs.astype(jnp.bfloat16), input_grads.astype(jnp.bfloat16)))
    start_totals = tuple((jnp.zeros(item.shape, jnp.float32) for item in params))
    totals, (outputs, input_grads) = lax.scan(one_group, start_totals, (tok_groups, seg_groups, cot_groups))
    return (outputs.reshape(SEQS, LENGTH, D), input_grads.reshape(SEQS, LENGTH, D), totals[0], totals[1], totals[2], totals[3], totals[4], totals[5], totals[6], totals[7], totals[8], totals[9], totals[10], totals[11], totals[12], totals[13], totals[14])
```

```python
import jax
import jax.numpy as jnp
from jax import lax
from jax.sharding import PartitionSpec as P

epsilon = 1e-06
decay_scale = 8.0
GROUP = ("seq", "shard")
ROWS = ("shard", "seq")
f32 = jnp.float32
bf16 = jnp.bfloat16


def link(earlier, later):
    return (earlier[0] * later[0], earlier[1] * later[0] + later[1])


def mm(left, right):
    return jnp.dot(left, right, preferred_element_type=f32)


def mm_nt(left, right):
    return lax.dot_general(left, right, (((1,), (1,)), ((), ())), preferred_element_type=f32)


def mm_tn(left, right):
    return lax.dot_general(left, right, (((0,), (0,)), ((), ())), preferred_element_type=f32)


def gather_rows(part):
    return lax.all_gather(part, ROWS, axis=0, tiled=True)


def scatter_rows(partial):
    return lax.psum_scatter(
        partial.astype(bf16), ROWS, scatter_dimension=0, tiled=True
    ).astype(f32)


def to_columns(weight):
    return lax.all_to_all(weight.astype(bf16), GROUP, split_axis=1, concat_axis=0, tiled=True)


def reduce_rows(grad):
    return lax.psum(grad.astype(bf16), "replica").astype(f32)


def reduce_columns(grad):
    owners = lax.axis_size(GROUP)
    copies = lax.axis_size("replica")
    depth, width = grad.shape
    piece = depth // (owners * copies)
    cut = grad.astype(bf16).reshape(owners, copies, piece, width)
    cut = jnp.swapaxes(cut, 0, 1).reshape(depth, width)
    cut = lax.psum_scatter(cut, "replica", scatter_dimension=0, tiled=True)
    cut = lax.all_to_all(cut, GROUP, split_axis=0, concat_axis=1, tiled=True)
    return lax.all_gather(cut, "replica", axis=0, tiled=True).astype(f32)


def norm_backward(grad_unit, unit, inverse):
    return inverse * (grad_unit - unit * jnp.mean(grad_unit * unit, axis=-1, keepdims=True))


def shift_down(array, distance):
    if distance == 0:
        return array
    return jnp.pad(array, ((0, 0), (distance, 0), (0, 0)))[:, : array.shape[1]]


def shift_up(array, distance):
    if distance == 0:
        return array
    return jnp.pad(array, ((0, 0), (0, distance), (0, 0)))[:, distance:]


def body(
    tokens,
    segments,
    cotangent,
    norm_gain,
    branch_weight,
    input_weight,
    conv_weight,
    conv_bias,
    recur_gate_weight,
    recur_gate_bias,
    input_gate_weight,
    input_gate_bias,
    decay_param,
    output_weight,
    mlp_norm_gain,
    gate_weight,
    up_weight,
    down_weight,
):
    def low(item):
        return item.astype(bf16).astype(f32)

    gains = lax.all_gather(
        jnp.stack([norm_gain, mlp_norm_gain]).astype(bf16), GROUP, axis=1, tiled=True
    ).astype(f32)
    gain_f, mlp_gain_f = gains[0], gains[1]
    rows = tokens[0].astype(f32)
    count_rows = rows.shape[0]
    halves = lax.axis_size("seq")
    inverse = lax.rsqrt(jnp.mean(rows * rows, axis=-1, keepdims=True) + epsilon)
    unit = rows * inverse
    normed = (unit * gain_f).astype(bf16)
    normed_all = gather_rows(normed)
    branch_w = to_columns(branch_weight)
    input_w = to_columns(input_weight)
    labels = gather_rows(segments).reshape(-1, halves * count_rows) + 1
    out_low = gather_rows(cotangent[0])
    gate_w = to_columns(gate_weight)
    up_w = to_columns(up_weight)
    recur_w = recur_gate_weight.astype(bf16)
    inject_w = input_gate_weight.astype(bf16)
    output_w = output_weight.astype(bf16)
    down_w = down_weight.astype(bf16)
    total = normed_all.shape[0]
    sequences, length = labels.shape
    width = branch_w.shape[1]
    blocks_count = recur_w.shape[0]

    branch_pre = mm(normed_all, branch_w)
    branch_act, branch_pull = jax.vjp(jax.nn.gelu, branch_pre)
    conv_in = mm(normed_all, input_w).astype(bf16)
    conv_f = low(conv_weight)
    taps = conv_f.shape[0]
    shaped_in = conv_in.astype(f32).reshape(sequences, length, width)
    masks = []
    conv_out = jnp.zeros_like(shaped_in) + low(conv_bias)
    for offset in range(taps):
        earlier = jnp.pad(labels, ((0, 0), (offset, 0)))[:, :length]
        mask = (earlier == labels).astype(f32)[..., None]
        masks.append(mask)
        conv_out = conv_out + conv_f[offset] * shift_down(shaped_in, offset) * mask
    values = conv_out.astype(bf16).reshape(total, width)
    values_f = values.astype(f32)
    blocks = values.reshape(total, blocks_count, -1)
    recur_pre = jnp.einsum("thi,hij->thj", blocks, recur_w, preferred_element_type=f32)
    recur_gate = jax.nn.sigmoid(recur_pre.reshape(total, width) + low(recur_gate_bias))
    inject_pre = jnp.einsum("thi,hij->thj", blocks, inject_w, preferred_element_type=f32)
    inject_gate = jax.nn.sigmoid(inject_pre.reshape(total, width) + low(input_gate_bias))
    starts = (labels != jnp.pad(labels, ((0, 0), (1, 0)))[:, :length]).reshape(total, 1)
    decay_f = low(decay_param)
    rate = jax.nn.softplus(-decay_f)
    log_decay = -decay_scale * rate * recur_gate
    decay = jnp.where(starts, 0.0, jnp.exp(log_decay))
    scale = jnp.where(starts, 1.0, jnp.sqrt(-jnp.expm1(2.0 * log_decay)))
    driven = scale * inject_gate * values_f
    decay3 = decay.reshape(sequences, length, width)
    _, states3 = lax.associative_scan(
        link, (decay3, driven.reshape(sequences, length, width)), axis=1
    )
    states = states3.reshape(total, width)
    product = (branch_act * states).astype(bf16)
    middle = rows + scatter_rows(mm(product, output_w))
    inverse_two = lax.rsqrt(jnp.mean(middle * middle, axis=-1, keepdims=True) + epsilon)
    unit_two = middle * inverse_two
    normed_two = gather_rows((unit_two * mlp_gain_f).astype(bf16))
    gate_pre = mm(normed_two, gate_w)
    up_pre = mm(normed_two, up_w)
    gate_act, gate_pull = jax.vjp(jax.nn.gelu, gate_pre)
    hidden = (gate_act * up_pre).astype(bf16)
    block_out = (middle + scatter_rows(mm(hidden, down_w))).astype(bf16)

    grad_out = cotangent[0].astype(f32)
    hidden_grad = mm_nt(out_low, down_w)
    gate_low = gate_pull(hidden_grad * up_pre)[0].astype(bf16)
    up_low = (hidden_grad * gate_act).astype(bf16)
    down_weight_grad = reduce_rows(mm_tn(hidden, out_low))
    gate_weight_grad = reduce_columns(mm_tn(normed_two, gate_low))
    up_weight_grad = reduce_columns(mm_tn(normed_two, up_low))
    two_grad = scatter_rows(mm_nt(gate_low, gate_w) + mm_nt(up_low, up_w))
    mlp_gain_grad = jnp.sum(two_grad * unit_two, axis=0)
    middle_grad = grad_out + norm_backward(two_grad * mlp_gain_f, unit_two, inverse_two)
    mid_low = gather_rows(middle_grad.astype(bf16))
    output_weight_grad = reduce_rows(mm_tn(product, mid_low))
    product_grad = mm_nt(mid_low, output_w)
    branch_low = branch_pull(product_grad * states)[0].astype(bf16)
    states_grad = (product_grad * branch_act).reshape(sequences, length, width)
    _, adjoint3 = lax.associative_scan(
        link, (shift_up(decay3, 1)[:, ::-1], states_grad[:, ::-1]), axis=1
    )
    adjoint = adjoint3[:, ::-1].reshape(total, width)
    previous = shift_down(states3, 1).reshape(total, width)
    scale_grad = adjoint * inject_gate * values_f
    log_grad = jnp.where(
        starts, 0.0, adjoint * previous * decay - scale_grad * decay * decay / scale
    )
    decay_param_grad = jnp.sum(log_grad * decay_scale * recur_gate, axis=0) * jax.nn.sigmoid(
        -decay_f
    )
    recur_low = (log_grad * (-decay_scale * rate) * recur_gate * (1.0 - recur_gate)).astype(bf16)
    inject_low = (adjoint * scale * values_f * inject_gate * (1.0 - inject_gate)).astype(bf16)
    recur_bias_grad = jnp.sum(recur_low.astype(f32), axis=0)
    inject_bias_grad = jnp.sum(inject_low.astype(f32), axis=0)
    recur_blocks = recur_low.reshape(total, blocks_count, -1)
    inject_blocks = inject_low.reshape(total, blocks_count, -1)
    recur_weight_grad = jnp.einsum("thi,thj->hij", blocks, recur_blocks, preferred_element_type=f32)
    inject_weight_grad = jnp.einsum(
        "thi,thj->hij", blocks, inject_blocks, preferred_element_type=f32
    )
    values_grad = adjoint * scale * inject_gate
    values_grad = values_grad + jnp.einsum(
        "thj,hij->thi", recur_blocks, recur_w, preferred_element_type=f32
    ).reshape(total, width)
    values_grad = values_grad + jnp.einsum(
        "thj,hij->thi", inject_blocks, inject_w, preferred_element_type=f32
    ).reshape(total, width)
    conv_bias_grad = jnp.sum(values_grad, axis=0)
    shaped_grad = values_grad.reshape(sequences, length, width)
    tap_grads = []
    conv_in_grad = jnp.zeros_like(shaped_grad)
    for offset in range(taps):
        masked = shaped_grad * masks[offset]
        tap_grads.append(jnp.sum(masked * shift_down(shaped_in, offset), axis=(0, 1)))
        conv_in_grad = conv_in_grad + shift_up(masked * conv_f[offset], offset)
    conv_weight_grad = jnp.stack(tap_grads, 0)
    conv_low = conv_in_grad.reshape(total, width).astype(bf16)
    normed_grad = scatter_rows(mm_nt(branch_low, branch_w) + mm_nt(conv_low, input_w))
    gain_grad = jnp.sum(normed_grad * unit, axis=0)
    tokens_grad = (middle_grad + norm_backward(normed_grad * gain_f, unit, inverse)).astype(bf16)
    branch_weight_grad = reduce_columns(mm_tn(normed_all, branch_low))
    input_weight_grad = reduce_columns(mm_tn(normed_all, conv_low))
    gain_pair = lax.psum_scatter(
        jnp.stack([gain_grad, mlp_gain_grad]), GROUP, scatter_dimension=1, tiled=True
    )
    small = (
        gain_pair,
        conv_weight_grad,
        conv_bias_grad,
        recur_weight_grad,
        recur_bias_grad,
        inject_weight_grad,
        inject_bias_grad,
        decay_param_grad,
    )
    small = lax.psum(tuple(item.astype(bf16) for item in small), "replica")
    small = [item.astype(f32) for item in small]
    return (
        block_out[None],
        tokens_grad[None],
        small[0][0],
        branch_weight_grad,
        input_weight_grad,
        small[1],
        small[2],
        small[3],
        small[4],
        small[5],
        small[6],
        small[7],
        output_weight_grad,
        small[0][1],
        gate_weight_grad,
        up_weight_grad,
        down_weight_grad,
    )


def solution(mesh):
    row3 = P(("shard", "replica"), "seq", None)
    vec = P(("seq", "shard"))
    mat = P(("seq", "shard"), None)
    cube = P(("seq", "shard"), None, None)
    taps = P(None, ("seq", "shard"))
    params = (vec, mat, mat, taps, vec, cube, vec, cube, vec, vec, mat, vec, mat, mat, mat)
    in_specs = (row3, P(("shard", "replica"), "seq"), row3) + params
    out_specs = (row3, row3) + params
    return jax.shard_map(body, mesh=mesh, in_specs=in_specs, out_specs=out_specs, check_vma=False)
```

```python
import functools

import jax
import jax.numpy as jnp
from jax import lax
from jax.experimental import pallas as pl
from jax.experimental.pallas import tpu as pltpu
from jax.sharding import PartitionSpec as P

epsilon = 1e-06
decay_scale = 8.0
GROUP = ("seq", "shard")
ROWS = ("shard", "seq")
f32 = jnp.float32
bf16 = jnp.bfloat16
VM = pl.BlockSpec(memory_space=pltpu.VMEM)


def mm(left, right):
    return jnp.dot(left, right, preferred_element_type=f32)


def mm_nt(left, right):
    return lax.dot_general(left, right, (((1,), (1,)), ((), ())), preferred_element_type=f32)


def mm_tn(left, right):
    return lax.dot_general(left, right, (((0,), (0,)), ((), ())), preferred_element_type=f32)


def gather_rows(part):
    return lax.all_gather(part, ROWS, axis=0, tiled=True)


def scatter_rows(partial):
    return lax.psum_scatter(
        partial.astype(bf16), ROWS, scatter_dimension=0, tiled=True
    ).astype(f32)


def to_columns(weight):
    return lax.all_to_all(weight.astype(bf16), GROUP, split_axis=1, concat_axis=0, tiled=True)


def reduce_rows(grad):
    return lax.psum(grad.astype(bf16), "replica").astype(f32)


def reduce_columns(grad):
    owners = lax.axis_size(GROUP)
    copies = lax.axis_size("replica")
    depth, width = grad.shape
    piece = depth // (owners * copies)
    cut = grad.astype(bf16).reshape(owners, copies, piece, width)
    cut = jnp.swapaxes(cut, 0, 1).reshape(depth, width)
    cut = lax.psum_scatter(cut, "replica", scatter_dimension=0, tiled=True)
    cut = lax.all_to_all(cut, GROUP, split_axis=0, concat_axis=1, tiled=True)
    return lax.all_gather(cut, "replica", axis=0, tiled=True).astype(f32)


def norm_backward(grad_unit, unit, inverse):
    return inverse * (grad_unit - unit * jnp.mean(grad_unit * unit, axis=-1, keepdims=True))


def token_masks(labels, taps):
    length = labels.shape[1]
    masks = [
        (jnp.pad(labels, ((0, 0), (offset, 0)))[:, :length] == labels) for offset in range(taps)
    ]
    return jnp.stack(masks, -1).astype(f32).reshape(-1, taps)


def gelu_parts(x):
    inner = 0.7978845608028654 * (x + 0.044715 * x * x * x)
    t = jnp.tanh(inner)
    value = 0.5 * x * (1.0 + t)
    slope = 0.5 * (1.0 + t) + 0.5 * x * (1.0 - t * t) * 0.7978845608028654 * (
        1.0 + 3.0 * 0.044715 * x * x
    )
    return value, slope


def minus_expm1(y):
    poly = 1.0 + y * (1.0 / 8.0)
    for order in (7.0, 6.0, 5.0, 4.0, 3.0, 2.0):
        poly = 1.0 + y * (1.0 / order) * poly
    return jnp.where(y > -0.5, -y * poly, 1.0 - jnp.exp(y))


def dot_nn(a, b):
    return lax.dot_general(a, b, (((1,), (0,)), ((), ())), preferred_element_type=f32)


def dot_nt(a, b):
    return lax.dot_general(a, b, (((1,), (1,)), ((), ())), preferred_element_type=f32)


def dot_tn(a, b):
    return lax.dot_general(a, b, (((0,), (0,)), ((), ())), preferred_element_type=f32)


def fill_blocks(target, source):
    target[...] = jnp.zeros_like(target)
    count, size = source.shape[0], source.shape[1]
    for h in range(count):
        target[h * size : (h + 1) * size, h * size : (h + 1) * size] = source[h].astype(bf16).astype(f32)


def put_tiles(ref, here, value):
    width = value.shape[1]
    for tile in range(ref.shape[0]):
        lanes = min(128, width - 128 * tile)
        ref[tile, here, 0:lanes] = value[:, 128 * tile : 128 * tile + lanes]


def get_tiles(ref, here, width):
    parts = [ref[tile, here, 0 : min(128, width - 128 * tile)] for tile in range(ref.shape[0])]
    return jnp.concatenate(parts, axis=1)


def clear_tail(ref, width):
    tail = ref.shape[0] * 128 - width
    if tail:
        ref[ref.shape[0] - 1, :, 128 - tail :] = jnp.zeros((ref.shape[1], tail), f32)


def seq_scan(decay_ref, value_ref, sequences, length, reverse):
    tiles = decay_ref.shape[0]
    unroll = 8

    def step(i, states):
        states = list(states)
        for j in range(unroll):
            at = i * unroll + j
            if reverse:
                at = length - 1 - at
            here = pl.ds(at, sequences, stride=length)
            for tile in range(tiles):
                value = value_ref[tile, here, :]
                decay = decay_ref[tile, here, :]
                if reverse:
                    new = value + states[tile]
                    value_ref[tile, here, :] = new
                    states[tile] = decay * new
                else:
                    states[tile] = value + decay * states[tile]
                    value_ref[tile, here, :] = states[tile]
        return tuple(states)

    lax.fori_loop(0, length // unroll, step, (jnp.zeros((sequences, 128), f32),) * tiles)


def mix_forward_kernel(
    sequences, length, n_ref, wb_ref, wi_ref, mask_ref, conv_ref, bias_ref, rw_ref, iw_ref, ow_ref,
    partial_ref, product_ref, pre_ref, conv_in_ref, values_ref, recur_ref, inject_ref, decay_ref, states_ref,
    pad, rbig, ibig,
):
    fill_blocks(rbig, rw_ref)
    fill_blocks(ibig, iw_ref)
    pad[0:8, :] = jnp.zeros((8, pad.shape[1]), f32)
    taps = conv_ref.shape[0]
    width = pad.shape[1]
    clear_tail(decay_ref, width)
    clear_tail(states_ref, width)

    def one(s, _):
        base = pl.multiple_of(s * length, length)
        here = pl.ds(base, length)
        rows = n_ref[here, :]
        pre_ref[here, :] = dot_nn(rows, wb_ref[...])
        conv_in = dot_nn(rows, wi_ref[...]).astype(bf16)
        conv_in_ref[here, :] = conv_in
        pad[8 : 8 + length, :] = conv_in.astype(f32)
        total = bias_ref[0:1, :] + conv_ref[0:1, :] * pad[8 : 8 + length, :]
        for k in range(1, taps):
            total = total + conv_ref[k : k + 1, :] * pad[8 - k : 8 - k + length, :] * mask_ref[here, k : k + 1]
        values = total.astype(bf16)
        values_ref[here, :] = values
        recur = jax.nn.sigmoid(dot_nn(values, rbig[...].astype(bf16)) + bias_ref[1:2, :])
        inject = jax.nn.sigmoid(dot_nn(values, ibig[...].astype(bf16)) + bias_ref[2:3, :])
        recur_ref[here, :] = recur
        inject_ref[here, :] = inject
        log_decay = -decay_scale * bias_ref[3:4, :] * recur
        inside = mask_ref[here, 1:2] > 0.5
        put_tiles(decay_ref, here, jnp.where(inside, jnp.exp(log_decay), 0.0))
        scale = jnp.where(inside, jnp.sqrt(minus_expm1(2.0 * log_decay)), 1.0)
        put_tiles(states_ref, here, scale * inject * values.astype(f32))
        return 0

    lax.fori_loop(0, sequences, one, 0)
    seq_scan(decay_ref, states_ref, sequences, length, False)

    def two(s, _):
        base = pl.multiple_of(s * length, length)
        here = pl.ds(base, length)
        act, _unused = gelu_parts(pre_ref[here, :])
        product = (act * get_tiles(states_ref, here, width)).astype(bf16)
        product_ref[here, :] = product
        partial_ref[here, :] = dot_nn(product, ow_ref[...]).astype(bf16)
        return 0

    lax.fori_loop(0, sequences, two, 0)


def mix_forward(sequences, normed, wb, wi, mask, conv, bias, rw, iw, ow):
    total, width = normed.shape[0], wb.shape[1]
    length = total // sequences
    depth = ow.shape[1]
    shape = jax.ShapeDtypeStruct
    like = lambda dt: shape((total, width), dt)
    tiled = shape((-(-width // 128), total, 128), f32)
    return pl.pallas_call(
        functools.partial(mix_forward_kernel, sequences, length),
        out_shape=(
            shape((total, depth), bf16), like(bf16), like(f32), like(bf16), like(bf16), like(f32), like(f32), tiled, tiled,
        ),
        in_specs=[VM] * 9,
        out_specs=[VM] * 9,
        scratch_shapes=[
            pltpu.VMEM((8 + length, width), f32),
            pltpu.VMEM((width, width), f32),
            pltpu.VMEM((width, width), f32),
        ],
        compiler_params=pltpu.CompilerParams(vmem_limit_bytes=56 * 2**20),
        cost_estimate=pl.CostEstimate(flops=2 * total * width * 3 * depth, bytes_accessed=20 * 2**20, transcendentals=total * width * 5),
    )(normed, wb, wi, mask, conv, bias, rw, iw, ow)


def mix_backward_kernel(
    sequences, length, mid_ref, ow_ref, wb_ref, wi_ref, pre_ref, conv_in_ref, values_ref, recur_ref, inject_ref, decay_ref, states_ref,
    mask_ref, conv_ref, bias_ref, rw_ref, iw_ref,
    partial_ref, branch_low_ref, conv_low_ref, dconv_ref, sums_ref, drw_ref, diw_ref,
    adj, pad, rbig, ibig, dr, di,
):
    fill_blocks(rbig, rw_ref)
    fill_blocks(ibig, iw_ref)
    dr[...] = jnp.zeros_like(dr)
    di[...] = jnp.zeros_like(di)
    sums_ref[...] = jnp.zeros_like(sums_ref)
    dconv_ref[...] = jnp.zeros_like(dconv_ref)
    taps = conv_ref.shape[0]
    width = pad.shape[1]
    clear_tail(adj, width)

    def one(s, _):
        base = pl.multiple_of(s * length, length)
        here = pl.ds(base, length)
        product_grad = dot_nt(mid_ref[here, :], ow_ref[...])
        act, slope = gelu_parts(pre_ref[here, :])
        branch_low_ref[here, :] = (product_grad * get_tiles(states_ref, here, width) * slope).astype(bf16)
        put_tiles(adj, here, product_grad * act)
        return 0

    lax.fori_loop(0, sequences, one, 0)
    seq_scan(decay_ref, adj, sequences, length, True)

    def two(s, _):
        base = pl.multiple_of(s * length, length)
        here = pl.ds(base, length)
        adjoint = get_tiles(adj, here, width)
        recur = recur_ref[here, :]
        inject = inject_ref[here, :]
        decay = get_tiles(decay_ref, here, width)
        values = values_ref[here, :]
        values_f = values.astype(f32)
        inside = mask_ref[here, 1:2] > 0.5
        rate = bias_ref[3:4, :]
        log_decay = -decay_scale * rate * recur
        scale = jnp.where(inside, jnp.sqrt(minus_expm1(2.0 * log_decay)), 1.0)
        pad[0:8, :] = jnp.zeros((8, width), f32)
        pad[8 : 8 + length, :] = get_tiles(states_ref, here, width)
        previous = pad[7 : 7 + length, :]
        driven = adjoint * inject * values_f
        log_grad = jnp.where(inside, adjoint * previous * decay - driven * decay * decay / scale, 0.0)
        recur_low = (log_grad * (-decay_scale * rate) * recur * (1.0 - recur)).astype(bf16)
        inject_low = (driven * scale * (1.0 - inject)).astype(bf16)
        sums_ref[1:2, :] += jnp.sum(recur_low.astype(f32), axis=0, keepdims=True)
        sums_ref[2:3, :] += jnp.sum(inject_low.astype(f32), axis=0, keepdims=True)
        sums_ref[3:4, :] += jnp.sum(log_grad * recur, axis=0, keepdims=True)
        dr[...] += dot_tn(values, recur_low)
        di[...] += dot_tn(values, inject_low)
        grad = adjoint * scale * inject
        grad = grad + dot_nt(recur_low, rbig[...].astype(bf16)) + dot_nt(inject_low, ibig[...].astype(bf16))
        sums_ref[0:1, :] += jnp.sum(grad, axis=0, keepdims=True)
        pad[8 : 8 + length, :] = conv_in_ref[here, :].astype(f32)
        dconv_ref[0:1, :] += jnp.sum(grad * pad[8 : 8 + length, :], axis=0, keepdims=True)
        masked = []
        for k in range(1, taps):
            part = grad * mask_ref[here, k : k + 1]
            masked.append(part)
            dconv_ref[k : k + 1, :] += jnp.sum(part * pad[8 - k : 8 - k + length, :], axis=0, keepdims=True)
        total = grad * conv_ref[0:1, :]
        pad[length : length + 8, :] = jnp.zeros((8, width), f32)
        for k in range(1, taps):
            pad[0:length, :] = masked[k - 1] * conv_ref[k : k + 1, :]
            total = total + pad[k : k + length, :]
        conv_low = total.astype(bf16)
        conv_low_ref[here, :] = conv_low
        partial_ref[here, :] = (dot_nt(branch_low_ref[here, :], wb_ref[...]) + dot_nt(conv_low, wi_ref[...])).astype(bf16)
        return 0

    lax.fori_loop(0, sequences, two, 0)
    size = drw_ref.shape[1]
    for h in range(drw_ref.shape[0]):
        cut = slice(h * size, (h + 1) * size)
        drw_ref[h] = dr[cut, cut]
        diw_ref[h] = di[cut, cut]


def mix_backward(sequences, mid_low, ow, wb, wi, pre, conv_in, values, recur, inject, decay, states, mask, conv, bias, rw, iw):
    total, depth = mid_low.shape
    width = ow.shape[0]
    length = total // sequences
    shape = jax.ShapeDtypeStruct
    return pl.pallas_call(
        functools.partial(mix_backward_kernel, sequences, length),
        out_shape=(
            shape((total, depth), bf16), shape((total, width), bf16), shape((total, width), bf16),
            shape(conv.shape, f32), shape((4, width), f32), shape(rw.shape, f32), shape(iw.shape, f32),
        ),
        in_specs=[VM] * 16,
        out_specs=[VM] * 7,
        scratch_shapes=[
            pltpu.VMEM(states.shape, f32),
            pltpu.VMEM((8 + length, width), f32),
            pltpu.VMEM((width, width), f32),
            pltpu.VMEM((width, width), f32),
            pltpu.VMEM((width, width), f32),
            pltpu.VMEM((width, width), f32),
        ],
        compiler_params=pltpu.CompilerParams(vmem_limit_bytes=56 * 2**20),
        cost_estimate=pl.CostEstimate(flops=2 * total * width * 3 * depth, bytes_accessed=25 * 2**20, transcendentals=total * width * 5),
    )(mid_low, ow, wb, wi, pre, conv_in, values, recur, inject, decay, states, mask, conv, bias, rw, iw)


def body(
    tokens,
    segments,
    cotangent,
    norm_gain,
    branch_weight,
    input_weight,
    conv_weight,
    conv_bias,
    recur_gate_weight,
    recur_gate_bias,
    input_gate_weight,
    input_gate_bias,
    decay_param,
    output_weight,
    mlp_norm_gain,
    gate_weight,
    up_weight,
    down_weight,
):
    def low(item):
        return item.astype(bf16).astype(f32)

    gains = lax.all_gather(
        jnp.stack([norm_gain, mlp_norm_gain]).astype(bf16), GROUP, axis=1, tiled=True
    ).astype(f32)
    gain_f, mlp_gain_f = gains[0], gains[1]
    rows = tokens[0].astype(f32)
    count_rows = rows.shape[0]
    halves = lax.axis_size("seq")
    inverse = lax.rsqrt(jnp.mean(rows * rows, axis=-1, keepdims=True) + epsilon)
    unit = rows * inverse
    normed = (unit * gain_f).astype(bf16)
    normed_all = gather_rows(normed)
    branch_w = to_columns(branch_weight)
    input_w = to_columns(input_weight)
    labels = gather_rows(segments).reshape(-1, halves * count_rows) + 1
    out_low = gather_rows(cotangent[0])
    gate_w = to_columns(gate_weight)
    up_w = to_columns(up_weight)
    output_w = output_weight.astype(bf16)
    down_w = down_weight.astype(bf16)
    sequences = labels.shape[0]

    mask = token_masks(labels, conv_weight.shape[0])
    conv_f = low(conv_weight)
    decay_f = low(decay_param)
    bias = jnp.stack([low(conv_bias), low(recur_gate_bias), low(input_gate_bias), jax.nn.softplus(-decay_f)])
    mixed = mix_forward(
        sequences, normed_all, branch_w, input_w, mask, conv_f, bias, recur_gate_weight, input_gate_weight, output_w
    )
    partial, product = mixed[:2]
    middle = rows + scatter_rows(partial)
    inverse_two = lax.rsqrt(jnp.mean(middle * middle, axis=-1, keepdims=True) + epsilon)
    unit_two = middle * inverse_two
    normed_two = gather_rows((unit_two * mlp_gain_f).astype(bf16))
    gate_pre = mm(normed_two, gate_w)
    up_pre = mm(normed_two, up_w)
    gate_act, gate_pull = jax.vjp(jax.nn.gelu, gate_pre)
    hidden = (gate_act * up_pre).astype(bf16)
    block_out = (middle + scatter_rows(mm(hidden, down_w))).astype(bf16)

    grad_out = cotangent[0].astype(f32)
    hidden_grad = mm_nt(out_low, down_w)
    gate_low = gate_pull(hidden_grad * up_pre)[0].astype(bf16)
    up_low = (hidden_grad * gate_act).astype(bf16)
    down_weight_grad = reduce_rows(mm_tn(hidden, out_low))
    gate_weight_grad = reduce_columns(mm_tn(normed_two, gate_low))
    up_weight_grad = reduce_columns(mm_tn(normed_two, up_low))
    two_grad = scatter_rows(mm_nt(gate_low, gate_w) + mm_nt(up_low, up_w))
    mlp_gain_grad = jnp.sum(two_grad * unit_two, axis=0)
    middle_grad = grad_out + norm_backward(two_grad * mlp_gain_f, unit_two, inverse_two)
    mid_low = gather_rows(middle_grad.astype(bf16))
    output_weight_grad = reduce_rows(mm_tn(product, mid_low))
    back = mix_backward(
        sequences, mid_low, output_w, branch_w, input_w, *mixed[2:], mask, conv_f, bias, recur_gate_weight, input_gate_weight
    )
    partial, branch_low, conv_low, conv_weight_grad, sums, recur_weight_grad, inject_weight_grad = back
    conv_bias_grad, recur_bias_grad, inject_bias_grad = sums[0], sums[1], sums[2]
    decay_param_grad = sums[3] * decay_scale * jax.nn.sigmoid(-decay_f)
    normed_grad = scatter_rows(partial)
    gain_grad = jnp.sum(normed_grad * unit, axis=0)
    tokens_grad = (middle_grad + norm_backward(normed_grad * gain_f, unit, inverse)).astype(bf16)
    branch_weight_grad = reduce_columns(mm_tn(normed_all, branch_low))
    input_weight_grad = reduce_columns(mm_tn(normed_all, conv_low))
    gain_pair = lax.psum_scatter(
        jnp.stack([gain_grad, mlp_gain_grad]), GROUP, scatter_dimension=1, tiled=True
    )
    small = (
        gain_pair,
        conv_weight_grad,
        conv_bias_grad,
        recur_weight_grad,
        recur_bias_grad,
        inject_weight_grad,
        inject_bias_grad,
        decay_param_grad,
    )
    small = lax.psum(tuple(item.astype(bf16) for item in small), "replica")
    small = [item.astype(f32) for item in small]
    return (
        block_out[None],
        tokens_grad[None],
        small[0][0],
        branch_weight_grad,
        input_weight_grad,
        small[1],
        small[2],
        small[3],
        small[4],
        small[5],
        small[6],
        small[7],
        output_weight_grad,
        small[0][1],
        gate_weight_grad,
        up_weight_grad,
        down_weight_grad,
    )


def solution(mesh):
    row3 = P(("shard", "replica"), "seq", None)
    vec = P(("seq", "shard"))
    mat = P(("seq", "shard"), None)
    cube = P(("seq", "shard"), None, None)
    taps = P(None, ("seq", "shard"))
    params = (vec, mat, mat, taps, vec, cube, vec, cube, vec, vec, mat, vec, mat, mat, mat)
    in_specs = (row3, P(("shard", "replica"), "seq"), row3) + params
    out_specs = (row3, row3) + params
    return jax.shard_map(body, mesh=mesh, in_specs=in_specs, out_specs=out_specs, check_vma=False)
```

```python
import functools

import jax
import jax.numpy as jnp
from jax import lax
from jax.experimental import pallas as pl
from jax.experimental.pallas import tpu as pltpu
from jax.sharding import PartitionSpec as P

epsilon = 1e-06
decay_scale = 8.0
GROUP = ("seq", "shard")
ROWS = ("shard", "seq")
f32 = jnp.float32
bf16 = jnp.bfloat16
VM = pl.BlockSpec(memory_space=pltpu.VMEM)
ANY = pl.BlockSpec(memory_space=pl.ANY)
MESH = pl.DeviceIdType.MESH


def mm(left, right):
    return jnp.dot(left, right, preferred_element_type=f32)


def mm_nt(left, right):
    return lax.dot_general(left, right, (((1,), (1,)), ((), ())), preferred_element_type=f32)


def mm_tn(left, right):
    return lax.dot_general(left, right, (((0,), (0,)), ((), ())), preferred_element_type=f32)


def gather_rows(part):
    return lax.all_gather(part, ROWS, axis=0, tiled=True)


def scatter_rows(partial):
    return lax.psum_scatter(
        partial.astype(bf16), ROWS, scatter_dimension=0, tiled=True
    ).astype(f32)


def to_columns(weight):
    return lax.all_to_all(weight.astype(bf16), GROUP, split_axis=1, concat_axis=0, tiled=True)


def swap_columns(grad):
    owners = lax.axis_size(GROUP)
    cut = grad.astype(bf16).reshape(owners, grad.shape[0] // owners, grad.shape[1])
    return lax.all_to_all(cut, GROUP, split_axis=0, concat_axis=0, tiled=True)


def side_by_side(cut):
    return jnp.swapaxes(cut, 0, 1).reshape(1, cut.shape[1], -1)


def norm_backward(grad_unit, unit, inverse):
    return inverse * (grad_unit - unit * jnp.mean(grad_unit * unit, axis=-1, keepdims=True))


def token_masks(labels, taps):
    length = labels.shape[1]
    masks = [
        (jnp.pad(labels, ((0, 0), (offset, 0)))[:, :length] == labels) for offset in range(taps)
    ]
    return jnp.stack(masks, -1).astype(f32).reshape(-1, taps)


def gelu_parts(x):
    inner = 0.7978845608028654 * (x + 0.044715 * x * x * x)
    t = jnp.tanh(inner)
    value = 0.5 * x * (1.0 + t)
    slope = 0.5 * (1.0 + t) + 0.5 * x * (1.0 - t * t) * 0.7978845608028654 * (
        1.0 + 3.0 * 0.044715 * x * x
    )
    return value, slope


def minus_expm1(y):
    poly = 1.0 + y * (1.0 / 8.0)
    for order in (7.0, 6.0, 5.0, 4.0, 3.0, 2.0):
        poly = 1.0 + y * (1.0 / order) * poly
    return jnp.where(y > -0.5, -y * poly, 1.0 - jnp.exp(y))


def dot_nn(a, b):
    return lax.dot_general(a, b, (((1,), (0,)), ((), ())), preferred_element_type=f32)


def dot_nt(a, b):
    return lax.dot_general(a, b, (((1,), (1,)), ((), ())), preferred_element_type=f32)


def dot_tn(a, b):
    return lax.dot_general(a, b, (((0,), (0,)), ((), ())), preferred_element_type=f32)


def fill_blocks(target, source):
    target[...] = jnp.zeros_like(target)
    count, size = source.shape[0], source.shape[1]
    for h in range(count):
        target[h * size : (h + 1) * size, h * size : (h + 1) * size] = source[h].astype(bf16).astype(f32)


def put_tiles(ref, here, value):
    width = value.shape[1]
    for tile in range(ref.shape[0]):
        lanes = min(128, width - 128 * tile)
        ref[tile, here, 0:lanes] = value[:, 128 * tile : 128 * tile + lanes]


def get_tiles(ref, here, width):
    parts = [ref[tile, here, 0 : min(128, width - 128 * tile)] for tile in range(ref.shape[0])]
    return jnp.concatenate(parts, axis=1)


def clear_tail(ref, width):
    tail = ref.shape[0] * 128 - width
    if tail:
        ref[ref.shape[0] - 1, :, 128 - tail :] = jnp.zeros((ref.shape[1], tail), f32)


def seq_scan(decay_ref, value_ref, sequences, length, reverse):
    tiles = decay_ref.shape[0]
    unroll = 8

    def step(i, states):
        states = list(states)
        for j in range(unroll):
            at = i * unroll + j
            if reverse:
                at = length - 1 - at
            here = pl.ds(at, sequences, stride=length)
            for tile in range(tiles):
                value = value_ref[tile, here, :]
                decay = decay_ref[tile, here, :]
                if reverse:
                    new = value + states[tile]
                    value_ref[tile, here, :] = new
                    states[tile] = decay * new
                else:
                    states[tile] = value + decay * states[tile]
                    value_ref[tile, here, :] = states[tile]
        return tuple(states)

    lax.fori_loop(0, length // unroll, step, (jnp.zeros((sequences, 128), f32),) * tiles)


def mix_forward_kernel(
    sequences, length, n_ref, wb_ref, wi_ref, mask_ref, conv_ref, bias_ref, rw_ref, iw_ref, ow_ref,
    partial_ref, product_ref, pre_ref, conv_in_ref, values_ref, recur_ref, inject_ref, decay_ref, states_ref,
    pad, rbig, ibig,
):
    fill_blocks(rbig, rw_ref)
    fill_blocks(ibig, iw_ref)
    pad[0:8, :] = jnp.zeros((8, pad.shape[1]), f32)
    taps = conv_ref.shape[0]
    width = pad.shape[1]
    clear_tail(decay_ref, width)
    clear_tail(states_ref, width)

    def one(s, _):
        base = pl.multiple_of(s * length, length)
        here = pl.ds(base, length)
        rows = n_ref[here, :]
        pre_ref[here, :] = dot_nn(rows, wb_ref[...])
        conv_in = dot_nn(rows, wi_ref[...]).astype(bf16)
        conv_in_ref[here, :] = conv_in
        pad[8 : 8 + length, :] = conv_in.astype(f32)
        total = bias_ref[0:1, :] + conv_ref[0:1, :] * pad[8 : 8 + length, :]
        for k in range(1, taps):
            total = total + conv_ref[k : k + 1, :] * pad[8 - k : 8 - k + length, :] * mask_ref[here, k : k + 1]
        values = total.astype(bf16)
        values_ref[here, :] = values
        recur = jax.nn.sigmoid(dot_nn(values, rbig[...].astype(bf16)) + bias_ref[1:2, :])
        inject = jax.nn.sigmoid(dot_nn(values, ibig[...].astype(bf16)) + bias_ref[2:3, :])
        recur_ref[here, :] = recur
        inject_ref[here, :] = inject
        log_decay = -decay_scale * bias_ref[3:4, :] * recur
        inside = mask_ref[here, 1:2] > 0.5
        put_tiles(decay_ref, here, jnp.where(inside, jnp.exp(log_decay), 0.0))
        scale = jnp.where(inside, jnp.sqrt(minus_expm1(2.0 * log_decay)), 1.0)
        put_tiles(states_ref, here, scale * inject * values.astype(f32))
        return 0

    lax.fori_loop(0, sequences, one, 0)
    seq_scan(decay_ref, states_ref, sequences, length, False)

    def two(s, _):
        base = pl.multiple_of(s * length, length)
        here = pl.ds(base, length)
        act, _unused = gelu_parts(pre_ref[here, :])
        product = (act * get_tiles(states_ref, here, width)).astype(bf16)
        product_ref[here, :] = product
        partial_ref[here, :] = dot_nn(product, ow_ref[...]).astype(bf16)
        return 0

    lax.fori_loop(0, sequences, two, 0)


def mix_forward(sequences, normed, wb, wi, mask, conv, bias, rw, iw, ow):
    total, width = normed.shape[0], wb.shape[1]
    length = total // sequences
    depth = ow.shape[1]
    shape = jax.ShapeDtypeStruct
    like = lambda dt: shape((total, width), dt)
    tiled = shape((-(-width // 128), total, 128), f32)
    return pl.pallas_call(
        functools.partial(mix_forward_kernel, sequences, length),
        out_shape=(
            shape((total, depth), bf16), like(bf16), like(f32), like(bf16), like(bf16), like(f32), like(f32), tiled, tiled,
        ),
        in_specs=[VM] * 9,
        out_specs=[VM] * 9,
        scratch_shapes=[
            pltpu.VMEM((8 + length, width), f32),
            pltpu.VMEM((width, width), f32),
            pltpu.VMEM((width, width), f32),
        ],
        compiler_params=pltpu.CompilerParams(vmem_limit_bytes=56 * 2**20),
        cost_estimate=pl.CostEstimate(flops=2 * total * width * 3 * depth, bytes_accessed=20 * 2**20, transcendentals=total * width * 5),
    )(normed, wb, wi, mask, conv, bias, rw, iw, ow)


def mix_backward_kernel(
    sequences, length, mid_ref, ow_ref, wb_ref, wi_ref, pre_ref, conv_in_ref, values_ref, recur_ref, inject_ref, decay_ref, states_ref,
    mask_ref, conv_ref, bias_ref, rw_ref, iw_ref,
    partial_ref, branch_low_ref, conv_low_ref, dconv_ref, sums_ref, drw_ref, diw_ref,
    adj, pad, rbig, ibig, dr, di,
):
    fill_blocks(rbig, rw_ref)
    fill_blocks(ibig, iw_ref)
    dr[...] = jnp.zeros_like(dr)
    di[...] = jnp.zeros_like(di)
    sums_ref[...] = jnp.zeros_like(sums_ref)
    dconv_ref[...] = jnp.zeros_like(dconv_ref)
    taps = conv_ref.shape[0]
    width = pad.shape[1]
    clear_tail(adj, width)

    def one(s, _):
        base = pl.multiple_of(s * length, length)
        here = pl.ds(base, length)
        product_grad = dot_nt(mid_ref[here, :], ow_ref[...])
        act, slope = gelu_parts(pre_ref[here, :])
        branch_low_ref[here, :] = (product_grad * get_tiles(states_ref, here, width) * slope).astype(bf16)
        put_tiles(adj, here, product_grad * act)
        return 0

    lax.fori_loop(0, sequences, one, 0)
    seq_scan(decay_ref, adj, sequences, length, True)

    def two(s, _):
        base = pl.multiple_of(s * length, length)
        here = pl.ds(base, length)
        adjoint = get_tiles(adj, here, width)
        recur = recur_ref[here, :]
        inject = inject_ref[here, :]
        decay = get_tiles(decay_ref, here, width)
        values = values_ref[here, :]
        values_f = values.astype(f32)
        inside = mask_ref[here, 1:2] > 0.5
        rate = bias_ref[3:4, :]
        log_decay = -decay_scale * rate * recur
        scale = jnp.where(inside, jnp.sqrt(minus_expm1(2.0 * log_decay)), 1.0)
        pad[0:8, :] = jnp.zeros((8, width), f32)
        pad[8 : 8 + length, :] = get_tiles(states_ref, here, width)
        previous = pad[7 : 7 + length, :]
        driven = adjoint * inject * values_f
        log_grad = jnp.where(inside, adjoint * previous * decay - driven * decay * decay / scale, 0.0)
        recur_low = (log_grad * (-decay_scale * rate) * recur * (1.0 - recur)).astype(bf16)
        inject_low = (driven * scale * (1.0 - inject)).astype(bf16)
        sums_ref[1:2, :] += jnp.sum(recur_low.astype(f32), axis=0, keepdims=True)
        sums_ref[2:3, :] += jnp.sum(inject_low.astype(f32), axis=0, keepdims=True)
        sums_ref[3:4, :] += jnp.sum(log_grad * recur, axis=0, keepdims=True)
        dr[...] += dot_tn(values, recur_low)
        di[...] += dot_tn(values, inject_low)
        grad = adjoint * scale * inject
        grad = grad + dot_nt(recur_low, rbig[...].astype(bf16)) + dot_nt(inject_low, ibig[...].astype(bf16))
        sums_ref[0:1, :] += jnp.sum(grad, axis=0, keepdims=True)
        pad[8 : 8 + length, :] = conv_in_ref[here, :].astype(f32)
        dconv_ref[0:1, :] += jnp.sum(grad * pad[8 : 8 + length, :], axis=0, keepdims=True)
        masked = []
        for k in range(1, taps):
            part = grad * mask_ref[here, k : k + 1]
            masked.append(part)
            dconv_ref[k : k + 1, :] += jnp.sum(part * pad[8 - k : 8 - k + length, :], axis=0, keepdims=True)
        total = grad * conv_ref[0:1, :]
        pad[length : length + 8, :] = jnp.zeros((8, width), f32)
        for k in range(1, taps):
            pad[0:length, :] = masked[k - 1] * conv_ref[k : k + 1, :]
            total = total + pad[k : k + length, :]
        conv_low = total.astype(bf16)
        conv_low_ref[here, :] = conv_low
        partial_ref[here, :] = (dot_nt(branch_low_ref[here, :], wb_ref[...]) + dot_nt(conv_low, wi_ref[...])).astype(bf16)
        return 0

    lax.fori_loop(0, sequences, two, 0)
    size = drw_ref.shape[1]
    for h in range(drw_ref.shape[0]):
        cut = slice(h * size, (h + 1) * size)
        drw_ref[h] = dr[cut, cut]
        diw_ref[h] = di[cut, cut]


def mix_backward(sequences, mid_low, ow, wb, wi, pre, conv_in, values, recur, inject, decay, states, mask, conv, bias, rw, iw):
    total, depth = mid_low.shape
    width = ow.shape[0]
    length = total // sequences
    shape = jax.ShapeDtypeStruct
    return pl.pallas_call(
        functools.partial(mix_backward_kernel, sequences, length),
        out_shape=(
            shape((total, depth), bf16), shape((total, width), bf16), shape((total, width), bf16),
            shape(conv.shape, f32), shape((4, width), f32), shape(rw.shape, f32), shape(iw.shape, f32),
        ),
        in_specs=[VM] * 16,
        out_specs=[VM] * 7,
        scratch_shapes=[
            pltpu.VMEM(states.shape, f32),
            pltpu.VMEM((8 + length, width), f32),
            pltpu.VMEM((width, width), f32),
            pltpu.VMEM((width, width), f32),
            pltpu.VMEM((width, width), f32),
            pltpu.VMEM((width, width), f32),
        ],
        compiler_params=pltpu.CompilerParams(vmem_limit_bytes=56 * 2**20),
        cost_estimate=pl.CostEstimate(flops=2 * total * width * 3 * depth, bytes_accessed=25 * 2**20, transcendentals=total * width * 5),
    )(mid_low, ow, wb, wi, pre, conv_in, values, recur, inject, decay, states, mask, conv, bias, rw, iw)


def pieces(rows, most):
    count = -(-rows // most)
    while rows % count or (rows // count) % 16:
        count += 1
    return count


def line_kernel(n, cuts, paired, *refs):
    ins = len(cuts)
    own_hbm = refs[:ins]
    outs = refs[ins : ins + ins + 1]
    scratch = refs[ins + ins + 1 :]
    own, from_out, from_in = scratch[:ins], scratch[ins : 2 * ins], scratch[2 * ins : 3 * ins]
    stage, load_sem, stage_sem, sent_in, sent_out, got_out, got_in = scratch[3 * ins :]
    me = lax.axis_index("replica")
    left = me < n // 2
    inward = jnp.where(left, me + 1, me - 1)
    outward = jnp.where(left, me - 1, me + 1)
    has_out = jnp.logical_and(me > 0, me < n - 1)
    middle = jnp.logical_or(me == n // 2 - 1, me == n // 2)

    loads = [pltpu.make_async_copy(own_hbm[k], own[k], load_sem.at[k]) for k in range(ins)]
    for load in loads:
        load.start()
    barrier = pltpu.get_barrier_semaphore()
    pl.semaphore_signal(barrier, inc=1, device_id={"replica": inward}, device_id_type=MESH)

    @pl.when(has_out)
    def _():
        pl.semaphore_signal(barrier, inc=1, device_id={"replica": outward}, device_id_type=MESH)
        pl.semaphore_wait(barrier, 2)

    @pl.when(jnp.logical_not(has_out))
    def _():
        pl.semaphore_wait(barrier, 1)

    chunks = []
    for k, (lead, count, rows) in enumerate(cuts):
        for j in range(lead):
            for i in range(count):
                chunks.append((k, j, i * rows, rows))
    slots = stage.shape[0]
    ready = set()

    def view(group, c):
        k, j, start, rows = chunks[c]
        return group[k].at[j, pl.ds(start, rows), :]

    def push(group, target, c, sent, got, device):
        return pltpu.make_async_remote_copy(
            src_ref=view(group, c),
            dst_ref=view(target, c),
            send_sem=sent.at[c],
            recv_sem=got.at[c],
            device_id={"replica": device},
            device_id_type=MESH,
        )

    def add(target, other, c):
        k, j, start, rows = chunks[c]

        def tile(i, _):
            here = pl.ds(pl.multiple_of(start + i * 16, 16), 16)
            total = target[k][j, here, :].astype(f32) + other[k][j, here, :].astype(f32)
            target[k][j, here, :] = total.astype(bf16)
            return 0

        lax.fori_loop(0, rows // 16, tile, 0)

    def gather_in(c):
        k = chunks[c][0]
        if k not in ready:
            loads[k].wait()
            ready.add(k)

        @pl.when(has_out)
        def _():
            push(from_out, from_out, c, sent_in, got_out, inward).wait_recv()
            add(own, from_out, c)

        @pl.when(middle)
        def _():
            push(own, from_in, c, sent_in, got_in, inward).start()

        @pl.when(jnp.logical_not(middle))
        def _():
            push(own, from_out, c, sent_in, got_out, inward).start()

    def stage_copies(c):
        k, j, start, rows = chunks[c]
        slot = c % slots
        columns = own[k].shape[2]
        if k == paired:
            half = columns // 2
            return [
                pltpu.make_async_copy(
                    stage.at[slot, pl.ds(0, rows), pl.ds(side * half, half)],
                    outs[k + side].at[pl.ds(start, rows), pl.ds(j * half, half)],
                    stage_sem.at[slot, side],
                )
                for side in range(2)
            ]
        where = k if k < paired else k + 1
        return [
            pltpu.make_async_copy(
                stage.at[slot, pl.ds(0, rows), pl.ds(0, columns)],
                outs[where].at[pl.ds(start, rows), :],
                stage_sem.at[slot, 0],
            )
        ]

    def give_back(c):
        k, j, start, rows = chunks[c]
        push(own, from_in, c, sent_out, got_in, inward).wait_recv()

        @pl.when(middle)
        def _():
            add(from_in, own, c)

        @pl.when(has_out)
        def _():
            push(from_in, from_in, c, sent_out, got_in, outward).start()

        if c >= slots:
            for copy in stage_copies(c - slots):
                copy.wait()
        slot = c % slots
        columns = own[k].shape[2]

        def tile(i, _):
            step = pl.multiple_of(i * 16, 16)
            stage[slot, pl.ds(step, 16), 0:columns] = from_in[k][
                j, pl.ds(pl.multiple_of(start + step, 16), 16), :
            ].astype(f32)
            return 0

        lax.fori_loop(0, rows // 16, tile, 0)
        for copy in stage_copies(c):
            copy.start()

    lag = 2
    for c in range(len(chunks) + lag):
        if c < len(chunks):
            gather_in(c)
        if c >= lag:
            give_back(c - lag)
    for c in range(max(0, len(chunks) - slots), len(chunks)):
        for copy in stage_copies(c):
            copy.wait()
    for c in range(len(chunks)):
        push(own, from_in, c, sent_in, got_in, inward).wait_send()

        @pl.when(has_out)
        def _():
            push(from_in, from_in, c, sent_out, got_in, outward).wait_send()


def replica_sum(arrays, paired, copies):
    cuts, outs = [], []
    stage_rows = stage_columns = 0
    for k, item in enumerate(arrays):
        lead, rows, columns = item.shape
        count = pieces(rows, max(16, (210 * 1024) // columns // 16 * 16))
        cuts.append((lead, count, rows // count))
        stage_rows, stage_columns = max(stage_rows, rows // count), max(stage_columns, columns)
        if k == paired:
            outs += [jax.ShapeDtypeStruct((rows, lead * columns // 2), f32)] * 2
        else:
            outs.append(jax.ShapeDtypeStruct((rows, columns), f32))
    count = sum(lead * cut for lead, cut, _ in cuts)
    buffers = [pltpu.VMEM(item.shape, bf16) for item in arrays]
    return pl.pallas_call(
        functools.partial(line_kernel, copies, tuple(cuts), paired),
        out_shape=tuple(outs),
        in_specs=[ANY] * len(arrays),
        out_specs=[ANY] * len(outs),
        scratch_shapes=buffers * 3
        + [
            pltpu.VMEM((3, stage_rows, stage_columns), f32),
            pltpu.SemaphoreType.DMA((len(arrays),)),
            pltpu.SemaphoreType.DMA((3, 2)),
        ]
        + [pltpu.SemaphoreType.DMA((count,))] * 4,
        compiler_params=pltpu.CompilerParams(
            collective_id=7, has_side_effects=True, vmem_limit_bytes=60 * 2**20
        ),
    )(*arrays)


def body(
    tokens,
    segments,
    cotangent,
    norm_gain,
    branch_weight,
    input_weight,
    conv_weight,
    conv_bias,
    recur_gate_weight,
    recur_gate_bias,
    input_gate_weight,
    input_gate_bias,
    decay_param,
    output_weight,
    mlp_norm_gain,
    gate_weight,
    up_weight,
    down_weight,
):
    def low(item):
        return item.astype(bf16).astype(f32)

    gains = lax.all_gather(
        jnp.stack([norm_gain, mlp_norm_gain]).astype(bf16), GROUP, axis=1, tiled=True
    ).astype(f32)
    gain_f, mlp_gain_f = gains[0], gains[1]
    rows = tokens[0].astype(f32)
    count_rows = rows.shape[0]
    halves = lax.axis_size("seq")
    inverse = lax.rsqrt(jnp.mean(rows * rows, axis=-1, keepdims=True) + epsilon)
    unit = rows * inverse
    normed = (unit * gain_f).astype(bf16)
    normed_all = gather_rows(normed)
    branch_w = to_columns(branch_weight)
    input_w = to_columns(input_weight)
    labels = gather_rows(segments).reshape(-1, halves * count_rows) + 1
    out_low = gather_rows(cotangent[0])
    gate_w = to_columns(gate_weight)
    up_w = to_columns(up_weight)
    output_w = output_weight.astype(bf16)
    down_w = down_weight.astype(bf16)
    sequences = labels.shape[0]

    mask = token_masks(labels, conv_weight.shape[0])
    conv_f = low(conv_weight)
    decay_f = low(decay_param)
    bias = jnp.stack([low(conv_bias), low(recur_gate_bias), low(input_gate_bias), jax.nn.softplus(-decay_f)])
    mixed = mix_forward(
        sequences, normed_all, branch_w, input_w, mask, conv_f, bias, recur_gate_weight, input_gate_weight, output_w
    )
    partial, product = mixed[:2]
    middle = rows + scatter_rows(partial)
    inverse_two = lax.rsqrt(jnp.mean(middle * middle, axis=-1, keepdims=True) + epsilon)
    unit_two = middle * inverse_two
    normed_two = gather_rows((unit_two * mlp_gain_f).astype(bf16))
    gate_pre = mm(normed_two, gate_w)
    up_pre = mm(normed_two, up_w)
    gate_act, gate_pull = jax.vjp(jax.nn.gelu, gate_pre)
    hidden = (gate_act * up_pre).astype(bf16)
    block_out = (middle + scatter_rows(mm(hidden, down_w))).astype(bf16)

    grad_out = cotangent[0].astype(f32)
    hidden_grad = mm_nt(out_low, down_w)
    gate_low = gate_pull(hidden_grad * up_pre)[0].astype(bf16)
    up_low = (hidden_grad * gate_act).astype(bf16)
    down_partial = mm_tn(hidden, out_low).astype(bf16)[None]
    pair_partial = swap_columns(mm_tn(normed_two, jnp.concatenate([gate_low, up_low], 1)))
    two_grad = scatter_rows(mm_nt(gate_low, gate_w) + mm_nt(up_low, up_w))
    middle_grad = grad_out + norm_backward(two_grad * mlp_gain_f, unit_two, inverse_two)
    mid_low = gather_rows(middle_grad.astype(bf16))
    output_partial = mm_tn(product, mid_low).astype(bf16)[None]
    back = mix_backward(
        sequences, mid_low, output_w, branch_w, input_w, *mixed[2:], mask, conv_f, bias, recur_gate_weight, input_gate_weight
    )
    partial, branch_low, conv_low, conv_weight_grad, sums, recur_weight_grad, inject_weight_grad = back
    conv_bias_grad, recur_bias_grad, inject_bias_grad = sums[0], sums[1], sums[2]
    decay_param_grad = sums[3] * decay_scale * jax.nn.sigmoid(-decay_f)
    normed_grad = scatter_rows(partial)
    tokens_grad = (middle_grad + norm_backward(normed_grad * gain_f, unit, inverse)).astype(bf16)
    branch_partial = side_by_side(swap_columns(mm_tn(normed_all, branch_low)))
    input_partial = side_by_side(swap_columns(mm_tn(normed_all, conv_low)))
    down_weight_grad, gate_weight_grad, up_weight_grad, output_weight_grad, branch_weight_grad, input_weight_grad = (
        replica_sum(
            [down_partial, pair_partial, output_partial, branch_partial, input_partial], 1, lax.axis_size("replica")
        )
    )
    gain_grad = (
        jnp.sum(branch_weight_grad * low(branch_weight) + input_weight_grad * low(input_weight), axis=1) / low(norm_gain)
    )
    mlp_gain_grad = (
        jnp.sum(gate_weight_grad * low(gate_weight) + up_weight_grad * low(up_weight), axis=1) / low(mlp_norm_gain)
    )
    small = (
        conv_weight_grad,
        conv_bias_grad,
        recur_weight_grad,
        recur_bias_grad,
        inject_weight_grad,
        inject_bias_grad,
        decay_param_grad,
    )
    small = lax.psum(tuple(item.astype(bf16) for item in small), "replica")
    small = [item.astype(f32) for item in small]
    return (
        block_out[None],
        tokens_grad[None],
        gain_grad,
        branch_weight_grad,
        input_weight_grad,
        small[0],
        small[1],
        small[2],
        small[3],
        small[4],
        small[5],
        small[6],
        output_weight_grad,
        mlp_gain_grad,
        gate_weight_grad,
        up_weight_grad,
        down_weight_grad,
    )


def solution(mesh):
    row3 = P(("shard", "replica"), "seq", None)
    vec = P(("seq", "shard"))
    mat = P(("seq", "shard"), None)
    cube = P(("seq", "shard"), None, None)
    taps = P(None, ("seq", "shard"))
    params = (vec, mat, mat, taps, vec, cube, vec, cube, vec, vec, mat, vec, mat, mat, mat)
    in_specs = (row3, P(("shard", "replica"), "seq"), row3) + params
    out_specs = (row3, row3) + params
    return jax.shard_map(body, mesh=mesh, in_specs=in_specs, out_specs=out_specs, check_vma=False)
```

```python
import functools

import jax
import jax.numpy as jnp
from jax import lax
from jax.experimental import pallas as pl
from jax.experimental.pallas import tpu as pltpu
from jax.sharding import PartitionSpec as P

epsilon = 1e-06
decay_scale = 8.0
GROUP = ("seq", "shard")
ROWS = ("shard", "seq")
f32 = jnp.float32
bf16 = jnp.bfloat16
VM = pl.BlockSpec(memory_space=pltpu.VMEM)
ANY = pl.BlockSpec(memory_space=pl.ANY)
MESH = pl.DeviceIdType.MESH


def mm(left, right):
    return jnp.dot(left, right, preferred_element_type=f32)


def mm_nt(left, right):
    return lax.dot_general(left, right, (((1,), (1,)), ((), ())), preferred_element_type=f32)


def mm_tn(left, right):
    return lax.dot_general(left, right, (((0,), (0,)), ((), ())), preferred_element_type=f32)


def low(item):
    return item.astype(bf16).astype(f32)


def swap_columns(grad):
    owners = lax.axis_size(GROUP)
    cut = grad.astype(bf16).reshape(owners, grad.shape[0] // owners, grad.shape[1])
    return lax.all_to_all(cut, GROUP, split_axis=0, concat_axis=0, tiled=True)


def side_by_side(cut):
    return jnp.swapaxes(cut, 0, 1).reshape(1, cut.shape[1], -1)


def to_columns(weights, gain):
    owners = lax.axis_size(GROUP)
    rows = weights[0].shape[0]
    scaled = [(low(item) * gain).astype(bf16).reshape(rows, owners, -1) for item in weights]
    cut = jnp.swapaxes(jnp.concatenate(scaled, 2), 0, 1)
    return lax.all_to_all(cut, GROUP, split_axis=0, concat_axis=0, tiled=True).reshape(rows * owners, -1)


def gelu_parts(x):
    inner = 0.7978845608028654 * (x + 0.044715 * x * x * x)
    t = jnp.tanh(inner)
    value = 0.5 * x * (1.0 + t)
    slope = 0.5 * (1.0 + t) + 0.5 * x * (1.0 - t * t) * 0.7978845608028654 * (
        1.0 + 3.0 * 0.044715 * x * x
    )
    return value, slope


def minus_expm1(y):
    poly = 1.0 + y * (1.0 / 8.0)
    for order in (7.0, 6.0, 5.0, 4.0, 3.0, 2.0):
        poly = 1.0 + y * (1.0 / order) * poly
    return jnp.where(y > -0.5, -y * poly, 1.0 - jnp.exp(y))


def dot_nn(a, b):
    return lax.dot_general(a, b, (((1,), (0,)), ((), ())), preferred_element_type=f32)


def dot_nt(a, b):
    return lax.dot_general(a, b, (((1,), (1,)), ((), ())), preferred_element_type=f32)


def dot_tn(a, b):
    return lax.dot_general(a, b, (((0,), (0,)), ((), ())), preferred_element_type=f32)


def fill_blocks(target, source):
    target[...] = jnp.zeros_like(target)
    count, size = source.shape[0], source.shape[1]
    for h in range(count):
        target[h * size : (h + 1) * size, h * size : (h + 1) * size] = source[h].astype(bf16).astype(f32)


def put_tiles(ref, here, value):
    width = value.shape[1]
    for tile in range(ref.shape[0]):
        lanes = min(128, width - 128 * tile)
        ref[tile, here, 0:lanes] = value[:, 128 * tile : 128 * tile + lanes]


def get_tiles(ref, here, width):
    parts = [ref[tile, here, 0 : min(128, width - 128 * tile)] for tile in range(ref.shape[0])]
    return jnp.concatenate(parts, axis=1)


def clear_tail(ref, width):
    tail = ref.shape[0] * 128 - width
    if tail:
        ref[ref.shape[0] - 1, :, 128 - tail :] = jnp.zeros((ref.shape[1], tail), f32)


def label_masks(label_ref, here, length, width, taps, lines):
    own = label_ref[here, :].astype(f32)
    lines[0:8, :] = jnp.full((8, 128), -1.0, f32)
    lines[8 : 8 + length, :] = own
    masks = []
    for k in range(1, taps):
        same = jnp.where(lines[8 - k : 8 - k + length, :] == own, 1.0, 0.0)
        masks.append(jnp.concatenate([same] * -(-width // 128), axis=1)[:, :width])
    return masks


def seq_scan(decay_ref, value_ref, sequences, length, reverse):
    tiles = decay_ref.shape[0]
    unroll = 8

    def step(i, states):
        states = list(states)
        for j in range(unroll):
            at = i * unroll + j
            if reverse:
                at = length - 1 - at
            here = pl.ds(at, sequences, stride=length)
            for tile in range(tiles):
                value = value_ref[tile, here, :]
                decay = decay_ref[tile, here, :]
                if reverse:
                    new = value + states[tile]
                    value_ref[tile, here, :] = new
                    states[tile] = decay * new
                else:
                    states[tile] = value + decay * states[tile]
                    value_ref[tile, here, :] = states[tile]
        return tuple(states)

    lax.fori_loop(0, length // unroll, step, (jnp.zeros((sequences, 128), f32),) * tiles)


def mix_forward_kernel(
    sequences, length, n_ref, wb_ref, wi_ref, label_ref, conv_ref, bias_ref, rw_ref, iw_ref, ow_ref,
    partial_ref, product_ref, pre_ref, conv_in_ref, values_ref, recur_ref, inject_ref, decay_ref, states_ref,
    pad, lines, rbig, ibig,
):
    fill_blocks(rbig, rw_ref)
    fill_blocks(ibig, iw_ref)
    pad[0:8, :] = jnp.zeros((8, pad.shape[1]), f32)
    taps = conv_ref.shape[0]
    width = pad.shape[1]
    clear_tail(decay_ref, width)
    clear_tail(states_ref, width)

    def one(s, _):
        base = pl.multiple_of(s * length, length)
        here = pl.ds(base, length)
        rows = n_ref[here, :]
        masks = label_masks(label_ref, here, length, width, taps, lines)
        pre_ref[here, :] = dot_nn(rows, wb_ref[...])
        conv_in = dot_nn(rows, wi_ref[...]).astype(bf16)
        conv_in_ref[here, :] = conv_in
        pad[8 : 8 + length, :] = conv_in.astype(f32)
        total = bias_ref[0:1, :] + conv_ref[0:1, :] * pad[8 : 8 + length, :]
        for k in range(1, taps):
            total = total + conv_ref[k : k + 1, :] * pad[8 - k : 8 - k + length, :] * masks[k - 1]
        values = total.astype(bf16)
        values_ref[here, :] = values
        recur = jax.nn.sigmoid(dot_nn(values, rbig[...].astype(bf16)) + bias_ref[1:2, :])
        inject = jax.nn.sigmoid(dot_nn(values, ibig[...].astype(bf16)) + bias_ref[2:3, :])
        recur_ref[here, :] = recur
        inject_ref[here, :] = inject
        log_decay = -decay_scale * bias_ref[3:4, :] * recur
        inside = masks[0] > 0.5
        put_tiles(decay_ref, here, jnp.where(inside, jnp.exp(log_decay), 0.0))
        scale = jnp.where(inside, jnp.sqrt(minus_expm1(2.0 * log_decay)), 1.0)
        put_tiles(states_ref, here, scale * inject * values.astype(f32))
        return 0

    lax.fori_loop(0, sequences, one, 0)
    seq_scan(decay_ref, states_ref, sequences, length, False)

    def two(s, _):
        base = pl.multiple_of(s * length, length)
        here = pl.ds(base, length)
        act, _unused = gelu_parts(pre_ref[here, :])
        product = (act * get_tiles(states_ref, here, width)).astype(bf16)
        product_ref[here, :] = product
        partial_ref[here, :] = dot_nn(product, ow_ref[...]).astype(bf16)
        return 0

    lax.fori_loop(0, sequences, two, 0)


def mix_forward(sequences, normed, wb, wi, labels, conv, bias, rw, iw, ow):
    total, width = normed.shape[0], wb.shape[1]
    length = total // sequences
    depth = ow.shape[1]
    shape = jax.ShapeDtypeStruct
    like = lambda dt: shape((total, width), dt)
    tiled = shape((-(-width // 128), total, 128), f32)
    return pl.pallas_call(
        functools.partial(mix_forward_kernel, sequences, length),
        out_shape=(
            shape((total, depth), bf16), like(bf16), like(f32), like(bf16), like(bf16), like(f32), like(f32), tiled, tiled,
        ),
        in_specs=[VM] * 9,
        out_specs=[VM] * 9,
        scratch_shapes=[
            pltpu.VMEM((8 + length, width), f32),
            pltpu.VMEM((8 + length, 128), f32),
            pltpu.VMEM((width, width), f32),
            pltpu.VMEM((width, width), f32),
        ],
        compiler_params=pltpu.CompilerParams(vmem_limit_bytes=56 * 2**20),
        cost_estimate=pl.CostEstimate(flops=2 * total * width * 3 * depth, bytes_accessed=20 * 2**20, transcendentals=total * width * 5),
    )(normed, wb, wi, labels, conv, bias, rw, iw, ow)


def mix_backward_kernel(
    sequences, length, mid_ref, ow_ref, wb_ref, wi_ref, pre_ref, conv_in_ref, values_ref, recur_ref, inject_ref, decay_ref, states_ref,
    label_ref, conv_ref, bias_ref, rw_ref, iw_ref,
    partial_ref, branch_low_ref, conv_low_ref, dconv_ref, sums_ref, drw_ref, diw_ref,
    adj, pad, lines, rbig, ibig, dr, di,
):
    fill_blocks(rbig, rw_ref)
    fill_blocks(ibig, iw_ref)
    dr[...] = jnp.zeros_like(dr)
    di[...] = jnp.zeros_like(di)
    sums_ref[...] = jnp.zeros_like(sums_ref)
    dconv_ref[...] = jnp.zeros_like(dconv_ref)
    taps = conv_ref.shape[0]
    width = pad.shape[1]
    clear_tail(adj, width)

    def one(s, _):
        base = pl.multiple_of(s * length, length)
        here = pl.ds(base, length)
        product_grad = dot_nt(mid_ref[here, :], ow_ref[...])
        act, slope = gelu_parts(pre_ref[here, :])
        branch_low_ref[here, :] = (product_grad * get_tiles(states_ref, here, width) * slope).astype(bf16)
        put_tiles(adj, here, product_grad * act)
        return 0

    lax.fori_loop(0, sequences, one, 0)
    seq_scan(decay_ref, adj, sequences, length, True)

    def two(s, _):
        base = pl.multiple_of(s * length, length)
        here = pl.ds(base, length)
        adjoint = get_tiles(adj, here, width)
        recur = recur_ref[here, :]
        inject = inject_ref[here, :]
        decay = get_tiles(decay_ref, here, width)
        values = values_ref[here, :]
        values_f = values.astype(f32)
        masks = label_masks(label_ref, here, length, width, taps, lines)
        inside = masks[0] > 0.5
        rate = bias_ref[3:4, :]
        log_decay = -decay_scale * rate * recur
        scale = jnp.where(inside, jnp.sqrt(minus_expm1(2.0 * log_decay)), 1.0)
        pad[0:8, :] = jnp.zeros((8, width), f32)
        pad[8 : 8 + length, :] = get_tiles(states_ref, here, width)
        previous = pad[7 : 7 + length, :]
        driven = adjoint * inject * values_f
        log_grad = jnp.where(inside, adjoint * previous * decay - driven * decay * decay / scale, 0.0)
        recur_low = (log_grad * (-decay_scale * rate) * recur * (1.0 - recur)).astype(bf16)
        inject_low = (driven * scale * (1.0 - inject)).astype(bf16)
        sums_ref[1:2, :] += jnp.sum(recur_low.astype(f32), axis=0, keepdims=True)
        sums_ref[2:3, :] += jnp.sum(inject_low.astype(f32), axis=0, keepdims=True)
        sums_ref[3:4, :] += jnp.sum(log_grad * recur, axis=0, keepdims=True)
        dr[...] += dot_tn(values, recur_low)
        di[...] += dot_tn(values, inject_low)
        grad = adjoint * scale * inject
        grad = grad + dot_nt(recur_low, rbig[...].astype(bf16)) + dot_nt(inject_low, ibig[...].astype(bf16))
        sums_ref[0:1, :] += jnp.sum(grad, axis=0, keepdims=True)
        pad[8 : 8 + length, :] = conv_in_ref[here, :].astype(f32)
        dconv_ref[0:1, :] += jnp.sum(grad * pad[8 : 8 + length, :], axis=0, keepdims=True)
        masked = []
        for k in range(1, taps):
            part = grad * masks[k - 1]
            masked.append(part)
            dconv_ref[k : k + 1, :] += jnp.sum(part * pad[8 - k : 8 - k + length, :], axis=0, keepdims=True)
        total = grad * conv_ref[0:1, :]
        pad[length : length + 8, :] = jnp.zeros((8, width), f32)
        for k in range(1, taps):
            pad[0:length, :] = masked[k - 1] * conv_ref[k : k + 1, :]
            total = total + pad[k : k + length, :]
        conv_low = total.astype(bf16)
        conv_low_ref[here, :] = conv_low
        partial_ref[here, :] = (dot_nt(branch_low_ref[here, :], wb_ref[...]) + dot_nt(conv_low, wi_ref[...])).astype(bf16)
        return 0

    lax.fori_loop(0, sequences, two, 0)
    size = drw_ref.shape[1]
    for h in range(drw_ref.shape[0]):
        cut = slice(h * size, (h + 1) * size)
        drw_ref[h] = dr[cut, cut]
        diw_ref[h] = di[cut, cut]


def mix_backward(sequences, mid_low, ow, wb, wi, pre, conv_in, values, recur, inject, decay, states, labels, conv, bias, rw, iw):
    total, depth = mid_low.shape
    width = ow.shape[0]
    length = total // sequences
    shape = jax.ShapeDtypeStruct
    return pl.pallas_call(
        functools.partial(mix_backward_kernel, sequences, length),
        out_shape=(
            shape((total, depth), bf16), shape((total, width), bf16), shape((total, width), bf16),
            shape(conv.shape, f32), shape((4, width), f32), shape(rw.shape, f32), shape(iw.shape, f32),
        ),
        in_specs=[VM] * 16,
        out_specs=[VM] * 7,
        scratch_shapes=[
            pltpu.VMEM(states.shape, f32),
            pltpu.VMEM((8 + length, width), f32),
            pltpu.VMEM((8 + length, 128), f32),
            pltpu.VMEM((width, width), f32),
            pltpu.VMEM((width, width), f32),
            pltpu.VMEM((width, width), f32),
            pltpu.VMEM((width, width), f32),
        ],
        compiler_params=pltpu.CompilerParams(vmem_limit_bytes=56 * 2**20),
        cost_estimate=pl.CostEstimate(flops=2 * total * width * 3 * depth, bytes_accessed=25 * 2**20, transcendentals=total * width * 5),
    )(mid_low, ow, wb, wi, pre, conv_in, values, recur, inject, decay, states, labels, conv, bias, rw, iw)


def plane():
    halves, shards = lax.axis_size("seq"), lax.axis_size("shard")
    y, s = lax.axis_index("seq"), lax.axis_index("shard")
    offsets = [(dy, ds) for ds in range(0, shards, 2) for dy in range(halves)]

    def at(dy, ds):
        return {"seq": jnp.bitwise_xor(y, dy), "shard": jnp.bitwise_xor(s, ds)}

    def block(dy, ds):
        return jnp.bitwise_xor(s, ds) * halves + jnp.bitwise_xor(y, dy)

    return offsets, at, block


def greet(offsets, at):
    barrier = pltpu.get_barrier_semaphore()
    partners = [(0, 1)] + offsets[1:]
    for dy, ds in partners:
        pl.semaphore_signal(barrier, inc=1, device_id=at(dy, ds), device_id_type=MESH)
    pl.semaphore_wait(barrier, len(partners))


def remote(src, dst, sent, got, device):
    return pltpu.make_async_remote_copy(
        src_ref=src, dst_ref=dst, send_sem=sent, recv_sem=got, device_id=device, device_id_type=MESH
    )


def row_block(ref, index, rows):
    return ref.at[pl.ds(pl.multiple_of(index * rows, rows), rows), :]


def scatter_sum(rows, partial, near, far, stage, acc, sems):
    offsets, at, block = plane()
    near_sent, near_got, far_sent, far_got = sems
    count = len(offsets)
    order = list(range(count - 1, -1, -1))
    firsts = {}
    for q in order:
        dy, ds = offsets[q]
        firsts[q] = remote(
            row_block(partial, block(dy, ds ^ 1), rows), near.at[q], near_sent.at[q], near_got.at[q], at(0, 1)
        )
        firsts[q].start()
    seconds = {}
    for q in order:
        dy, ds = offsets[q]
        firsts[q].wait_recv()
        base = block(dy, ds) * rows

        def tile(i, _):
            step = pl.multiple_of(i * 16, 16)
            here = pl.ds(step, 16)
            total = partial[pl.ds(pl.multiple_of(base + step, 16), 16), :].astype(f32) + near[q, here, :].astype(f32)
            if q:
                stage[q - 1, here, :] = total.astype(bf16)
            else:
                acc[here, :] = total
            return 0

        lax.fori_loop(0, rows // 16, tile, 0)
        if q:
            seconds[q] = remote(stage.at[q - 1], far.at[q - 1], far_sent.at[q - 1], far_got.at[q - 1], at(dy, ds))
            seconds[q].start()
    for q in order[:-1]:
        seconds[q].wait_recv()

        def more(i, _):
            here = pl.ds(pl.multiple_of(i * 16, 16), 16)
            acc[here, :] += far[q - 1, here, :].astype(f32)
            return 0

        lax.fori_loop(0, rows // 16, more, 0)
    return [firsts[q].wait_send for q in order] + [seconds[q].wait_send for q in order[:-1]]


def gather_blocks(rows, whole, sems):
    offsets, at, block = plane()
    near_sent, near_got, far_sent, far_got = sems
    count = len(offsets)
    own = row_block(whole, block(0, 0), rows)
    sends = []
    outs = {}
    for q in range(count - 1, 0, -1):
        dy, ds = offsets[q]
        outs[q] = remote(own, own, far_sent.at[q - 1], far_got.at[q - 1], at(dy, ds))
        outs[q].start()
        sends.append(outs[q].wait_send)
    hand = remote(own, own, near_sent.at[0], near_got.at[0], at(0, 1))
    hand.start()
    sends.append(hand.wait_send)
    arrivals = [hand.wait_recv]
    for q in list(range(1, count)):
        dy, ds = offsets[q]
        outs[q].wait_recv()
        block_q = row_block(whole, block(dy, ds), rows)
        hand = remote(block_q, block_q, near_sent.at[q], near_got.at[q], at(0, 1))
        hand.start()
        sends.append(hand.wait_send)
        arrivals.append(hand.wait_recv)
    return arrivals + sends


def root_mean(rows):
    return lax.rsqrt(jnp.mean(rows * rows, axis=-1, keepdims=True) + epsilon)


def norm_backward(grad_unit, unit, inverse):
    return inverse * (grad_unit - unit * jnp.mean(grad_unit * unit, axis=-1, keepdims=True))


def by_tiles(rows, work):
    def tile(i, _):
        work(pl.ds(pl.multiple_of(i * 16, 16), 16), i)
        return 0

    lax.fori_loop(0, rows // 16, tile, 0)


def start_kernel(x_ref, label_ref, unit_ref, labels_ref, *sems):
    rows = x_ref.shape[0]
    offsets, at, block = plane()
    greet(offsets, at)
    base = block(0, 0) * rows

    def unit(here, i):
        value = x_ref[here, :].astype(f32)
        there = pl.ds(pl.multiple_of(base + i * 16, 16), 16)
        unit_ref[there, :] = (value * root_mean(value)).astype(bf16)
        labels_ref[there, :] = label_ref[here, :]

    by_tiles(rows, unit)
    waits = gather_blocks(rows, labels_ref, sems[4:])
    waits = waits + gather_blocks(rows, unit_ref, sems[:4])
    for wait in waits:
        wait()


def forward_kernel(partial, x_ref, unit_ref, middle_ref, near, far, stage, acc, *sems):
    rows = x_ref.shape[0]
    offsets, at, block = plane()
    greet(offsets, at)
    waits = scatter_sum(rows, partial, near, far, stage, acc, sems[:4])
    base = block(0, 0) * rows

    def norm(here, i):
        middle = x_ref[here, :].astype(f32) + acc[here, :]
        middle_ref[here, :] = middle
        there = pl.ds(pl.multiple_of(base + i * 16, 16), 16)
        unit_ref[there, :] = (middle * root_mean(middle)).astype(bf16)

    by_tiles(rows, norm)
    waits = waits + gather_blocks(rows, unit_ref, sems[4:])
    for wait in waits:
        wait()


def backward_kernel(partial, middle_ref, cot_ref, low_ref, grad_ref, near, far, stage, acc, *sems):
    rows = middle_ref.shape[0]
    offsets, at, block = plane()
    greet(offsets, at)
    waits = scatter_sum(rows, partial, near, far, stage, acc, sems[:4])
    base = block(0, 0) * rows

    def norm(here, i):
        middle = middle_ref[here, :]
        inverse = root_mean(middle)
        grad = cot_ref[here, :].astype(f32) + norm_backward(acc[here, :], middle * inverse, inverse)
        grad_ref[here, :] = grad
        there = pl.ds(pl.multiple_of(base + i * 16, 16), 16)
        low_ref[there, :] = grad.astype(bf16)

    by_tiles(rows, norm)
    waits = waits + gather_blocks(rows, low_ref, sems[4:])
    for wait in waits:
        wait()


def last_kernel(partial, grad_ref, x_ref, out_ref, near, far, stage, acc, *sems):
    rows = x_ref.shape[0]
    offsets, at, block = plane()
    greet(offsets, at)
    waits = scatter_sum(rows, partial, near, far, stage, acc, sems[:4])

    def norm(here, i):
        value = x_ref[here, :].astype(f32)
        inverse = root_mean(value)
        grad = grad_ref[here, :] + norm_backward(acc[here, :], value * inverse, inverse)
        out_ref[here, :] = grad.astype(bf16)

    by_tiles(rows, norm)
    for wait in waits:
        wait()


def exchange(kernel, identity, inputs, outs, rows, depth, gathers, scatters):
    count = lax.axis_size("seq") * lax.axis_size("shard") // 2
    block = (rows, depth)
    scratch = []
    if scatters:
        scratch = [
            pltpu.VMEM((count,) + block, bf16),
            pltpu.VMEM((count - 1,) + block, bf16),
            pltpu.VMEM((count - 1,) + block, bf16),
            pltpu.VMEM(block, f32),
        ]
    for _ in range(scatters + gathers):
        scratch += [pltpu.SemaphoreType.DMA((count,))] * 2 + [pltpu.SemaphoreType.DMA((count - 1,))] * 2
    return pl.pallas_call(
        kernel,
        out_shape=tuple(jax.ShapeDtypeStruct(shape, kind) for shape, kind in outs),
        in_specs=[VM] * len(inputs),
        out_specs=[VM] * len(outs),
        scratch_shapes=scratch,
        compiler_params=pltpu.CompilerParams(
            collective_id=identity, has_side_effects=True, vmem_limit_bytes=40 * 2**20
        ),
        cost_estimate=pl.CostEstimate(flops=10**6, bytes_accessed=60 * 2**20, transcendentals=0),
    )(*inputs)


def pieces(rows, most):
    count = -(-rows // most)
    while rows % count or (rows // count) % 16:
        count += 1
    return count


def line_kernel(n, cuts, paired, *refs):
    ins = len(cuts)
    own_hbm = refs[:ins]
    outs = refs[ins : ins + ins + 1]
    scratch = refs[ins + ins + 1 :]
    own, from_out, from_in = scratch[:ins], scratch[ins : 2 * ins], scratch[2 * ins : 3 * ins]
    stage, load_sem, stage_sem, sent_in, sent_out, got_out, got_in = scratch[3 * ins :]
    me = lax.axis_index("replica")
    left = me < n // 2
    inward = jnp.where(left, me + 1, me - 1)
    outward = jnp.where(left, me - 1, me + 1)
    has_out = jnp.logical_and(me > 0, me < n - 1)
    middle = jnp.logical_or(me == n // 2 - 1, me == n // 2)

    loads = [pltpu.make_async_copy(own_hbm[k], own[k], load_sem.at[k]) for k in range(ins)]
    for load in loads:
        load.start()
    barrier = pltpu.get_barrier_semaphore()
    pl.semaphore_signal(barrier, inc=1, device_id={"replica": inward}, device_id_type=MESH)

    @pl.when(has_out)
    def _():
        pl.semaphore_signal(barrier, inc=1, device_id={"replica": outward}, device_id_type=MESH)
        pl.semaphore_wait(barrier, 2)

    @pl.when(jnp.logical_not(has_out))
    def _():
        pl.semaphore_wait(barrier, 1)

    chunks = []
    for k, (lead, count, rows) in enumerate(cuts):
        for j in range(lead):
            for i in range(count):
                chunks.append((k, j, i * rows, rows))
    slots = stage.shape[0]
    ready = set()

    def view(group, c):
        k, j, start, rows = chunks[c]
        return group[k].at[j, pl.ds(start, rows), :]

    def push(group, target, c, sent, got, device):
        return pltpu.make_async_remote_copy(
            src_ref=view(group, c),
            dst_ref=view(target, c),
            send_sem=sent.at[c],
            recv_sem=got.at[c],
            device_id={"replica": device},
            device_id_type=MESH,
        )

    def add(target, other, c):
        k, j, start, rows = chunks[c]

        def tile(i, _):
            here = pl.ds(pl.multiple_of(start + i * 16, 16), 16)
            total = target[k][j, here, :].astype(f32) + other[k][j, here, :].astype(f32)
            target[k][j, here, :] = total.astype(bf16)
            return 0

        lax.fori_loop(0, rows // 16, tile, 0)

    def pass_in(c):
        @pl.when(middle)
        def _():
            push(own, from_in, c, sent_in, got_in, inward).start()

        @pl.when(jnp.logical_not(middle))
        def _():
            push(own, from_out, c, sent_in, got_out, inward).start()

    def gather_in(c):
        @pl.when(has_out)
        def _():
            if chunks[c][0] not in ready:
                loads[chunks[c][0]].wait()
                ready.add(chunks[c][0])
            push(from_out, from_out, c, sent_in, got_out, inward).wait_recv()
            add(own, from_out, c)
            pass_in(c)

    @pl.when(jnp.logical_not(has_out))
    def _():
        seen = set()
        for c in range(len(chunks)):
            if chunks[c][0] not in seen:
                loads[chunks[c][0]].wait()
                seen.add(chunks[c][0])
            pass_in(c)

    def stage_copies(c):
        k, j, start, rows = chunks[c]
        slot = c % slots
        columns = own[k].shape[2]
        if k == paired:
            half = columns // 2
            return [
                pltpu.make_async_copy(
                    stage.at[slot, pl.ds(0, rows), pl.ds(side * half, half)],
                    outs[k + side].at[pl.ds(start, rows), pl.ds(j * half, half)],
                    stage_sem.at[slot, side],
                )
                for side in range(2)
            ]
        where = k if k < paired else k + 1
        return [
            pltpu.make_async_copy(
                stage.at[slot, pl.ds(0, rows), pl.ds(0, columns)],
                outs[where].at[pl.ds(start, rows), :],
                stage_sem.at[slot, 0],
            )
        ]

    def give_back(c):
        k, j, start, rows = chunks[c]
        push(own, from_in, c, sent_out, got_in, inward).wait_recv()

        @pl.when(middle)
        def _():
            add(from_in, own, c)

        @pl.when(has_out)
        def _():
            push(from_in, from_in, c, sent_out, got_in, outward).start()

        if c >= slots:
            for copy in stage_copies(c - slots):
                copy.wait()
        slot = c % slots
        columns = own[k].shape[2]

        def tile(i, _):
            step = pl.multiple_of(i * 16, 16)
            stage[slot, pl.ds(step, 16), 0:columns] = from_in[k][
                j, pl.ds(pl.multiple_of(start + step, 16), 16), :
            ].astype(f32)
            return 0

        lax.fori_loop(0, rows // 16, tile, 0)
        for copy in stage_copies(c):
            copy.start()

    lag = 2
    for c in range(len(chunks) + lag):
        if c < len(chunks):
            gather_in(c)
        if c >= lag:
            give_back(c - lag)
    for c in range(max(0, len(chunks) - slots), len(chunks)):
        for copy in stage_copies(c):
            copy.wait()
    for c in range(len(chunks)):
        push(own, from_in, c, sent_in, got_in, inward).wait_send()

        @pl.when(has_out)
        def _():
            push(from_in, from_in, c, sent_out, got_in, outward).wait_send()


def replica_sum(arrays, paired, copies):
    cuts, outs = [], []
    stage_rows = stage_columns = 0
    for k, item in enumerate(arrays):
        lead, rows, columns = item.shape
        count = pieces(rows, max(16, (210 * 1024) // columns // 16 * 16))
        cuts.append((lead, count, rows // count))
        stage_rows, stage_columns = max(stage_rows, rows // count), max(stage_columns, columns)
        if k == paired:
            outs += [jax.ShapeDtypeStruct((rows, lead * columns // 2), f32)] * 2
        else:
            outs.append(jax.ShapeDtypeStruct((rows, columns), f32))
    count = sum(lead * cut for lead, cut, _ in cuts)
    buffers = [pltpu.VMEM(item.shape, bf16) for item in arrays]
    return pl.pallas_call(
        functools.partial(line_kernel, copies, tuple(cuts), paired),
        out_shape=tuple(outs),
        in_specs=[ANY] * len(arrays),
        out_specs=[ANY] * len(outs),
        scratch_shapes=buffers * 3
        + [
            pltpu.VMEM((3, stage_rows, stage_columns), f32),
            pltpu.SemaphoreType.DMA((len(arrays),)),
            pltpu.SemaphoreType.DMA((3, 2)),
        ]
        + [pltpu.SemaphoreType.DMA((count,))] * 4,
        compiler_params=pltpu.CompilerParams(
            collective_id=7, has_side_effects=True, vmem_limit_bytes=60 * 2**20
        ),
    )(*arrays)


def body(
    tokens,
    segments,
    cotangent,
    norm_gain,
    branch_weight,
    input_weight,
    conv_weight,
    conv_bias,
    recur_gate_weight,
    recur_gate_bias,
    input_gate_weight,
    input_gate_bias,
    decay_param,
    output_weight,
    mlp_norm_gain,
    gate_weight,
    up_weight,
    down_weight,
):
    x, cot = tokens[0], cotangent[0]
    rows, depth = x.shape
    members = lax.axis_size(GROUP)
    sequences = lax.axis_size("shard")
    total = members * rows
    gain, mlp_gain = low(norm_gain)[:, None], low(mlp_norm_gain)[:, None]
    own_labels = jnp.broadcast_to(segments[0].astype(bf16)[:, None], (rows, 128))
    unit_all, labels = exchange(
        start_kernel, 1, (x, own_labels), (((total, depth), bf16), ((total, 128), bf16)), rows, depth, 2, 0
    )
    mix_w = to_columns([branch_weight, input_weight], gain)
    pair_w = to_columns([gate_weight, up_weight], mlp_gain)
    width = branch_weight.shape[1] // members
    branch_w, input_w = mix_w[:, :width], mix_w[:, width:]
    out_low = lax.all_gather(cot, ROWS, axis=0, tiled=True)
    output_w = output_weight.astype(bf16)
    down_w = down_weight.astype(bf16)

    conv_f = low(conv_weight)
    decay_f = low(decay_param)
    bias = jnp.stack([low(conv_bias), low(recur_gate_bias), low(input_gate_bias), jax.nn.softplus(-decay_f)])
    mixed = mix_forward(
        sequences, unit_all, branch_w, input_w, labels, conv_f, bias, recur_gate_weight, input_gate_weight, output_w
    )
    partial, product = mixed[:2]
    whole = ((total, depth), bf16)
    unit_two, middle = exchange(
        forward_kernel, 2, (partial, x), (whole, ((rows, depth), f32)), rows, depth, 1, 1
    )
    ff = pair_w.shape[1] // 2
    gate_pre = mm(unit_two, pair_w[:, :ff])
    up_pre = mm(unit_two, pair_w[:, ff:])
    hidden_grad = mm_nt(out_low, down_w)
    gate_act, gate_slope = gelu_parts(gate_pre)
    hidden = (gate_act * up_pre).astype(bf16)
    gate_low = (hidden_grad * up_pre * gate_slope).astype(bf16)
    up_low = (hidden_grad * gate_act).astype(bf16)
    pair_low = jnp.concatenate([gate_low, up_low], 1)
    partial = mm_nt(pair_low, pair_w).astype(bf16)
    mid_low, middle_grad = exchange(
        backward_kernel, 3, (partial, middle, cot), (whole, ((rows, depth), f32)), rows, depth, 1, 1
    )
    pair_partial = swap_columns(mm_tn(unit_two, pair_low))
    down_partial = mm_tn(hidden, out_low).astype(bf16)[None]
    block_sum = lax.psum_scatter(mm(hidden, down_w).astype(bf16), ROWS, scatter_dimension=0, tiled=True)
    block_out = (middle + block_sum.astype(f32)).astype(bf16)
    output_partial = mm_tn(product, mid_low).astype(bf16)[None]
    back = mix_backward(
        sequences, mid_low, output_w, branch_w, input_w, *mixed[2:], labels, conv_f, bias, recur_gate_weight, input_gate_weight
    )
    partial, branch_low, conv_low, conv_weight_grad, sums, recur_weight_grad, inject_weight_grad = back
    branch_partial = side_by_side(swap_columns(mm_tn(unit_all, branch_low)))
    input_partial = side_by_side(swap_columns(mm_tn(unit_all, conv_low)))
    (tokens_grad,) = exchange(
        last_kernel, 4, (partial, middle_grad, x), (((rows, depth), bf16),), rows, depth, 0, 1
    )
    decay_param_grad = sums[3] * decay_scale * jax.nn.sigmoid(-decay_f)
    small = (conv_weight_grad, sums[0], recur_weight_grad, sums[1], inject_weight_grad, sums[2], decay_param_grad)
    small = lax.psum(tuple(item.astype(bf16) for item in small), "replica")
    small = [item.astype(f32) for item in small]
    down_grad, gate_grad, up_grad, output_grad, branch_grad, input_grad = replica_sum(
        [down_partial, pair_partial, output_partial, branch_partial, input_partial], 1, lax.axis_size("replica")
    )
    gain_grad = jnp.sum(branch_grad * low(branch_weight) + input_grad * low(input_weight), axis=1)
    mlp_gain_grad = jnp.sum(gate_grad * low(gate_weight) + up_grad * low(up_weight), axis=1)
    return (
        block_out[None],
        tokens_grad[None],
        gain_grad,
        branch_grad * gain,
        input_grad * gain,
        *small,
        output_grad,
        mlp_gain_grad,
        gate_grad * mlp_gain,
        up_grad * mlp_gain,
        down_grad,
    )


def solution(mesh):
    row3 = P(("shard", "replica"), "seq", None)
    vec = P(("seq", "shard"))
    mat = P(("seq", "shard"), None)
    cube = P(("seq", "shard"), None, None)
    taps = P(None, ("seq", "shard"))
    params = (vec, mat, mat, taps, vec, cube, vec, cube, vec, vec, mat, vec, mat, mat, mat)
    in_specs = (row3, P(("shard", "replica"), "seq"), row3) + params
    out_specs = (row3, row3) + params
    return jax.shard_map(body, mesh=mesh, in_specs=in_specs, out_specs=out_specs, check_vma=False)
```

```python
import functools

import jax
import jax.numpy as jnp
from jax import lax
from jax.experimental import pallas as pl
from jax.experimental.pallas import tpu as pltpu
from jax.sharding import PartitionSpec as P

epsilon = 1e-06
decay_scale = 8.0
GROUP = ("seq", "shard")
ROWS = ("shard", "seq")
f32 = jnp.float32
bf16 = jnp.bfloat16
VM = pl.BlockSpec(memory_space=pltpu.VMEM)
ANY = pl.BlockSpec(memory_space=pl.ANY)
MESH = pl.DeviceIdType.MESH


def mm(left, right):
    return jnp.dot(left, right, preferred_element_type=f32)


def mm_nt(left, right):
    return lax.dot_general(left, right, (((1,), (1,)), ((), ())), preferred_element_type=f32)


def mm_tn(left, right):
    return lax.dot_general(left, right, (((0,), (0,)), ((), ())), preferred_element_type=f32)


def low(item):
    return item.astype(bf16).astype(f32)


def swap_columns(grad):
    owners = lax.axis_size(GROUP)
    cut = grad.astype(bf16).reshape(owners, grad.shape[0] // owners, grad.shape[1])
    return lax.all_to_all(cut, GROUP, split_axis=0, concat_axis=0, tiled=True)


def side_by_side(cut):
    return jnp.swapaxes(cut, 0, 1).reshape(1, cut.shape[1], -1)


def to_columns(weights, gain):
    owners = lax.axis_size(GROUP)
    rows = weights[0].shape[0]
    scaled = [(low(item) * gain).astype(bf16).reshape(rows, owners, -1) for item in weights]
    cut = jnp.swapaxes(jnp.concatenate(scaled, 2), 0, 1)
    return lax.all_to_all(cut, GROUP, split_axis=0, concat_axis=0, tiled=True).reshape(rows * owners, -1)


def gelu_parts(x):
    inner = 0.7978845608028654 * (x + 0.044715 * x * x * x)
    t = jnp.tanh(inner)
    value = 0.5 * x * (1.0 + t)
    slope = 0.5 * (1.0 + t) + 0.5 * x * (1.0 - t * t) * 0.7978845608028654 * (
        1.0 + 3.0 * 0.044715 * x * x
    )
    return value, slope


def minus_expm1(y):
    poly = 1.0 + y * (1.0 / 8.0)
    for order in (7.0, 6.0, 5.0, 4.0, 3.0, 2.0):
        poly = 1.0 + y * (1.0 / order) * poly
    return jnp.where(y > -0.5, -y * poly, 1.0 - jnp.exp(y))


def dot_nn(a, b):
    return lax.dot_general(a, b, (((1,), (0,)), ((), ())), preferred_element_type=f32)


def dot_nt(a, b):
    return lax.dot_general(a, b, (((1,), (1,)), ((), ())), preferred_element_type=f32)


def dot_tn(a, b):
    return lax.dot_general(a, b, (((0,), (0,)), ((), ())), preferred_element_type=f32)


def fill_blocks(target, source):
    target[...] = jnp.zeros_like(target)
    count, size = source.shape[0], source.shape[1]
    for h in range(count):
        target[h * size : (h + 1) * size, h * size : (h + 1) * size] = source[h].astype(bf16).astype(f32)


def put_tiles(ref, here, value):
    width = value.shape[1]
    for tile in range(ref.shape[0]):
        lanes = min(128, width - 128 * tile)
        ref[tile, here, 0:lanes] = value[:, 128 * tile : 128 * tile + lanes]


def get_tiles(ref, here, width):
    parts = [ref[tile, here, 0 : min(128, width - 128 * tile)] for tile in range(ref.shape[0])]
    return jnp.concatenate(parts, axis=1)


def clear_tail(ref, width):
    tail = ref.shape[0] * 128 - width
    if tail:
        ref[ref.shape[0] - 1, :, 128 - tail :] = jnp.zeros((ref.shape[1], tail), f32)


def label_masks(label_ref, here, length, width, taps, lines):
    own = label_ref[here, :].astype(f32)
    lines[0:8, :] = jnp.full((8, 128), -1.0, f32)
    lines[8 : 8 + length, :] = own
    masks = []
    for k in range(1, taps):
        same = jnp.where(lines[8 - k : 8 - k + length, :] == own, 1.0, 0.0)
        masks.append(jnp.concatenate([same] * -(-width // 128), axis=1)[:, :width])
    return masks


def seq_scan(decay_ref, value_ref, sequences, length, reverse):
    tiles = decay_ref.shape[0]
    unroll = 8

    def step(i, states):
        states = list(states)
        for j in range(unroll):
            at = i * unroll + j
            if reverse:
                at = length - 1 - at
            here = pl.ds(at, sequences, stride=length)
            for tile in range(tiles):
                value = value_ref[tile, here, :]
                decay = decay_ref[tile, here, :]
                if reverse:
                    new = value + states[tile]
                    value_ref[tile, here, :] = new
                    states[tile] = decay * new
                else:
                    states[tile] = value + decay * states[tile]
                    value_ref[tile, here, :] = states[tile]
        return tuple(states)

    lax.fori_loop(0, length // unroll, step, (jnp.zeros((sequences, 128), f32),) * tiles)


def mix_forward_kernel(
    sequences, length, n_ref, wb_ref, wi_ref, label_ref, conv_ref, bias_ref, rw_ref, iw_ref, ow_ref,
    partial_ref, product_ref, pre_ref, conv_in_ref, values_ref, recur_ref, inject_ref, decay_ref, states_ref,
    pad, lines, rbig, ibig,
):
    fill_blocks(rbig, rw_ref)
    fill_blocks(ibig, iw_ref)
    pad[0:8, :] = jnp.zeros((8, pad.shape[1]), f32)
    taps = conv_ref.shape[0]
    width = pad.shape[1]
    clear_tail(decay_ref, width)
    clear_tail(states_ref, width)

    def one(s, _):
        base = pl.multiple_of(s * length, length)
        here = pl.ds(base, length)
        rows = n_ref[here, :]
        masks = label_masks(label_ref, here, length, width, taps, lines)
        pre_ref[here, :] = dot_nn(rows, wb_ref[...])
        conv_in = dot_nn(rows, wi_ref[...]).astype(bf16)
        conv_in_ref[here, :] = conv_in
        pad[8 : 8 + length, :] = conv_in.astype(f32)
        total = bias_ref[0:1, :] + conv_ref[0:1, :] * pad[8 : 8 + length, :]
        for k in range(1, taps):
            total = total + conv_ref[k : k + 1, :] * pad[8 - k : 8 - k + length, :] * masks[k - 1]
        values = total.astype(bf16)
        values_ref[here, :] = values
        recur = jax.nn.sigmoid(dot_nn(values, rbig[...].astype(bf16)) + bias_ref[1:2, :])
        inject = jax.nn.sigmoid(dot_nn(values, ibig[...].astype(bf16)) + bias_ref[2:3, :])
        recur_ref[here, :] = recur
        inject_ref[here, :] = inject
        log_decay = -decay_scale * bias_ref[3:4, :] * recur
        inside = masks[0] > 0.5
        put_tiles(decay_ref, here, jnp.where(inside, jnp.exp(log_decay), 0.0))
        scale = jnp.where(inside, jnp.sqrt(minus_expm1(2.0 * log_decay)), 1.0)
        put_tiles(states_ref, here, scale * inject * values.astype(f32))
        return 0

    lax.fori_loop(0, sequences, one, 0)
    seq_scan(decay_ref, states_ref, sequences, length, False)

    def two(s, _):
        base = pl.multiple_of(s * length, length)
        here = pl.ds(base, length)
        act, _unused = gelu_parts(pre_ref[here, :])
        product = (act * get_tiles(states_ref, here, width)).astype(bf16)
        product_ref[here, :] = product
        partial_ref[here, :] = dot_nn(product, ow_ref[...]).astype(bf16)
        return 0

    lax.fori_loop(0, sequences, two, 0)


def mix_forward(sequences, normed, wb, wi, labels, conv, bias, rw, iw, ow):
    total, width = normed.shape[0], wb.shape[1]
    length = total // sequences
    depth = ow.shape[1]
    shape = jax.ShapeDtypeStruct
    like = lambda dt: shape((total, width), dt)
    tiled = shape((-(-width // 128), total, 128), f32)
    return pl.pallas_call(
        functools.partial(mix_forward_kernel, sequences, length),
        out_shape=(
            shape((total, depth), bf16), like(bf16), like(f32), like(bf16), like(bf16), like(f32), like(f32), tiled, tiled,
        ),
        in_specs=[VM] * 9,
        out_specs=[VM] * 9,
        scratch_shapes=[
            pltpu.VMEM((8 + length, width), f32),
            pltpu.VMEM((8 + length, 128), f32),
            pltpu.VMEM((width, width), f32),
            pltpu.VMEM((width, width), f32),
        ],
        compiler_params=pltpu.CompilerParams(vmem_limit_bytes=56 * 2**20),
        cost_estimate=pl.CostEstimate(flops=2 * total * width * 3 * depth, bytes_accessed=20 * 2**20, transcendentals=total * width * 5),
    )(normed, wb, wi, labels, conv, bias, rw, iw, ow)


def mix_backward_kernel(
    sequences, length, mid_ref, ow_ref, wb_ref, wi_ref, pre_ref, conv_in_ref, values_ref, recur_ref, inject_ref, decay_ref, states_ref,
    label_ref, conv_ref, bias_ref, rw_ref, iw_ref,
    partial_ref, branch_low_ref, conv_low_ref, dconv_ref, sums_ref, drw_ref, diw_ref,
    adj, pad, lines, rbig, ibig, dr, di,
):
    fill_blocks(rbig, rw_ref)
    fill_blocks(ibig, iw_ref)
    dr[...] = jnp.zeros_like(dr)
    di[...] = jnp.zeros_like(di)
    sums_ref[...] = jnp.zeros_like(sums_ref)
    dconv_ref[...] = jnp.zeros_like(dconv_ref)
    taps = conv_ref.shape[0]
    width = pad.shape[1]
    clear_tail(adj, width)

    def one(s, _):
        base = pl.multiple_of(s * length, length)
        here = pl.ds(base, length)
        product_grad = dot_nt(mid_ref[here, :], ow_ref[...])
        act, slope = gelu_parts(pre_ref[here, :])
        branch_low_ref[here, :] = (product_grad * get_tiles(states_ref, here, width) * slope).astype(bf16)
        put_tiles(adj, here, product_grad * act)
        return 0

    lax.fori_loop(0, sequences, one, 0)
    seq_scan(decay_ref, adj, sequences, length, True)

    def two(s, _):
        base = pl.multiple_of(s * length, length)
        here = pl.ds(base, length)
        adjoint = get_tiles(adj, here, width)
        recur = recur_ref[here, :]
        inject = inject_ref[here, :]
        decay = get_tiles(decay_ref, here, width)
        values = values_ref[here, :]
        values_f = values.astype(f32)
        masks = label_masks(label_ref, here, length, width, taps, lines)
        inside = masks[0] > 0.5
        rate = bias_ref[3:4, :]
        log_decay = -decay_scale * rate * recur
        scale = jnp.where(inside, jnp.sqrt(minus_expm1(2.0 * log_decay)), 1.0)
        pad[0:8, :] = jnp.zeros((8, width), f32)
        pad[8 : 8 + length, :] = get_tiles(states_ref, here, width)
        previous = pad[7 : 7 + length, :]
        driven = adjoint * inject * values_f
        log_grad = jnp.where(inside, adjoint * previous * decay - driven * decay * decay / scale, 0.0)
        recur_low = (log_grad * (-decay_scale * rate) * recur * (1.0 - recur)).astype(bf16)
        inject_low = (driven * scale * (1.0 - inject)).astype(bf16)
        sums_ref[1:2, :] += jnp.sum(recur_low.astype(f32), axis=0, keepdims=True)
        sums_ref[2:3, :] += jnp.sum(inject_low.astype(f32), axis=0, keepdims=True)
        sums_ref[3:4, :] += jnp.sum(log_grad * recur, axis=0, keepdims=True)
        dr[...] += dot_tn(values, recur_low)
        di[...] += dot_tn(values, inject_low)
        grad = adjoint * scale * inject
        grad = grad + dot_nt(recur_low, rbig[...].astype(bf16)) + dot_nt(inject_low, ibig[...].astype(bf16))
        sums_ref[0:1, :] += jnp.sum(grad, axis=0, keepdims=True)
        pad[8 : 8 + length, :] = conv_in_ref[here, :].astype(f32)
        dconv_ref[0:1, :] += jnp.sum(grad * pad[8 : 8 + length, :], axis=0, keepdims=True)
        masked = []
        for k in range(1, taps):
            part = grad * masks[k - 1]
            masked.append(part)
            dconv_ref[k : k + 1, :] += jnp.sum(part * pad[8 - k : 8 - k + length, :], axis=0, keepdims=True)
        total = grad * conv_ref[0:1, :]
        pad[length : length + 8, :] = jnp.zeros((8, width), f32)
        for k in range(1, taps):
            pad[0:length, :] = masked[k - 1] * conv_ref[k : k + 1, :]
            total = total + pad[k : k + length, :]
        conv_low = total.astype(bf16)
        conv_low_ref[here, :] = conv_low
        partial_ref[here, :] = (dot_nt(branch_low_ref[here, :], wb_ref[...]) + dot_nt(conv_low, wi_ref[...])).astype(bf16)
        return 0

    lax.fori_loop(0, sequences, two, 0)
    size = drw_ref.shape[1]
    for h in range(drw_ref.shape[0]):
        cut = slice(h * size, (h + 1) * size)
        drw_ref[h] = dr[cut, cut]
        diw_ref[h] = di[cut, cut]


def mix_backward(sequences, mid_low, ow, wb, wi, pre, conv_in, values, recur, inject, decay, states, labels, conv, bias, rw, iw):
    total, depth = mid_low.shape
    width = ow.shape[0]
    length = total // sequences
    shape = jax.ShapeDtypeStruct
    return pl.pallas_call(
        functools.partial(mix_backward_kernel, sequences, length),
        out_shape=(
            shape((total, depth), bf16), shape((total, width), bf16), shape((total, width), bf16),
            shape(conv.shape, f32), shape((4, width), f32), shape(rw.shape, f32), shape(iw.shape, f32),
        ),
        in_specs=[VM] * 16,
        out_specs=[VM] * 7,
        scratch_shapes=[
            pltpu.VMEM(states.shape, f32),
            pltpu.VMEM((8 + length, width), f32),
            pltpu.VMEM((8 + length, 128), f32),
            pltpu.VMEM((width, width), f32),
            pltpu.VMEM((width, width), f32),
            pltpu.VMEM((width, width), f32),
            pltpu.VMEM((width, width), f32),
        ],
        compiler_params=pltpu.CompilerParams(vmem_limit_bytes=56 * 2**20),
        cost_estimate=pl.CostEstimate(flops=2 * total * width * 3 * depth, bytes_accessed=25 * 2**20, transcendentals=total * width * 5),
    )(mid_low, ow, wb, wi, pre, conv_in, values, recur, inject, decay, states, labels, conv, bias, rw, iw)


def plane():
    halves, shards = lax.axis_size("seq"), lax.axis_size("shard")
    y, s = lax.axis_index("seq"), lax.axis_index("shard")
    offsets = [(dy, ds) for ds in range(0, shards, 2) for dy in range(halves)]

    def at(dy, ds):
        return {"seq": jnp.bitwise_xor(y, dy), "shard": jnp.bitwise_xor(s, ds)}

    def block(dy, ds):
        return jnp.bitwise_xor(s, ds) * halves + jnp.bitwise_xor(y, dy)

    return offsets, at, block


def greet(offsets, at):
    barrier = pltpu.get_barrier_semaphore()
    partners = [(0, 1)] + offsets[1:]
    for dy, ds in partners:
        pl.semaphore_signal(barrier, inc=1, device_id=at(dy, ds), device_id_type=MESH)
    pl.semaphore_wait(barrier, len(partners))


def remote(src, dst, sent, got, device):
    return pltpu.make_async_remote_copy(
        src_ref=src, dst_ref=dst, send_sem=sent, recv_sem=got, device_id=device, device_id_type=MESH
    )


def row_block(ref, index, rows):
    return ref.at[pl.ds(pl.multiple_of(index * rows, rows), rows), :]


def scatter_sum(rows, partial, near, far, stage, acc, sems):
    offsets, at, block = plane()
    near_sent, near_got, far_sent, far_got = sems
    count = len(offsets)
    order = list(range(count - 1, -1, -1))
    firsts = {}
    for q in order:
        dy, ds = offsets[q]
        firsts[q] = remote(
            row_block(partial, block(dy, ds ^ 1), rows), near.at[q], near_sent.at[q], near_got.at[q], at(0, 1)
        )
        firsts[q].start()
    seconds = {}
    for q in order:
        dy, ds = offsets[q]
        firsts[q].wait_recv()
        base = block(dy, ds) * rows

        def tile(i, _):
            step = pl.multiple_of(i * 16, 16)
            here = pl.ds(step, 16)
            total = partial[pl.ds(pl.multiple_of(base + step, 16), 16), :].astype(f32) + near[q, here, :].astype(f32)
            if q:
                stage[q - 1, here, :] = total.astype(bf16)
            else:
                acc[here, :] = total
            return 0

        lax.fori_loop(0, rows // 16, tile, 0)
        if q:
            seconds[q] = remote(stage.at[q - 1], far.at[q - 1], far_sent.at[q - 1], far_got.at[q - 1], at(dy, ds))
            seconds[q].start()
    for q in order[:-1]:
        seconds[q].wait_recv()

        def more(i, _):
            here = pl.ds(pl.multiple_of(i * 16, 16), 16)
            acc[here, :] += far[q - 1, here, :].astype(f32)
            return 0

        lax.fori_loop(0, rows // 16, more, 0)
    return [firsts[q].wait_send for q in order] + [seconds[q].wait_send for q in order[:-1]]


def gather_blocks(rows, whole, sems):
    offsets, at, block = plane()
    near_sent, near_got, far_sent, far_got = sems
    count = len(offsets)
    own = row_block(whole, block(0, 0), rows)
    sends = []
    outs = {}
    for q in range(count - 1, 0, -1):
        dy, ds = offsets[q]
        outs[q] = remote(own, own, far_sent.at[q - 1], far_got.at[q - 1], at(dy, ds))
        outs[q].start()
        sends.append(outs[q].wait_send)
    hand = remote(own, own, near_sent.at[0], near_got.at[0], at(0, 1))
    hand.start()
    sends.append(hand.wait_send)
    arrivals = [hand.wait_recv]
    for q in list(range(1, count)):
        dy, ds = offsets[q]
        outs[q].wait_recv()
        block_q = row_block(whole, block(dy, ds), rows)
        hand = remote(block_q, block_q, near_sent.at[q], near_got.at[q], at(0, 1))
        hand.start()
        sends.append(hand.wait_send)
        arrivals.append(hand.wait_recv)
    return arrivals + sends


def root_mean(rows):
    return lax.rsqrt(jnp.mean(rows * rows, axis=-1, keepdims=True) + epsilon)


def norm_backward(grad_unit, unit, inverse):
    return inverse * (grad_unit - unit * jnp.mean(grad_unit * unit, axis=-1, keepdims=True))


def by_tiles(rows, work):
    def tile(i, _):
        work(pl.ds(pl.multiple_of(i * 16, 16), 16), i)
        return 0

    lax.fori_loop(0, rows // 16, tile, 0)


def start_kernel(x_ref, label_ref, unit_ref, labels_ref, *sems):
    rows = x_ref.shape[0]
    offsets, at, block = plane()
    greet(offsets, at)
    base = block(0, 0) * rows

    def unit(here, i):
        value = x_ref[here, :].astype(f32)
        there = pl.ds(pl.multiple_of(base + i * 16, 16), 16)
        unit_ref[there, :] = (value * root_mean(value)).astype(bf16)
        labels_ref[there, :] = label_ref[here, :]

    by_tiles(rows, unit)
    waits = gather_blocks(rows, labels_ref, sems[4:])
    waits = waits + gather_blocks(rows, unit_ref, sems[:4])
    for wait in waits:
        wait()


def forward_kernel(partial, x_ref, unit_ref, middle_ref, near, far, stage, acc, *sems):
    rows = x_ref.shape[0]
    offsets, at, block = plane()
    greet(offsets, at)
    waits = scatter_sum(rows, partial, near, far, stage, acc, sems[:4])
    base = block(0, 0) * rows

    def norm(here, i):
        middle = x_ref[here, :].astype(f32) + acc[here, :]
        middle_ref[here, :] = middle
        there = pl.ds(pl.multiple_of(base + i * 16, 16), 16)
        unit_ref[there, :] = (middle * root_mean(middle)).astype(bf16)

    by_tiles(rows, norm)
    waits = waits + gather_blocks(rows, unit_ref, sems[4:])
    for wait in waits:
        wait()


def backward_kernel(partial, middle_ref, cot_ref, low_ref, grad_ref, near, far, stage, acc, *sems):
    rows = middle_ref.shape[0]
    offsets, at, block = plane()
    greet(offsets, at)
    waits = scatter_sum(rows, partial, near, far, stage, acc, sems[:4])
    base = block(0, 0) * rows

    def norm(here, i):
        middle = middle_ref[here, :]
        inverse = root_mean(middle)
        grad = cot_ref[here, :].astype(f32) + norm_backward(acc[here, :], middle * inverse, inverse)
        grad_ref[here, :] = grad
        there = pl.ds(pl.multiple_of(base + i * 16, 16), 16)
        low_ref[there, :] = grad.astype(bf16)

    by_tiles(rows, norm)
    waits = waits + gather_blocks(rows, low_ref, sems[4:])
    for wait in waits:
        wait()


def last_kernel(partial, grad_ref, x_ref, out_ref, near, far, stage, acc, *sems):
    rows = x_ref.shape[0]
    offsets, at, block = plane()
    greet(offsets, at)
    waits = scatter_sum(rows, partial, near, far, stage, acc, sems[:4])

    def norm(here, i):
        value = x_ref[here, :].astype(f32)
        inverse = root_mean(value)
        grad = grad_ref[here, :] + norm_backward(acc[here, :], value * inverse, inverse)
        out_ref[here, :] = grad.astype(bf16)

    by_tiles(rows, norm)
    for wait in waits:
        wait()


def exchange(kernel, identity, inputs, outs, rows, depth, gathers, scatters):
    count = lax.axis_size("seq") * lax.axis_size("shard") // 2
    block = (rows, depth)
    scratch = []
    if scatters:
        scratch = [
            pltpu.VMEM((count,) + block, bf16),
            pltpu.VMEM((count - 1,) + block, bf16),
            pltpu.VMEM((count - 1,) + block, bf16),
            pltpu.VMEM(block, f32),
        ]
    for _ in range(scatters + gathers):
        scratch += [pltpu.SemaphoreType.DMA((count,))] * 2 + [pltpu.SemaphoreType.DMA((count - 1,))] * 2
    return pl.pallas_call(
        kernel,
        out_shape=tuple(jax.ShapeDtypeStruct(shape, kind) for shape, kind in outs),
        in_specs=[VM] * len(inputs),
        out_specs=[VM] * len(outs),
        scratch_shapes=scratch,
        compiler_params=pltpu.CompilerParams(
            collective_id=identity, has_side_effects=True, vmem_limit_bytes=40 * 2**20
        ),
        cost_estimate=pl.CostEstimate(flops=10**6, bytes_accessed=60 * 2**20, transcendentals=0),
    )(*inputs)


def pieces(rows, most):
    count = -(-rows // most)
    while rows % count or (rows // count) % 16:
        count += 1
    return count


def line_kernel(n, cuts, paired, *refs):
    ins = len(cuts)
    own_hbm = refs[:ins]
    made = ins if paired is None else ins + 1
    outs = refs[ins : ins + made]
    scratch = refs[ins + made :]
    own, from_out, from_in = scratch[:ins], scratch[ins : 2 * ins], scratch[2 * ins : 3 * ins]
    stage, load_sem, stage_sem, sent_in, sent_out, got_out, got_in = scratch[3 * ins :]
    me = lax.axis_index("replica")
    left = me < n // 2
    inward = jnp.where(left, me + 1, me - 1)
    outward = jnp.where(left, me - 1, me + 1)
    has_out = jnp.logical_and(me > 0, me < n - 1)
    middle = jnp.logical_or(me == n // 2 - 1, me == n // 2)

    loads = [pltpu.make_async_copy(own_hbm[k], own[k], load_sem.at[k]) for k in range(ins)]
    for load in loads:
        load.start()
    barrier = pltpu.get_barrier_semaphore()
    pl.semaphore_signal(barrier, inc=1, device_id={"replica": inward}, device_id_type=MESH)

    @pl.when(has_out)
    def _():
        pl.semaphore_signal(barrier, inc=1, device_id={"replica": outward}, device_id_type=MESH)
        pl.semaphore_wait(barrier, 2)

    @pl.when(jnp.logical_not(has_out))
    def _():
        pl.semaphore_wait(barrier, 1)

    chunks = []
    for k, (lead, count, rows) in enumerate(cuts):
        for j in range(lead):
            for i in range(count):
                chunks.append((k, j, i * rows, rows))
    slots = stage.shape[0]
    ready = set()

    def view(group, c):
        k, j, start, rows = chunks[c]
        return group[k].at[j, pl.ds(start, rows), :]

    def push(group, target, c, sent, got, device):
        return pltpu.make_async_remote_copy(
            src_ref=view(group, c),
            dst_ref=view(target, c),
            send_sem=sent.at[c],
            recv_sem=got.at[c],
            device_id={"replica": device},
            device_id_type=MESH,
        )

    def add(target, other, c):
        k, j, start, rows = chunks[c]

        def tile(i, _):
            here = pl.ds(pl.multiple_of(start + i * 16, 16), 16)
            total = target[k][j, here, :].astype(f32) + other[k][j, here, :].astype(f32)
            target[k][j, here, :] = total.astype(bf16)
            return 0

        lax.fori_loop(0, rows // 16, tile, 0)

    def pass_in(c):
        @pl.when(middle)
        def _():
            push(own, from_in, c, sent_in, got_in, inward).start()

        @pl.when(jnp.logical_not(middle))
        def _():
            push(own, from_out, c, sent_in, got_out, inward).start()

    def gather_in(c):
        @pl.when(has_out)
        def _():
            if chunks[c][0] not in ready:
                loads[chunks[c][0]].wait()
                ready.add(chunks[c][0])
            push(from_out, from_out, c, sent_in, got_out, inward).wait_recv()
            add(own, from_out, c)
            pass_in(c)

    @pl.when(jnp.logical_not(has_out))
    def _():
        seen = set()
        for c in range(len(chunks)):
            if chunks[c][0] not in seen:
                loads[chunks[c][0]].wait()
                seen.add(chunks[c][0])
            pass_in(c)

    def stage_copies(c):
        k, j, start, rows = chunks[c]
        slot = c % slots
        columns = own[k].shape[2]
        if k == paired:
            half = columns // 2
            return [
                pltpu.make_async_copy(
                    stage.at[slot, pl.ds(0, rows), pl.ds(side * half, half)],
                    outs[k + side].at[pl.ds(start, rows), pl.ds(j * half, half)],
                    stage_sem.at[slot, side],
                )
                for side in range(2)
            ]
        where = k if paired is None or k < paired else k + 1
        return [
            pltpu.make_async_copy(
                stage.at[slot, pl.ds(0, rows), pl.ds(0, columns)],
                outs[where].at[pl.ds(start, rows), :],
                stage_sem.at[slot, 0],
            )
        ]

    def give_back(c):
        k, j, start, rows = chunks[c]
        push(own, from_in, c, sent_out, got_in, inward).wait_recv()

        @pl.when(middle)
        def _():
            add(from_in, own, c)

        @pl.when(has_out)
        def _():
            push(from_in, from_in, c, sent_out, got_in, outward).start()

        if c >= slots:
            for copy in stage_copies(c - slots):
                copy.wait()
        slot = c % slots
        columns = own[k].shape[2]

        def tile(i, _):
            step = pl.multiple_of(i * 16, 16)
            stage[slot, pl.ds(step, 16), 0:columns] = from_in[k][
                j, pl.ds(pl.multiple_of(start + step, 16), 16), :
            ].astype(f32)
            return 0

        lax.fori_loop(0, rows // 16, tile, 0)
        for copy in stage_copies(c):
            copy.start()

    lag = 2
    for c in range(len(chunks) + lag):
        if c < len(chunks):
            gather_in(c)
        if c >= lag:
            give_back(c - lag)
    for c in range(max(0, len(chunks) - slots), len(chunks)):
        for copy in stage_copies(c):
            copy.wait()
    for c in range(len(chunks)):
        push(own, from_in, c, sent_in, got_in, inward).wait_send()

        @pl.when(has_out)
        def _():
            push(from_in, from_in, c, sent_out, got_in, outward).wait_send()


def replica_sum(arrays, paired, copies):
    cuts, outs = [], []
    stage_rows = stage_columns = 0
    for k, item in enumerate(arrays):
        lead, rows, columns = item.shape
        count = pieces(rows, max(16, (210 * 1024) // columns // 16 * 16))
        cuts.append((lead, count, rows // count))
        stage_rows, stage_columns = max(stage_rows, rows // count), max(stage_columns, columns)
        if k == paired:
            outs += [jax.ShapeDtypeStruct((rows, lead * columns // 2), f32)] * 2
        else:
            outs.append(jax.ShapeDtypeStruct((rows, columns), f32))
    count = sum(lead * cut for lead, cut, _ in cuts)
    buffers = [pltpu.VMEM(item.shape, bf16) for item in arrays]
    return pl.pallas_call(
        functools.partial(line_kernel, copies, tuple(cuts), paired),
        out_shape=tuple(outs),
        in_specs=[ANY] * len(arrays),
        out_specs=[ANY] * len(outs),
        scratch_shapes=buffers * 3
        + [
            pltpu.VMEM((3, stage_rows, stage_columns), f32),
            pltpu.SemaphoreType.DMA((len(arrays),)),
            pltpu.SemaphoreType.DMA((3, 2)),
        ]
        + [pltpu.SemaphoreType.DMA((count,))] * 4,
        compiler_params=pltpu.CompilerParams(
            collective_id=7, has_side_effects=True, vmem_limit_bytes=60 * 2**20
        ),
    )(*arrays)


def body(
    tokens,
    segments,
    cotangent,
    norm_gain,
    branch_weight,
    input_weight,
    conv_weight,
    conv_bias,
    recur_gate_weight,
    recur_gate_bias,
    input_gate_weight,
    input_gate_bias,
    decay_param,
    output_weight,
    mlp_norm_gain,
    gate_weight,
    up_weight,
    down_weight,
):
    x, cot = tokens[0], cotangent[0]
    rows, depth = x.shape
    members = lax.axis_size(GROUP)
    sequences = lax.axis_size("shard")
    total = members * rows
    gain, mlp_gain = low(norm_gain)[:, None], low(mlp_norm_gain)[:, None]
    own_labels = jnp.broadcast_to(segments[0].astype(bf16)[:, None], (rows, 128))
    unit_all, labels = exchange(
        start_kernel, 1, (x, own_labels), (((total, depth), bf16), ((total, 128), bf16)), rows, depth, 2, 0
    )
    mix_w = to_columns([branch_weight, input_weight], gain)
    pair_w = to_columns([gate_weight, up_weight], mlp_gain)
    width = branch_weight.shape[1] // members
    branch_w, input_w = mix_w[:, :width], mix_w[:, width:]
    out_low = lax.all_gather(cot, ROWS, axis=0, tiled=True)
    output_w = output_weight.astype(bf16)
    down_w = down_weight.astype(bf16)

    conv_f = low(conv_weight)
    decay_f = low(decay_param)
    bias = jnp.stack([low(conv_bias), low(recur_gate_bias), low(input_gate_bias), jax.nn.softplus(-decay_f)])
    mixed = mix_forward(
        sequences, unit_all, branch_w, input_w, labels, conv_f, bias, recur_gate_weight, input_gate_weight, output_w
    )
    partial, product = mixed[:2]
    whole = ((total, depth), bf16)
    unit_two, middle = exchange(
        forward_kernel, 2, (partial, x), (whole, ((rows, depth), f32)), rows, depth, 1, 1
    )
    ff = pair_w.shape[1] // 2
    gate_pre = mm(unit_two, pair_w[:, :ff])
    up_pre = mm(unit_two, pair_w[:, ff:])
    hidden_grad = mm_nt(out_low, down_w)
    gate_act, gate_slope = gelu_parts(gate_pre)
    hidden = (gate_act * up_pre).astype(bf16)
    gate_low = (hidden_grad * up_pre * gate_slope).astype(bf16)
    up_low = (hidden_grad * gate_act).astype(bf16)
    pair_low = jnp.concatenate([gate_low, up_low], 1)
    partial = mm_nt(pair_low, pair_w).astype(bf16)
    down_sum = lax.psum(mm_tn(hidden, out_low).astype(bf16), "replica")
    pair_partial = swap_columns(mm_tn(unit_two, pair_low))
    mid_low, middle_grad = exchange(
        backward_kernel, 3, (partial, middle, cot), (whole, ((rows, depth), f32)), rows, depth, 1, 1
    )
    block_sum = lax.psum_scatter(mm(hidden, down_w).astype(bf16), ROWS, scatter_dimension=0, tiled=True)
    block_out = (middle + block_sum.astype(f32)).astype(bf16)
    output_partial = mm_tn(product, mid_low).astype(bf16)[None]
    back = mix_backward(
        sequences, mid_low, output_w, branch_w, input_w, *mixed[2:], labels, conv_f, bias, recur_gate_weight, input_gate_weight
    )
    partial, branch_low, conv_low, conv_weight_grad, sums, recur_weight_grad, inject_weight_grad = back
    down_sum, pair_partial, branch_low = lax.optimization_barrier((down_sum, pair_partial, branch_low))
    pair_sum = lax.psum(pair_partial, "replica").astype(f32)
    gate_grad = jnp.swapaxes(pair_sum[:, :, :ff], 0, 1).reshape(-1, members * ff)
    up_grad = jnp.swapaxes(pair_sum[:, :, ff:], 0, 1).reshape(-1, members * ff)
    branch_partial = side_by_side(swap_columns(mm_tn(unit_all, branch_low)))
    input_partial = side_by_side(swap_columns(mm_tn(unit_all, conv_low)))
    (tokens_grad,) = exchange(
        last_kernel, 4, (partial, middle_grad, x), (((rows, depth), bf16),), rows, depth, 0, 1
    )
    size = recur_gate_weight.shape[1]
    gates = jnp.concatenate([recur_weight_grad, inject_weight_grad], 2).reshape(width, 2 * size)
    lanes = -(-max(width, 2 * size) // 128) * 128
    lines = jnp.concatenate([conv_weight_grad, sums], 0)
    packed = jnp.concatenate(
        [
            jnp.pad(gates, ((0, 0), (0, lanes - 2 * size))),
            jnp.pad(lines, ((0, 16 - lines.shape[0]), (0, lanes - width))),
        ],
        0,
    ).astype(bf16)[None]
    output_grad, branch_grad, input_grad, packed = replica_sum(
        [output_partial, branch_partial, input_partial, packed], None, lax.axis_size("replica")
    )
    recur_weight_grad = packed[:width, :size].reshape(-1, size, size)
    inject_weight_grad = packed[:width, size : 2 * size].reshape(-1, size, size)
    conv_weight_grad = packed[width : width + conv_weight.shape[0], :width]
    conv_bias_grad, recur_bias_grad, inject_bias_grad, rate_grad = [packed[width + conv_weight.shape[0] + i, :width] for i in range(4)]
    decay_param_grad = rate_grad * decay_scale * jax.nn.sigmoid(-decay_f)
    gain_grad = jnp.sum(branch_grad * low(branch_weight) + input_grad * low(input_weight), axis=1)
    mlp_gain_grad = jnp.sum(gate_grad * low(gate_weight) + up_grad * low(up_weight), axis=1)
    return (
        block_out[None],
        tokens_grad[None],
        gain_grad,
        branch_grad * gain,
        input_grad * gain,
        conv_weight_grad,
        conv_bias_grad,
        recur_weight_grad,
        recur_bias_grad,
        inject_weight_grad,
        inject_bias_grad,
        decay_param_grad,
        output_grad,
        mlp_gain_grad,
        gate_grad * mlp_gain,
        up_grad * mlp_gain,
        down_sum.astype(f32),
    )


def solution(mesh):
    row3 = P(("shard", "replica"), "seq", None)
    vec = P(("seq", "shard"))
    mat = P(("seq", "shard"), None)
    cube = P(("seq", "shard"), None, None)
    taps = P(None, ("seq", "shard"))
    params = (vec, mat, mat, taps, vec, cube, vec, cube, vec, vec, mat, vec, mat, mat, mat)
    in_specs = (row3, P(("shard", "replica"), "seq"), row3) + params
    out_specs = (row3, row3) + params
    return jax.shard_map(body, mesh=mesh, in_specs=in_specs, out_specs=out_specs, check_vma=False)
```

```python
import functools

import jax
import jax.numpy as jnp
from jax import lax
from jax.experimental import pallas as pl
from jax.experimental.pallas import tpu as pltpu
from jax.sharding import PartitionSpec as P

epsilon = 1e-06
decay_scale = 8.0
GROUP = ("seq", "shard")
ROWS = ("shard", "seq")
f32 = jnp.float32
bf16 = jnp.bfloat16
VM = pl.BlockSpec(memory_space=pltpu.VMEM)
ANY = pl.BlockSpec(memory_space=pl.ANY)
MESH = pl.DeviceIdType.MESH


def mm(left, right):
    return jnp.dot(left, right, preferred_element_type=f32)


def mm_nt(left, right):
    return lax.dot_general(left, right, (((1,), (1,)), ((), ())), preferred_element_type=f32)


def mm_tn(left, right):
    return lax.dot_general(left, right, (((0,), (0,)), ((), ())), preferred_element_type=f32)


def low(item):
    return item.astype(bf16).astype(f32)


def by_owner(weight, gain):
    owners = lax.axis_size(GROUP)
    scaled = (low(weight) * gain).astype(bf16)
    return jnp.swapaxes(scaled.reshape(weight.shape[0], owners, -1), 0, 1)


def swap(cut):
    return lax.all_to_all(cut, GROUP, split_axis=0, concat_axis=0, tiled=True)


def gelu_parts(x):
    inner = 0.7978845608028654 * (x + 0.044715 * x * x * x)
    t = jnp.tanh(inner)
    value = 0.5 * x * (1.0 + t)
    slope = 0.5 * (1.0 + t) + 0.5 * x * (1.0 - t * t) * 0.7978845608028654 * (
        1.0 + 3.0 * 0.044715 * x * x
    )
    return value, slope


def minus_expm1(y):
    poly = 1.0 + y * (1.0 / 8.0)
    for order in (7.0, 6.0, 5.0, 4.0, 3.0, 2.0):
        poly = 1.0 + y * (1.0 / order) * poly
    return jnp.where(y > -0.5, -y * poly, 1.0 - jnp.exp(y))


def dot_nn(a, b):
    return lax.dot_general(a, b, (((1,), (0,)), ((), ())), preferred_element_type=f32)


def dot_nt(a, b):
    return lax.dot_general(a, b, (((1,), (1,)), ((), ())), preferred_element_type=f32)


def dot_tn(a, b):
    return lax.dot_general(a, b, (((0,), (0,)), ((), ())), preferred_element_type=f32)


def whole_weight(ref, part):
    owners, _, rows, width = ref.shape
    return ref[:, part].reshape(owners * rows, width)


def fill_blocks(target, source):
    target[...] = jnp.zeros_like(target)
    count, size = source.shape[0], source.shape[1]
    for h in range(count):
        target[h * size : (h + 1) * size, h * size : (h + 1) * size] = source[h].astype(bf16).astype(f32)


def put_tiles(ref, here, value):
    width = value.shape[1]
    for tile in range(ref.shape[0]):
        lanes = min(128, width - 128 * tile)
        ref[tile, here, 0:lanes] = value[:, 128 * tile : 128 * tile + lanes]


def get_tiles(ref, here, width):
    parts = [ref[tile, here, 0 : min(128, width - 128 * tile)] for tile in range(ref.shape[0])]
    return jnp.concatenate(parts, axis=1)


def clear_tail(ref, width):
    tail = ref.shape[0] * 128 - width
    if tail:
        ref[ref.shape[0] - 1, :, 128 - tail :] = jnp.zeros((ref.shape[1], tail), f32)


def label_masks(label_ref, here, length, width, taps, lines):
    own = label_ref[here, :].astype(f32)
    lines[0:8, :] = jnp.full((8, 128), -1.0, f32)
    lines[8 : 8 + length, :] = own
    masks = []
    for k in range(1, taps):
        same = jnp.where(lines[8 - k : 8 - k + length, :] == own, 1.0, 0.0)
        masks.append(jnp.concatenate([same] * -(-width // 128), axis=1)[:, :width])
    return masks


def seq_scan(decay_ref, value_ref, sequences, length, reverse):
    tiles = decay_ref.shape[0]
    unroll = 8

    def step(i, states):
        states = list(states)
        for j in range(unroll):
            at = i * unroll + j
            if reverse:
                at = length - 1 - at
            here = pl.ds(at, sequences, stride=length)
            for tile in range(tiles):
                value = value_ref[tile, here, :]
                decay = decay_ref[tile, here, :]
                if reverse:
                    new = value + states[tile]
                    value_ref[tile, here, :] = new
                    states[tile] = decay * new
                else:
                    states[tile] = value + decay * states[tile]
                    value_ref[tile, here, :] = states[tile]
        return tuple(states)

    lax.fori_loop(0, length // unroll, step, (jnp.zeros((sequences, 128), f32),) * tiles)


def mix_forward_kernel(
    sequences, length, n_ref, w_ref, label_ref, conv_ref, bias_ref, rw_ref, iw_ref, ow_ref,
    partial_ref, product_ref, pre_ref, conv_in_ref, values_ref, recur_ref, inject_ref, decay_ref, states_ref,
    pad, lines, rbig, ibig,
):
    fill_blocks(rbig, rw_ref)
    fill_blocks(ibig, iw_ref)
    pad[0:8, :] = jnp.zeros((8, pad.shape[1]), f32)
    taps = conv_ref.shape[0]
    width = pad.shape[1]
    clear_tail(decay_ref, width)
    clear_tail(states_ref, width)

    def one(s, _):
        base = pl.multiple_of(s * length, length)
        here = pl.ds(base, length)
        rows = n_ref[here, :]
        masks = label_masks(label_ref, here, length, width, taps, lines)
        pre_ref[here, :] = dot_nn(rows, whole_weight(w_ref, 0))
        conv_in = dot_nn(rows, whole_weight(w_ref, 1)).astype(bf16)
        conv_in_ref[here, :] = conv_in
        pad[8 : 8 + length, :] = conv_in.astype(f32)
        total = bias_ref[0:1, :] + conv_ref[0:1, :] * pad[8 : 8 + length, :]
        for k in range(1, taps):
            total = total + conv_ref[k : k + 1, :] * pad[8 - k : 8 - k + length, :] * masks[k - 1]
        values = total.astype(bf16)
        values_ref[here, :] = values
        recur = jax.nn.sigmoid(dot_nn(values, rbig[...].astype(bf16)) + bias_ref[1:2, :])
        inject = jax.nn.sigmoid(dot_nn(values, ibig[...].astype(bf16)) + bias_ref[2:3, :])
        recur_ref[here, :] = recur
        inject_ref[here, :] = inject
        log_decay = -decay_scale * bias_ref[3:4, :] * recur
        inside = masks[0] > 0.5
        put_tiles(decay_ref, here, jnp.where(inside, jnp.exp(log_decay), 0.0))
        scale = jnp.where(inside, jnp.sqrt(minus_expm1(2.0 * log_decay)), 1.0)
        put_tiles(states_ref, here, scale * inject * values.astype(f32))
        return 0

    lax.fori_loop(0, sequences, one, 0)
    seq_scan(decay_ref, states_ref, sequences, length, False)

    def two(s, _):
        base = pl.multiple_of(s * length, length)
        here = pl.ds(base, length)
        act, _unused = gelu_parts(pre_ref[here, :])
        product = (act * get_tiles(states_ref, here, width)).astype(bf16)
        product_ref[here, :] = product
        partial_ref[here, :] = dot_nn(product, ow_ref[...]).astype(bf16)
        return 0

    lax.fori_loop(0, sequences, two, 0)


def mix_forward(sequences, normed, weights, labels, conv, bias, rw, iw, ow):
    total, width = normed.shape[0], weights.shape[3]
    length = total // sequences
    depth = ow.shape[1]
    shape = jax.ShapeDtypeStruct
    like = lambda dt: shape((total, width), dt)
    tiled = shape((-(-width // 128), total, 128), f32)
    return pl.pallas_call(
        functools.partial(mix_forward_kernel, sequences, length),
        out_shape=(
            shape((total, depth), bf16), like(bf16), like(f32), like(bf16), like(bf16), like(f32), like(f32), tiled, tiled,
        ),
        in_specs=[VM] * 8,
        out_specs=[VM] * 9,
        scratch_shapes=[
            pltpu.VMEM((8 + length, width), f32),
            pltpu.VMEM((8 + length, 128), f32),
            pltpu.VMEM((width, width), f32),
            pltpu.VMEM((width, width), f32),
        ],
        compiler_params=pltpu.CompilerParams(vmem_limit_bytes=56 * 2**20),
        cost_estimate=pl.CostEstimate(flops=2 * total * width * 3 * depth, bytes_accessed=20 * 2**20, transcendentals=total * width * 5),
    )(normed, weights, labels, conv, bias, rw, iw, ow)


def mix_backward_kernel(
    sequences, length, mid_ref, ow_ref, w_ref, pre_ref, conv_in_ref, values_ref, recur_ref, inject_ref, decay_ref, states_ref,
    label_ref, conv_ref, bias_ref, rw_ref, iw_ref,
    partial_ref, branch_low_ref, conv_low_ref, dconv_ref, sums_ref, drw_ref, diw_ref,
    adj, pad, lines, rbig, ibig, dr, di,
):
    fill_blocks(rbig, rw_ref)
    fill_blocks(ibig, iw_ref)
    dr[...] = jnp.zeros_like(dr)
    di[...] = jnp.zeros_like(di)
    sums_ref[...] = jnp.zeros_like(sums_ref)
    dconv_ref[...] = jnp.zeros_like(dconv_ref)
    taps = conv_ref.shape[0]
    width = pad.shape[1]
    clear_tail(adj, width)

    def one(s, _):
        base = pl.multiple_of(s * length, length)
        here = pl.ds(base, length)
        product_grad = dot_nt(mid_ref[here, :], ow_ref[...])
        act, slope = gelu_parts(pre_ref[here, :])
        branch_low_ref[here, :] = (product_grad * get_tiles(states_ref, here, width) * slope).astype(bf16)
        put_tiles(adj, here, product_grad * act)
        return 0

    lax.fori_loop(0, sequences, one, 0)
    seq_scan(decay_ref, adj, sequences, length, True)

    def two(s, _):
        base = pl.multiple_of(s * length, length)
        here = pl.ds(base, length)
        adjoint = get_tiles(adj, here, width)
        recur = recur_ref[here, :]
        inject = inject_ref[here, :]
        decay = get_tiles(decay_ref, here, width)
        values = values_ref[here, :]
        values_f = values.astype(f32)
        masks = label_masks(label_ref, here, length, width, taps, lines)
        inside = masks[0] > 0.5
        rate = bias_ref[3:4, :]
        log_decay = -decay_scale * rate * recur
        scale = jnp.where(inside, jnp.sqrt(minus_expm1(2.0 * log_decay)), 1.0)
        pad[0:8, :] = jnp.zeros((8, width), f32)
        pad[8 : 8 + length, :] = get_tiles(states_ref, here, width)
        previous = pad[7 : 7 + length, :]
        driven = adjoint * inject * values_f
        log_grad = jnp.where(inside, adjoint * previous * decay - driven * decay * decay / scale, 0.0)
        recur_low = (log_grad * (-decay_scale * rate) * recur * (1.0 - recur)).astype(bf16)
        inject_low = (driven * scale * (1.0 - inject)).astype(bf16)
        sums_ref[1:2, :] += jnp.sum(recur_low.astype(f32), axis=0, keepdims=True)
        sums_ref[2:3, :] += jnp.sum(inject_low.astype(f32), axis=0, keepdims=True)
        sums_ref[3:4, :] += jnp.sum(log_grad * recur, axis=0, keepdims=True)
        dr[...] += dot_tn(values, recur_low)
        di[...] += dot_tn(values, inject_low)
        grad = adjoint * scale * inject
        grad = grad + dot_nt(recur_low, rbig[...].astype(bf16)) + dot_nt(inject_low, ibig[...].astype(bf16))
        sums_ref[0:1, :] += jnp.sum(grad, axis=0, keepdims=True)
        pad[8 : 8 + length, :] = conv_in_ref[here, :].astype(f32)
        dconv_ref[0:1, :] += jnp.sum(grad * pad[8 : 8 + length, :], axis=0, keepdims=True)
        masked = []
        for k in range(1, taps):
            part = grad * masks[k - 1]
            masked.append(part)
            dconv_ref[k : k + 1, :] += jnp.sum(part * pad[8 - k : 8 - k + length, :], axis=0, keepdims=True)
        total = grad * conv_ref[0:1, :]
        pad[length : length + 8, :] = jnp.zeros((8, width), f32)
        for k in range(1, taps):
            pad[0:length, :] = masked[k - 1] * conv_ref[k : k + 1, :]
            total = total + pad[k : k + length, :]
        conv_low = total.astype(bf16)
        conv_low_ref[here, :] = conv_low
        partial_ref[here, :] = (dot_nt(branch_low_ref[here, :], whole_weight(w_ref, 0)) + dot_nt(conv_low, whole_weight(w_ref, 1))).astype(bf16)
        return 0

    lax.fori_loop(0, sequences, two, 0)
    size = drw_ref.shape[1]
    for h in range(drw_ref.shape[0]):
        cut = slice(h * size, (h + 1) * size)
        drw_ref[h] = dr[cut, cut]
        diw_ref[h] = di[cut, cut]


def mix_backward(sequences, mid_low, ow, weights, pre, conv_in, values, recur, inject, decay, states, labels, conv, bias, rw, iw):
    total, depth = mid_low.shape
    width = ow.shape[0]
    length = total // sequences
    shape = jax.ShapeDtypeStruct
    return pl.pallas_call(
        functools.partial(mix_backward_kernel, sequences, length),
        out_shape=(
            shape((total, depth), bf16), shape((total, width), bf16), shape((total, width), bf16),
            shape(conv.shape, f32), shape((4, width), f32), shape(rw.shape, f32), shape(iw.shape, f32),
        ),
        in_specs=[VM] * 15,
        out_specs=[VM] * 7,
        scratch_shapes=[
            pltpu.VMEM(states.shape, f32),
            pltpu.VMEM((8 + length, width), f32),
            pltpu.VMEM((8 + length, 128), f32),
            pltpu.VMEM((width, width), f32),
            pltpu.VMEM((width, width), f32),
            pltpu.VMEM((width, width), f32),
            pltpu.VMEM((width, width), f32),
        ],
        compiler_params=pltpu.CompilerParams(vmem_limit_bytes=56 * 2**20),
        cost_estimate=pl.CostEstimate(flops=2 * total * width * 3 * depth, bytes_accessed=25 * 2**20, transcendentals=total * width * 5),
    )(mid_low, ow, weights, pre, conv_in, values, recur, inject, decay, states, labels, conv, bias, rw, iw)


def plane():
    halves, shards = lax.axis_size("seq"), lax.axis_size("shard")
    y, s = lax.axis_index("seq"), lax.axis_index("shard")
    offsets = [(dy, ds) for ds in range(0, shards, 2) for dy in range(halves)]

    def at(dy, ds):
        return {"seq": jnp.bitwise_xor(y, dy), "shard": jnp.bitwise_xor(s, ds)}

    def block(dy, ds):
        return jnp.bitwise_xor(s, ds) * halves + jnp.bitwise_xor(y, dy)

    return offsets, at, block


def greet(offsets, at):
    barrier = pltpu.get_barrier_semaphore()
    partners = [(0, 1)] + offsets[1:]
    for dy, ds in partners:
        pl.semaphore_signal(barrier, inc=1, device_id=at(dy, ds), device_id_type=MESH)
    pl.semaphore_wait(barrier, len(partners))


def remote(src, dst, sent, got, device):
    return pltpu.make_async_remote_copy(
        src_ref=src, dst_ref=dst, send_sem=sent, recv_sem=got, device_id=device, device_id_type=MESH
    )


def row_block(ref, index, rows):
    return ref.at[pl.ds(pl.multiple_of(index * rows, rows), rows), :]


def scatter_steps(rows, partial, near, far, stage, acc, sems):
    offsets, at, block = plane()
    near_sent, near_got, far_sent, far_got = sems
    count = len(offsets)
    order = list(range(count - 1, -1, -1))
    firsts = {}
    for q in order:
        dy, ds = offsets[q]
        firsts[q] = remote(
            row_block(partial, block(dy, ds ^ 1), rows), near.at[q], near_sent.at[q], near_got.at[q], at(0, 1)
        )
        firsts[q].start()
    seconds = {}
    for q in order:
        dy, ds = offsets[q]
        firsts[q].wait_recv()
        base = block(dy, ds) * rows

        def tile(i, _):
            step = pl.multiple_of(i * 16, 16)
            here = pl.ds(step, 16)
            total = partial[pl.ds(pl.multiple_of(base + step, 16), 16), :].astype(f32) + near[q, here, :].astype(f32)
            if q:
                stage[q - 1, here, :] = total.astype(bf16)
            else:
                acc[here, :] = total
            return 0

        lax.fori_loop(0, rows // 16, tile, 0)
        if q:
            seconds[q] = remote(stage.at[q - 1], far.at[q - 1], far_sent.at[q - 1], far_got.at[q - 1], at(dy, ds))
            seconds[q].start()
    yield None
    for q in order[:-1]:
        seconds[q].wait_recv()

        def more(i, _):
            here = pl.ds(pl.multiple_of(i * 16, 16), 16)
            acc[here, :] += far[q - 1, here, :].astype(f32)
            return 0

        lax.fori_loop(0, rows // 16, more, 0)
    yield [firsts[q].wait_send for q in order] + [seconds[q].wait_send for q in order[:-1]]


def scatter_sum(*args):
    *_, waits = scatter_steps(*args)
    return waits


def gather_steps(rows, whole, sems):
    offsets, at, block = plane()
    near_sent, near_got, far_sent, far_got = sems
    count = len(offsets)
    own = row_block(whole, block(0, 0), rows)
    sends = []
    outs = {}
    for q in range(count - 1, 0, -1):
        dy, ds = offsets[q]
        outs[q] = remote(own, own, far_sent.at[q - 1], far_got.at[q - 1], at(dy, ds))
        outs[q].start()
        sends.append(outs[q].wait_send)
    hand = remote(own, own, near_sent.at[0], near_got.at[0], at(0, 1))
    hand.start()
    sends.append(hand.wait_send)
    arrivals = [hand.wait_recv]
    yield None
    for q in list(range(1, count)):
        dy, ds = offsets[q]
        outs[q].wait_recv()
        block_q = row_block(whole, block(dy, ds), rows)
        hand = remote(block_q, block_q, near_sent.at[q], near_got.at[q], at(0, 1))
        hand.start()
        sends.append(hand.wait_send)
        arrivals.append(hand.wait_recv)
    yield arrivals + sends


def gather_blocks(*args):
    *_, waits = gather_steps(*args)
    return waits


def root_mean(rows):
    return lax.rsqrt(jnp.mean(rows * rows, axis=-1, keepdims=True) + epsilon)


def norm_backward(grad_unit, unit, inverse):
    return inverse * (grad_unit - unit * jnp.mean(grad_unit * unit, axis=-1, keepdims=True))


def by_tiles(rows, work):
    def tile(i, _):
        work(pl.ds(pl.multiple_of(i * 16, 16), 16), i)
        return 0

    lax.fori_loop(0, rows // 16, tile, 0)


def start_kernel(x_ref, label_ref, unit_ref, labels_ref, *sems):
    rows = x_ref.shape[0]
    offsets, at, block = plane()
    greet(offsets, at)
    base = block(0, 0) * rows

    def unit(here, i):
        value = x_ref[here, :].astype(f32)
        there = pl.ds(pl.multiple_of(base + i * 16, 16), 16)
        unit_ref[there, :] = (value * root_mean(value)).astype(bf16)
        labels_ref[there, :] = label_ref[here, :]

    by_tiles(rows, unit)
    waits = gather_blocks(rows, labels_ref, sems[4:])
    waits = waits + gather_blocks(rows, unit_ref, sems[:4])
    for wait in waits:
        wait()


def forward_kernel(partial, x_ref, unit_ref, middle_ref, near, far, stage, acc, *sems):
    rows = x_ref.shape[0]
    offsets, at, block = plane()
    greet(offsets, at)
    waits = scatter_sum(rows, partial, near, far, stage, acc, sems[:4])
    base = block(0, 0) * rows

    def norm(here, i):
        middle = x_ref[here, :].astype(f32) + acc[here, :]
        middle_ref[here, :] = middle
        there = pl.ds(pl.multiple_of(base + i * 16, 16), 16)
        unit_ref[there, :] = (middle * root_mean(middle)).astype(bf16)

    by_tiles(rows, norm)
    waits = waits + gather_blocks(rows, unit_ref, sems[4:])
    for wait in waits:
        wait()


def backward_steps(partial, middle_ref, cot_ref, low_ref, grad_ref, near, far, stage, acc, *sems):
    rows = middle_ref.shape[0]
    offsets, at, block = plane()
    scatter = scatter_steps(rows, partial, near, far, stage, acc, sems[:4])
    next(scatter)
    yield
    waits = next(scatter)
    base = block(0, 0) * rows

    def norm(here, i):
        middle = middle_ref[here, :]
        inverse = root_mean(middle)
        grad = cot_ref[here, :].astype(f32) + norm_backward(acc[here, :], middle * inverse, inverse)
        grad_ref[here, :] = grad
        there = pl.ds(pl.multiple_of(base + i * 16, 16), 16)
        low_ref[there, :] = grad.astype(bf16)

    by_tiles(rows, norm)
    gather = gather_steps(rows, low_ref, sems[4:])
    next(gather)
    yield
    waits = waits + next(gather)
    yield
    for wait in waits:
        wait()


def last_steps(partial, grad_ref, x_ref, out_ref, near, far, stage, acc, *sems):
    rows = x_ref.shape[0]
    scatter = scatter_steps(rows, partial, near, far, stage, acc, sems[:4])
    next(scatter)
    yield
    waits = next(scatter)

    def norm(here, i):
        value = x_ref[here, :].astype(f32)
        inverse = root_mean(value)
        grad = grad_ref[here, :] + norm_backward(acc[here, :], value * inverse, inverse)
        out_ref[here, :] = grad.astype(bf16)

    by_tiles(rows, norm)
    yield
    for wait in waits:
        wait()


def plane_scratch(rows, depth, gathers, scatters):
    count = lax.axis_size("seq") * lax.axis_size("shard") // 2
    block = (rows, depth)
    scratch = []
    if scatters:
        scratch = [
            pltpu.VMEM((count,) + block, bf16),
            pltpu.VMEM((count - 1,) + block, bf16),
            pltpu.VMEM((count - 1,) + block, bf16),
            pltpu.VMEM(block, f32),
        ]
    for _ in range(scatters + gathers):
        scratch += [pltpu.SemaphoreType.DMA((count,))] * 2 + [pltpu.SemaphoreType.DMA((count - 1,))] * 2
    return scratch


def exchange(kernel, identity, inputs, outs, rows, depth, gathers, scatters):
    return pl.pallas_call(
        kernel,
        out_shape=tuple(jax.ShapeDtypeStruct(shape, kind) for shape, kind in outs),
        in_specs=[VM] * len(inputs),
        out_specs=[VM] * len(outs),
        scratch_shapes=plane_scratch(rows, depth, gathers, scatters),
        compiler_params=pltpu.CompilerParams(
            collective_id=identity, has_side_effects=True, vmem_limit_bytes=40 * 2**20
        ),
        cost_estimate=pl.CostEstimate(flops=10**6, bytes_accessed=60 * 2**20, transcendentals=0),
    )(*inputs)


def pieces(rows, most):
    count = -(-rows // most)
    while rows % count or (rows // count) % 16:
        count += 1
    return count


def line_kernel(n, kinds, cuts, beside, turns, extra, *refs):
    ins = len(cuts)
    made = ins + kinds.count("pair")
    extra_ins, extra_outs, extra_scratch = extra
    refs = list(refs)

    def take(count):
        taken = refs[:count]
        del refs[:count]
        return taken

    own_hbm, side_in = take(ins), take(extra_ins)
    outs, side_out = take(made), take(extra_outs)
    side_scratch, scratch = take(extra_scratch), refs
    own, from_out, from_in = scratch[:ins], scratch[ins : 2 * ins], scratch[2 * ins : 3 * ins]
    columns = [k for k in range(ins) if kinds[k] != "row"]
    swapped = dict(zip(columns, scratch[3 * ins :]))
    load_sem, sent_in, sent_out, got_out, got_in, sent_x, got_x, out_sem = scratch[3 * ins + len(columns) :]
    me = lax.axis_index("replica")
    y, s = lax.axis_index("seq"), lax.axis_index("shard")
    shards = lax.axis_size("shard")
    owners = shards * lax.axis_size("seq")
    left = me < n // 2
    inward = jnp.where(left, me + 1, me - 1)
    outward = jnp.where(left, me - 1, me + 1)
    has_out = jnp.logical_and(me > 0, me < n - 1)
    middle = jnp.logical_or(me == n // 2 - 1, me == n // 2)

    def peer(i):
        return {"seq": jnp.bitwise_xor(y, i // shards), "shard": jnp.bitwise_xor(s, i % shards)}

    def place(i):
        return jnp.bitwise_xor(y, i // shards) * shards + jnp.bitwise_xor(s, i % shards)

    loads = [pltpu.make_async_copy(own_hbm[k], own[k], load_sem.at[k]) for k in range(ins)]
    for load in loads:
        load.start()
    barrier = pltpu.get_barrier_semaphore()
    for i in range(1, owners):
        pl.semaphore_signal(barrier, inc=1, device_id=peer(i), device_id_type=MESH)
    pl.semaphore_signal(barrier, inc=1, device_id={"replica": inward}, device_id_type=MESH)

    @pl.when(has_out)
    def _():
        pl.semaphore_signal(barrier, inc=1, device_id={"replica": outward}, device_id_type=MESH)
        pl.semaphore_wait(barrier, owners + 1)

    @pl.when(jnp.logical_not(has_out))
    def _():
        pl.semaphore_wait(barrier, owners)

    chunks = []
    for k, (lead, count, rows) in enumerate(cuts):
        for step in range(lead):
            for i in range(count):
                chunks.append((k, step if kinds[k] == "row" else (step + 1) % lead, i * rows, rows))
    total = len(chunks)
    ready = set()

    def view(group, c, index=None):
        k, i, start, rows = chunks[c]
        if index is None:
            index = 0 if kinds[k] == "row" else place(i)
        return group[k].at[index, pl.ds(start, rows), :]

    def push(group, target, c, sent, got, device):
        return remote(view(group, c), view(target, c), sent.at[c], got.at[c], {"replica": device})

    def add(target, other, c):
        k, i, start, rows = chunks[c]
        index = 0 if kinds[k] == "row" else place(i)

        def tile(t, _):
            here = pl.ds(pl.multiple_of(start + t * 16, 16), 16)
            both = target[k][index, here, :].astype(f32) + other[k][index, here, :].astype(f32)
            target[k][index, here, :] = both.astype(bf16)
            return 0

        lax.fori_loop(0, rows // 16, tile, 0)

    def pass_in(c):
        @pl.when(middle)
        def _():
            push(own, from_in, c, sent_in, got_in, inward).start()

        @pl.when(jnp.logical_not(middle))
        def _():
            push(own, from_out, c, sent_in, got_out, inward).start()

    def gather_in(c):
        @pl.when(has_out)
        def _():
            if chunks[c][0] not in ready:
                loads[chunks[c][0]].wait()
                ready.add(chunks[c][0])
            push(from_out, from_out, c, sent_in, got_out, inward).wait_recv()
            add(own, from_out, c)
            pass_in(c)

    @pl.when(jnp.logical_not(has_out))
    def _():
        seen = set()
        for c in range(total):
            if chunks[c][0] not in seen:
                loads[chunks[c][0]].wait()
                seen.add(chunks[c][0])
            pass_in(c)

    def crosses(c):
        return kinds[chunks[c][0]] != "row" and chunks[c][1] != 0

    def hand_over(c):
        k, i, start, rows = chunks[c]
        return remote(
            view(from_in, c), view(swapped, c, place(0)), sent_x.at[c], got_x.at[c], peer(i)
        )

    def stores(c):
        k, i, start, rows = chunks[c]
        here = pl.ds(start, rows)
        first = k + kinds[:k].count("pair")
        if kinds[k] == "row":
            return [pltpu.make_async_copy(from_in[k].at[0, here, :], outs[first].at[here, :], out_sem.at[c, 0])]
        source = swapped[k] if i else from_in[k]
        index = place(i)
        if kinds[k] == "side":
            return [pltpu.make_async_copy(source.at[index, here, :], outs[first].at[index, here, :], out_sem.at[c, 0])]
        half = source.shape[2] // 2
        there = pl.ds(pl.multiple_of(index * half, half), half)
        return [
            pltpu.make_async_copy(
                source.at[index, here, pl.ds(part * half, half)], outs[first + part].at[here, there], out_sem.at[c, part]
            )
            for part in range(2)
        ]

    def give_back(c):
        push(own, from_in, c, sent_out, got_in, inward).wait_recv()

        @pl.when(middle)
        def _():
            add(from_in, own, c)

        @pl.when(has_out)
        def _():
            push(from_in, from_in, c, sent_out, got_in, outward).start()

        if crosses(c):
            hand_over(c).start()
        else:
            for copy in stores(c):
                copy.start()

    def finish(c):
        if crosses(c):
            hand_over(c).wait_recv()
            for copy in stores(c):
                copy.start()

    lag, later = 2, 5
    work = beside(*side_in, *side_out, *side_scratch)
    for c in range(total + later):
        for turn in turns:
            if turn == c:
                next(work)
        if c < total:
            gather_in(c)
        if 0 <= c - lag < total:
            give_back(c - lag)
        if 0 <= c - later < total:
            finish(c - later)
    for _ in work:
        pass
    for c in range(total):
        for copy in stores(c):
            copy.wait()
        if crosses(c):
            hand_over(c).wait_send()
        push(own, from_in, c, sent_in, got_in, inward).wait_send()

        @pl.when(has_out)
        def _():
            push(from_in, from_in, c, sent_out, got_in, outward).wait_send()


def replica_sum(arrays, kinds, identity, beside, turns, inputs, results, rows, depth, gathers):
    cuts, outs, swaps = [], [], []
    for item, kind in zip(arrays, kinds):
        lead, height, columns = item.shape
        count = pieces(height, max(16, (210 * 1024) // columns // 16 * 16))
        cuts.append((lead, count, height // count))
        if kind == "pair":
            outs += [jax.ShapeDtypeStruct((height, lead * columns // 2), bf16)] * 2
        elif kind == "side":
            outs.append(jax.ShapeDtypeStruct(item.shape, bf16))
        else:
            outs.append(jax.ShapeDtypeStruct((height, columns), bf16))
        if kind != "row":
            swaps.append(pltpu.VMEM(item.shape, bf16))
    count = sum(lead * cut for lead, cut, _ in cuts)
    buffers = [pltpu.VMEM(item.shape, bf16) for item in arrays]
    side_scratch = plane_scratch(rows, depth, gathers, 1)
    return pl.pallas_call(
        functools.partial(
            line_kernel, lax.axis_size("replica"), tuple(kinds), tuple(cuts), beside, turns,
            (len(inputs), len(results), len(side_scratch)),
        ),
        out_shape=tuple(outs) + tuple(jax.ShapeDtypeStruct(shape, kind) for shape, kind in results),
        in_specs=[ANY] * len(arrays) + [VM] * len(inputs),
        out_specs=[ANY] * len(outs) + [VM] * len(results),
        scratch_shapes=side_scratch
        + buffers * 3
        + swaps
        + [pltpu.SemaphoreType.DMA((len(arrays),))]
        + [pltpu.SemaphoreType.DMA((count,))] * 6
        + [pltpu.SemaphoreType.DMA((count, 2))],
        compiler_params=pltpu.CompilerParams(
            collective_id=identity, has_side_effects=True, vmem_limit_bytes=60 * 2**20
        ),
        cost_estimate=pl.CostEstimate(flops=10**6, bytes_accessed=200 * 2**20, transcendentals=0),
    )(*arrays, *inputs)


def finish_pair_kernel(gain_ref, a_ref, b_ref, wa_ref, wb_ref, outa_ref, outb_ref, grad_ref):
    grad = jnp.zeros(gain_ref.shape, f32)
    for sum_ref, weight_ref, out_ref in ((a_ref, wa_ref, outa_ref), (b_ref, wb_ref, outb_ref)):
        total = sum_ref[...].astype(f32)
        out_ref[...] = total * gain_ref[...]
        grad = grad + jnp.sum(total * low(weight_ref[...]), axis=1, keepdims=True)
    grad_ref[...] = grad


def finish_pair(gain, a, b, wa, wb):
    rows, columns = wa.shape
    cut = min(rows, 32)
    wide = pl.BlockSpec((cut, columns), lambda i: (i, 0))
    thin = pl.BlockSpec((cut, 1), lambda i: (i, 0))
    out = jax.ShapeDtypeStruct((rows, columns), f32)
    return pl.pallas_call(
        finish_pair_kernel,
        grid=(rows // cut,),
        out_shape=(out, out, jax.ShapeDtypeStruct((rows, 1), f32)),
        in_specs=[thin, wide, wide, wide, wide],
        out_specs=[wide, wide, thin],
        compiler_params=pltpu.CompilerParams(vmem_limit_bytes=40 * 2**20),
        cost_estimate=pl.CostEstimate(flops=6 * rows * columns, bytes_accessed=20 * rows * columns, transcendentals=0),
    )(gain, a, b, wa, wb)


def finish_rest_kernel(gain_ref, mix_ref, wa_ref, wb_ref, out_sum_ref, down_sum_ref, outa_ref, outb_ref, grad_ref, out_ref, down_ref):
    owners, _, width = mix_ref.shape
    width = width // 2
    grad = jnp.zeros(gain_ref.shape, f32)
    for part, (weight_ref, target_ref) in enumerate(((wa_ref, outa_ref), (wb_ref, outb_ref))):
        total = jnp.concatenate(
            [mix_ref[j, :, part * width : (part + 1) * width].astype(f32) for j in range(owners)], axis=1
        )
        target_ref[...] = total * gain_ref[...]
        grad = grad + jnp.sum(total * low(weight_ref[...]), axis=1, keepdims=True)
    grad_ref[...] = grad
    out_ref[...] = out_sum_ref[...].astype(f32)
    down_ref[...] = down_sum_ref[...].astype(f32)


def finish_rest(gain, mix, wa, wb, out_sum, down_sum):
    rows, columns = wa.shape
    steps = 4
    while out_sum.shape[0] % (16 * steps) or down_sum.shape[0] % (16 * steps) or rows % (16 * steps):
        steps //= 2

    def tall(item):
        return pl.BlockSpec((item.shape[0] // steps, item.shape[1]), lambda i: (i, 0))

    owners, _, both = mix.shape
    wide, thin = tall(wa), tall(gain)
    return pl.pallas_call(
        finish_rest_kernel,
        grid=(steps,),
        out_shape=(
            jax.ShapeDtypeStruct(wa.shape, f32),
            jax.ShapeDtypeStruct(wa.shape, f32),
            jax.ShapeDtypeStruct((rows, 1), f32),
            jax.ShapeDtypeStruct(out_sum.shape, f32),
            jax.ShapeDtypeStruct(down_sum.shape, f32),
        ),
        in_specs=[
            thin,
            pl.BlockSpec((owners, rows // steps, both), lambda i: (0, i, 0)),
            wide,
            wide,
            tall(out_sum),
            tall(down_sum),
        ],
        out_specs=[wide, wide, thin, tall(out_sum), tall(down_sum)],
        compiler_params=pltpu.CompilerParams(vmem_limit_bytes=40 * 2**20),
        cost_estimate=pl.CostEstimate(flops=10**7, bytes_accessed=40 * 2**20, transcendentals=0),
    )(gain, mix, wa, wb, out_sum, down_sum)


def body(
    tokens,
    segments,
    cotangent,
    norm_gain,
    branch_weight,
    input_weight,
    conv_weight,
    conv_bias,
    recur_gate_weight,
    recur_gate_bias,
    input_gate_weight,
    input_gate_bias,
    decay_param,
    output_weight,
    mlp_norm_gain,
    gate_weight,
    up_weight,
    down_weight,
):
    x, cot = tokens[0], cotangent[0]
    rows, depth = x.shape
    members = lax.axis_size(GROUP)
    sequences = lax.axis_size("shard")
    total = members * rows
    gain, mlp_gain = low(norm_gain)[:, None], low(mlp_norm_gain)[:, None]
    own_labels = jnp.broadcast_to(segments[0].astype(bf16)[:, None], (rows, 128))
    unit_all, labels = exchange(
        start_kernel, 1, (x, own_labels), (((total, depth), bf16), ((total, 128), bf16)), rows, depth, 2, 0
    )
    mix_w = swap(jnp.stack([by_owner(branch_weight, gain), by_owner(input_weight, gain)], 1))
    pair_cut = jnp.concatenate([by_owner(gate_weight, mlp_gain), by_owner(up_weight, mlp_gain)], 2)
    unit_all, pair_cut = lax.optimization_barrier((unit_all, pair_cut))
    pair_w = swap(pair_cut).reshape(depth, -1)
    width = branch_weight.shape[1] // members
    out_low = lax.all_gather(cot, ROWS, axis=0, tiled=True)
    output_w = output_weight.astype(bf16)
    down_w = down_weight.astype(bf16)

    conv_f = low(conv_weight)
    decay_f = low(decay_param)
    bias = jnp.stack([low(conv_bias), low(recur_gate_bias), low(input_gate_bias), jax.nn.softplus(-decay_f)])
    mixed = mix_forward(
        sequences, unit_all, mix_w, labels, conv_f, bias, recur_gate_weight, input_gate_weight, output_w
    )
    partial, product = mixed[:2]
    whole = ((total, depth), bf16)
    unit_two, middle = exchange(
        forward_kernel, 2, (partial, x), (whole, ((rows, depth), f32)), rows, depth, 1, 1
    )
    ff = pair_w.shape[1] // 2
    gate_pre = mm(unit_two, pair_w[:, :ff])
    up_pre = mm(unit_two, pair_w[:, ff:])
    hidden_grad = mm_nt(out_low, down_w)
    gate_act, gate_slope = gelu_parts(gate_pre)
    hidden = (gate_act * up_pre).astype(bf16)
    gate_low = (hidden_grad * up_pre * gate_slope).astype(bf16)
    up_low = (hidden_grad * gate_act).astype(bf16)
    pair_low = jnp.concatenate([gate_low, up_low], 1)
    partial = mm_nt(pair_low, pair_w).astype(bf16)
    pair_partial = mm_tn(unit_two, pair_low).astype(bf16).reshape(members, -1, 2 * ff)
    down_partial = mm_tn(hidden, out_low).astype(bf16)
    gate_sum, up_sum, mid_low, middle_grad = replica_sum(
        [pair_partial], ["pair"], 3, backward_steps, (0, 3, 6),
        (partial, middle, cot), (whole, ((rows, depth), f32)), rows, depth, 1,
    )
    mid_low, down_partial = lax.optimization_barrier((mid_low, down_partial))
    down_sum = lax.psum(down_partial, "replica")
    gate_grad, up_grad, mlp_gain_grad = finish_pair(mlp_gain, gate_sum, up_sum, gate_weight, up_weight)
    block_sum = lax.psum_scatter(mm(hidden, down_w).astype(bf16), ROWS, scatter_dimension=0, tiled=True)
    block_out = (middle + block_sum.astype(f32)).astype(bf16)
    output_partial = mm_tn(product, mid_low).astype(bf16)[None]
    back = mix_backward(
        sequences, mid_low, output_w, mix_w, *mixed[2:], labels, conv_f, bias, recur_gate_weight, input_gate_weight
    )
    partial, branch_low, conv_low, conv_weight_grad, sums, recur_weight_grad, inject_weight_grad = back
    mix_low = jnp.concatenate([branch_low, conv_low], 1)
    mix_partial = mm_tn(unit_all, mix_low).astype(bf16).reshape(members, -1, 2 * width)
    size = recur_gate_weight.shape[1]
    gates = jnp.concatenate([recur_weight_grad, inject_weight_grad], 2).reshape(width, 2 * size)
    lanes = -(-max(width, 2 * size) // 128) * 128
    lines = jnp.concatenate([conv_weight_grad, sums], 0)
    packed = jnp.concatenate(
        [
            jnp.pad(gates, ((0, 0), (0, lanes - 2 * size))),
            jnp.pad(lines, ((0, 16 - lines.shape[0]), (0, lanes - width))),
        ],
        0,
    ).astype(bf16)[None]
    output_sum, mix_sum, packed, tokens_grad = replica_sum(
        [output_partial, mix_partial, packed], ["row", "side", "row"], 4, last_steps, (0, 3),
        (partial, middle_grad, x), (((rows, depth), bf16),), rows, depth, 0,
    )
    packed = packed.astype(f32)
    branch_grad, input_grad, gain_grad, output_grad, down_grad = finish_rest(
        gain, mix_sum, branch_weight, input_weight, output_sum, down_sum
    )
    recur_weight_grad = packed[:width, :size].reshape(-1, size, size)
    inject_weight_grad = packed[:width, size : 2 * size].reshape(-1, size, size)
    conv_weight_grad = packed[width : width + conv_weight.shape[0], :width]
    conv_bias_grad, recur_bias_grad, inject_bias_grad, rate_grad = [packed[width + conv_weight.shape[0] + i, :width] for i in range(4)]
    decay_param_grad = rate_grad * decay_scale * jax.nn.sigmoid(-decay_f)
    return (
        block_out[None],
        tokens_grad[None],
        gain_grad[:, 0],
        branch_grad,
        input_grad,
        conv_weight_grad,
        conv_bias_grad,
        recur_weight_grad,
        recur_bias_grad,
        inject_weight_grad,
        inject_bias_grad,
        decay_param_grad,
        output_grad,
        mlp_gain_grad[:, 0],
        gate_grad,
        up_grad,
        down_grad,
    )


def solution(mesh):
    row3 = P(("shard", "replica"), "seq", None)
    vec = P(("seq", "shard"))
    mat = P(("seq", "shard"), None)
    cube = P(("seq", "shard"), None, None)
    taps = P(None, ("seq", "shard"))
    params = (vec, mat, mat, taps, vec, cube, vec, cube, vec, vec, mat, vec, mat, mat, mat)
    in_specs = (row3, P(("shard", "replica"), "seq"), row3) + params
    out_specs = (row3, row3) + params
    return jax.shard_map(body, mesh=mesh, in_specs=in_specs, out_specs=out_specs, check_vma=False)
```

```python
import functools

import jax
import jax.numpy as jnp
from jax import lax
from jax.experimental import pallas as pl
from jax.experimental.pallas import tpu as pltpu
from jax.sharding import PartitionSpec as P

epsilon = 1e-06
decay_scale = 8.0
GROUP = ("seq", "shard")
ROWS = ("shard", "seq")
f32 = jnp.float32
bf16 = jnp.bfloat16
VM = pl.BlockSpec(memory_space=pltpu.VMEM)
ANY = pl.BlockSpec(memory_space=pl.ANY)
MESH = pl.DeviceIdType.MESH


def mm(left, right):
    return jnp.dot(left, right, preferred_element_type=f32)


def mm_nt(left, right):
    return lax.dot_general(left, right, (((1,), (1,)), ((), ())), preferred_element_type=f32)


def mm_tn(left, right):
    return lax.dot_general(left, right, (((0,), (0,)), ((), ())), preferred_element_type=f32)


def low(item):
    return item.astype(bf16).astype(f32)


def by_owner(weight, gain):
    owners = lax.axis_size(GROUP)
    scaled = (low(weight) * gain).astype(bf16)
    return jnp.swapaxes(scaled.reshape(weight.shape[0], owners, -1), 0, 1)


def swap(cut):
    return lax.all_to_all(cut, GROUP, split_axis=0, concat_axis=0, tiled=True)


def gelu_parts(x):
    inner = 0.7978845608028654 * (x + 0.044715 * x * x * x)
    t = jnp.tanh(inner)
    value = 0.5 * x * (1.0 + t)
    slope = 0.5 * (1.0 + t) + 0.5 * x * (1.0 - t * t) * 0.7978845608028654 * (
        1.0 + 3.0 * 0.044715 * x * x
    )
    return value, slope


def minus_expm1(y):
    poly = 1.0 + y * (1.0 / 8.0)
    for order in (7.0, 6.0, 5.0, 4.0, 3.0, 2.0):
        poly = 1.0 + y * (1.0 / order) * poly
    return jnp.where(y > -0.5, -y * poly, 1.0 - jnp.exp(y))


def dot_nn(a, b):
    return lax.dot_general(a, b, (((1,), (0,)), ((), ())), preferred_element_type=f32)


def dot_nt(a, b):
    return lax.dot_general(a, b, (((1,), (1,)), ((), ())), preferred_element_type=f32)


def dot_tn(a, b):
    return lax.dot_general(a, b, (((0,), (0,)), ((), ())), preferred_element_type=f32)


def whole_weight(ref, part):
    owners, _, rows, width = ref.shape
    return ref[:, part].reshape(owners * rows, width)


def fill_blocks(target, source):
    target[...] = jnp.zeros_like(target)
    count, size = source.shape[0], source.shape[1]
    for h in range(count):
        target[h * size : (h + 1) * size, h * size : (h + 1) * size] = source[h].astype(bf16).astype(f32)


def put_tiles(ref, here, value):
    width = value.shape[1]
    for tile in range(ref.shape[0]):
        lanes = min(128, width - 128 * tile)
        ref[tile, here, 0:lanes] = value[:, 128 * tile : 128 * tile + lanes]


def get_tiles(ref, here, width):
    parts = [ref[tile, here, 0 : min(128, width - 128 * tile)] for tile in range(ref.shape[0])]
    return jnp.concatenate(parts, axis=1)


def clear_tail(ref, width):
    tail = ref.shape[0] * 128 - width
    if tail:
        ref[ref.shape[0] - 1, :, 128 - tail :] = jnp.zeros((ref.shape[1], tail), f32)


def label_masks(label_ref, here, length, width, taps, lines):
    own = label_ref[here, :].astype(f32)
    lines[0:8, :] = jnp.full((8, 128), -1.0, f32)
    lines[8 : 8 + length, :] = own
    masks = []
    for k in range(1, taps):
        same = jnp.where(lines[8 - k : 8 - k + length, :] == own, 1.0, 0.0)
        masks.append(jnp.concatenate([same] * -(-width // 128), axis=1)[:, :width])
    return masks


def seq_scan(decay_ref, value_ref, sequences, length, reverse):
    tiles = decay_ref.shape[0]
    unroll = 8

    def step(i, states):
        states = list(states)
        for j in range(unroll):
            at = i * unroll + j
            if reverse:
                at = length - 1 - at
            here = pl.ds(at, sequences, stride=length)
            for tile in range(tiles):
                value = value_ref[tile, here, :]
                decay = decay_ref[tile, here, :]
                if reverse:
                    new = value + states[tile]
                    value_ref[tile, here, :] = new
                    states[tile] = decay * new
                else:
                    states[tile] = value + decay * states[tile]
                    value_ref[tile, here, :] = states[tile]
        return tuple(states)

    lax.fori_loop(0, length // unroll, step, (jnp.zeros((sequences, 128), f32),) * tiles)


def mix_backward_kernel(
    sequences, length, mid_ref, ow_ref, w_ref, pre_ref, conv_in_ref, values_ref, recur_ref, inject_ref, decay_ref, states_ref,
    label_ref, conv_ref, bias_ref, rw_ref, iw_ref,
    partial_ref, branch_low_ref, conv_low_ref, dconv_ref, sums_ref, drw_ref, diw_ref,
    adj, pad, lines, rbig, ibig, dr, di,
):
    fill_blocks(rbig, rw_ref)
    fill_blocks(ibig, iw_ref)
    dr[...] = jnp.zeros_like(dr)
    di[...] = jnp.zeros_like(di)
    sums_ref[...] = jnp.zeros_like(sums_ref)
    dconv_ref[...] = jnp.zeros_like(dconv_ref)
    taps = conv_ref.shape[0]
    width = pad.shape[1]
    clear_tail(adj, width)

    def one(s, _):
        base = pl.multiple_of(s * length, length)
        here = pl.ds(base, length)
        product_grad = dot_nt(mid_ref[here, :], ow_ref[...])
        act, slope = gelu_parts(pre_ref[here, :])
        branch_low_ref[here, :] = (product_grad * get_tiles(states_ref, here, width) * slope).astype(bf16)
        put_tiles(adj, here, product_grad * act)
        return 0

    lax.fori_loop(0, sequences, one, 0)
    seq_scan(decay_ref, adj, sequences, length, True)

    def two(s, _):
        base = pl.multiple_of(s * length, length)
        here = pl.ds(base, length)
        adjoint = get_tiles(adj, here, width)
        recur = recur_ref[here, :]
        inject = inject_ref[here, :]
        decay = get_tiles(decay_ref, here, width)
        values = values_ref[here, :]
        values_f = values.astype(f32)
        masks = label_masks(label_ref, here, length, width, taps, lines)
        inside = masks[0] > 0.5
        rate = bias_ref[3:4, :]
        log_decay = -decay_scale * rate * recur
        scale = jnp.where(inside, jnp.sqrt(minus_expm1(2.0 * log_decay)), 1.0)
        pad[0:8, :] = jnp.zeros((8, width), f32)
        pad[8 : 8 + length, :] = get_tiles(states_ref, here, width)
        previous = pad[7 : 7 + length, :]
        driven = adjoint * inject * values_f
        log_grad = jnp.where(inside, adjoint * previous * decay - driven * decay * decay / scale, 0.0)
        recur_low = (log_grad * (-decay_scale * rate) * recur * (1.0 - recur)).astype(bf16)
        inject_low = (driven * scale * (1.0 - inject)).astype(bf16)
        sums_ref[1:2, :] += jnp.sum(recur_low.astype(f32), axis=0, keepdims=True)
        sums_ref[2:3, :] += jnp.sum(inject_low.astype(f32), axis=0, keepdims=True)
        sums_ref[3:4, :] += jnp.sum(log_grad * recur, axis=0, keepdims=True)
        dr[...] += dot_tn(values, recur_low)
        di[...] += dot_tn(values, inject_low)
        grad = adjoint * scale * inject
        grad = grad + dot_nt(recur_low, rbig[...].astype(bf16)) + dot_nt(inject_low, ibig[...].astype(bf16))
        sums_ref[0:1, :] += jnp.sum(grad, axis=0, keepdims=True)
        pad[8 : 8 + length, :] = conv_in_ref[here, :].astype(f32)
        dconv_ref[0:1, :] += jnp.sum(grad * pad[8 : 8 + length, :], axis=0, keepdims=True)
        masked = []
        for k in range(1, taps):
            part = grad * masks[k - 1]
            masked.append(part)
            dconv_ref[k : k + 1, :] += jnp.sum(part * pad[8 - k : 8 - k + length, :], axis=0, keepdims=True)
        total = grad * conv_ref[0:1, :]
        pad[length : length + 8, :] = jnp.zeros((8, width), f32)
        for k in range(1, taps):
            pad[0:length, :] = masked[k - 1] * conv_ref[k : k + 1, :]
            total = total + pad[k : k + length, :]
        conv_low = total.astype(bf16)
        conv_low_ref[here, :] = conv_low
        partial_ref[here, :] = (dot_nt(branch_low_ref[here, :], whole_weight(w_ref, 0)) + dot_nt(conv_low, whole_weight(w_ref, 1))).astype(bf16)
        return 0

    lax.fori_loop(0, sequences, two, 0)
    size = drw_ref.shape[1]
    for h in range(drw_ref.shape[0]):
        cut = slice(h * size, (h + 1) * size)
        drw_ref[h] = dr[cut, cut]
        diw_ref[h] = di[cut, cut]


def mix_backward(sequences, mid_low, ow, weights, pre, conv_in, values, recur, inject, decay, states, labels, conv, bias, rw, iw):
    total, depth = mid_low.shape
    width = ow.shape[0]
    length = total // sequences
    shape = jax.ShapeDtypeStruct
    return pl.pallas_call(
        functools.partial(mix_backward_kernel, sequences, length),
        out_shape=(
            shape((total, depth), bf16), shape((total, width), bf16), shape((total, width), bf16),
            shape(conv.shape, f32), shape((4, width), f32), shape(rw.shape, f32), shape(iw.shape, f32),
        ),
        in_specs=[VM] * 15,
        out_specs=[VM] * 7,
        scratch_shapes=[
            pltpu.VMEM(states.shape, f32),
            pltpu.VMEM((8 + length, width), f32),
            pltpu.VMEM((8 + length, 128), f32),
            pltpu.VMEM((width, width), f32),
            pltpu.VMEM((width, width), f32),
            pltpu.VMEM((width, width), f32),
            pltpu.VMEM((width, width), f32),
        ],
        compiler_params=pltpu.CompilerParams(vmem_limit_bytes=56 * 2**20),
        cost_estimate=pl.CostEstimate(flops=2 * total * width * 3 * depth, bytes_accessed=25 * 2**20, transcendentals=total * width * 5),
    )(mid_low, ow, weights, pre, conv_in, values, recur, inject, decay, states, labels, conv, bias, rw, iw)


def plane():
    halves, shards = lax.axis_size("seq"), lax.axis_size("shard")
    y, s = lax.axis_index("seq"), lax.axis_index("shard")
    offsets = [(dy, ds) for ds in range(0, shards, 2) for dy in range(halves)]

    def at(dy, ds):
        return {"seq": jnp.bitwise_xor(y, dy), "shard": jnp.bitwise_xor(s, ds)}

    def block(dy, ds):
        return jnp.bitwise_xor(s, ds) * halves + jnp.bitwise_xor(y, dy)

    return offsets, at, block


def remote(src, dst, sent, got, device):
    return pltpu.make_async_remote_copy(
        src_ref=src, dst_ref=dst, send_sem=sent, recv_sem=got, device_id=device, device_id_type=MESH
    )


def row_block(ref, index, rows):
    return ref.at[pl.ds(pl.multiple_of(index * rows, rows), rows), :]


def scatter_steps(rows, partial, near, far, acc, sems):
    offsets, at, block = plane()
    near_sent, near_got, far_sent, far_got = sems
    count = len(offsets)
    order = list(range(count - 1, -1, -1))
    firsts = {}
    for q in order:
        dy, ds = offsets[q]
        firsts[q] = remote(
            row_block(partial, block(dy, ds ^ 1), rows), near.at[q], near_sent.at[q], near_got.at[q], at(0, 1)
        )
        firsts[q].start()
    seconds = {}
    for q in order:
        dy, ds = offsets[q]
        firsts[q].wait_recv()
        base = block(dy, ds) * rows

        def tile(i, _):
            step = pl.multiple_of(i * 16, 16)
            here = pl.ds(step, 16)
            total = partial[pl.ds(pl.multiple_of(base + step, 16), 16), :].astype(f32) + near[q, here, :].astype(f32)
            if q:
                near[q, here, :] = total.astype(bf16)
            else:
                acc[here, :] = total
            return 0

        lax.fori_loop(0, rows // 16, tile, 0)
        if q:
            seconds[q] = remote(near.at[q], far.at[q - 1], far_sent.at[q - 1], far_got.at[q - 1], at(dy, ds))
            seconds[q].start()
    yield None
    for q in order[:-1]:
        seconds[q].wait_recv()

        def more(i, _):
            here = pl.ds(pl.multiple_of(i * 16, 16), 16)
            acc[here, :] += far[q - 1, here, :].astype(f32)
            return 0

        lax.fori_loop(0, rows // 16, more, 0)
    yield [firsts[q].wait_send for q in order] + [seconds[q].wait_send for q in order[:-1]]


def gather_steps(rows, whole, sems):
    offsets, at, block = plane()
    near_sent, near_got, far_sent, far_got = sems
    count = len(offsets)
    own = row_block(whole, block(0, 0), rows)
    sends = []
    outs = {}
    for q in range(count - 1, 0, -1):
        dy, ds = offsets[q]
        outs[q] = remote(own, own, far_sent.at[q - 1], far_got.at[q - 1], at(dy, ds))
        outs[q].start()
        sends.append(outs[q].wait_send)
    hand = remote(own, own, near_sent.at[0], near_got.at[0], at(0, 1))
    hand.start()
    sends.append(hand.wait_send)
    arrivals = [hand.wait_recv]
    yield None
    for q in list(range(1, count)):
        dy, ds = offsets[q]
        outs[q].wait_recv()
        block_q = row_block(whole, block(dy, ds), rows)
        hand = remote(block_q, block_q, near_sent.at[q], near_got.at[q], at(0, 1))
        hand.start()
        sends.append(hand.wait_send)
        arrivals.append(hand.wait_recv)
    yield arrivals + sends


def root_mean(rows):
    return lax.rsqrt(jnp.mean(rows * rows, axis=-1, keepdims=True) + epsilon)


def norm_backward(grad_unit, unit, inverse):
    return inverse * (grad_unit - unit * jnp.mean(grad_unit * unit, axis=-1, keepdims=True))


def by_tiles(rows, work):
    def tile(i, _):
        work(pl.ds(pl.multiple_of(i * 16, 16), 16), i)
        return 0

    lax.fori_loop(0, rows // 16, tile, 0)


def backward_steps(partial, middle_ref, cot_ref, low_ref, grad_ref, near, far, acc, *sems):
    rows = middle_ref.shape[0]
    offsets, at, block = plane()
    scatter = scatter_steps(rows, partial, near, far, acc, sems[:4])
    next(scatter)
    yield
    waits = next(scatter)
    base = block(0, 0) * rows

    def norm(here, i):
        middle = middle_ref[here, :]
        inverse = root_mean(middle)
        grad = cot_ref[here, :].astype(f32) + norm_backward(acc[here, :], middle * inverse, inverse)
        grad_ref[here, :] = grad
        there = pl.ds(pl.multiple_of(base + i * 16, 16), 16)
        low_ref[there, :] = grad.astype(bf16)

    by_tiles(rows, norm)
    gather = gather_steps(rows, low_ref, sems[4:])
    next(gather)
    yield
    waits = waits + next(gather)
    yield
    for wait in waits:
        wait()


def last_steps(partial, grad_ref, x_ref, out_ref, near, far, acc, *sems):
    rows = x_ref.shape[0]
    scatter = scatter_steps(rows, partial, near, far, acc, sems[:4])
    next(scatter)
    yield
    waits = next(scatter)

    def norm(here, i):
        value = x_ref[here, :].astype(f32)
        inverse = root_mean(value)
        grad = grad_ref[here, :] + norm_backward(acc[here, :], value * inverse, inverse)
        out_ref[here, :] = grad.astype(bf16)

    by_tiles(rows, norm)
    yield
    for wait in waits:
        wait()


def plane_scratch(rows, depth, gathers, scatters):
    count = lax.axis_size("seq") * lax.axis_size("shard") // 2
    block = (rows, depth)
    scratch = []
    if scatters:
        scratch = [
            pltpu.VMEM((count,) + block, bf16),
            pltpu.VMEM((count - 1,) + block, bf16),
            pltpu.VMEM(block, f32),
        ]
    for _ in range(scatters + gathers):
        scratch += [pltpu.SemaphoreType.DMA((count,))] * 2 + [pltpu.SemaphoreType.DMA((count - 1,))] * 2
    return scratch


def cut_columns(weight_ref, gain, target, start, lanes):
    owners = weight_ref.shape[1] // lanes

    def tile(i, _):
        step = pl.multiple_of(i * 16, 16)
        here = pl.ds(step, 16)
        scaled = low(weight_ref[here, :]) * gain(step)
        for j in range(owners):
            target(j)[here, start : start + lanes] = scaled[:, j * lanes : (j + 1) * lanes].astype(bf16)
        return 0

    lax.fori_loop(0, weight_ref.shape[0] // 16, tile, 0)


def quarter_steps(n, part, whole, sems):
    me = lax.axis_index("replica")
    right_sent, right_got, left_sent, left_got = sems

    def rows(q):
        return whole.at[:, pl.ds(pl.multiple_of(q * part, 16), part), :]

    def to_right(hop):
        block = rows(me - hop)
        return remote(block, block, right_sent.at[hop], right_got.at[hop], {"replica": me + 1})

    def to_left(hop):
        block = rows(me + hop)
        return remote(block, block, left_sent.at[hop], left_got.at[hop], {"replica": me - 1})

    def from_left(hop):
        block = rows(me - hop - 1)
        return remote(block, block, right_sent.at[hop], right_got.at[hop], {"replica": me + 1})

    def from_right(hop):
        block = rows(me + hop + 1)
        return remote(block, block, left_sent.at[hop], left_got.at[hop], {"replica": me - 1})

    for hop in range(n - 1):
        if hop:

            @pl.when(me >= hop)
            def _():
                from_left(hop - 1).wait_recv()

            @pl.when(me + hop < n)
            def _():
                from_right(hop - 1).wait_recv()

        @pl.when(jnp.logical_and(me >= hop, me < n - 1))
        def _():
            to_right(hop).start()

        @pl.when(jnp.logical_and(me + hop < n, me > 0))
        def _():
            to_left(hop).start()

        yield

    @pl.when(me >= n - 1)
    def _():
        from_left(n - 2).wait_recv()

    @pl.when(me + n - 1 < n)
    def _():
        from_right(n - 2).wait_recv()

    for hop in range(n - 1):

        @pl.when(jnp.logical_and(me >= hop, me < n - 1))
        def _():
            to_right(hop).wait_send()

        @pl.when(jnp.logical_and(me + hop < n, me > 0))
        def _():
            to_left(hop).wait_send()

    yield


def front_kernel(
    n, sequences, length,
    x_ref, label_ref, cot_ref, gains_ref, conv_ref, bias_ref, rw_ref, iw_ref,
    branch_hbm, input_hbm, gate_hbm, up_hbm, ow_hbm,
    unit_out, labels_out, low_out, product_out, pre_out, conv_in_out, values_out, recur_out, inject_out, decay_out,
    states_out, mix_out, ow_out, two_out, middle_out, pair_out,
    unit_ref, labels_ref, product_ref, pre_ref, conv_in_ref, values_ref, recur_ref, inject_ref, decay_ref,
    states_ref, mix_ref, ow_ref, two_ref, middle_ref,
    wide, tall, ow_f, mix_cut, pair_cut, pad, lines, rbig, ibig, partial,
    near, far, acc, *sems,
):
    rows = x_ref.shape[0]
    scatter_sems, sems = sems[:4], sems[4:]
    unit_sems, label_sems, low_sems, two_sems, sems = sems[:4], sems[4:8], sems[8:12], sems[12:16], sems[16:]
    load_sem, save_sem, mix_sent, mix_got, pair_sent, pair_got = sems[:6]
    line_sems = sems[6:]
    offsets, at, block = plane()
    z = lax.axis_index("replica")
    y, s = lax.axis_index("seq"), lax.axis_index("shard")
    shards = lax.axis_size("shard")
    owners = shards * lax.axis_size("seq")
    part = gate_hbm.shape[0] // n
    width = pad.shape[1]
    ff = gate_hbm.shape[1] // owners

    def peer(i):
        return {"seq": jnp.bitwise_xor(y, i // shards), "shard": jnp.bitwise_xor(s, i % shards)}

    def place(i):
        return jnp.bitwise_xor(y, i // shards) * shards + jnp.bitwise_xor(s, i % shards)

    own_rows = pl.ds(pl.multiple_of(z * part, 16), part)
    loads = [
        pltpu.make_async_copy(gate_hbm.at[own_rows, :], tall.at[0], load_sem.at[0]),
        pltpu.make_async_copy(up_hbm.at[own_rows, :], tall.at[1], load_sem.at[1]),
        pltpu.make_async_copy(branch_hbm, wide.at[0], load_sem.at[2]),
        pltpu.make_async_copy(input_hbm, wide.at[1], load_sem.at[3]),
        pltpu.make_async_copy(ow_hbm, ow_f, load_sem.at[4]),
    ]
    for load in loads:
        load.start()
    saves = []

    def save(source, target):
        copy = pltpu.make_async_copy(source, target, save_sem.at[len(saves)])
        copy.start()
        saves.append(copy)

    low_own = pltpu.make_async_copy(cot_ref, row_block(low_out, block(0, 0), rows), load_sem.at[5])
    low_own.start()
    barrier = pltpu.get_barrier_semaphore()
    for i in range(1, owners):
        pl.semaphore_signal(barrier, inc=1, device_id=peer(i), device_id_type=MESH)

    @pl.when(z > 0)
    def _():
        pl.semaphore_signal(barrier, inc=1, device_id={"replica": z - 1}, device_id_type=MESH)

    @pl.when(z < n - 1)
    def _():
        pl.semaphore_signal(barrier, inc=1, device_id={"replica": z + 1}, device_id_type=MESH)

    base = block(0, 0) * rows

    def unit(here, i):
        value = x_ref[here, :].astype(f32)
        there = pl.ds(pl.multiple_of(base + i * 16, 16), 16)
        unit_ref[there, :] = (value * root_mean(value)).astype(bf16)
        labels_ref[there, :] = label_ref[here, :]

    by_tiles(rows, unit)
    inside_line = jnp.logical_and(z > 0, z < n - 1)

    @pl.when(inside_line)
    def _():
        pl.semaphore_wait(barrier, owners + 1)

    @pl.when(jnp.logical_not(inside_line))
    def _():
        pl.semaphore_wait(barrier, owners)

    label_gather = gather_steps(rows, labels_ref, label_sems)
    unit_gather = gather_steps(rows, unit_ref, unit_sems)
    next(label_gather)
    next(unit_gather)

    for side in range(2):
        loads[side].wait()

        cut_columns(
            tall.at[side],
            lambda step: gains_ref[pl.ds(pl.multiple_of(z * part + step, 16), 16), 1:2],
            lambda j: pair_cut.at[j],
            side * ff,
            ff,
        )
    me = place(0)
    pair_there = pair_out.at[me, own_rows, :]
    pair_moves = [
        remote(pair_cut.at[place(i)], pair_there, pair_sent.at[i], pair_got.at[i], peer(i)) for i in range(1, owners)
    ]
    for move in pair_moves:
        move.start()
    pair_own = pltpu.make_async_copy(pair_cut.at[me], pair_there, pair_sent.at[0])
    pair_own.start()

    for side in range(2):
        loads[2 + side].wait()
        cut_columns(
            wide.at[side], lambda step: gains_ref[pl.ds(step, 16), 0:1], lambda j: mix_cut.at[j, side], 0, width
        )
    mix_moves = [
        remote(mix_cut.at[place(i)], mix_ref.at[me], mix_sent.at[i], mix_got.at[i], peer(i)) for i in range(1, owners)
    ]
    for move in mix_moves:
        move.start()
    mix_own = pltpu.make_async_copy(mix_cut.at[me], mix_ref.at[me], mix_sent.at[0])
    mix_own.start()
    loads[4].wait()
    ow_ref[...] = ow_f[...].astype(bf16)
    save(ow_ref, ow_out)
    fill_blocks(rbig, rw_ref)
    fill_blocks(ibig, iw_ref)
    pad[0:8, :] = jnp.zeros((8, width), f32)
    taps = conv_ref.shape[0]
    clear_tail(decay_ref, width)
    clear_tail(states_ref, width)

    waits = next(label_gather)
    waits = waits + next(unit_gather)
    pair_own.wait()
    for move in pair_moves:
        move.wait_recv()
    line = quarter_steps(n, part, pair_out, line_sems)
    next(line)
    for wait in waits:
        wait()
    mix_own.wait()
    for move in mix_moves:
        move.wait_recv()
    save(unit_ref, unit_out)
    save(labels_ref, labels_out)
    save(mix_ref, mix_out)

    low_own.wait()
    low_gather = gather_steps(rows, low_out, low_sems)
    next(low_gather)

    def one(q, _):
        here = pl.ds(pl.multiple_of(q * length, length), length)
        sequence = unit_ref[here, :]
        masks = label_masks(labels_ref, here, length, width, taps, lines)
        pre_ref[here, :] = dot_nn(sequence, whole_weight(mix_ref, 0))
        conv_in = dot_nn(sequence, whole_weight(mix_ref, 1)).astype(bf16)
        conv_in_ref[here, :] = conv_in
        pad[8 : 8 + length, :] = conv_in.astype(f32)
        total = bias_ref[0:1, :] + conv_ref[0:1, :] * pad[8 : 8 + length, :]
        for k in range(1, taps):
            total = total + conv_ref[k : k + 1, :] * pad[8 - k : 8 - k + length, :] * masks[k - 1]
        values = total.astype(bf16)
        values_ref[here, :] = values
        recur = jax.nn.sigmoid(dot_nn(values, rbig[...].astype(bf16)) + bias_ref[1:2, :])
        inject = jax.nn.sigmoid(dot_nn(values, ibig[...].astype(bf16)) + bias_ref[2:3, :])
        recur_ref[here, :] = recur
        inject_ref[here, :] = inject
        log_decay = -decay_scale * bias_ref[3:4, :] * recur
        inside = masks[0] > 0.5
        put_tiles(decay_ref, here, jnp.where(inside, jnp.exp(log_decay), 0.0))
        scale = jnp.where(inside, jnp.sqrt(minus_expm1(2.0 * log_decay)), 1.0)
        put_tiles(states_ref, here, scale * inject * values.astype(f32))
        return 0

    lax.fori_loop(0, sequences, one, 0)
    seq_scan(decay_ref, states_ref, sequences, length, False)

    def two(q, _):
        here = pl.ds(pl.multiple_of(q * length, length), length)
        act, _unused = gelu_parts(pre_ref[here, :])
        product = (act * get_tiles(states_ref, here, width)).astype(bf16)
        product_ref[here, :] = product
        partial[here, :] = dot_nn(product, ow_ref[...]).astype(bf16)
        return 0

    lax.fori_loop(0, sequences, two, 0)
    scatter = scatter_steps(rows, partial, near, far, acc, scatter_sems)
    next(scatter)
    for source, target in (
        (product_ref, product_out), (pre_ref, pre_out), (conv_in_ref, conv_in_out), (values_ref, values_out),
        (recur_ref, recur_out), (inject_ref, inject_out), (decay_ref, decay_out), (states_ref, states_out),
    ):
        save(source, target)
    next(line)
    waits = next(low_gather)
    waits = waits + next(scatter)

    def norm(here, i):
        middle = x_ref[here, :].astype(f32) + acc[here, :]
        middle_ref[here, :] = middle
        there = pl.ds(pl.multiple_of(base + i * 16, 16), 16)
        two_ref[there, :] = (middle * root_mean(middle)).astype(bf16)

    by_tiles(rows, norm)
    two_gather = gather_steps(rows, two_ref, two_sems)
    next(two_gather)
    save(middle_ref, middle_out)
    for _ in range(n - 3):
        next(line)
    for wait in waits:
        wait()
    waits = next(two_gather)
    for wait in waits:
        wait()
    save(two_ref, two_out)
    for _ in line:
        pass
    for move in pair_moves + mix_moves:
        move.wait_send()
    for copy in saves:
        copy.wait()


def front(sequences, x, label, cot, gains, conv, bias, rw, iw, branch_w, input_w, gate_w, up_w, output_w):
    rows, depth = x.shape
    own, n = branch_w.shape[0], lax.axis_size("replica")
    owners = lax.axis_size(GROUP)
    total, width, ff = owners * rows, branch_w.shape[1] // owners, gate_w.shape[1] // owners
    part = own // n
    length = total // sequences
    tiles = -(-width // 128)
    kept = [
        ((total, depth), bf16), ((total, 128), bf16), ((total, depth), bf16), ((total, width), bf16),
        ((total, width), f32), ((total, width), bf16), ((total, width), bf16), ((total, width), f32),
        ((total, width), f32), ((tiles, total, 128), f32), ((tiles, total, 128), f32), ((owners, 2, own, width), bf16),
        ((width, depth), bf16), ((total, depth), bf16), ((rows, depth), f32),
    ]
    vm = pltpu.VMEM
    dma = pltpu.SemaphoreType.DMA
    scratch = [vm(*item) for k, item in enumerate(kept) if k != 2] + [
        vm((2,) + branch_w.shape, f32),
        vm((2, part, gate_w.shape[1]), f32),
        vm(output_w.shape, f32),
        vm((owners, 2, own, width), bf16),
        vm((owners, part, 2 * ff), bf16),
        vm((8 + length, width), f32),
        vm((8 + length, 128), f32),
        vm((width, width), f32),
        vm((width, width), f32),
        vm((total, depth), bf16),
    ]
    scratch += plane_scratch(rows, depth, 4, 1)
    scratch += [dma((6,)), dma((len(kept),))] + [dma((owners,))] * 4 + [dma((n - 1,))] * 4
    outs = kept + [((owners, own, 2 * ff), bf16)]
    return pl.pallas_call(
        functools.partial(front_kernel, n, sequences, length),
        out_shape=tuple(jax.ShapeDtypeStruct(*item) for item in outs),
        in_specs=[VM] * 8 + [ANY] * 5,
        out_specs=[ANY] * len(outs),
        scratch_shapes=scratch,
        compiler_params=pltpu.CompilerParams(
            collective_id=1, has_side_effects=True, vmem_limit_bytes=60 * 2**20
        ),
        cost_estimate=pl.CostEstimate(flops=10**6, bytes_accessed=200 * 2**20, transcendentals=0),
    )(x, label, cot, gains, conv, bias, rw, iw, branch_w, input_w, gate_w, up_w, output_w)


def pieces(rows, most):
    count = -(-rows // most)
    while rows % count or (rows // count) % 16:
        count += 1
    return count


def line_kernel(n, kinds, cuts, beside, turns, extra, *refs):
    ins = len(cuts)
    made = ins + kinds.count("pair")
    extra_ins, extra_outs, extra_scratch = extra
    refs = list(refs)

    def take(count):
        taken = refs[:count]
        del refs[:count]
        return taken

    own_hbm, side_in = take(ins), take(extra_ins)
    outs, side_out = take(made), take(extra_outs)
    side_scratch, scratch = take(extra_scratch), refs
    own, from_out, from_in = scratch[:ins], scratch[ins : 2 * ins], scratch[2 * ins : 3 * ins]
    columns = [k for k in range(ins) if kinds[k] != "row"]
    swapped = dict(zip(columns, scratch[3 * ins :]))
    load_sem, sent_in, sent_out, got_out, got_in, sent_x, got_x, out_sem = scratch[3 * ins + len(columns) :]
    me = lax.axis_index("replica")
    y, s = lax.axis_index("seq"), lax.axis_index("shard")
    shards = lax.axis_size("shard")
    owners = shards * lax.axis_size("seq")
    left = me < n // 2
    inward = jnp.where(left, me + 1, me - 1)
    outward = jnp.where(left, me - 1, me + 1)
    has_out = jnp.logical_and(me > 0, me < n - 1)
    middle = jnp.logical_or(me == n // 2 - 1, me == n // 2)

    def peer(i):
        return {"seq": jnp.bitwise_xor(y, i // shards), "shard": jnp.bitwise_xor(s, i % shards)}

    def place(i):
        return jnp.bitwise_xor(y, i // shards) * shards + jnp.bitwise_xor(s, i % shards)

    loads = [pltpu.make_async_copy(own_hbm[k], own[k], load_sem.at[k]) for k in range(ins)]
    for load in loads:
        load.start()
    barrier = pltpu.get_barrier_semaphore()
    for i in range(1, owners):
        pl.semaphore_signal(barrier, inc=1, device_id=peer(i), device_id_type=MESH)
    pl.semaphore_signal(barrier, inc=1, device_id={"replica": inward}, device_id_type=MESH)

    @pl.when(has_out)
    def _():
        pl.semaphore_signal(barrier, inc=1, device_id={"replica": outward}, device_id_type=MESH)
        pl.semaphore_wait(barrier, owners + 1)

    @pl.when(jnp.logical_not(has_out))
    def _():
        pl.semaphore_wait(barrier, owners)

    chunks = []
    for k, (lead, count, rows) in enumerate(cuts):
        for step in range(lead):
            for i in range(count):
                chunks.append((k, step if kinds[k] == "row" else (step + 1) % lead, i * rows, rows))
    total = len(chunks)
    ready = set()

    def view(group, c, index=None):
        k, i, start, rows = chunks[c]
        if index is None:
            index = 0 if kinds[k] == "row" else place(i)
        return group[k].at[index, pl.ds(start, rows), :]

    def push(group, target, c, sent, got, device):
        return remote(view(group, c), view(target, c), sent.at[c], got.at[c], {"replica": device})

    def add(target, other, c):
        k, i, start, rows = chunks[c]
        index = 0 if kinds[k] == "row" else place(i)

        def tile(t, _):
            here = pl.ds(pl.multiple_of(start + t * 16, 16), 16)
            both = target[k][index, here, :].astype(f32) + other[k][index, here, :].astype(f32)
            target[k][index, here, :] = both.astype(bf16)
            return 0

        lax.fori_loop(0, rows // 16, tile, 0)

    def pass_in(c):
        @pl.when(middle)
        def _():
            push(own, from_in, c, sent_in, got_in, inward).start()

        @pl.when(jnp.logical_not(middle))
        def _():
            push(own, from_out, c, sent_in, got_out, inward).start()

    def gather_in(c):
        @pl.when(has_out)
        def _():
            if chunks[c][0] not in ready:
                loads[chunks[c][0]].wait()
                ready.add(chunks[c][0])
            push(from_out, from_out, c, sent_in, got_out, inward).wait_recv()
            add(own, from_out, c)
            pass_in(c)

    @pl.when(jnp.logical_not(has_out))
    def _():
        seen = set()
        for c in range(total):
            if chunks[c][0] not in seen:
                loads[chunks[c][0]].wait()
                seen.add(chunks[c][0])
            pass_in(c)

    def crosses(c):
        return kinds[chunks[c][0]] != "row" and chunks[c][1] != 0

    def hand_over(c):
        k, i, start, rows = chunks[c]
        return remote(
            view(from_in, c), view(swapped, c, place(0)), sent_x.at[c], got_x.at[c], peer(i)
        )

    def stores(c):
        k, i, start, rows = chunks[c]
        here = pl.ds(start, rows)
        first = k + kinds[:k].count("pair")
        if kinds[k] == "row":
            return [pltpu.make_async_copy(from_in[k].at[0, here, :], outs[first].at[here, :], out_sem.at[c, 0])]
        source = swapped[k] if i else from_in[k]
        index = place(i)
        if kinds[k] == "side":
            return [pltpu.make_async_copy(source.at[index, here, :], outs[first].at[index, here, :], out_sem.at[c, 0])]
        half = source.shape[2] // 2
        there = pl.ds(pl.multiple_of(index * half, half), half)
        return [
            pltpu.make_async_copy(
                source.at[index, here, pl.ds(part * half, half)], outs[first + part].at[here, there], out_sem.at[c, part]
            )
            for part in range(2)
        ]

    def give_back(c):
        push(own, from_in, c, sent_out, got_in, inward).wait_recv()

        @pl.when(middle)
        def _():
            add(from_in, own, c)

        @pl.when(has_out)
        def _():
            push(from_in, from_in, c, sent_out, got_in, outward).start()

        if crosses(c):
            hand_over(c).start()
        else:
            for copy in stores(c):
                copy.start()

    def finish(c):
        if crosses(c):
            hand_over(c).wait_recv()
            for copy in stores(c):
                copy.start()

    lag, later = 2, 5
    work = beside(*side_in, *side_out, *side_scratch)
    for c in range(total + later):
        for turn in turns:
            if turn == c:
                next(work)
        if c < total:
            gather_in(c)
        if 0 <= c - lag < total:
            give_back(c - lag)
        if 0 <= c - later < total:
            finish(c - later)
    for _ in work:
        pass
    for c in range(total):
        for copy in stores(c):
            copy.wait()
        if crosses(c):
            hand_over(c).wait_send()
        push(own, from_in, c, sent_in, got_in, inward).wait_send()

        @pl.when(has_out)
        def _():
            push(from_in, from_in, c, sent_out, got_in, outward).wait_send()


def replica_sum(arrays, kinds, identity, beside, turns, inputs, results, rows, depth, gathers):
    cuts, outs, swaps = [], [], []
    for item, kind in zip(arrays, kinds):
        lead, height, columns = item.shape
        count = pieces(height, max(16, (210 * 1024) // columns // 16 * 16))
        cuts.append((lead, count, height // count))
        if kind == "pair":
            outs += [jax.ShapeDtypeStruct((height, lead * columns // 2), bf16)] * 2
        elif kind == "side":
            outs.append(jax.ShapeDtypeStruct(item.shape, bf16))
        else:
            outs.append(jax.ShapeDtypeStruct((height, columns), bf16))
        if kind != "row":
            swaps.append(pltpu.VMEM(item.shape, bf16))
    count = sum(lead * cut for lead, cut, _ in cuts)
    buffers = [pltpu.VMEM(item.shape, bf16) for item in arrays]
    side_scratch = plane_scratch(rows, depth, gathers, 1)
    return pl.pallas_call(
        functools.partial(
            line_kernel, lax.axis_size("replica"), tuple(kinds), tuple(cuts), beside, turns,
            (len(inputs), len(results), len(side_scratch)),
        ),
        out_shape=tuple(outs) + tuple(jax.ShapeDtypeStruct(shape, kind) for shape, kind in results),
        in_specs=[ANY] * len(arrays) + [VM] * len(inputs),
        out_specs=[ANY] * len(outs) + [VM] * len(results),
        scratch_shapes=side_scratch
        + buffers * 3
        + swaps
        + [pltpu.SemaphoreType.DMA((len(arrays),))]
        + [pltpu.SemaphoreType.DMA((count,))] * 6
        + [pltpu.SemaphoreType.DMA((count, 2))],
        compiler_params=pltpu.CompilerParams(
            collective_id=identity, has_side_effects=True, vmem_limit_bytes=60 * 2**20
        ),
        cost_estimate=pl.CostEstimate(flops=10**6, bytes_accessed=200 * 2**20, transcendentals=0),
    )(*arrays, *inputs)


def finish_pair_kernel(gain_ref, a_ref, b_ref, wa_ref, wb_ref, outa_ref, outb_ref, grad_ref):
    grad = jnp.zeros(gain_ref.shape, f32)
    for sum_ref, weight_ref, out_ref in ((a_ref, wa_ref, outa_ref), (b_ref, wb_ref, outb_ref)):
        total = sum_ref[...].astype(f32)
        out_ref[...] = total * gain_ref[...]
        grad = grad + jnp.sum(total * low(weight_ref[...]), axis=1, keepdims=True)
    grad_ref[...] = grad


def finish_pair(gain, a, b, wa, wb):
    rows, columns = wa.shape
    cut = min(rows, 32)
    wide = pl.BlockSpec((cut, columns), lambda i: (i, 0))
    thin = pl.BlockSpec((cut, 1), lambda i: (i, 0))
    out = jax.ShapeDtypeStruct((rows, columns), f32)
    return pl.pallas_call(
        finish_pair_kernel,
        grid=(rows // cut,),
        out_shape=(out, out, jax.ShapeDtypeStruct((rows, 1), f32)),
        in_specs=[thin, wide, wide, wide, wide],
        out_specs=[wide, wide, thin],
        compiler_params=pltpu.CompilerParams(vmem_limit_bytes=40 * 2**20),
        cost_estimate=pl.CostEstimate(flops=6 * rows * columns, bytes_accessed=20 * rows * columns, transcendentals=0),
    )(gain, a, b, wa, wb)


def finish_rest_kernel(gain_ref, mix_ref, wa_ref, wb_ref, out_sum_ref, down_sum_ref, outa_ref, outb_ref, grad_ref, out_ref, down_ref):
    owners, _, width = mix_ref.shape
    width = width // 2
    grad = jnp.zeros(gain_ref.shape, f32)
    for part, (weight_ref, target_ref) in enumerate(((wa_ref, outa_ref), (wb_ref, outb_ref))):
        total = jnp.concatenate(
            [mix_ref[j, :, part * width : (part + 1) * width].astype(f32) for j in range(owners)], axis=1
        )
        target_ref[...] = total * gain_ref[...]
        grad = grad + jnp.sum(total * low(weight_ref[...]), axis=1, keepdims=True)
    grad_ref[...] = grad
    out_ref[...] = out_sum_ref[...].astype(f32)
    down_ref[...] = down_sum_ref[...].astype(f32)


def finish_rest(gain, mix, wa, wb, out_sum, down_sum):
    rows, columns = wa.shape
    steps = 4
    while out_sum.shape[0] % (16 * steps) or down_sum.shape[0] % (16 * steps) or rows % (16 * steps):
        steps //= 2

    def tall(item):
        return pl.BlockSpec((item.shape[0] // steps, item.shape[1]), lambda i: (i, 0))

    owners, _, both = mix.shape
    wide, thin = tall(wa), tall(gain)
    return pl.pallas_call(
        finish_rest_kernel,
        grid=(steps,),
        out_shape=(
            jax.ShapeDtypeStruct(wa.shape, f32),
            jax.ShapeDtypeStruct(wa.shape, f32),
            jax.ShapeDtypeStruct((rows, 1), f32),
            jax.ShapeDtypeStruct(out_sum.shape, f32),
            jax.ShapeDtypeStruct(down_sum.shape, f32),
        ),
        in_specs=[
            thin,
            pl.BlockSpec((owners, rows // steps, both), lambda i: (0, i, 0)),
            wide,
            wide,
            tall(out_sum),
            tall(down_sum),
        ],
        out_specs=[wide, wide, thin, tall(out_sum), tall(down_sum)],
        compiler_params=pltpu.CompilerParams(vmem_limit_bytes=40 * 2**20),
        cost_estimate=pl.CostEstimate(flops=10**7, bytes_accessed=40 * 2**20, transcendentals=0),
    )(gain, mix, wa, wb, out_sum, down_sum)


def body(
    tokens,
    segments,
    cotangent,
    norm_gain,
    branch_weight,
    input_weight,
    conv_weight,
    conv_bias,
    recur_gate_weight,
    recur_gate_bias,
    input_gate_weight,
    input_gate_bias,
    decay_param,
    output_weight,
    mlp_norm_gain,
    gate_weight,
    up_weight,
    down_weight,
):
    x, cot = tokens[0], cotangent[0]
    rows, depth = x.shape
    members = lax.axis_size(GROUP)
    sequences = lax.axis_size("shard")
    total = members * rows
    gain, mlp_gain = low(norm_gain)[:, None], low(mlp_norm_gain)[:, None]
    own_labels = jnp.broadcast_to(segments[0].astype(bf16)[:, None], (rows, 128))
    width = branch_weight.shape[1] // members
    conv_f = low(conv_weight)
    decay_f = low(decay_param)
    bias = jnp.stack([low(conv_bias), low(recur_gate_bias), low(input_gate_bias), jax.nn.softplus(-decay_f)])
    (
        unit_all, labels, out_low, product, *mixed, mix_w, output_w, unit_two, middle, pair_w,
    ) = front(
        sequences, x, own_labels, cot, low(jnp.stack([norm_gain, mlp_norm_gain], 1)), conv_f, bias,
        recur_gate_weight, input_gate_weight, branch_weight, input_weight, gate_weight, up_weight, output_weight,
    )
    pair_w = pair_w.reshape(depth, -1)
    down_w = down_weight.astype(bf16)
    whole = ((total, depth), bf16)
    ff = pair_w.shape[1] // 2
    gate_pre = mm(unit_two, pair_w[:, :ff])
    up_pre = mm(unit_two, pair_w[:, ff:])
    hidden_grad = mm_nt(out_low, down_w)
    gate_act, gate_slope = gelu_parts(gate_pre)
    hidden = (gate_act * up_pre).astype(bf16)
    gate_low = (hidden_grad * up_pre * gate_slope).astype(bf16)
    up_low = (hidden_grad * gate_act).astype(bf16)
    pair_low = jnp.concatenate([gate_low, up_low], 1)
    partial = mm_nt(pair_low, pair_w).astype(bf16)
    pair_partial = mm_tn(unit_two, pair_low).astype(bf16).reshape(members, -1, 2 * ff)
    down_partial = mm_tn(hidden, out_low).astype(bf16)
    gate_sum, up_sum, mid_low, middle_grad = replica_sum(
        [pair_partial], ["pair"], 3, backward_steps, (0, 3, 6),
        (partial, middle, cot), (whole, ((rows, depth), f32)), rows, depth, 1,
    )
    mid_low, down_partial = lax.optimization_barrier((mid_low, down_partial))
    down_sum = lax.psum(down_partial, "replica")
    gate_grad, up_grad, mlp_gain_grad = finish_pair(mlp_gain, gate_sum, up_sum, gate_weight, up_weight)
    block_sum = lax.psum_scatter(mm(hidden, down_w).astype(bf16), ROWS, scatter_dimension=0, tiled=True)
    block_out = (middle + block_sum.astype(f32)).astype(bf16)
    output_partial = mm_tn(product, mid_low).astype(bf16)[None]
    back = mix_backward(
        sequences, mid_low, output_w, mix_w, *mixed, labels, conv_f, bias, recur_gate_weight, input_gate_weight
    )
    partial, branch_low, conv_low, conv_weight_grad, sums, recur_weight_grad, inject_weight_grad = back
    mix_low = jnp.concatenate([branch_low, conv_low], 1)
    mix_partial = mm_tn(unit_all, mix_low).astype(bf16).reshape(members, -1, 2 * width)
    size = recur_gate_weight.shape[1]
    gates = jnp.concatenate([recur_weight_grad, inject_weight_grad], 2).reshape(width, 2 * size)
    lanes = -(-max(width, 2 * size) // 128) * 128
    lines = jnp.concatenate([conv_weight_grad, sums], 0)
    packed = jnp.concatenate(
        [
            jnp.pad(gates, ((0, 0), (0, lanes - 2 * size))),
            jnp.pad(lines, ((0, 16 - lines.shape[0]), (0, lanes - width))),
        ],
        0,
    ).astype(bf16)[None]
    output_sum, mix_sum, packed, tokens_grad = replica_sum(
        [output_partial, mix_partial, packed], ["row", "side", "row"], 4, last_steps, (0, 3),
        (partial, middle_grad, x), (((rows, depth), bf16),), rows, depth, 0,
    )
    packed = packed.astype(f32)
    branch_grad, input_grad, gain_grad, output_grad, down_grad = finish_rest(
        gain, mix_sum, branch_weight, input_weight, output_sum, down_sum
    )
    recur_weight_grad = packed[:width, :size].reshape(-1, size, size)
    inject_weight_grad = packed[:width, size : 2 * size].reshape(-1, size, size)
    conv_weight_grad = packed[width : width + conv_weight.shape[0], :width]
    conv_bias_grad, recur_bias_grad, inject_bias_grad, rate_grad = [packed[width + conv_weight.shape[0] + i, :width] for i in range(4)]
    decay_param_grad = rate_grad * decay_scale * jax.nn.sigmoid(-decay_f)
    return (
        block_out[None],
        tokens_grad[None],
        gain_grad[:, 0],
        branch_grad,
        input_grad,
        conv_weight_grad,
        conv_bias_grad,
        recur_weight_grad,
        recur_bias_grad,
        inject_weight_grad,
        inject_bias_grad,
        decay_param_grad,
        output_grad,
        mlp_gain_grad[:, 0],
        gate_grad,
        up_grad,
        down_grad,
    )


def solution(mesh):
    row3 = P(("shard", "replica"), "seq", None)
    vec = P(("seq", "shard"))
    mat = P(("seq", "shard"), None)
    cube = P(("seq", "shard"), None, None)
    taps = P(None, ("seq", "shard"))
    params = (vec, mat, mat, taps, vec, cube, vec, cube, vec, vec, mat, vec, mat, mat, mat)
    in_specs = (row3, P(("shard", "replica"), "seq"), row3) + params
    out_specs = (row3, row3) + params
    return jax.shard_map(body, mesh=mesh, in_specs=in_specs, out_specs=out_specs, check_vma=False)
```

```python
import functools

import jax
import jax.numpy as jnp
from jax import lax
from jax.experimental import pallas as pl
from jax.experimental.pallas import tpu as pltpu
from jax.sharding import PartitionSpec as P

epsilon = 1e-06
decay_scale = 8.0
GROUP = ("seq", "shard")
ROWS = ("shard", "seq")
f32 = jnp.float32
bf16 = jnp.bfloat16
VM = pl.BlockSpec(memory_space=pltpu.VMEM)
ANY = pl.BlockSpec(memory_space=pl.ANY)
MESH = pl.DeviceIdType.MESH


def mm(left, right):
    return jnp.dot(left, right, preferred_element_type=f32)


def mm_nt(left, right):
    return lax.dot_general(left, right, (((1,), (1,)), ((), ())), preferred_element_type=f32)


def mm_tn(left, right):
    return lax.dot_general(left, right, (((0,), (0,)), ((), ())), preferred_element_type=f32)


def low(item):
    return item.astype(bf16).astype(f32)


def by_owner(weight, gain):
    owners = lax.axis_size(GROUP)
    scaled = (low(weight) * gain).astype(bf16)
    return jnp.swapaxes(scaled.reshape(weight.shape[0], owners, -1), 0, 1)


def swap(cut):
    return lax.all_to_all(cut, GROUP, split_axis=0, concat_axis=0, tiled=True)


def gelu_parts(x):
    inner = 0.7978845608028654 * (x + 0.044715 * x * x * x)
    t = jnp.tanh(inner)
    value = 0.5 * x * (1.0 + t)
    slope = 0.5 * (1.0 + t) + 0.5 * x * (1.0 - t * t) * 0.7978845608028654 * (
        1.0 + 3.0 * 0.044715 * x * x
    )
    return value, slope


def minus_expm1(y):
    poly = 1.0 + y * (1.0 / 8.0)
    for order in (7.0, 6.0, 5.0, 4.0, 3.0, 2.0):
        poly = 1.0 + y * (1.0 / order) * poly
    return jnp.where(y > -0.5, -y * poly, 1.0 - jnp.exp(y))


def dot_nn(a, b):
    return lax.dot_general(a, b, (((1,), (0,)), ((), ())), preferred_element_type=f32)


def dot_nt(a, b):
    return lax.dot_general(a, b, (((1,), (1,)), ((), ())), preferred_element_type=f32)


def dot_tn(a, b):
    return lax.dot_general(a, b, (((0,), (0,)), ((), ())), preferred_element_type=f32)


def whole_weight(ref, part):
    owners, _, rows, width = ref.shape
    return ref[:, part].reshape(owners * rows, width)


def fill_blocks(target, source):
    target[...] = jnp.zeros_like(target)
    count, size = source.shape[0], source.shape[1]
    for h in range(count):
        target[h * size : (h + 1) * size, h * size : (h + 1) * size] = source[h].astype(bf16).astype(f32)


def put_tiles(ref, here, value):
    width = value.shape[1]
    for tile in range(ref.shape[0]):
        lanes = min(128, width - 128 * tile)
        ref[tile, here, 0:lanes] = value[:, 128 * tile : 128 * tile + lanes]


def get_tiles(ref, here, width):
    parts = [ref[tile, here, 0 : min(128, width - 128 * tile)] for tile in range(ref.shape[0])]
    return jnp.concatenate(parts, axis=1)


def clear_tail(ref, width):
    tail = ref.shape[0] * 128 - width
    if tail:
        ref[ref.shape[0] - 1, :, 128 - tail :] = jnp.zeros((ref.shape[1], tail), f32)


def label_masks(label_ref, here, length, width, taps, lines):
    own = label_ref[here, :].astype(f32)
    lines[0:8, :] = jnp.full((8, 128), -1.0, f32)
    lines[8 : 8 + length, :] = own
    masks = []
    for k in range(1, taps):
        same = jnp.where(lines[8 - k : 8 - k + length, :] == own, 1.0, 0.0)
        masks.append(jnp.concatenate([same] * -(-width // 128), axis=1)[:, :width])
    return masks


def seq_scan(decay_ref, value_ref, sequences, length, reverse):
    tiles = decay_ref.shape[0]
    unroll = 8

    def step(i, states):
        states = list(states)
        for j in range(unroll):
            at = i * unroll + j
            if reverse:
                at = length - 1 - at
            here = pl.ds(at, sequences, stride=length)
            for tile in range(tiles):
                value = value_ref[tile, here, :]
                decay = decay_ref[tile, here, :]
                if reverse:
                    new = value + states[tile]
                    value_ref[tile, here, :] = new
                    states[tile] = decay * new
                else:
                    states[tile] = value + decay * states[tile]
                    value_ref[tile, here, :] = states[tile]
        return tuple(states)

    lax.fori_loop(0, length // unroll, step, (jnp.zeros((sequences, 128), f32),) * tiles)


def plane():
    halves, shards = lax.axis_size("seq"), lax.axis_size("shard")
    y, s = lax.axis_index("seq"), lax.axis_index("shard")
    offsets = [(dy, ds) for ds in range(0, shards, 2) for dy in range(halves)]

    def at(dy, ds):
        return {"seq": jnp.bitwise_xor(y, dy), "shard": jnp.bitwise_xor(s, ds)}

    def block(dy, ds):
        return jnp.bitwise_xor(s, ds) * halves + jnp.bitwise_xor(y, dy)

    return offsets, at, block


def remote(src, dst, sent, got, device):
    return pltpu.make_async_remote_copy(
        src_ref=src, dst_ref=dst, send_sem=sent, recv_sem=got, device_id=device, device_id_type=MESH
    )


def row_block(ref, index, rows):
    return ref.at[pl.ds(pl.multiple_of(index * rows, rows), rows), :]


def scatter_steps(rows, partial, near, far, acc, sems):
    offsets, at, block = plane()
    near_sent, near_got, far_sent, far_got = sems
    count = len(offsets)
    order = list(range(count - 1, -1, -1))
    firsts = {}
    for q in order:
        dy, ds = offsets[q]
        firsts[q] = remote(
            row_block(partial, block(dy, ds ^ 1), rows), near.at[q], near_sent.at[q], near_got.at[q], at(0, 1)
        )
        firsts[q].start()
    seconds = {}
    for q in order:
        dy, ds = offsets[q]
        firsts[q].wait_recv()
        base = block(dy, ds) * rows

        def tile(i, _):
            step = pl.multiple_of(i * 16, 16)
            here = pl.ds(step, 16)
            total = partial[pl.ds(pl.multiple_of(base + step, 16), 16), :].astype(f32) + near[q, here, :].astype(f32)
            if q:
                near[q, here, :] = total.astype(bf16)
            else:
                acc[here, :] = total
            return 0

        lax.fori_loop(0, rows // 16, tile, 0)
        if q:
            seconds[q] = remote(near.at[q], far.at[q - 1], far_sent.at[q - 1], far_got.at[q - 1], at(dy, ds))
            seconds[q].start()
    yield None
    for q in order[:-1]:
        seconds[q].wait_recv()

        def more(i, _):
            here = pl.ds(pl.multiple_of(i * 16, 16), 16)
            acc[here, :] += far[q - 1, here, :].astype(f32)
            return 0

        lax.fori_loop(0, rows // 16, more, 0)
    yield [firsts[q].wait_send for q in order] + [seconds[q].wait_send for q in order[:-1]]


def gather_steps(rows, whole, sems):
    offsets, at, block = plane()
    near_sent, near_got, far_sent, far_got = sems
    count = len(offsets)
    own = row_block(whole, block(0, 0), rows)
    sends = []
    outs = {}
    for q in range(count - 1, 0, -1):
        dy, ds = offsets[q]
        outs[q] = remote(own, own, far_sent.at[q - 1], far_got.at[q - 1], at(dy, ds))
        outs[q].start()
        sends.append(outs[q].wait_send)
    hand = remote(own, own, near_sent.at[0], near_got.at[0], at(0, 1))
    hand.start()
    sends.append(hand.wait_send)
    arrivals = [hand.wait_recv]
    yield None
    for q in list(range(1, count)):
        dy, ds = offsets[q]
        outs[q].wait_recv()
        block_q = row_block(whole, block(dy, ds), rows)
        hand = remote(block_q, block_q, near_sent.at[q], near_got.at[q], at(0, 1))
        hand.start()
        sends.append(hand.wait_send)
        arrivals.append(hand.wait_recv)
    yield arrivals + sends


def root_mean(rows):
    return lax.rsqrt(jnp.mean(rows * rows, axis=-1, keepdims=True) + epsilon)


def norm_backward(grad_unit, unit, inverse):
    return inverse * (grad_unit - unit * jnp.mean(grad_unit * unit, axis=-1, keepdims=True))


def by_tiles(rows, work):
    def tile(i, _):
        work(pl.ds(pl.multiple_of(i * 16, 16), 16), i)
        return 0

    lax.fori_loop(0, rows // 16, tile, 0)


def plane_scratch(rows, depth, gathers, scatters):
    count = lax.axis_size("seq") * lax.axis_size("shard") // 2
    block = (rows, depth)
    scratch = []
    if scatters:
        scratch = [
            pltpu.VMEM((count,) + block, bf16),
            pltpu.VMEM((count - 1,) + block, bf16),
            pltpu.VMEM(block, f32),
        ]
    for _ in range(scatters + gathers):
        scratch += [pltpu.SemaphoreType.DMA((count,))] * 2 + [pltpu.SemaphoreType.DMA((count - 1,))] * 2
    return scratch


def cut_columns(weight_ref, gain, target, start, lanes):
    owners = weight_ref.shape[1] // lanes

    def tile(i, _):
        step = pl.multiple_of(i * 16, 16)
        here = pl.ds(step, 16)
        scaled = low(weight_ref[here, :]) * gain(step)
        for j in range(owners):
            target(j)[here, start : start + lanes] = scaled[:, j * lanes : (j + 1) * lanes].astype(bf16)
        return 0

    lax.fori_loop(0, weight_ref.shape[0] // 16, tile, 0)


def quarter_steps(n, part, whole, sems):
    me = lax.axis_index("replica")
    right_sent, right_got, left_sent, left_got = sems

    def rows(q):
        return whole.at[:, pl.ds(pl.multiple_of(q * part, 16), part), :]

    def to_right(hop):
        block = rows(me - hop)
        return remote(block, block, right_sent.at[hop], right_got.at[hop], {"replica": me + 1})

    def to_left(hop):
        block = rows(me + hop)
        return remote(block, block, left_sent.at[hop], left_got.at[hop], {"replica": me - 1})

    def from_left(hop):
        block = rows(me - hop - 1)
        return remote(block, block, right_sent.at[hop], right_got.at[hop], {"replica": me + 1})

    def from_right(hop):
        block = rows(me + hop + 1)
        return remote(block, block, left_sent.at[hop], left_got.at[hop], {"replica": me - 1})

    for hop in range(n - 1):
        if hop:

            @pl.when(me >= hop)
            def _():
                from_left(hop - 1).wait_recv()

            @pl.when(me + hop < n)
            def _():
                from_right(hop - 1).wait_recv()

        @pl.when(jnp.logical_and(me >= hop, me < n - 1))
        def _():
            to_right(hop).start()

        @pl.when(jnp.logical_and(me + hop < n, me > 0))
        def _():
            to_left(hop).start()

        yield

    @pl.when(me >= n - 1)
    def _():
        from_left(n - 2).wait_recv()

    @pl.when(me + n - 1 < n)
    def _():
        from_right(n - 2).wait_recv()

    for hop in range(n - 1):

        @pl.when(jnp.logical_and(me >= hop, me < n - 1))
        def _():
            to_right(hop).wait_send()

        @pl.when(jnp.logical_and(me + hop < n, me > 0))
        def _():
            to_left(hop).wait_send()

    yield


def front_kernel(
    n, sequences, length,
    x_ref, label_ref, cot_ref, gains_ref, conv_ref, bias_ref, rw_ref, iw_ref,
    branch_hbm, input_hbm, gate_hbm, up_hbm, ow_hbm,
    unit_out, labels_out, low_out, product_out, pre_out, conv_in_out, values_out, recur_out, inject_out, decay_out,
    states_out, mix_out, ow_out, two_out, middle_out, pair_out,
    unit_ref, labels_ref, product_ref, pre_ref, conv_in_ref, values_ref, recur_ref, inject_ref, decay_ref,
    states_ref, mix_ref, ow_ref, two_ref, middle_ref,
    wide, tall, ow_f, mix_cut, pair_cut, pad, lines, rbig, ibig, partial,
    near, far, acc, *sems,
):
    rows = x_ref.shape[0]
    scatter_sems, sems = sems[:4], sems[4:]
    unit_sems, label_sems, low_sems, two_sems, sems = sems[:4], sems[4:8], sems[8:12], sems[12:16], sems[16:]
    load_sem, save_sem, mix_sent, mix_got, pair_sent, pair_got = sems[:6]
    line_sems = sems[6:]
    offsets, at, block = plane()
    z = lax.axis_index("replica")
    y, s = lax.axis_index("seq"), lax.axis_index("shard")
    shards = lax.axis_size("shard")
    owners = shards * lax.axis_size("seq")
    part = gate_hbm.shape[0] // n
    width = pad.shape[1]
    ff = gate_hbm.shape[1] // owners

    def peer(i):
        return {"seq": jnp.bitwise_xor(y, i // shards), "shard": jnp.bitwise_xor(s, i % shards)}

    def place(i):
        return jnp.bitwise_xor(y, i // shards) * shards + jnp.bitwise_xor(s, i % shards)

    own_rows = pl.ds(pl.multiple_of(z * part, 16), part)
    loads = [
        pltpu.make_async_copy(gate_hbm.at[own_rows, :], tall.at[0], load_sem.at[0]),
        pltpu.make_async_copy(up_hbm.at[own_rows, :], tall.at[1], load_sem.at[1]),
        pltpu.make_async_copy(branch_hbm, wide.at[0], load_sem.at[2]),
        pltpu.make_async_copy(input_hbm, wide.at[1], load_sem.at[3]),
        pltpu.make_async_copy(ow_hbm, ow_f, load_sem.at[4]),
    ]
    for load in loads:
        load.start()
    saves = []

    def save(source, target):
        copy = pltpu.make_async_copy(source, target, save_sem.at[len(saves)])
        copy.start()
        saves.append(copy)

    low_own = pltpu.make_async_copy(cot_ref, row_block(low_out, block(0, 0), rows), load_sem.at[5])
    low_own.start()
    barrier = pltpu.get_barrier_semaphore()
    for i in range(1, owners):
        pl.semaphore_signal(barrier, inc=1, device_id=peer(i), device_id_type=MESH)

    @pl.when(z > 0)
    def _():
        pl.semaphore_signal(barrier, inc=1, device_id={"replica": z - 1}, device_id_type=MESH)

    @pl.when(z < n - 1)
    def _():
        pl.semaphore_signal(barrier, inc=1, device_id={"replica": z + 1}, device_id_type=MESH)

    base = block(0, 0) * rows

    def unit(here, i):
        value = x_ref[here, :].astype(f32)
        there = pl.ds(pl.multiple_of(base + i * 16, 16), 16)
        unit_ref[there, :] = (value * root_mean(value)).astype(bf16)
        labels_ref[there, :] = label_ref[here, :]

    by_tiles(rows, unit)
    inside_line = jnp.logical_and(z > 0, z < n - 1)

    @pl.when(inside_line)
    def _():
        pl.semaphore_wait(barrier, owners + 1)

    @pl.when(jnp.logical_not(inside_line))
    def _():
        pl.semaphore_wait(barrier, owners)

    label_gather = gather_steps(rows, labels_ref, label_sems)
    unit_gather = gather_steps(rows, unit_ref, unit_sems)
    next(label_gather)
    next(unit_gather)

    for side in range(2):
        loads[side].wait()

        cut_columns(
            tall.at[side],
            lambda step: gains_ref[pl.ds(pl.multiple_of(z * part + step, 16), 16), 1:2],
            lambda j: pair_cut.at[j],
            side * ff,
            ff,
        )
    me = place(0)
    pair_there = pair_out.at[me, own_rows, :]
    pair_moves = [
        remote(pair_cut.at[place(i)], pair_there, pair_sent.at[i], pair_got.at[i], peer(i)) for i in range(1, owners)
    ]
    for move in pair_moves:
        move.start()
    pair_own = pltpu.make_async_copy(pair_cut.at[me], pair_there, pair_sent.at[0])
    pair_own.start()

    for side in range(2):
        loads[2 + side].wait()
        cut_columns(
            wide.at[side], lambda step: gains_ref[pl.ds(step, 16), 0:1], lambda j: mix_cut.at[j, side], 0, width
        )
    mix_moves = [
        remote(mix_cut.at[place(i)], mix_ref.at[me], mix_sent.at[i], mix_got.at[i], peer(i)) for i in range(1, owners)
    ]
    for move in mix_moves:
        move.start()
    mix_own = pltpu.make_async_copy(mix_cut.at[me], mix_ref.at[me], mix_sent.at[0])
    mix_own.start()
    loads[4].wait()
    ow_ref[...] = ow_f[...].astype(bf16)
    save(ow_ref, ow_out)
    fill_blocks(rbig, rw_ref)
    fill_blocks(ibig, iw_ref)
    pad[0:8, :] = jnp.zeros((8, width), f32)
    taps = conv_ref.shape[0]
    clear_tail(decay_ref, width)
    clear_tail(states_ref, width)

    waits = next(label_gather)
    waits = waits + next(unit_gather)
    pair_own.wait()
    for move in pair_moves:
        move.wait_recv()
    line = quarter_steps(n, part, pair_out, line_sems)
    next(line)
    for wait in waits:
        wait()
    mix_own.wait()
    for move in mix_moves:
        move.wait_recv()
    save(unit_ref, unit_out)
    save(labels_ref, labels_out)
    save(mix_ref, mix_out)

    low_own.wait()
    low_gather = gather_steps(rows, low_out, low_sems)
    next(low_gather)

    def one(q, _):
        here = pl.ds(pl.multiple_of(q * length, length), length)
        sequence = unit_ref[here, :]
        masks = label_masks(labels_ref, here, length, width, taps, lines)
        pre_ref[here, :] = dot_nn(sequence, whole_weight(mix_ref, 0))
        conv_in = dot_nn(sequence, whole_weight(mix_ref, 1)).astype(bf16)
        conv_in_ref[here, :] = conv_in
        pad[8 : 8 + length, :] = conv_in.astype(f32)
        total = bias_ref[0:1, :] + conv_ref[0:1, :] * pad[8 : 8 + length, :]
        for k in range(1, taps):
            total = total + conv_ref[k : k + 1, :] * pad[8 - k : 8 - k + length, :] * masks[k - 1]
        values = total.astype(bf16)
        values_ref[here, :] = values
        recur = jax.nn.sigmoid(dot_nn(values, rbig[...].astype(bf16)) + bias_ref[1:2, :])
        inject = jax.nn.sigmoid(dot_nn(values, ibig[...].astype(bf16)) + bias_ref[2:3, :])
        recur_ref[here, :] = recur
        inject_ref[here, :] = inject
        log_decay = -decay_scale * bias_ref[3:4, :] * recur
        inside = masks[0] > 0.5
        put_tiles(decay_ref, here, jnp.where(inside, jnp.exp(log_decay), 0.0))
        scale = jnp.where(inside, jnp.sqrt(minus_expm1(2.0 * log_decay)), 1.0)
        put_tiles(states_ref, here, scale * inject * values.astype(f32))
        return 0

    lax.fori_loop(0, sequences, one, 0)
    seq_scan(decay_ref, states_ref, sequences, length, False)

    def two(q, _):
        here = pl.ds(pl.multiple_of(q * length, length), length)
        act, _unused = gelu_parts(pre_ref[here, :])
        product = (act * get_tiles(states_ref, here, width)).astype(bf16)
        product_ref[here, :] = product
        partial[here, :] = dot_nn(product, ow_ref[...]).astype(bf16)
        return 0

    lax.fori_loop(0, sequences, two, 0)
    scatter = scatter_steps(rows, partial, near, far, acc, scatter_sems)
    next(scatter)
    for source, target in (
        (product_ref, product_out), (pre_ref, pre_out), (conv_in_ref, conv_in_out), (values_ref, values_out),
        (recur_ref, recur_out), (inject_ref, inject_out), (decay_ref, decay_out), (states_ref, states_out),
    ):
        save(source, target)
    next(line)
    waits = next(low_gather)
    waits = waits + next(scatter)

    def norm(here, i):
        middle = x_ref[here, :].astype(f32) + acc[here, :]
        middle_ref[here, :] = middle
        there = pl.ds(pl.multiple_of(base + i * 16, 16), 16)
        two_ref[there, :] = (middle * root_mean(middle)).astype(bf16)

    by_tiles(rows, norm)
    two_gather = gather_steps(rows, two_ref, two_sems)
    next(two_gather)
    save(middle_ref, middle_out)
    for _ in range(n - 3):
        next(line)
    for wait in waits:
        wait()
    waits = next(two_gather)
    for wait in waits:
        wait()
    save(two_ref, two_out)
    for _ in line:
        pass
    for move in pair_moves + mix_moves:
        move.wait_send()
    for copy in saves:
        copy.wait()


def front(sequences, x, label, cot, gains, conv, bias, rw, iw, branch_w, input_w, gate_w, up_w, output_w):
    rows, depth = x.shape
    own, n = branch_w.shape[0], lax.axis_size("replica")
    owners = lax.axis_size(GROUP)
    total, width, ff = owners * rows, branch_w.shape[1] // owners, gate_w.shape[1] // owners
    part = own // n
    length = total // sequences
    tiles = -(-width // 128)
    kept = [
        ((total, depth), bf16), ((total, 128), bf16), ((total, depth), bf16), ((total, width), bf16),
        ((total, width), f32), ((total, width), bf16), ((total, width), bf16), ((total, width), f32),
        ((total, width), f32), ((tiles, total, 128), f32), ((tiles, total, 128), f32), ((owners, 2, own, width), bf16),
        ((width, depth), bf16), ((total, depth), bf16), ((rows, depth), f32),
    ]
    vm = pltpu.VMEM
    dma = pltpu.SemaphoreType.DMA
    scratch = [vm(*item) for k, item in enumerate(kept) if k != 2] + [
        vm((2,) + branch_w.shape, f32),
        vm((2, part, gate_w.shape[1]), f32),
        vm(output_w.shape, f32),
        vm((owners, 2, own, width), bf16),
        vm((owners, part, 2 * ff), bf16),
        vm((8 + length, width), f32),
        vm((8 + length, 128), f32),
        vm((width, width), f32),
        vm((width, width), f32),
        vm((total, depth), bf16),
    ]
    scratch += plane_scratch(rows, depth, 4, 1)
    scratch += [dma((6,)), dma((len(kept),))] + [dma((owners,))] * 4 + [dma((n - 1,))] * 4
    outs = kept + [((owners, own, 2 * ff), bf16)]
    return pl.pallas_call(
        functools.partial(front_kernel, n, sequences, length),
        out_shape=tuple(jax.ShapeDtypeStruct(*item) for item in outs),
        in_specs=[VM] * 8 + [ANY] * 5,
        out_specs=[ANY] * len(outs),
        scratch_shapes=scratch,
        compiler_params=pltpu.CompilerParams(
            collective_id=1, has_side_effects=True, vmem_limit_bytes=60 * 2**20
        ),
        cost_estimate=pl.CostEstimate(flops=10**6, bytes_accessed=200 * 2**20, transcendentals=0),
    )(x, label, cot, gains, conv, bias, rw, iw, branch_w, input_w, gate_w, up_w, output_w)


def turn_steps(
    sequences, length,
    partial_hbm, middle_ref, cot_ref, label_ref, conv_ref, bias_ref, rw_ref, iw_ref, *rest,
):
    kept_hbm, rest = rest[:9], rest[9:]
    low_out, grad_out, partial_out, branch_low_out, conv_low_out, dconv_ref, sums_ref, drw_ref, diw_ref = rest[:9]
    scatter_sems, gather_sems = rest[9 + 3 : 9 + 7], rest[9 + 7 : 9 + 11]
    near, far, acc = rest[9:12]
    rest = rest[20:]
    kept, rest = rest[:9], rest[9:]
    ow_ref, w_ref, pre_ref, conv_in_ref, values_ref, recur_ref, inject_ref, decay_ref, states_ref = kept
    partial, low_ref, grad_ref, branch_low_ref, conv_low_ref, adj, pad, lines, rbig, ibig, dr, di, load_sem, save_sem = rest
    rows = middle_ref.shape[0]
    offsets, at, block = plane()
    first = pltpu.make_async_copy(partial_hbm, partial, load_sem.at[9])
    first.start()
    loads = [pltpu.make_async_copy(kept_hbm[k], kept[k], load_sem.at[k]) for k in range(9)]
    for load in loads:
        load.start()
    first.wait()
    scatter = scatter_steps(rows, partial, near, far, acc, scatter_sems)
    next(scatter)
    yield
    waits = next(scatter)
    base = block(0, 0) * rows

    def norm(here, i):
        middle = middle_ref[here, :]
        inverse = root_mean(middle)
        grad = cot_ref[here, :].astype(f32) + norm_backward(acc[here, :], middle * inverse, inverse)
        grad_ref[here, :] = grad
        there = pl.ds(pl.multiple_of(base + i * 16, 16), 16)
        low_ref[there, :] = grad.astype(bf16)

    by_tiles(rows, norm)
    gather = gather_steps(rows, low_ref, gather_sems)
    next(gather)
    yield
    waits = waits + next(gather)
    yield
    for wait in waits:
        wait()
    for load in loads:
        load.wait()
    saves = [pltpu.make_async_copy(low_ref, low_out, save_sem.at[0]), pltpu.make_async_copy(grad_ref, grad_out, save_sem.at[1])]
    for save in saves:
        save.start()
    fill_blocks(rbig, rw_ref)
    fill_blocks(ibig, iw_ref)
    dr[...] = jnp.zeros_like(dr)
    di[...] = jnp.zeros_like(di)
    sums_ref[...] = jnp.zeros_like(sums_ref)
    dconv_ref[...] = jnp.zeros_like(dconv_ref)
    taps = conv_ref.shape[0]
    width = pad.shape[1]
    clear_tail(adj, width)

    def one(s):
        here = pl.ds(s * length, length)
        product_grad = dot_nt(low_ref[here, :], ow_ref[...])
        act, slope = gelu_parts(pre_ref[here, :])
        branch_low_ref[here, :] = (product_grad * get_tiles(states_ref, here, width) * slope).astype(bf16)
        put_tiles(adj, here, product_grad * act)

    for s in range(sequences):
        one(s)
        yield
    seq_scan(decay_ref, adj, sequences, length, True)
    yield

    def two(s):
        here = pl.ds(s * length, length)
        adjoint = get_tiles(adj, here, width)
        recur = recur_ref[here, :]
        inject = inject_ref[here, :]
        decay = get_tiles(decay_ref, here, width)
        values = values_ref[here, :]
        values_f = values.astype(f32)
        masks = label_masks(label_ref, here, length, width, taps, lines)
        inside = masks[0] > 0.5
        rate = bias_ref[3:4, :]
        log_decay = -decay_scale * rate * recur
        scale = jnp.where(inside, jnp.sqrt(minus_expm1(2.0 * log_decay)), 1.0)
        pad[0:8, :] = jnp.zeros((8, width), f32)
        pad[8 : 8 + length, :] = get_tiles(states_ref, here, width)
        previous = pad[7 : 7 + length, :]
        driven = adjoint * inject * values_f
        log_grad = jnp.where(inside, adjoint * previous * decay - driven * decay * decay / scale, 0.0)
        recur_low = (log_grad * (-decay_scale * rate) * recur * (1.0 - recur)).astype(bf16)
        inject_low = (driven * scale * (1.0 - inject)).astype(bf16)
        sums_ref[1:2, :] += jnp.sum(recur_low.astype(f32), axis=0, keepdims=True)
        sums_ref[2:3, :] += jnp.sum(inject_low.astype(f32), axis=0, keepdims=True)
        sums_ref[3:4, :] += jnp.sum(log_grad * recur, axis=0, keepdims=True)
        dr[...] += dot_tn(values, recur_low)
        di[...] += dot_tn(values, inject_low)
        grad = adjoint * scale * inject
        grad = grad + dot_nt(recur_low, rbig[...].astype(bf16)) + dot_nt(inject_low, ibig[...].astype(bf16))
        sums_ref[0:1, :] += jnp.sum(grad, axis=0, keepdims=True)
        pad[8 : 8 + length, :] = conv_in_ref[here, :].astype(f32)
        dconv_ref[0:1, :] += jnp.sum(grad * pad[8 : 8 + length, :], axis=0, keepdims=True)
        masked = []
        for k in range(1, taps):
            part = grad * masks[k - 1]
            masked.append(part)
            dconv_ref[k : k + 1, :] += jnp.sum(part * pad[8 - k : 8 - k + length, :], axis=0, keepdims=True)
        total = grad * conv_ref[0:1, :]
        pad[length : length + 8, :] = jnp.zeros((8, width), f32)
        for k in range(1, taps):
            pad[0:length, :] = masked[k - 1] * conv_ref[k : k + 1, :]
            total = total + pad[k : k + length, :]
        conv_low = total.astype(bf16)
        conv_low_ref[here, :] = conv_low
        partial[here, :] = (dot_nt(branch_low_ref[here, :], whole_weight(w_ref, 0)) + dot_nt(conv_low, whole_weight(w_ref, 1))).astype(bf16)

    for s in range(sequences):
        two(s)
        yield
    size = drw_ref.shape[1]
    for h in range(drw_ref.shape[0]):
        cut = slice(h * size, (h + 1) * size)
        drw_ref[h] = dr[cut, cut]
        diw_ref[h] = di[cut, cut]
    ends = [(partial, partial_out), (branch_low_ref, branch_low_out), (conv_low_ref, conv_low_out)]
    for k, pair in enumerate(ends):
        saves.append(pltpu.make_async_copy(*pair, save_sem.at[2 + k]))
        saves[-1].start()
    yield
    for save in saves:
        save.wait()


def end_steps(
    partial_hbm, grad_ref, x_ref, middle_ref, hidden_hbm, down_hbm, tokens_ref, block_ref, *rest,
):
    near, far, acc = rest[:3]
    scatter_sems = rest[3:7]
    more_sems = rest[7:11]
    near_two, far_two, partial, partial_two, hidden, down, load_sem = rest[11:]
    rows = x_ref.shape[0]
    loads = [
        pltpu.make_async_copy(source, target, load_sem.at[k])
        for k, (source, target) in enumerate(((partial_hbm, partial), (hidden_hbm, hidden), (down_hbm, down)))
    ]
    for load in loads:
        load.start()
    loads[0].wait()
    scatter = scatter_steps(rows, partial, near, far, acc, scatter_sems)
    next(scatter)
    yield
    loads[1].wait()
    loads[2].wait()
    pieces_of = 4
    height = hidden.shape[0] // pieces_of
    for k in range(pieces_of):
        here = pl.ds(k * height, height)
        partial_two[here, :] = dot_nn(hidden[here, :], down[...]).astype(bf16)
        yield
    waits = next(scatter)

    def norm(here, i):
        value = x_ref[here, :].astype(f32)
        inverse = root_mean(value)
        grad = grad_ref[here, :] + norm_backward(acc[here, :], value * inverse, inverse)
        tokens_ref[here, :] = grad.astype(bf16)

    by_tiles(rows, norm)
    yield
    scatter = scatter_steps(rows, partial_two, near_two, far_two, acc, more_sems)
    next(scatter)
    yield
    waits = waits + next(scatter)

    def out(here, i):
        block_ref[here, :] = (middle_ref[here, :] + acc[here, :]).astype(bf16)

    by_tiles(rows, out)
    yield
    for wait in waits:
        wait()


def pieces(rows, most):
    count = -(-rows // most)
    while rows % count or (rows // count) % 16:
        count += 1
    return count


def line_kernel(n, kinds, cuts, beside, turns, extra, *refs):
    ins = len(cuts)
    made = ins + kinds.count("pair")
    extra_ins, extra_outs, extra_scratch = extra
    refs = list(refs)

    def take(count):
        taken = refs[:count]
        del refs[:count]
        return taken

    own_hbm, side_in = take(ins), take(extra_ins)
    outs, side_out = take(made), take(extra_outs)
    side_scratch = take(extra_scratch)
    from_out, from_in = take(ins), take(ins)
    slots, whole_sem, slot_sem, sent_in, sent_out, got_out, got_in, sent_x, got_x = refs
    depth = slots.shape[0]
    me = lax.axis_index("replica")
    y, s = lax.axis_index("seq"), lax.axis_index("shard")
    shards = lax.axis_size("shard")
    owners = shards * lax.axis_size("seq")
    left = me < n // 2
    inward = jnp.where(left, me + 1, me - 1)
    outward = jnp.where(left, me - 1, me + 1)
    has_out = jnp.logical_and(me > 0, me < n - 1)
    at_end = jnp.logical_not(has_out)
    middle = jnp.logical_or(me == n // 2 - 1, me == n // 2)

    def peer(i):
        return {"seq": jnp.bitwise_xor(y, i // shards), "shard": jnp.bitwise_xor(s, i % shards)}

    def place(i):
        return jnp.bitwise_xor(y, i // shards) * shards + jnp.bitwise_xor(s, i % shards)

    chunks = []
    for k, (lead, count, rows) in enumerate(cuts):
        for step in range(lead):
            for i in range(count):
                chunks.append((k, step if kinds[k] == "row" else (step + 1) % lead, i * rows, rows))
    total = len(chunks)

    def view(group, c):
        k, i, start, rows = chunks[c]
        return group[k].at[0 if kinds[k] == "row" else place(i), pl.ds(start, rows), :]

    def slot(c):
        k, i, start, rows = chunks[c]
        return slots.at[c % depth, pl.ds(0, rows), pl.ds(0, from_in[k].shape[2])]

    def load(c):
        return pltpu.make_async_copy(view(own_hbm, c), slot(c), slot_sem.at[c % depth])

    wholes = [pltpu.make_async_copy(own_hbm[k], from_out[k], whole_sem.at[k]) for k in range(ins)]

    @pl.when(at_end)
    def _():
        for item in wholes:
            item.start()

    @pl.when(has_out)
    def _():
        for c in range(min(depth - 1, total)):
            load(c).start()

    barrier = pltpu.get_barrier_semaphore()
    for i in range(1, owners):
        pl.semaphore_signal(barrier, inc=1, device_id=peer(i), device_id_type=MESH)
    pl.semaphore_signal(barrier, inc=1, device_id={"replica": inward}, device_id_type=MESH)

    @pl.when(has_out)
    def _():
        pl.semaphore_signal(barrier, inc=1, device_id={"replica": outward}, device_id_type=MESH)
        pl.semaphore_wait(barrier, owners + 1)

    @pl.when(at_end)
    def _():
        pl.semaphore_wait(barrier, owners)

    def push(group, target, c, sent, got, device):
        return remote(view(group, c), view(target, c), sent.at[c], got.at[c], {"replica": device})

    def add(target, other, c):
        k, i, start, rows = chunks[c]
        into, more = view(target, c), slot(c) if other is None else view(other, c)

        def tile(t, _):
            here = pl.ds(pl.multiple_of(t * 16, 16), 16)
            into[here, :] = (into[here, :].astype(f32) + more[here, :].astype(f32)).astype(bf16)
            return 0

        lax.fori_loop(0, rows // 16, tile, 0)

    def pass_in(c):
        @pl.when(middle)
        def _():
            push(from_out, from_in, c, sent_in, got_in, inward).start()

        @pl.when(jnp.logical_not(middle))
        def _():
            push(from_out, from_out, c, sent_in, got_out, inward).start()

    def gather_in(c):
        @pl.when(has_out)
        def _():
            load(c).wait()
            push(from_out, from_out, c, sent_in, got_out, inward).wait_recv()
            add(from_out, None, c)
            pass_in(c)
            if c + depth - 1 < total:
                load(c + depth - 1).start()

    work = beside(*side_in, *side_out, *side_scratch)
    next(work)

    @pl.when(at_end)
    def _():
        for c in range(total):
            if c == 0 or chunks[c][0] != chunks[c - 1][0]:
                wholes[chunks[c][0]].wait()
            pass_in(c)

    def deliveries(c):
        k, i, start, rows = chunks[c]
        here = pl.ds(start, rows)
        first = k + kinds[:k].count("pair")
        source = view(from_in, c)
        if kinds[k] == "row":
            ends = [(source, outs[first].at[here, :])]
        elif kinds[k] == "side":
            ends = [(source, outs[first].at[place(0), here, :])]
        else:
            half = source.shape[1] // 2
            there = pl.ds(pl.multiple_of(place(0) * half, half), half)
            ends = [
                (source.at[:, pl.ds(part * half, half)], outs[first + part].at[here, there]) for part in range(2)
            ]
        if kinds[k] == "row" or i == 0:
            return [pltpu.make_async_copy(*pair, sent_x.at[c, p]) for p, pair in enumerate(ends)], False
        return [remote(*pair, sent_x.at[c, p], got_x.at[c, p], peer(i)) for p, pair in enumerate(ends)], True

    def give_back(c):
        push(from_out, from_in, c, sent_out, got_in, inward).wait_recv()

        @pl.when(middle)
        def _():
            add(from_in, from_out, c)

        @pl.when(has_out)
        def _():
            push(from_in, from_in, c, sent_out, got_in, outward).start()

        for copy in deliveries(c)[0]:
            copy.start()

    lag = 2
    for c in range(total + lag):
        for _ in range(turns.count(c)):
            next(work)
        if c < total:
            gather_in(c)
        if c >= lag:
            give_back(c - lag)
    for _ in work:
        pass
    for c in range(total):
        copies, away = deliveries(c)
        for copy in copies:
            if away:
                copy.wait_recv()
                copy.wait_send()
            else:
                copy.wait()
        push(from_out, from_in, c, sent_in, got_in, inward).wait_send()

        @pl.when(has_out)
        def _():
            push(from_in, from_in, c, sent_out, got_in, outward).wait_send()


def replica_sum(arrays, kinds, identity, beside, turns, inputs, results, side_scratch):
    cuts, outs = [], []
    tall = broad = 0
    for item, kind in zip(arrays, kinds):
        lead, height, columns = item.shape
        count = pieces(height, max(16, (105 * 1024) // columns // 16 * 16))
        cuts.append((lead, count, height // count))
        tall, broad = max(tall, height // count), max(broad, columns)
        if kind == "pair":
            outs += [jax.ShapeDtypeStruct((height, lead * columns // 2), bf16)] * 2
        elif kind == "side":
            outs.append(jax.ShapeDtypeStruct(item.shape, bf16))
        else:
            outs.append(jax.ShapeDtypeStruct((height, columns), bf16))
    count = sum(lead * cut for lead, cut, _ in cuts)
    buffers = [pltpu.VMEM(item.shape, bf16) for item in arrays]
    dma = pltpu.SemaphoreType.DMA
    return pl.pallas_call(
        functools.partial(
            line_kernel, lax.axis_size("replica"), tuple(kinds), tuple(cuts), beside, turns,
            (len(inputs), len(results), len(side_scratch)),
        ),
        out_shape=tuple(outs) + tuple(jax.ShapeDtypeStruct(shape, kind) for shape, kind, _ in results),
        in_specs=[ANY] * len(arrays) + [spec for _, spec in inputs],
        out_specs=[ANY] * len(outs) + [spec for _, _, spec in results],
        scratch_shapes=list(side_scratch)
        + buffers * 2
        + [pltpu.VMEM((4, tall, broad), bf16), dma((len(arrays),)), dma((4,))]
        + [dma((count,))] * 4
        + [dma((count, 2))] * 2,
        compiler_params=pltpu.CompilerParams(
            collective_id=identity, has_side_effects=True, vmem_limit_bytes=61 * 2**20
        ),
        cost_estimate=pl.CostEstimate(flops=10**6, bytes_accessed=200 * 2**20, transcendentals=0),
    )(*arrays, *[item for item, _ in inputs])


def finish_pair_kernel(gain_ref, a_ref, b_ref, wa_ref, wb_ref, outa_ref, outb_ref, grad_ref):
    grad = jnp.zeros(gain_ref.shape, f32)
    for sum_ref, weight_ref, out_ref in ((a_ref, wa_ref, outa_ref), (b_ref, wb_ref, outb_ref)):
        total = sum_ref[...].astype(f32)
        out_ref[...] = total * gain_ref[...]
        grad = grad + jnp.sum(total * low(weight_ref[...]), axis=1, keepdims=True)
    grad_ref[...] = grad


def finish_pair(gain, a, b, wa, wb):
    rows, columns = wa.shape
    cut = min(rows, 32)
    wide = pl.BlockSpec((cut, columns), lambda i: (i, 0))
    thin = pl.BlockSpec((cut, 1), lambda i: (i, 0))
    out = jax.ShapeDtypeStruct((rows, columns), f32)
    return pl.pallas_call(
        finish_pair_kernel,
        grid=(rows // cut,),
        out_shape=(out, out, jax.ShapeDtypeStruct((rows, 1), f32)),
        in_specs=[thin, wide, wide, wide, wide],
        out_specs=[wide, wide, thin],
        compiler_params=pltpu.CompilerParams(vmem_limit_bytes=61 * 2**20),
        cost_estimate=pl.CostEstimate(flops=6 * rows * columns, bytes_accessed=20 * rows * columns, transcendentals=0),
    )(gain, a, b, wa, wb)


def finish_rest_kernel(gain_ref, mix_ref, wa_ref, wb_ref, out_sum_ref, down_sum_ref, outa_ref, outb_ref, grad_ref, out_ref, down_ref):
    owners = mix_ref.shape[0]
    width = wa_ref.shape[1] // owners
    grad = jnp.zeros(gain_ref.shape, f32)
    for part, (weight_ref, target_ref) in enumerate(((wa_ref, outa_ref), (wb_ref, outb_ref))):
        total = jnp.concatenate(
            [mix_ref[j, :, part * width : (part + 1) * width].astype(f32) for j in range(owners)], axis=1
        )
        target_ref[...] = total * gain_ref[...]
        grad = grad + jnp.sum(total * low(weight_ref[...]), axis=1, keepdims=True)
    grad_ref[...] = grad
    out_ref[...] = out_sum_ref[...].astype(f32)
    down_ref[...] = down_sum_ref[...].astype(f32)


def finish_rest(gain, mix, wa, wb, out_sum, down_sum):
    rows, columns = wa.shape
    steps = 4
    while out_sum.shape[0] % (16 * steps) or down_sum.shape[0] % (16 * steps) or rows % (16 * steps):
        steps //= 2

    def tall(item):
        return pl.BlockSpec((item.shape[0] // steps, item.shape[1]), lambda i: (i, 0))

    owners, _, both = mix.shape
    wide, thin = tall(wa), tall(gain)
    return pl.pallas_call(
        finish_rest_kernel,
        grid=(steps,),
        out_shape=(
            jax.ShapeDtypeStruct(wa.shape, f32),
            jax.ShapeDtypeStruct(wa.shape, f32),
            jax.ShapeDtypeStruct((rows, 1), f32),
            jax.ShapeDtypeStruct(out_sum.shape, f32),
            jax.ShapeDtypeStruct(down_sum.shape, f32),
        ),
        in_specs=[
            thin,
            pl.BlockSpec((owners, rows // steps, both), lambda i: (0, i, 0)),
            wide,
            wide,
            tall(out_sum),
            tall(down_sum),
        ],
        out_specs=[wide, wide, thin, tall(out_sum), tall(down_sum)],
        compiler_params=pltpu.CompilerParams(vmem_limit_bytes=61 * 2**20),
        cost_estimate=pl.CostEstimate(flops=10**7, bytes_accessed=40 * 2**20, transcendentals=0),
    )(gain, mix, wa, wb, out_sum, down_sum)


def body(
    tokens,
    segments,
    cotangent,
    norm_gain,
    branch_weight,
    input_weight,
    conv_weight,
    conv_bias,
    recur_gate_weight,
    recur_gate_bias,
    input_gate_weight,
    input_gate_bias,
    decay_param,
    output_weight,
    mlp_norm_gain,
    gate_weight,
    up_weight,
    down_weight,
):
    x, cot = tokens[0], cotangent[0]
    rows, depth = x.shape
    members = lax.axis_size(GROUP)
    sequences = lax.axis_size("shard")
    total = members * rows
    gain, mlp_gain = low(norm_gain)[:, None], low(mlp_norm_gain)[:, None]
    own_labels = jnp.broadcast_to(segments[0].astype(bf16)[:, None], (rows, 128))
    width = branch_weight.shape[1] // members
    conv_f = low(conv_weight)
    decay_f = low(decay_param)
    bias = jnp.stack([low(conv_bias), low(recur_gate_bias), low(input_gate_bias), jax.nn.softplus(-decay_f)])
    (
        unit_all, labels, out_low, product, *mixed, mix_w, output_w, unit_two, middle, pair_w,
    ) = front(
        sequences, x, own_labels, cot, low(jnp.stack([norm_gain, mlp_norm_gain], 1)), conv_f, bias,
        recur_gate_weight, input_gate_weight, branch_weight, input_weight, gate_weight, up_weight, output_weight,
    )
    pair_w = pair_w.reshape(depth, -1)
    down_w = down_weight.astype(bf16)
    whole = ((total, depth), bf16)
    ff = pair_w.shape[1] // 2
    gate_pre = mm(unit_two, pair_w[:, :ff])
    up_pre = mm(unit_two, pair_w[:, ff:])
    hidden_grad = mm_nt(out_low, down_w)
    gate_act, gate_slope = gelu_parts(gate_pre)
    hidden = (gate_act * up_pre).astype(bf16)
    gate_low = (hidden_grad * up_pre * gate_slope).astype(bf16)
    up_low = (hidden_grad * gate_act).astype(bf16)
    pair_low = jnp.concatenate([gate_low, up_low], 1)
    partial = mm_nt(pair_low, pair_w).astype(bf16)
    pair_partial = mm_tn(unit_two, pair_low).astype(bf16).reshape(members, -1, 2 * ff)
    down_partial = mm_tn(hidden, out_low).astype(bf16)[None]
    kept = (output_w, mix_w, *mixed)
    narrow = ((total, width), bf16)
    vm, dma = pltpu.VMEM, pltpu.SemaphoreType.DMA
    length = total // sequences
    back = replica_sum(
        [down_partial, pair_partial], ["row", "pair"], 3,
        functools.partial(turn_steps, sequences, length),
        (6, 12) + tuple(range(14, 14 + 2 * sequences + 2)),
        [(partial, ANY)] + [(item, VM) for item in (middle, cot, labels, conv_f, bias, recur_gate_weight, input_gate_weight)]
        + [(item, ANY) for item in kept],
        [whole + (ANY,), ((rows, depth), f32, ANY), whole + (ANY,), narrow + (ANY,), narrow + (ANY,)]
        + [(conv_f.shape, f32, VM), ((4, width), f32, VM), (recur_gate_weight.shape, f32, VM), (input_gate_weight.shape, f32, VM)],
        plane_scratch(rows, depth, 1, 1)
        + [vm(item.shape, item.dtype) for item in kept]
        + [vm(*whole), vm(*whole), vm((rows, depth), f32), vm(*narrow), vm(*narrow), vm(mixed[-1].shape, f32)]
        + [vm((8 + length, width), f32), vm((8 + length, 128), f32)]
        + [vm((width, width), f32)] * 4
        + [dma((10,)), dma((5,))],
    )
    down_sum, gate_sum, up_sum, mid_low, middle_grad, partial, branch_low, conv_low = back[:8]
    conv_weight_grad, sums, recur_weight_grad, inject_weight_grad = back[8:]
    gate_grad, up_grad, mlp_gain_grad = finish_pair(mlp_gain, gate_sum, up_sum, gate_weight, up_weight)
    output_partial = mm_tn(product, mid_low).astype(bf16)[None]
    mix_low = jnp.concatenate([branch_low, conv_low], 1)
    mix_low = jnp.pad(mix_low, ((0, 0), (0, -2 * width % 128)))
    mix_partial = mm_tn(unit_all, mix_low).astype(bf16).reshape(members, -1, mix_low.shape[1])
    size = recur_gate_weight.shape[1]
    gates = jnp.concatenate([recur_weight_grad, inject_weight_grad], 2).reshape(width, 2 * size)
    lanes = -(-max(width, 2 * size) // 128) * 128
    lines = jnp.concatenate([conv_weight_grad, sums], 0)
    packed = jnp.concatenate(
        [
            jnp.pad(gates, ((0, 0), (0, lanes - 2 * size))),
            jnp.pad(lines, ((0, 16 - lines.shape[0]), (0, lanes - width))),
        ],
        0,
    ).astype(bf16)[None]
    again = plane_scratch(rows, depth, 1, 1)
    output_sum, mix_sum, packed, tokens_grad, block_out = replica_sum(
        [output_partial, mix_partial, packed], ["row", "side", "row"], 4, end_steps, (1, 2, 3, 4, 6, 7, 14),
        [(partial, ANY), (middle_grad, VM), (x, VM), (middle, VM), (hidden, ANY), (down_w, ANY)],
        [((rows, depth), bf16, VM), ((rows, depth), bf16, VM)],
        again + again[:2] + [vm(*whole), vm(*whole), vm(hidden.shape, bf16), vm(down_w.shape, bf16), dma((3,))],
    )
    packed = packed.astype(f32)
    branch_grad, input_grad, gain_grad, output_grad, down_grad = finish_rest(
        gain, mix_sum, branch_weight, input_weight, output_sum, down_sum
    )
    recur_weight_grad = packed[:width, :size].reshape(-1, size, size)
    inject_weight_grad = packed[:width, size : 2 * size].reshape(-1, size, size)
    conv_weight_grad = packed[width : width + conv_weight.shape[0], :width]
    conv_bias_grad, recur_bias_grad, inject_bias_grad, rate_grad = [packed[width + conv_weight.shape[0] + i, :width] for i in range(4)]
    decay_param_grad = rate_grad * decay_scale * jax.nn.sigmoid(-decay_f)
    return (
        block_out[None],
        tokens_grad[None],
        gain_grad[:, 0],
        branch_grad,
        input_grad,
        conv_weight_grad,
        conv_bias_grad,
        recur_weight_grad,
        recur_bias_grad,
        inject_weight_grad,
        inject_bias_grad,
        decay_param_grad,
        output_grad,
        mlp_gain_grad[:, 0],
        gate_grad,
        up_grad,
        down_grad,
    )


def solution(mesh):
    row3 = P(("shard", "replica"), "seq", None)
    vec = P(("seq", "shard"))
    mat = P(("seq", "shard"), None)
    cube = P(("seq", "shard"), None, None)
    taps = P(None, ("seq", "shard"))
    params = (vec, mat, mat, taps, vec, cube, vec, cube, vec, vec, mat, vec, mat, mat, mat)
    in_specs = (row3, P(("shard", "replica"), "seq"), row3) + params
    out_specs = (row3, row3) + params
    return jax.shard_map(body, mesh=mesh, in_specs=in_specs, out_specs=out_specs, check_vma=False)
```

```python
import functools

import jax
import jax.numpy as jnp
from jax import lax
from jax.experimental import pallas as pl
from jax.experimental.pallas import tpu as pltpu
from jax.sharding import PartitionSpec as P

epsilon = 1e-06
decay_scale = 8.0
GROUP = ("seq", "shard")
ROWS = ("shard", "seq")
f32 = jnp.float32
bf16 = jnp.bfloat16
VM = pl.BlockSpec(memory_space=pltpu.VMEM)
ANY = pl.BlockSpec(memory_space=pl.ANY)
MESH = pl.DeviceIdType.MESH


def mm(left, right):
    return jnp.dot(left, right, preferred_element_type=f32)


def mm_nt(left, right):
    return lax.dot_general(left, right, (((1,), (1,)), ((), ())), preferred_element_type=f32)


def mm_tn(left, right):
    return lax.dot_general(left, right, (((0,), (0,)), ((), ())), preferred_element_type=f32)


def low(item):
    return item.astype(bf16).astype(f32)


def by_owner(weight, gain):
    owners = lax.axis_size(GROUP)
    scaled = (low(weight) * gain).astype(bf16)
    return jnp.swapaxes(scaled.reshape(weight.shape[0], owners, -1), 0, 1)


def swap(cut):
    return lax.all_to_all(cut, GROUP, split_axis=0, concat_axis=0, tiled=True)


def gelu_parts(x):
    inner = 0.7978845608028654 * (x + 0.044715 * x * x * x)
    t = jnp.tanh(inner)
    value = 0.5 * x * (1.0 + t)
    slope = 0.5 * (1.0 + t) + 0.5 * x * (1.0 - t * t) * 0.7978845608028654 * (
        1.0 + 3.0 * 0.044715 * x * x
    )
    return value, slope


def minus_expm1(y):
    poly = 1.0 + y * (1.0 / 8.0)
    for order in (7.0, 6.0, 5.0, 4.0, 3.0, 2.0):
        poly = 1.0 + y * (1.0 / order) * poly
    return jnp.where(y > -0.5, -y * poly, 1.0 - jnp.exp(y))


def dot_nn(a, b):
    return lax.dot_general(a, b, (((1,), (0,)), ((), ())), preferred_element_type=f32)


def dot_nt(a, b):
    return lax.dot_general(a, b, (((1,), (1,)), ((), ())), preferred_element_type=f32)


def dot_tn(a, b):
    return lax.dot_general(a, b, (((0,), (0,)), ((), ())), preferred_element_type=f32)


def whole_weight(ref, part):
    owners, _, rows, width = ref.shape
    return ref[:, part].reshape(owners * rows, width)


def fill_blocks(target, source):
    target[...] = jnp.zeros_like(target)
    count, size = source.shape[0], source.shape[1]
    for h in range(count):
        target[h * size : (h + 1) * size, h * size : (h + 1) * size] = source[h].astype(bf16).astype(f32)


def put_tiles(ref, here, value):
    width = value.shape[1]
    for tile in range(ref.shape[0]):
        lanes = min(128, width - 128 * tile)
        ref[tile, here, 0:lanes] = value[:, 128 * tile : 128 * tile + lanes]


def get_tiles(ref, here, width):
    parts = [ref[tile, here, 0 : min(128, width - 128 * tile)] for tile in range(ref.shape[0])]
    return jnp.concatenate(parts, axis=1)


def clear_tail(ref, width):
    tail = ref.shape[0] * 128 - width
    if tail:
        ref[ref.shape[0] - 1, :, 128 - tail :] = jnp.zeros((ref.shape[1], tail), f32)


def label_masks(label_ref, here, length, width, taps, lines):
    own = label_ref[here, :].astype(f32)
    lines[0:8, :] = jnp.full((8, 128), -1.0, f32)
    lines[8 : 8 + length, :] = own
    masks = []
    for k in range(1, taps):
        same = jnp.where(lines[8 - k : 8 - k + length, :] == own, 1.0, 0.0)
        masks.append(jnp.concatenate([same] * -(-width // 128), axis=1)[:, :width])
    return masks


def seq_scan(decay_ref, value_ref, sequences, length, reverse):
    tiles = decay_ref.shape[0]
    unroll = 8

    def step(i, states):
        states = list(states)
        for j in range(unroll):
            at = i * unroll + j
            if reverse:
                at = length - 1 - at
            here = pl.ds(at, sequences, stride=length)
            for tile in range(tiles):
                value = value_ref[tile, here, :]
                decay = decay_ref[tile, here, :]
                if reverse:
                    new = value + states[tile]
                    value_ref[tile, here, :] = new
                    states[tile] = decay * new
                else:
                    states[tile] = value + decay * states[tile]
                    value_ref[tile, here, :] = states[tile]
        return tuple(states)

    lax.fori_loop(0, length // unroll, step, (jnp.zeros((sequences, 128), f32),) * tiles)


def plane():
    halves, shards = lax.axis_size("seq"), lax.axis_size("shard")
    y, s = lax.axis_index("seq"), lax.axis_index("shard")
    offsets = [(dy, ds) for ds in range(0, shards, 2) for dy in range(halves)]

    def at(dy, ds):
        return {"seq": jnp.bitwise_xor(y, dy), "shard": jnp.bitwise_xor(s, ds)}

    def block(dy, ds):
        return jnp.bitwise_xor(s, ds) * halves + jnp.bitwise_xor(y, dy)

    return offsets, at, block


def remote(src, dst, sent, got, device):
    return pltpu.make_async_remote_copy(
        src_ref=src, dst_ref=dst, send_sem=sent, recv_sem=got, device_id=device, device_id_type=MESH
    )


def row_block(ref, index, rows):
    return ref.at[pl.ds(pl.multiple_of(index * rows, rows), rows), :]


def scatter_steps(rows, partial, near, far, acc, sems):
    offsets, at, block = plane()
    near_sent, near_got, far_sent, far_got = sems
    count = len(offsets)
    order = list(range(count - 1, -1, -1))
    firsts = {}
    for q in order:
        dy, ds = offsets[q]
        firsts[q] = remote(
            row_block(partial, block(dy, ds ^ 1), rows), near.at[q], near_sent.at[q], near_got.at[q], at(0, 1)
        )
        firsts[q].start()
    seconds = {}
    for q in order:
        dy, ds = offsets[q]
        firsts[q].wait_recv()
        base = block(dy, ds) * rows

        def tile(i, _):
            step = pl.multiple_of(i * 16, 16)
            here = pl.ds(step, 16)
            total = partial[pl.ds(pl.multiple_of(base + step, 16), 16), :].astype(f32) + near[q, here, :].astype(f32)
            if q:
                near[q, here, :] = total.astype(bf16)
            else:
                acc[here, :] = total
            return 0

        lax.fori_loop(0, rows // 16, tile, 0)
        if q:
            seconds[q] = remote(near.at[q], far.at[q - 1], far_sent.at[q - 1], far_got.at[q - 1], at(dy, ds))
            seconds[q].start()
    yield None
    for q in order[:-1]:
        seconds[q].wait_recv()

        def more(i, _):
            here = pl.ds(pl.multiple_of(i * 16, 16), 16)
            acc[here, :] += far[q - 1, here, :].astype(f32)
            return 0

        lax.fori_loop(0, rows // 16, more, 0)
    yield [firsts[q].wait_send for q in order] + [seconds[q].wait_send for q in order[:-1]]


def gather_steps(rows, whole, sems):
    offsets, at, block = plane()
    near_sent, near_got, far_sent, far_got = sems
    count = len(offsets)
    half = rows // 2

    def piece(q, part):
        start = pl.multiple_of(block(*offsets[q]) * rows + part * half, 16)
        return whole.at[pl.ds(start, half), :]

    own = row_block(whole, block(0, 0), rows)
    straight = [q for q in range(1, count) if offsets[q][0] == 0 or offsets[q][1] == 0]
    across = [q for q in range(1, count) if q not in straight]
    upright = [q for q in straight if offsets[q][0]]
    sends, arrivals = [], []
    outs = {}
    for q in straight:
        outs[q] = remote(own, own, far_sent.at[q], far_got.at[q], at(*offsets[q]))
        outs[q].start()
        sends.append(outs[q].wait_send)

    def hand(q, part=None):
        source = row_block(whole, block(*offsets[q]), rows) if part is None else piece(q, part)
        place = q if part is None or part == 0 else count + q
        copy = remote(source, source, near_sent.at[place], near_got.at[place], at(0, 1))
        copy.start()
        sends.append(copy.wait_send)
        arrivals.append(copy.wait_recv)

    hand(0)
    yield None
    onward = {}
    for q in straight:
        outs[q].wait_recv()
        if q in upright:
            targets = [(1, t) for t in straight if t not in upright]
        else:
            targets = [(0, t) for t in upright]
        for part, t in targets:
            dy, ds = offsets[q][0] | offsets[t][0], offsets[q][1] | offsets[t][1]
            a = offsets.index((dy, ds))
            source = piece(q, part)
            onward[a, part] = remote(source, source, far_sent.at[part * count + a], far_got.at[part * count + a], at(*offsets[t]))
            onward[a, part].start()
            sends.append(onward[a, part].wait_send)
        hand(q)
    yield None
    for a in across:
        for part in range(2):
            onward[a, part].wait_recv()
            hand(a, part)
    yield arrivals + sends


def root_mean(rows):
    return lax.rsqrt(jnp.mean(rows * rows, axis=-1, keepdims=True) + epsilon)


def norm_backward(grad_unit, unit, inverse):
    return inverse * (grad_unit - unit * jnp.mean(grad_unit * unit, axis=-1, keepdims=True))


def by_tiles(rows, work):
    def tile(i, _):
        work(pl.ds(pl.multiple_of(i * 16, 16), 16), i)
        return 0

    lax.fori_loop(0, rows // 16, tile, 0)


def plane_scratch(rows, depth, gathers, scatters):
    count = lax.axis_size("seq") * lax.axis_size("shard") // 2
    block = (rows, depth)
    scratch = []
    if scatters:
        scratch = [
            pltpu.VMEM((count,) + block, bf16),
            pltpu.VMEM((count - 1,) + block, bf16),
            pltpu.VMEM(block, f32),
        ]
    dma = pltpu.SemaphoreType.DMA
    for _ in range(scatters):
        scratch += [dma((count,))] * 2 + [dma((count - 1,))] * 2
    for _ in range(gathers):
        scratch += [dma((2 * count,))] * 4
    return scratch


def cut_columns(weight_ref, gain, target, start, lanes):
    owners = weight_ref.shape[1] // lanes

    def tile(i, _):
        step = pl.multiple_of(i * 16, 16)
        here = pl.ds(step, 16)
        scaled = low(weight_ref[here, :]) * gain(step)
        for j in range(owners):
            target(j)[here, start : start + lanes] = scaled[:, j * lanes : (j + 1) * lanes].astype(bf16)
        return 0

    lax.fori_loop(0, weight_ref.shape[0] // 16, tile, 0)


def quarter_steps(n, part, whole, sems):
    me = lax.axis_index("replica")
    right_sent, right_got, left_sent, left_got = sems

    def rows(q):
        return whole.at[:, pl.ds(pl.multiple_of(q * part, 16), part), :]

    def to_right(hop):
        block = rows(me - hop)
        return remote(block, block, right_sent.at[hop], right_got.at[hop], {"replica": me + 1})

    def to_left(hop):
        block = rows(me + hop)
        return remote(block, block, left_sent.at[hop], left_got.at[hop], {"replica": me - 1})

    def from_left(hop):
        block = rows(me - hop - 1)
        return remote(block, block, right_sent.at[hop], right_got.at[hop], {"replica": me + 1})

    def from_right(hop):
        block = rows(me + hop + 1)
        return remote(block, block, left_sent.at[hop], left_got.at[hop], {"replica": me - 1})

    for hop in range(n - 1):
        if hop:

            @pl.when(me >= hop)
            def _():
                from_left(hop - 1).wait_recv()

            @pl.when(me + hop < n)
            def _():
                from_right(hop - 1).wait_recv()

        @pl.when(jnp.logical_and(me >= hop, me < n - 1))
        def _():
            to_right(hop).start()

        @pl.when(jnp.logical_and(me + hop < n, me > 0))
        def _():
            to_left(hop).start()

        yield

    @pl.when(me >= n - 1)
    def _():
        from_left(n - 2).wait_recv()

    @pl.when(me + n - 1 < n)
    def _():
        from_right(n - 2).wait_recv()

    for hop in range(n - 1):

        @pl.when(jnp.logical_and(me >= hop, me < n - 1))
        def _():
            to_right(hop).wait_send()

        @pl.when(jnp.logical_and(me + hop < n, me > 0))
        def _():
            to_left(hop).wait_send()

    yield


def front_kernel(
    n, sequences, length,
    x_ref, label_ref, cot_ref, gains_ref, conv_ref, bias_ref, rw_ref, iw_ref,
    branch_hbm, input_hbm, gate_hbm, up_hbm, ow_hbm,
    unit_out, labels_out, low_out, product_out, pre_out, conv_in_out, values_out, recur_out, inject_out, decay_out,
    states_out, mix_out, ow_out, two_out, middle_out, pair_out,
    unit_ref, labels_ref, product_ref, pre_ref, conv_in_ref, values_ref, recur_ref, inject_ref, decay_ref,
    states_ref, mix_ref, ow_ref, two_ref, middle_ref,
    wide, tall, ow_f, mix_cut, pair_cut, pad, lines, rbig, ibig, partial,
    near, far, acc, *sems,
):
    rows = x_ref.shape[0]
    scatter_sems, sems = sems[:4], sems[4:]
    unit_sems, label_sems, low_sems, two_sems, sems = sems[:4], sems[4:8], sems[8:12], sems[12:16], sems[16:]
    load_sem, save_sem, mix_sent, mix_got, pair_sent, pair_got = sems[:6]
    line_sems = sems[6:]
    offsets, at, block = plane()
    z = lax.axis_index("replica")
    y, s = lax.axis_index("seq"), lax.axis_index("shard")
    shards = lax.axis_size("shard")
    owners = shards * lax.axis_size("seq")
    part = gate_hbm.shape[0] // n
    width = pad.shape[1]
    ff = gate_hbm.shape[1] // owners

    def peer(i):
        return {"seq": jnp.bitwise_xor(y, i // shards), "shard": jnp.bitwise_xor(s, i % shards)}

    def place(i):
        return jnp.bitwise_xor(y, i // shards) * shards + jnp.bitwise_xor(s, i % shards)

    own_rows = pl.ds(pl.multiple_of(z * part, 16), part)
    loads = [
        pltpu.make_async_copy(gate_hbm.at[own_rows, :], tall.at[0], load_sem.at[0]),
        pltpu.make_async_copy(up_hbm.at[own_rows, :], tall.at[1], load_sem.at[1]),
        pltpu.make_async_copy(branch_hbm, wide.at[0], load_sem.at[2]),
        pltpu.make_async_copy(input_hbm, wide.at[1], load_sem.at[3]),
        pltpu.make_async_copy(ow_hbm, ow_f, load_sem.at[4]),
    ]
    for load in loads:
        load.start()
    saves = []

    def save(source, target):
        copy = pltpu.make_async_copy(source, target, save_sem.at[len(saves)])
        copy.start()
        saves.append(copy)

    low_own = pltpu.make_async_copy(cot_ref, row_block(low_out, block(0, 0), rows), load_sem.at[5])
    low_own.start()
    barrier = pltpu.get_barrier_semaphore()
    for i in range(1, owners):
        pl.semaphore_signal(barrier, inc=1, device_id=peer(i), device_id_type=MESH)

    @pl.when(z > 0)
    def _():
        pl.semaphore_signal(barrier, inc=1, device_id={"replica": z - 1}, device_id_type=MESH)

    @pl.when(z < n - 1)
    def _():
        pl.semaphore_signal(barrier, inc=1, device_id={"replica": z + 1}, device_id_type=MESH)

    for side in range(2):
        loads[side].wait()

        cut_columns(
            tall.at[side],
            lambda step: gains_ref[pl.ds(pl.multiple_of(z * part + step, 16), 16), 1:2],
            lambda j: pair_cut.at[j],
            side * ff,
            ff,
        )

    inside_line = jnp.logical_and(z > 0, z < n - 1)

    @pl.when(inside_line)
    def _():
        pl.semaphore_wait(barrier, owners + 1)

    @pl.when(jnp.logical_not(inside_line))
    def _():
        pl.semaphore_wait(barrier, owners)

    me = place(0)
    pair_there = pair_out.at[me, own_rows, :]
    pair_moves = [
        remote(pair_cut.at[place(i)], pair_there, pair_sent.at[i], pair_got.at[i], peer(i)) for i in range(1, owners)
    ]
    for move in pair_moves:
        move.start()
    pair_own = pltpu.make_async_copy(pair_cut.at[me], pair_there, pair_sent.at[0])
    pair_own.start()

    base = block(0, 0) * rows

    def unit(here, i):
        value = x_ref[here, :].astype(f32)
        there = pl.ds(pl.multiple_of(base + i * 16, 16), 16)
        unit_ref[there, :] = (value * root_mean(value)).astype(bf16)
        labels_ref[there, :] = label_ref[here, :]

    by_tiles(rows, unit)
    label_gather = gather_steps(rows, labels_ref, label_sems)
    unit_gather = gather_steps(rows, unit_ref, unit_sems)
    next(label_gather)
    next(unit_gather)

    for side in range(2):
        loads[2 + side].wait()
        cut_columns(
            wide.at[side], lambda step: gains_ref[pl.ds(step, 16), 0:1], lambda j: mix_cut.at[j, side], 0, width
        )
    mix_moves = [
        remote(mix_cut.at[place(i)], mix_ref.at[me], mix_sent.at[i], mix_got.at[i], peer(i)) for i in range(1, owners)
    ]
    for move in mix_moves:
        move.start()
    mix_own = pltpu.make_async_copy(mix_cut.at[me], mix_ref.at[me], mix_sent.at[0])
    mix_own.start()
    loads[4].wait()
    ow_ref[...] = ow_f[...].astype(bf16)
    save(ow_ref, ow_out)
    fill_blocks(rbig, rw_ref)
    fill_blocks(ibig, iw_ref)
    pad[0:8, :] = jnp.zeros((8, width), f32)
    taps = conv_ref.shape[0]
    clear_tail(decay_ref, width)
    clear_tail(states_ref, width)

    pair_own.wait()
    for move in pair_moves:
        move.wait_recv()
    line = quarter_steps(n, part, pair_out, line_sems)
    next(line)
    next(label_gather)
    next(unit_gather)
    waits = next(label_gather) + next(unit_gather)
    for wait in waits:
        wait()
    mix_own.wait()
    for move in mix_moves:
        move.wait_recv()
    save(unit_ref, unit_out)
    save(labels_ref, labels_out)
    save(mix_ref, mix_out)

    low_own.wait()
    low_gather = gather_steps(rows, low_out, low_sems)
    next(low_gather)
    next(line)

    def one(q, _):
        here = pl.ds(pl.multiple_of(q * length, length), length)
        sequence = unit_ref[here, :]
        masks = label_masks(labels_ref, here, length, width, taps, lines)
        pre_ref[here, :] = dot_nn(sequence, whole_weight(mix_ref, 0))
        conv_in = dot_nn(sequence, whole_weight(mix_ref, 1)).astype(bf16)
        conv_in_ref[here, :] = conv_in
        pad[8 : 8 + length, :] = conv_in.astype(f32)
        total = bias_ref[0:1, :] + conv_ref[0:1, :] * pad[8 : 8 + length, :]
        for k in range(1, taps):
            total = total + conv_ref[k : k + 1, :] * pad[8 - k : 8 - k + length, :] * masks[k - 1]
        values = total.astype(bf16)
        values_ref[here, :] = values
        recur = jax.nn.sigmoid(dot_nn(values, rbig[...].astype(bf16)) + bias_ref[1:2, :])
        inject = jax.nn.sigmoid(dot_nn(values, ibig[...].astype(bf16)) + bias_ref[2:3, :])
        recur_ref[here, :] = recur
        inject_ref[here, :] = inject
        log_decay = -decay_scale * bias_ref[3:4, :] * recur
        inside = masks[0] > 0.5
        put_tiles(decay_ref, here, jnp.where(inside, jnp.exp(log_decay), 0.0))
        scale = jnp.where(inside, jnp.sqrt(minus_expm1(2.0 * log_decay)), 1.0)
        put_tiles(states_ref, here, scale * inject * values.astype(f32))
        return 0

    lax.fori_loop(0, sequences, one, 0)
    seq_scan(decay_ref, states_ref, sequences, length, False)

    def two(q, _):
        here = pl.ds(pl.multiple_of(q * length, length), length)
        act, _unused = gelu_parts(pre_ref[here, :])
        product = (act * get_tiles(states_ref, here, width)).astype(bf16)
        product_ref[here, :] = product
        partial[here, :] = dot_nn(product, ow_ref[...]).astype(bf16)
        return 0

    lax.fori_loop(0, sequences, two, 0)
    scatter = scatter_steps(rows, partial, near, far, acc, scatter_sems)
    next(scatter)
    for source, target in (
        (product_ref, product_out), (pre_ref, pre_out), (conv_in_ref, conv_in_out), (values_ref, values_out),
        (recur_ref, recur_out), (inject_ref, inject_out), (decay_ref, decay_out), (states_ref, states_out),
    ):
        save(source, target)
    next(line)
    next(low_gather)
    waits = next(low_gather) + next(scatter)

    def norm(here, i):
        middle = x_ref[here, :].astype(f32) + acc[here, :]
        middle_ref[here, :] = middle
        there = pl.ds(pl.multiple_of(base + i * 16, 16), 16)
        two_ref[there, :] = (middle * root_mean(middle)).astype(bf16)

    by_tiles(rows, norm)
    two_gather = gather_steps(rows, two_ref, two_sems)
    next(two_gather)
    save(middle_ref, middle_out)
    for _ in range(n - 4):
        next(line)
    for wait in waits:
        wait()
    next(two_gather)
    for wait in next(two_gather):
        wait()
    save(two_ref, two_out)
    for _ in line:
        pass
    for move in pair_moves + mix_moves:
        move.wait_send()
    for copy in saves:
        copy.wait()


def front(sequences, x, label, cot, gains, conv, bias, rw, iw, branch_w, input_w, gate_w, up_w, output_w):
    rows, depth = x.shape
    own, n = branch_w.shape[0], lax.axis_size("replica")
    owners = lax.axis_size(GROUP)
    total, width, ff = owners * rows, branch_w.shape[1] // owners, gate_w.shape[1] // owners
    part = own // n
    length = total // sequences
    tiles = -(-width // 128)
    kept = [
        ((total, depth), bf16), ((total, 128), bf16), ((total, depth), bf16), ((total, width), bf16),
        ((total, width), f32), ((total, width), bf16), ((total, width), bf16), ((total, width), f32),
        ((total, width), f32), ((tiles, total, 128), f32), ((tiles, total, 128), f32), ((owners, 2, own, width), bf16),
        ((width, depth), bf16), ((total, depth), bf16), ((rows, depth), f32),
    ]
    vm = pltpu.VMEM
    dma = pltpu.SemaphoreType.DMA
    scratch = [vm(*item) for k, item in enumerate(kept) if k != 2] + [
        vm((2,) + branch_w.shape, f32),
        vm((2, part, gate_w.shape[1]), f32),
        vm(output_w.shape, f32),
        vm((owners, 2, own, width), bf16),
        vm((owners, part, 2 * ff), bf16),
        vm((8 + length, width), f32),
        vm((8 + length, 128), f32),
        vm((width, width), f32),
        vm((width, width), f32),
        vm((total, depth), bf16),
    ]
    scratch += plane_scratch(rows, depth, 4, 1)
    scratch += [dma((6,)), dma((len(kept),))] + [dma((owners,))] * 4 + [dma((n - 1,))] * 4
    outs = kept + [((owners, own, 2 * ff), bf16)]
    return pl.pallas_call(
        functools.partial(front_kernel, n, sequences, length),
        out_shape=tuple(jax.ShapeDtypeStruct(*item) for item in outs),
        in_specs=[VM] * 8 + [ANY] * 5,
        out_specs=[ANY] * len(outs),
        scratch_shapes=scratch,
        compiler_params=pltpu.CompilerParams(
            collective_id=1, has_side_effects=True, vmem_limit_bytes=60 * 2**20
        ),
        cost_estimate=pl.CostEstimate(flops=10**6, bytes_accessed=200 * 2**20, transcendentals=0),
    )(x, label, cot, gains, conv, bias, rw, iw, branch_w, input_w, gate_w, up_w, output_w)


def turn_steps(
    sequences, length,
    partial_hbm, middle_ref, cot_ref, label_ref, conv_ref, bias_ref, rw_ref, iw_ref, *rest,
):
    kept_hbm, rest = rest[:9], rest[9:]
    low_out, grad_out, partial_out, branch_low_out, conv_low_out, dconv_ref, sums_ref, drw_ref, diw_ref = rest[:9]
    scatter_sems, gather_sems = rest[9 + 3 : 9 + 7], rest[9 + 7 : 9 + 11]
    near, far, acc = rest[9:12]
    rest = rest[20:]
    kept, rest = rest[:9], rest[9:]
    ow_ref, w_ref, pre_ref, conv_in_ref, values_ref, recur_ref, inject_ref, decay_ref, states_ref = kept
    partial, low_ref, grad_ref, branch_low_ref, conv_low_ref, adj, pad, lines, rbig, ibig, dr, di, load_sem, save_sem = rest
    rows = middle_ref.shape[0]
    offsets, at, block = plane()
    first = pltpu.make_async_copy(partial_hbm, partial, load_sem.at[9])
    first.start()
    loads = [pltpu.make_async_copy(kept_hbm[k], kept[k], load_sem.at[k]) for k in range(9)]
    for load in loads:
        load.start()
    first.wait()
    scatter = scatter_steps(rows, partial, near, far, acc, scatter_sems)
    next(scatter)
    yield
    waits = next(scatter)
    base = block(0, 0) * rows

    def norm(here, i):
        middle = middle_ref[here, :]
        inverse = root_mean(middle)
        grad = cot_ref[here, :].astype(f32) + norm_backward(acc[here, :], middle * inverse, inverse)
        grad_ref[here, :] = grad
        there = pl.ds(pl.multiple_of(base + i * 16, 16), 16)
        low_ref[there, :] = grad.astype(bf16)

    by_tiles(rows, norm)
    gather = gather_steps(rows, low_ref, gather_sems)
    next(gather)
    yield
    next(gather)
    yield
    waits = waits + next(gather)
    yield
    for wait in waits:
        wait()
    for load in loads:
        load.wait()
    saves = [pltpu.make_async_copy(low_ref, low_out, save_sem.at[0]), pltpu.make_async_copy(grad_ref, grad_out, save_sem.at[1])]
    for save in saves:
        save.start()
    fill_blocks(rbig, rw_ref)
    fill_blocks(ibig, iw_ref)
    dr[...] = jnp.zeros_like(dr)
    di[...] = jnp.zeros_like(di)
    sums_ref[...] = jnp.zeros_like(sums_ref)
    dconv_ref[...] = jnp.zeros_like(dconv_ref)
    taps = conv_ref.shape[0]
    width = pad.shape[1]
    clear_tail(adj, width)

    def one(s):
        here = pl.ds(s * length, length)
        product_grad = dot_nt(low_ref[here, :], ow_ref[...])
        act, slope = gelu_parts(pre_ref[here, :])
        branch_low_ref[here, :] = (product_grad * get_tiles(states_ref, here, width) * slope).astype(bf16)
        put_tiles(adj, here, product_grad * act)

    for s in range(sequences):
        one(s)
        yield
    seq_scan(decay_ref, adj, sequences, length, True)
    yield

    def two(s):
        here = pl.ds(s * length, length)
        adjoint = get_tiles(adj, here, width)
        recur = recur_ref[here, :]
        inject = inject_ref[here, :]
        decay = get_tiles(decay_ref, here, width)
        values = values_ref[here, :]
        values_f = values.astype(f32)
        masks = label_masks(label_ref, here, length, width, taps, lines)
        inside = masks[0] > 0.5
        rate = bias_ref[3:4, :]
        log_decay = -decay_scale * rate * recur
        scale = jnp.where(inside, jnp.sqrt(minus_expm1(2.0 * log_decay)), 1.0)
        pad[0:8, :] = jnp.zeros((8, width), f32)
        pad[8 : 8 + length, :] = get_tiles(states_ref, here, width)
        previous = pad[7 : 7 + length, :]
        driven = adjoint * inject * values_f
        log_grad = jnp.where(inside, adjoint * previous * decay - driven * decay * decay / scale, 0.0)
        recur_low = (log_grad * (-decay_scale * rate) * recur * (1.0 - recur)).astype(bf16)
        inject_low = (driven * scale * (1.0 - inject)).astype(bf16)
        sums_ref[1:2, :] += jnp.sum(recur_low.astype(f32), axis=0, keepdims=True)
        sums_ref[2:3, :] += jnp.sum(inject_low.astype(f32), axis=0, keepdims=True)
        sums_ref[3:4, :] += jnp.sum(log_grad * recur, axis=0, keepdims=True)
        dr[...] += dot_tn(values, recur_low)
        di[...] += dot_tn(values, inject_low)
        grad = adjoint * scale * inject
        grad = grad + dot_nt(recur_low, rbig[...].astype(bf16)) + dot_nt(inject_low, ibig[...].astype(bf16))
        sums_ref[0:1, :] += jnp.sum(grad, axis=0, keepdims=True)
        pad[8 : 8 + length, :] = conv_in_ref[here, :].astype(f32)
        dconv_ref[0:1, :] += jnp.sum(grad * pad[8 : 8 + length, :], axis=0, keepdims=True)
        masked = []
        for k in range(1, taps):
            part = grad * masks[k - 1]
            masked.append(part)
            dconv_ref[k : k + 1, :] += jnp.sum(part * pad[8 - k : 8 - k + length, :], axis=0, keepdims=True)
        total = grad * conv_ref[0:1, :]
        pad[length : length + 8, :] = jnp.zeros((8, width), f32)
        for k in range(1, taps):
            pad[0:length, :] = masked[k - 1] * conv_ref[k : k + 1, :]
            total = total + pad[k : k + length, :]
        conv_low = total.astype(bf16)
        conv_low_ref[here, :] = conv_low
        partial[here, :] = (dot_nt(branch_low_ref[here, :], whole_weight(w_ref, 0)) + dot_nt(conv_low, whole_weight(w_ref, 1))).astype(bf16)

    for s in range(sequences):
        two(s)
        yield
    size = drw_ref.shape[1]
    for h in range(drw_ref.shape[0]):
        cut = slice(h * size, (h + 1) * size)
        drw_ref[h] = dr[cut, cut]
        diw_ref[h] = di[cut, cut]
    ends = [(partial, partial_out), (branch_low_ref, branch_low_out), (conv_low_ref, conv_low_out)]
    for k, pair in enumerate(ends):
        saves.append(pltpu.make_async_copy(*pair, save_sem.at[2 + k]))
        saves[-1].start()
    yield
    for save in saves:
        save.wait()


def end_steps(
    partial_hbm, grad_ref, x_ref, middle_ref, hidden_hbm, down_hbm, tokens_ref, block_ref, *rest,
):
    near, far, acc = rest[:3]
    scatter_sems = rest[3:7]
    more_sems = rest[7:11]
    near_two, far_two, partial, partial_two, hidden, down, load_sem = rest[11:]
    rows = x_ref.shape[0]
    loads = [
        pltpu.make_async_copy(source, target, load_sem.at[k])
        for k, (source, target) in enumerate(((partial_hbm, partial), (hidden_hbm, hidden), (down_hbm, down)))
    ]
    for load in loads:
        load.start()
    loads[0].wait()
    scatter = scatter_steps(rows, partial, near, far, acc, scatter_sems)
    next(scatter)
    yield
    loads[1].wait()
    loads[2].wait()
    pieces_of = 4
    height = hidden.shape[0] // pieces_of
    for k in range(pieces_of):
        here = pl.ds(k * height, height)
        partial_two[here, :] = dot_nn(hidden[here, :], down[...]).astype(bf16)
        yield
    waits = next(scatter)

    def norm(here, i):
        value = x_ref[here, :].astype(f32)
        inverse = root_mean(value)
        grad = grad_ref[here, :] + norm_backward(acc[here, :], value * inverse, inverse)
        tokens_ref[here, :] = grad.astype(bf16)

    by_tiles(rows, norm)
    yield
    scatter = scatter_steps(rows, partial_two, near_two, far_two, acc, more_sems)
    next(scatter)
    yield
    waits = waits + next(scatter)

    def out(here, i):
        block_ref[here, :] = (middle_ref[here, :] + acc[here, :]).astype(bf16)

    by_tiles(rows, out)
    yield
    for wait in waits:
        wait()


def pieces(rows, most):
    count = -(-rows // most)
    while rows % count or (rows // count) % 16:
        count += 1
    return count


def line_kernel(n, kinds, cuts, beside, turns, extra, *refs):
    ins = len(cuts)
    made = ins + kinds.count("pair")
    extra_ins, extra_outs, extra_scratch = extra
    refs = list(refs)

    def take(count):
        taken = refs[:count]
        del refs[:count]
        return taken

    own_hbm, side_in = take(ins), take(extra_ins)
    outs, side_out = take(made), take(extra_outs)
    side_scratch = take(extra_scratch)
    from_out, from_in = take(ins), take(ins)
    slots, whole_sem, slot_sem, sent_in, sent_out, got_out, got_in, sent_x, got_x = refs
    depth = slots.shape[0]
    me = lax.axis_index("replica")
    y, s = lax.axis_index("seq"), lax.axis_index("shard")
    shards = lax.axis_size("shard")
    owners = shards * lax.axis_size("seq")
    left = me < n // 2
    inward = jnp.where(left, me + 1, me - 1)
    outward = jnp.where(left, me - 1, me + 1)
    has_out = jnp.logical_and(me > 0, me < n - 1)
    at_end = jnp.logical_not(has_out)
    middle = jnp.logical_or(me == n // 2 - 1, me == n // 2)

    def peer(i):
        return {"seq": jnp.bitwise_xor(y, i // shards), "shard": jnp.bitwise_xor(s, i % shards)}

    def place(i):
        return jnp.bitwise_xor(y, i // shards) * shards + jnp.bitwise_xor(s, i % shards)

    chunks = []
    for k, (lead, count, rows) in enumerate(cuts):
        for step in range(lead):
            for i in range(count):
                chunks.append((k, step if kinds[k] == "row" else (step + 1) % lead, i * rows, rows))
    total = len(chunks)

    def view(group, c):
        k, i, start, rows = chunks[c]
        return group[k].at[0 if kinds[k] == "row" else place(i), pl.ds(start, rows), :]

    def slot(c):
        k, i, start, rows = chunks[c]
        return slots.at[c % depth, pl.ds(0, rows), pl.ds(0, from_in[k].shape[2])]

    def load(c):
        return pltpu.make_async_copy(view(own_hbm, c), slot(c), slot_sem.at[c % depth])

    wholes = [pltpu.make_async_copy(own_hbm[k], from_out[k], whole_sem.at[k]) for k in range(ins)]

    @pl.when(at_end)
    def _():
        for item in wholes:
            item.start()

    @pl.when(has_out)
    def _():
        for c in range(min(depth - 1, total)):
            load(c).start()

    barrier = pltpu.get_barrier_semaphore()
    for i in range(1, owners):
        pl.semaphore_signal(barrier, inc=1, device_id=peer(i), device_id_type=MESH)
    pl.semaphore_signal(barrier, inc=1, device_id={"replica": inward}, device_id_type=MESH)

    @pl.when(has_out)
    def _():
        pl.semaphore_signal(barrier, inc=1, device_id={"replica": outward}, device_id_type=MESH)
        pl.semaphore_wait(barrier, owners + 1)

    @pl.when(at_end)
    def _():
        pl.semaphore_wait(barrier, owners)

    def push(group, target, c, sent, got, device):
        return remote(view(group, c), view(target, c), sent.at[c], got.at[c], {"replica": device})

    def add(target, other, c):
        k, i, start, rows = chunks[c]
        into, more = view(target, c), slot(c) if other is None else view(other, c)

        def tile(t, _):
            here = pl.ds(pl.multiple_of(t * 16, 16), 16)
            into[here, :] = (into[here, :].astype(f32) + more[here, :].astype(f32)).astype(bf16)
            return 0

        lax.fori_loop(0, rows // 16, tile, 0)

    def pass_in(c):
        @pl.when(middle)
        def _():
            push(from_out, from_in, c, sent_in, got_in, inward).start()

        @pl.when(jnp.logical_not(middle))
        def _():
            push(from_out, from_out, c, sent_in, got_out, inward).start()

    def gather_in(c):
        @pl.when(has_out)
        def _():
            load(c).wait()
            push(from_out, from_out, c, sent_in, got_out, inward).wait_recv()
            add(from_out, None, c)
            pass_in(c)
            if c + depth - 1 < total:
                load(c + depth - 1).start()

    @pl.when(at_end)
    def _():
        for c in range(total):
            if c == 0 or chunks[c][0] != chunks[c - 1][0]:
                wholes[chunks[c][0]].wait()
            pass_in(c)

    work = beside(*side_in, *side_out, *side_scratch)
    next(work)

    def deliveries(c):
        k, i, start, rows = chunks[c]
        here = pl.ds(start, rows)
        first = k + kinds[:k].count("pair")
        source = view(from_in, c)
        if kinds[k] == "row":
            ends = [(source, outs[first].at[here, :])]
        elif kinds[k] == "side":
            ends = [(source, outs[first].at[place(0), here, :])]
        else:
            half = source.shape[1] // 2
            there = pl.ds(pl.multiple_of(place(0) * half, half), half)
            ends = [
                (source.at[:, pl.ds(part * half, half)], outs[first + part].at[here, there]) for part in range(2)
            ]
        if kinds[k] == "row" or i == 0:
            return [pltpu.make_async_copy(*pair, sent_x.at[c, p]) for p, pair in enumerate(ends)], False
        return [remote(*pair, sent_x.at[c, p], got_x.at[c, p], peer(i)) for p, pair in enumerate(ends)], True

    def give_back(c):
        push(from_out, from_in, c, sent_out, got_in, inward).wait_recv()

        @pl.when(middle)
        def _():
            add(from_in, from_out, c)

        @pl.when(has_out)
        def _():
            push(from_in, from_in, c, sent_out, got_in, outward).start()

        for copy in deliveries(c)[0]:
            copy.start()

    lag = 2
    for c in range(total + lag):
        for _ in range(turns.count(c)):
            next(work)
        if c < total:
            gather_in(c)
        if c >= lag:
            give_back(c - lag)
    for _ in work:
        pass
    for c in range(total):
        copies, away = deliveries(c)
        for copy in copies:
            if away:
                copy.wait_recv()
                copy.wait_send()
            else:
                copy.wait()
        push(from_out, from_in, c, sent_in, got_in, inward).wait_send()

        @pl.when(has_out)
        def _():
            push(from_in, from_in, c, sent_out, got_in, outward).wait_send()


def replica_sum(arrays, kinds, identity, beside, turns, inputs, results, side_scratch):
    cuts, outs = [], []
    tall = broad = 0
    for item, kind in zip(arrays, kinds):
        lead, height, columns = item.shape
        count = pieces(height, max(16, (105 * 1024) // columns // 16 * 16))
        cuts.append((lead, count, height // count))
        tall, broad = max(tall, height // count), max(broad, columns)
        if kind == "pair":
            outs += [jax.ShapeDtypeStruct((height, lead * columns // 2), bf16)] * 2
        elif kind == "side":
            outs.append(jax.ShapeDtypeStruct(item.shape, bf16))
        else:
            outs.append(jax.ShapeDtypeStruct((height, columns), bf16))
    count = sum(lead * cut for lead, cut, _ in cuts)
    buffers = [pltpu.VMEM(item.shape, bf16) for item in arrays]
    dma = pltpu.SemaphoreType.DMA
    return pl.pallas_call(
        functools.partial(
            line_kernel, lax.axis_size("replica"), tuple(kinds), tuple(cuts), beside, turns,
            (len(inputs), len(results), len(side_scratch)),
        ),
        out_shape=tuple(outs) + tuple(jax.ShapeDtypeStruct(shape, kind) for shape, kind, _ in results),
        in_specs=[ANY] * len(arrays) + [spec for _, spec in inputs],
        out_specs=[ANY] * len(outs) + [spec for _, _, spec in results],
        scratch_shapes=list(side_scratch)
        + buffers * 2
        + [pltpu.VMEM((4, tall, broad), bf16), dma((len(arrays),)), dma((4,))]
        + [dma((count,))] * 4
        + [dma((count, 2))] * 2,
        compiler_params=pltpu.CompilerParams(
            collective_id=identity, has_side_effects=True, vmem_limit_bytes=61 * 2**20
        ),
        cost_estimate=pl.CostEstimate(flops=10**6, bytes_accessed=200 * 2**20, transcendentals=0),
    )(*arrays, *[item for item, _ in inputs])


def finish_pair_kernel(gain_ref, a_ref, b_ref, wa_ref, wb_ref, outa_ref, outb_ref, grad_ref):
    grad = jnp.zeros(gain_ref.shape, f32)
    for sum_ref, weight_ref, out_ref in ((a_ref, wa_ref, outa_ref), (b_ref, wb_ref, outb_ref)):
        total = sum_ref[...].astype(f32)
        out_ref[...] = total * gain_ref[...]
        grad = grad + jnp.sum(total * low(weight_ref[...]), axis=1, keepdims=True)
    grad_ref[...] = grad


def finish_pair(gain, a, b, wa, wb):
    rows, columns = wa.shape
    cut = min(rows, 32)
    wide = pl.BlockSpec((cut, columns), lambda i: (i, 0))
    thin = pl.BlockSpec((cut, 1), lambda i: (i, 0))
    out = jax.ShapeDtypeStruct((rows, columns), f32)
    return pl.pallas_call(
        finish_pair_kernel,
        grid=(rows // cut,),
        out_shape=(out, out, jax.ShapeDtypeStruct((rows, 1), f32)),
        in_specs=[thin, wide, wide, wide, wide],
        out_specs=[wide, wide, thin],
        compiler_params=pltpu.CompilerParams(vmem_limit_bytes=61 * 2**20),
        cost_estimate=pl.CostEstimate(flops=6 * rows * columns, bytes_accessed=20 * rows * columns, transcendentals=0),
    )(gain, a, b, wa, wb)


def finish_rest_kernel(gain_ref, mix_ref, wa_ref, wb_ref, out_sum_ref, down_sum_ref, outa_ref, outb_ref, grad_ref, out_ref, down_ref):
    owners = mix_ref.shape[0]
    width = wa_ref.shape[1] // owners
    grad = jnp.zeros(gain_ref.shape, f32)
    for part, (weight_ref, target_ref) in enumerate(((wa_ref, outa_ref), (wb_ref, outb_ref))):
        total = jnp.concatenate(
            [mix_ref[j, :, part * width : (part + 1) * width].astype(f32) for j in range(owners)], axis=1
        )
        target_ref[...] = total * gain_ref[...]
        grad = grad + jnp.sum(total * low(weight_ref[...]), axis=1, keepdims=True)
    grad_ref[...] = grad
    out_ref[...] = out_sum_ref[...].astype(f32)
    down_ref[...] = down_sum_ref[...].astype(f32)


def finish_rest(gain, mix, wa, wb, out_sum, down_sum):
    rows, columns = wa.shape
    steps = 4
    while out_sum.shape[0] % (16 * steps) or down_sum.shape[0] % (16 * steps) or rows % (16 * steps):
        steps //= 2

    def tall(item):
        return pl.BlockSpec((item.shape[0] // steps, item.shape[1]), lambda i: (i, 0))

    owners, _, both = mix.shape
    wide, thin = tall(wa), tall(gain)
    return pl.pallas_call(
        finish_rest_kernel,
        grid=(steps,),
        out_shape=(
            jax.ShapeDtypeStruct(wa.shape, f32),
            jax.ShapeDtypeStruct(wa.shape, f32),
            jax.ShapeDtypeStruct((rows, 1), f32),
            jax.ShapeDtypeStruct(out_sum.shape, f32),
            jax.ShapeDtypeStruct(down_sum.shape, f32),
        ),
        in_specs=[
            thin,
            pl.BlockSpec((owners, rows // steps, both), lambda i: (0, i, 0)),
            wide,
            wide,
            tall(out_sum),
            tall(down_sum),
        ],
        out_specs=[wide, wide, thin, tall(out_sum), tall(down_sum)],
        compiler_params=pltpu.CompilerParams(vmem_limit_bytes=61 * 2**20),
        cost_estimate=pl.CostEstimate(flops=10**7, bytes_accessed=40 * 2**20, transcendentals=0),
    )(gain, mix, wa, wb, out_sum, down_sum)


def body(
    tokens,
    segments,
    cotangent,
    norm_gain,
    branch_weight,
    input_weight,
    conv_weight,
    conv_bias,
    recur_gate_weight,
    recur_gate_bias,
    input_gate_weight,
    input_gate_bias,
    decay_param,
    output_weight,
    mlp_norm_gain,
    gate_weight,
    up_weight,
    down_weight,
):
    x, cot = tokens[0], cotangent[0]
    rows, depth = x.shape
    members = lax.axis_size(GROUP)
    sequences = lax.axis_size("shard")
    total = members * rows
    gain, mlp_gain = low(norm_gain)[:, None], low(mlp_norm_gain)[:, None]
    own_labels = jnp.broadcast_to(segments[0].astype(bf16)[:, None], (rows, 128))
    width = branch_weight.shape[1] // members
    conv_f = low(conv_weight)
    decay_f = low(decay_param)
    bias = jnp.stack([low(conv_bias), low(recur_gate_bias), low(input_gate_bias), jax.nn.softplus(-decay_f)])
    (
        unit_all, labels, out_low, product, *mixed, mix_w, output_w, unit_two, middle, pair_w,
    ) = front(
        sequences, x, own_labels, cot, low(jnp.stack([norm_gain, mlp_norm_gain], 1)), conv_f, bias,
        recur_gate_weight, input_gate_weight, branch_weight, input_weight, gate_weight, up_weight, output_weight,
    )
    pair_w = pair_w.reshape(depth, -1)
    down_w = down_weight.astype(bf16)
    whole = ((total, depth), bf16)
    ff = pair_w.shape[1] // 2
    gate_pre = mm(unit_two, pair_w[:, :ff])
    up_pre = mm(unit_two, pair_w[:, ff:])
    hidden_grad = mm_nt(out_low, down_w)
    gate_act, gate_slope = gelu_parts(gate_pre)
    hidden = (gate_act * up_pre).astype(bf16)
    gate_low = (hidden_grad * up_pre * gate_slope).astype(bf16)
    up_low = (hidden_grad * gate_act).astype(bf16)
    pair_low = jnp.concatenate([gate_low, up_low], 1)
    partial = mm_nt(pair_low, pair_w).astype(bf16)
    pair_partial = mm_tn(unit_two, pair_low).astype(bf16).reshape(members, -1, 2 * ff)
    down_partial = mm_tn(hidden, out_low).astype(bf16)[None]
    kept = (output_w, mix_w, *mixed)
    narrow = ((total, width), bf16)
    vm, dma = pltpu.VMEM, pltpu.SemaphoreType.DMA
    length = total // sequences
    back = replica_sum(
        [down_partial, pair_partial], ["row", "pair"], 3,
        functools.partial(turn_steps, sequences, length),
        (6, 9, 12) + tuple(range(14, 14 + 2 * sequences + 2)),
        [(partial, ANY)] + [(item, VM) for item in (middle, cot, labels, conv_f, bias, recur_gate_weight, input_gate_weight)]
        + [(item, ANY) for item in kept],
        [whole + (ANY,), ((rows, depth), f32, ANY), whole + (ANY,), narrow + (ANY,), narrow + (ANY,)]
        + [(conv_f.shape, f32, VM), ((4, width), f32, VM), (recur_gate_weight.shape, f32, VM), (input_gate_weight.shape, f32, VM)],
        plane_scratch(rows, depth, 1, 1)
        + [vm(item.shape, item.dtype) for item in kept]
        + [vm(*whole), vm(*whole), vm((rows, depth), f32), vm(*narrow), vm(*narrow), vm(mixed[-1].shape, f32)]
        + [vm((8 + length, width), f32), vm((8 + length, 128), f32)]
        + [vm((width, width), f32)] * 4
        + [dma((10,)), dma((5,))],
    )
    down_sum, gate_sum, up_sum, mid_low, middle_grad, partial, branch_low, conv_low = back[:8]
    conv_weight_grad, sums, recur_weight_grad, inject_weight_grad = back[8:]
    gate_grad, up_grad, mlp_gain_grad = finish_pair(mlp_gain, gate_sum, up_sum, gate_weight, up_weight)
    output_partial = mm_tn(product, mid_low).astype(bf16)[None]
    mix_low = jnp.concatenate([branch_low, conv_low], 1)
    mix_low = jnp.pad(mix_low, ((0, 0), (0, -2 * width % 128)))
    mix_partial = mm_tn(unit_all, mix_low).astype(bf16).reshape(members, -1, mix_low.shape[1])
    size = recur_gate_weight.shape[1]
    gates = jnp.concatenate([recur_weight_grad, inject_weight_grad], 2).reshape(width, 2 * size)
    lanes = -(-max(width, 2 * size) // 128) * 128
    lines = jnp.concatenate([conv_weight_grad, sums], 0)
    packed = jnp.concatenate(
        [
            jnp.pad(gates, ((0, 0), (0, lanes - 2 * size))),
            jnp.pad(lines, ((0, 16 - lines.shape[0]), (0, lanes - width))),
        ],
        0,
    ).astype(bf16)[None]
    again = plane_scratch(rows, depth, 1, 1)
    output_sum, mix_sum, packed, tokens_grad, block_out = replica_sum(
        [output_partial, mix_partial, packed], ["row", "side", "row"], 4, end_steps, (1, 2, 3, 4, 6, 7, 14),
        [(partial, ANY), (middle_grad, VM), (x, VM), (middle, VM), (hidden, ANY), (down_w, ANY)],
        [((rows, depth), bf16, VM), ((rows, depth), bf16, VM)],
        again + again[:2] + [vm(*whole), vm(*whole), vm(hidden.shape, bf16), vm(down_w.shape, bf16), dma((3,))],
    )
    packed = packed.astype(f32)
    branch_grad, input_grad, gain_grad, output_grad, down_grad = finish_rest(
        gain, mix_sum, branch_weight, input_weight, output_sum, down_sum
    )
    recur_weight_grad = packed[:width, :size].reshape(-1, size, size)
    inject_weight_grad = packed[:width, size : 2 * size].reshape(-1, size, size)
    conv_weight_grad = packed[width : width + conv_weight.shape[0], :width]
    conv_bias_grad, recur_bias_grad, inject_bias_grad, rate_grad = [packed[width + conv_weight.shape[0] + i, :width] for i in range(4)]
    decay_param_grad = rate_grad * decay_scale * jax.nn.sigmoid(-decay_f)
    return (
        block_out[None],
        tokens_grad[None],
        gain_grad[:, 0],
        branch_grad,
        input_grad,
        conv_weight_grad,
        conv_bias_grad,
        recur_weight_grad,
        recur_bias_grad,
        inject_weight_grad,
        inject_bias_grad,
        decay_param_grad,
        output_grad,
        mlp_gain_grad[:, 0],
        gate_grad,
        up_grad,
        down_grad,
    )


def solution(mesh):
    row3 = P(("shard", "replica"), "seq", None)
    vec = P(("seq", "shard"))
    mat = P(("seq", "shard"), None)
    cube = P(("seq", "shard"), None, None)
    taps = P(None, ("seq", "shard"))
    params = (vec, mat, mat, taps, vec, cube, vec, cube, vec, vec, mat, vec, mat, mat, mat)
    in_specs = (row3, P(("shard", "replica"), "seq"), row3) + params
    out_specs = (row3, row3) + params
    return jax.shard_map(body, mesh=mesh, in_specs=in_specs, out_specs=out_specs, check_vma=False)
```

```python
import functools

import jax
import jax.numpy as jnp
from jax import lax
from jax.experimental import pallas as pl
from jax.experimental.pallas import tpu as pltpu
from jax.sharding import PartitionSpec as P

epsilon = 1e-06
decay_scale = 8.0
GROUP = ("seq", "shard")
ROWS = ("shard", "seq")
f32 = jnp.float32
bf16 = jnp.bfloat16
VM = pl.BlockSpec(memory_space=pltpu.VMEM)
ANY = pl.BlockSpec(memory_space=pl.ANY)
MESH = pl.DeviceIdType.MESH


def mm(left, right):
    return jnp.dot(left, right, preferred_element_type=f32)


def mm_nt(left, right):
    return lax.dot_general(left, right, (((1,), (1,)), ((), ())), preferred_element_type=f32)


def mm_tn(left, right):
    return lax.dot_general(left, right, (((0,), (0,)), ((), ())), preferred_element_type=f32)


def low(item):
    return item.astype(bf16).astype(f32)


def by_owner(weight, gain):
    owners = lax.axis_size(GROUP)
    scaled = (low(weight) * gain).astype(bf16)
    return jnp.swapaxes(scaled.reshape(weight.shape[0], owners, -1), 0, 1)


def swap(cut):
    return lax.all_to_all(cut, GROUP, split_axis=0, concat_axis=0, tiled=True)


def gelu_parts(x):
    inner = 0.7978845608028654 * (x + 0.044715 * x * x * x)
    t = jnp.tanh(inner)
    value = 0.5 * x * (1.0 + t)
    slope = 0.5 * (1.0 + t) + 0.5 * x * (1.0 - t * t) * 0.7978845608028654 * (
        1.0 + 3.0 * 0.044715 * x * x
    )
    return value, slope


def minus_expm1(y):
    poly = 1.0 + y * (1.0 / 8.0)
    for order in (7.0, 6.0, 5.0, 4.0, 3.0, 2.0):
        poly = 1.0 + y * (1.0 / order) * poly
    return jnp.where(y > -0.5, -y * poly, 1.0 - jnp.exp(y))


def dot_nn(a, b):
    return lax.dot_general(a, b, (((1,), (0,)), ((), ())), preferred_element_type=f32)


def dot_nt(a, b):
    return lax.dot_general(a, b, (((1,), (1,)), ((), ())), preferred_element_type=f32)


def dot_tn(a, b):
    return lax.dot_general(a, b, (((0,), (0,)), ((), ())), preferred_element_type=f32)


def whole_weight(ref, part):
    owners, _, rows, width = ref.shape
    return ref[:, part].reshape(owners * rows, width)


def fill_blocks(target, source):
    target[...] = jnp.zeros_like(target)
    count, size = source.shape[0], source.shape[1]
    for h in range(count):
        target[h * size : (h + 1) * size, h * size : (h + 1) * size] = source[h].astype(bf16).astype(f32)


def put_tiles(ref, here, value):
    width = value.shape[1]
    for tile in range(ref.shape[0]):
        lanes = min(128, width - 128 * tile)
        ref[tile, here, 0:lanes] = value[:, 128 * tile : 128 * tile + lanes]


def get_tiles(ref, here, width):
    parts = [ref[tile, here, 0 : min(128, width - 128 * tile)] for tile in range(ref.shape[0])]
    return jnp.concatenate(parts, axis=1)


def clear_tail(ref, width):
    tail = ref.shape[0] * 128 - width
    if tail:
        ref[ref.shape[0] - 1, :, 128 - tail :] = jnp.zeros((ref.shape[1], tail), f32)


def label_masks(label_ref, here, length, width, taps, lines):
    own = label_ref[here, :].astype(f32)
    lines[0:8, :] = jnp.full((8, 128), -1.0, f32)
    lines[8 : 8 + length, :] = own
    masks = []
    for k in range(1, taps):
        same = jnp.where(lines[8 - k : 8 - k + length, :] == own, 1.0, 0.0)
        masks.append(jnp.concatenate([same] * -(-width // 128), axis=1)[:, :width])
    return masks


def seq_scan(decay_ref, value_ref, sequences, length, reverse):
    tiles = decay_ref.shape[0]
    unroll = 8

    def step(i, states):
        states = list(states)
        for j in range(unroll):
            at = i * unroll + j
            if reverse:
                at = length - 1 - at
            here = pl.ds(at, sequences, stride=length)
            for tile in range(tiles):
                value = value_ref[tile, here, :]
                decay = decay_ref[tile, here, :]
                if reverse:
                    new = value + states[tile]
                    value_ref[tile, here, :] = new
                    states[tile] = decay * new
                else:
                    states[tile] = value + decay * states[tile]
                    value_ref[tile, here, :] = states[tile]
        return tuple(states)

    lax.fori_loop(0, length // unroll, step, (jnp.zeros((sequences, 128), f32),) * tiles)


def plane():
    halves, shards = lax.axis_size("seq"), lax.axis_size("shard")
    y, s = lax.axis_index("seq"), lax.axis_index("shard")
    offsets = [(dy, ds) for ds in range(0, shards, 2) for dy in range(halves)]

    def at(dy, ds):
        return {"seq": jnp.bitwise_xor(y, dy), "shard": jnp.bitwise_xor(s, ds)}

    def block(dy, ds):
        return jnp.bitwise_xor(s, ds) * halves + jnp.bitwise_xor(y, dy)

    return offsets, at, block


def remote(src, dst, sent, got, device):
    return pltpu.make_async_remote_copy(
        src_ref=src, dst_ref=dst, send_sem=sent, recv_sem=got, device_id=device, device_id_type=MESH
    )


def row_block(ref, index, rows):
    return ref.at[pl.ds(pl.multiple_of(index * rows, rows), rows), :]


def scatter_steps(rows, partial, near, far, acc, sems):
    offsets, at, block = plane()
    near_sent, near_got, far_sent, far_got = sems
    count = len(offsets)
    order = list(range(count - 1, -1, -1))
    firsts = {}
    for q in order:
        dy, ds = offsets[q]
        firsts[q] = remote(
            row_block(partial, block(dy, ds ^ 1), rows), near.at[q], near_sent.at[q], near_got.at[q], at(0, 1)
        )
        firsts[q].start()
    seconds = {}
    for q in order:
        dy, ds = offsets[q]
        firsts[q].wait_recv()
        base = block(dy, ds) * rows

        def tile(i, _):
            step = pl.multiple_of(i * 16, 16)
            here = pl.ds(step, 16)
            total = partial[pl.ds(pl.multiple_of(base + step, 16), 16), :].astype(f32) + near[q, here, :].astype(f32)
            if q:
                near[q, here, :] = total.astype(bf16)
            else:
                acc[here, :] = total
            return 0

        lax.fori_loop(0, rows // 16, tile, 0)
        if q:
            seconds[q] = remote(near.at[q], far.at[q - 1], far_sent.at[q - 1], far_got.at[q - 1], at(dy, ds))
            seconds[q].start()
    yield None
    for q in order[:-1]:
        seconds[q].wait_recv()

        def more(i, _):
            here = pl.ds(pl.multiple_of(i * 16, 16), 16)
            acc[here, :] += far[q - 1, here, :].astype(f32)
            return 0

        lax.fori_loop(0, rows // 16, more, 0)
    yield [firsts[q].wait_send for q in order] + [seconds[q].wait_send for q in order[:-1]]


def gather_steps(rows, whole, sems):
    offsets, at, block = plane()
    near_sent, near_got, far_sent, far_got = sems
    count = len(offsets)
    half = rows // 2

    def piece(q, part):
        start = pl.multiple_of(block(*offsets[q]) * rows + part * half, 16)
        return whole.at[pl.ds(start, half), :]

    own = row_block(whole, block(0, 0), rows)
    straight = [q for q in range(1, count) if offsets[q][0] == 0 or offsets[q][1] == 0]
    across = [q for q in range(1, count) if q not in straight]
    upright = [q for q in straight if offsets[q][0]]
    sends, arrivals = [], []
    outs = {}
    for q in straight:
        outs[q] = remote(own, own, far_sent.at[q], far_got.at[q], at(*offsets[q]))
        outs[q].start()
        sends.append(outs[q].wait_send)

    def hand(q, part=None):
        source = row_block(whole, block(*offsets[q]), rows) if part is None else piece(q, part)
        place = q if part is None or part == 0 else count + q
        copy = remote(source, source, near_sent.at[place], near_got.at[place], at(0, 1))
        copy.start()
        sends.append(copy.wait_send)
        arrivals.append(copy.wait_recv)

    hand(0)
    yield None
    onward = {}
    for q in straight:
        outs[q].wait_recv()
        if q in upright:
            targets = [(1, t) for t in straight if t not in upright]
        else:
            targets = [(0, t) for t in upright]
        for part, t in targets:
            dy, ds = offsets[q][0] | offsets[t][0], offsets[q][1] | offsets[t][1]
            a = offsets.index((dy, ds))
            source = piece(q, part)
            onward[a, part] = remote(source, source, far_sent.at[part * count + a], far_got.at[part * count + a], at(*offsets[t]))
            onward[a, part].start()
            sends.append(onward[a, part].wait_send)
        hand(q)
    yield None
    for a in across:
        for part in range(2):
            onward[a, part].wait_recv()
            hand(a, part)
    yield arrivals + sends


def root_mean(rows):
    return lax.rsqrt(jnp.mean(rows * rows, axis=-1, keepdims=True) + epsilon)


def norm_backward(grad_unit, unit, inverse):
    return inverse * (grad_unit - unit * jnp.mean(grad_unit * unit, axis=-1, keepdims=True))


def by_tiles(rows, work):
    def tile(i, _):
        work(pl.ds(pl.multiple_of(i * 16, 16), 16), i)
        return 0

    lax.fori_loop(0, rows // 16, tile, 0)


def plane_scratch(rows, depth, gathers, scatters):
    count = lax.axis_size("seq") * lax.axis_size("shard") // 2
    block = (rows, depth)
    scratch = []
    if scatters:
        scratch = [
            pltpu.VMEM((count,) + block, bf16),
            pltpu.VMEM((count - 1,) + block, bf16),
            pltpu.VMEM(block, f32),
        ]
    dma = pltpu.SemaphoreType.DMA
    for _ in range(scatters):
        scratch += [dma((count,))] * 2 + [dma((count - 1,))] * 2
    for _ in range(gathers):
        scratch += [dma((2 * count,))] * 4
    return scratch


def cut_columns(weight_ref, gain, target, start, lanes):
    owners = weight_ref.shape[1] // lanes

    def tile(i, _):
        step = pl.multiple_of(i * 16, 16)
        here = pl.ds(step, 16)
        scaled = low(weight_ref[here, :]) * gain(step)
        for j in range(owners):
            target(j)[here, start : start + lanes] = scaled[:, j * lanes : (j + 1) * lanes].astype(bf16)
        return 0

    lax.fori_loop(0, weight_ref.shape[0] // 16, tile, 0)


def quarter_steps(n, part, whole, sems):
    me = lax.axis_index("replica")
    right_sent, right_got, left_sent, left_got = sems

    def rows(q):
        return whole.at[:, pl.ds(pl.multiple_of(q * part, 16), part), :]

    def to_right(hop):
        block = rows(me - hop)
        return remote(block, block, right_sent.at[hop], right_got.at[hop], {"replica": me + 1})

    def to_left(hop):
        block = rows(me + hop)
        return remote(block, block, left_sent.at[hop], left_got.at[hop], {"replica": me - 1})

    def from_left(hop):
        block = rows(me - hop - 1)
        return remote(block, block, right_sent.at[hop], right_got.at[hop], {"replica": me + 1})

    def from_right(hop):
        block = rows(me + hop + 1)
        return remote(block, block, left_sent.at[hop], left_got.at[hop], {"replica": me - 1})

    for hop in range(n - 1):
        if hop:

            @pl.when(me >= hop)
            def _():
                from_left(hop - 1).wait_recv()

            @pl.when(me + hop < n)
            def _():
                from_right(hop - 1).wait_recv()

        @pl.when(jnp.logical_and(me >= hop, me < n - 1))
        def _():
            to_right(hop).start()

        @pl.when(jnp.logical_and(me + hop < n, me > 0))
        def _():
            to_left(hop).start()

        yield

    @pl.when(me >= n - 1)
    def _():
        from_left(n - 2).wait_recv()

    @pl.when(me + n - 1 < n)
    def _():
        from_right(n - 2).wait_recv()

    for hop in range(n - 1):

        @pl.when(jnp.logical_and(me >= hop, me < n - 1))
        def _():
            to_right(hop).wait_send()

        @pl.when(jnp.logical_and(me + hop < n, me > 0))
        def _():
            to_left(hop).wait_send()

    yield


def front_kernel(
    n, sequences, length,
    x_ref, label_ref, cot_ref, gains_ref, conv_ref, bias_ref, rw_ref, iw_ref,
    branch_hbm, input_hbm, gate_hbm, up_hbm, ow_hbm,
    unit_out, labels_out, low_out, product_out, pre_out, conv_in_out, values_out, recur_out, inject_out, decay_out,
    states_out, mix_out, ow_out, two_out, middle_out, pair_out,
    unit_ref, labels_ref, product_ref, pre_ref, conv_in_ref, values_ref, recur_ref, inject_ref, decay_ref,
    states_ref, mix_ref, ow_ref, two_ref, middle_ref,
    wide, tall, ow_f, mix_cut, pair_cut, pad, lines, rbig, ibig, partial,
    near, far, acc, *sems,
):
    rows = x_ref.shape[0]
    scatter_sems, sems = sems[:4], sems[4:]
    unit_sems, label_sems, low_sems, two_sems, sems = sems[:4], sems[4:8], sems[8:12], sems[12:16], sems[16:]
    load_sem, save_sem, mix_sent, mix_got, pair_sent, pair_got = sems[:6]
    line_sems = sems[6:]
    offsets, at, block = plane()
    z = lax.axis_index("replica")
    y, s = lax.axis_index("seq"), lax.axis_index("shard")
    shards = lax.axis_size("shard")
    owners = shards * lax.axis_size("seq")
    part = gate_hbm.shape[0] // n
    width = pad.shape[1]
    ff = gate_hbm.shape[1] // owners

    def peer(i):
        return {"seq": jnp.bitwise_xor(y, i // shards), "shard": jnp.bitwise_xor(s, i % shards)}

    def place(i):
        return jnp.bitwise_xor(y, i // shards) * shards + jnp.bitwise_xor(s, i % shards)

    own_rows = pl.ds(pl.multiple_of(z * part, 16), part)
    loads = [
        pltpu.make_async_copy(gate_hbm.at[own_rows, :], tall.at[0], load_sem.at[0]),
        pltpu.make_async_copy(up_hbm.at[own_rows, :], tall.at[1], load_sem.at[1]),
        pltpu.make_async_copy(branch_hbm, wide.at[0], load_sem.at[2]),
        pltpu.make_async_copy(input_hbm, wide.at[1], load_sem.at[3]),
        pltpu.make_async_copy(ow_hbm, ow_f, load_sem.at[4]),
    ]
    for load in loads:
        load.start()
    saves = []

    def save(source, target):
        copy = pltpu.make_async_copy(source, target, save_sem.at[len(saves)])
        copy.start()
        saves.append(copy)

    low_own = pltpu.make_async_copy(cot_ref, row_block(low_out, block(0, 0), rows), load_sem.at[5])
    low_own.start()
    barrier = pltpu.get_barrier_semaphore()
    for i in range(1, owners):
        pl.semaphore_signal(barrier, inc=1, device_id=peer(i), device_id_type=MESH)

    @pl.when(z > 0)
    def _():
        pl.semaphore_signal(barrier, inc=1, device_id={"replica": z - 1}, device_id_type=MESH)

    @pl.when(z < n - 1)
    def _():
        pl.semaphore_signal(barrier, inc=1, device_id={"replica": z + 1}, device_id_type=MESH)

    for side in range(2):
        loads[side].wait()

        cut_columns(
            tall.at[side],
            lambda step: gains_ref[pl.ds(pl.multiple_of(z * part + step, 16), 16), 1:2],
            lambda j: pair_cut.at[j],
            side * ff,
            ff,
        )

    inside_line = jnp.logical_and(z > 0, z < n - 1)

    @pl.when(inside_line)
    def _():
        pl.semaphore_wait(barrier, owners + 1)

    @pl.when(jnp.logical_not(inside_line))
    def _():
        pl.semaphore_wait(barrier, owners)

    me = place(0)
    pair_there = pair_out.at[me, own_rows, :]
    pair_moves = [
        remote(pair_cut.at[place(i)], pair_there, pair_sent.at[i], pair_got.at[i], peer(i)) for i in range(1, owners)
    ]
    for move in pair_moves:
        move.start()
    pair_own = pltpu.make_async_copy(pair_cut.at[me], pair_there, pair_sent.at[0])
    pair_own.start()

    base = block(0, 0) * rows

    def unit(here, i):
        value = x_ref[here, :].astype(f32)
        there = pl.ds(pl.multiple_of(base + i * 16, 16), 16)
        unit_ref[there, :] = (value * root_mean(value)).astype(bf16)
        labels_ref[there, :] = label_ref[here, :]

    by_tiles(rows, unit)
    label_gather = gather_steps(rows, labels_ref, label_sems)
    unit_gather = gather_steps(rows, unit_ref, unit_sems)
    next(label_gather)
    next(unit_gather)

    for side in range(2):
        loads[2 + side].wait()
        cut_columns(
            wide.at[side], lambda step: gains_ref[pl.ds(step, 16), 0:1], lambda j: mix_cut.at[j, side], 0, width
        )
    mix_moves = [
        remote(mix_cut.at[place(i)], mix_ref.at[me], mix_sent.at[i], mix_got.at[i], peer(i)) for i in range(1, owners)
    ]
    for move in mix_moves:
        move.start()
    mix_own = pltpu.make_async_copy(mix_cut.at[me], mix_ref.at[me], mix_sent.at[0])
    mix_own.start()
    loads[4].wait()
    ow_ref[...] = ow_f[...].astype(bf16)
    save(ow_ref, ow_out)
    fill_blocks(rbig, rw_ref)
    fill_blocks(ibig, iw_ref)
    pad[0:8, :] = jnp.zeros((8, width), f32)
    taps = conv_ref.shape[0]
    clear_tail(decay_ref, width)
    clear_tail(states_ref, width)

    pair_own.wait()
    for move in pair_moves:
        move.wait_recv()
    line = quarter_steps(n, part, pair_out, line_sems)
    next(line)
    next(label_gather)
    next(unit_gather)
    waits = next(label_gather) + next(unit_gather)
    for wait in waits:
        wait()
    mix_own.wait()
    for move in mix_moves:
        move.wait_recv()
    save(unit_ref, unit_out)
    save(labels_ref, labels_out)
    save(mix_ref, mix_out)

    low_own.wait()
    low_gather = gather_steps(rows, low_out, low_sems)
    next(low_gather)
    next(line)

    def one(q, _):
        here = pl.ds(pl.multiple_of(q * length, length), length)
        sequence = unit_ref[here, :]
        masks = label_masks(labels_ref, here, length, width, taps, lines)
        pre_ref[here, :] = dot_nn(sequence, whole_weight(mix_ref, 0))
        conv_in = dot_nn(sequence, whole_weight(mix_ref, 1)).astype(bf16)
        conv_in_ref[here, :] = conv_in
        pad[8 : 8 + length, :] = conv_in.astype(f32)
        total = bias_ref[0:1, :] + conv_ref[0:1, :] * pad[8 : 8 + length, :]
        for k in range(1, taps):
            total = total + conv_ref[k : k + 1, :] * pad[8 - k : 8 - k + length, :] * masks[k - 1]
        values = total.astype(bf16)
        values_ref[here, :] = values
        recur = jax.nn.sigmoid(dot_nn(values, rbig[...].astype(bf16)) + bias_ref[1:2, :])
        inject = jax.nn.sigmoid(dot_nn(values, ibig[...].astype(bf16)) + bias_ref[2:3, :])
        recur_ref[here, :] = recur
        inject_ref[here, :] = inject
        log_decay = -decay_scale * bias_ref[3:4, :] * recur
        inside = masks[0] > 0.5
        put_tiles(decay_ref, here, jnp.where(inside, jnp.exp(log_decay), 0.0))
        scale = jnp.where(inside, jnp.sqrt(minus_expm1(2.0 * log_decay)), 1.0)
        put_tiles(states_ref, here, scale * inject * values.astype(f32))
        return 0

    lax.fori_loop(0, sequences, one, 0)
    seq_scan(decay_ref, states_ref, sequences, length, False)

    def two(q, _):
        here = pl.ds(pl.multiple_of(q * length, length), length)
        act, _unused = gelu_parts(pre_ref[here, :])
        product = (act * get_tiles(states_ref, here, width)).astype(bf16)
        product_ref[here, :] = product
        partial[here, :] = dot_nn(product, ow_ref[...]).astype(bf16)
        return 0

    lax.fori_loop(0, sequences, two, 0)
    scatter = scatter_steps(rows, partial, near, far, acc, scatter_sems)
    next(scatter)
    for source, target in (
        (product_ref, product_out), (pre_ref, pre_out), (conv_in_ref, conv_in_out), (values_ref, values_out),
        (recur_ref, recur_out), (inject_ref, inject_out), (decay_ref, decay_out), (states_ref, states_out),
    ):
        save(source, target)
    next(line)
    next(low_gather)
    waits = next(low_gather) + next(scatter)

    def norm(here, i):
        middle = x_ref[here, :].astype(f32) + acc[here, :]
        middle_ref[here, :] = middle
        there = pl.ds(pl.multiple_of(base + i * 16, 16), 16)
        two_ref[there, :] = (middle * root_mean(middle)).astype(bf16)

    by_tiles(rows, norm)
    two_gather = gather_steps(rows, two_ref, two_sems)
    next(two_gather)
    save(middle_ref, middle_out)
    for _ in range(n - 4):
        next(line)
    for wait in waits:
        wait()
    next(two_gather)
    for wait in next(two_gather):
        wait()
    save(two_ref, two_out)
    for _ in line:
        pass
    for move in pair_moves + mix_moves:
        move.wait_send()
    for copy in saves:
        copy.wait()


def front(sequences, x, label, cot, gains, conv, bias, rw, iw, branch_w, input_w, gate_w, up_w, output_w):
    rows, depth = x.shape
    own, n = branch_w.shape[0], lax.axis_size("replica")
    owners = lax.axis_size(GROUP)
    total, width, ff = owners * rows, branch_w.shape[1] // owners, gate_w.shape[1] // owners
    part = own // n
    length = total // sequences
    tiles = -(-width // 128)
    kept = [
        ((total, depth), bf16), ((total, 128), bf16), ((total, depth), bf16), ((total, width), bf16),
        ((total, width), f32), ((total, width), bf16), ((total, width), bf16), ((total, width), f32),
        ((total, width), f32), ((tiles, total, 128), f32), ((tiles, total, 128), f32), ((owners, 2, own, width), bf16),
        ((width, depth), bf16), ((total, depth), bf16), ((rows, depth), f32),
    ]
    vm = pltpu.VMEM
    dma = pltpu.SemaphoreType.DMA
    scratch = [vm(*item) for k, item in enumerate(kept) if k != 2] + [
        vm((2,) + branch_w.shape, f32),
        vm((2, part, gate_w.shape[1]), f32),
        vm(output_w.shape, f32),
        vm((owners, 2, own, width), bf16),
        vm((owners, part, 2 * ff), bf16),
        vm((8 + length, width), f32),
        vm((8 + length, 128), f32),
        vm((width, width), f32),
        vm((width, width), f32),
        vm((total, depth), bf16),
    ]
    scratch += plane_scratch(rows, depth, 4, 1)
    scratch += [dma((6,)), dma((len(kept),))] + [dma((owners,))] * 4 + [dma((n - 1,))] * 4
    outs = kept + [((owners, own, 2 * ff), bf16)]
    return pl.pallas_call(
        functools.partial(front_kernel, n, sequences, length),
        out_shape=tuple(jax.ShapeDtypeStruct(*item) for item in outs),
        in_specs=[VM] * 8 + [ANY] * 5,
        out_specs=[ANY] * len(outs),
        scratch_shapes=scratch,
        compiler_params=pltpu.CompilerParams(
            collective_id=1, has_side_effects=True, vmem_limit_bytes=60 * 2**20
        ),
        cost_estimate=pl.CostEstimate(flops=10**6, bytes_accessed=200 * 2**20, transcendentals=0),
    )(x, label, cot, gains, conv, bias, rw, iw, branch_w, input_w, gate_w, up_w, output_w)


def turn_steps(
    sequences, length,
    partial_hbm, middle_ref, cot_ref, label_ref, conv_ref, bias_ref, rw_ref, iw_ref, *rest,
):
    kept_hbm, rest = rest[:9], rest[9:]
    low_out, grad_out, partial_out, branch_low_out, conv_low_out, dconv_ref, sums_ref, drw_ref, diw_ref = rest[:9]
    scatter_sems, gather_sems = rest[9 + 3 : 9 + 7], rest[9 + 7 : 9 + 11]
    near, far, acc = rest[9:12]
    rest = rest[20:]
    kept, rest = rest[:9], rest[9:]
    ow_ref, w_ref, pre_ref, conv_in_ref, values_ref, recur_ref, inject_ref, decay_ref, states_ref = kept
    partial, low_ref, grad_ref, branch_low_ref, conv_low_ref, adj, pad, lines, rbig, ibig, dr, di, load_sem, save_sem = rest
    rows = middle_ref.shape[0]
    offsets, at, block = plane()
    first = pltpu.make_async_copy(partial_hbm, partial, load_sem.at[9])
    first.start()
    loads = [pltpu.make_async_copy(kept_hbm[k], kept[k], load_sem.at[k]) for k in range(9)]
    for load in loads:
        load.start()
    first.wait()
    scatter = scatter_steps(rows, partial, near, far, acc, scatter_sems)
    next(scatter)
    yield
    waits = next(scatter)
    base = block(0, 0) * rows

    def norm(here, i):
        middle = middle_ref[here, :]
        inverse = root_mean(middle)
        grad = cot_ref[here, :].astype(f32) + norm_backward(acc[here, :], middle * inverse, inverse)
        grad_ref[here, :] = grad
        there = pl.ds(pl.multiple_of(base + i * 16, 16), 16)
        low_ref[there, :] = grad.astype(bf16)

    by_tiles(rows, norm)
    gather = gather_steps(rows, low_ref, gather_sems)
    next(gather)
    yield
    next(gather)
    yield
    waits = waits + next(gather)
    yield
    for wait in waits:
        wait()
    for load in loads:
        load.wait()
    saves = [pltpu.make_async_copy(low_ref, low_out, save_sem.at[0]), pltpu.make_async_copy(grad_ref, grad_out, save_sem.at[1])]
    for save in saves:
        save.start()
    fill_blocks(rbig, rw_ref)
    fill_blocks(ibig, iw_ref)
    dr[...] = jnp.zeros_like(dr)
    di[...] = jnp.zeros_like(di)
    sums_ref[...] = jnp.zeros_like(sums_ref)
    dconv_ref[...] = jnp.zeros_like(dconv_ref)
    taps = conv_ref.shape[0]
    width = pad.shape[1]
    clear_tail(adj, width)

    def one(s):
        here = pl.ds(s * length, length)
        product_grad = dot_nt(low_ref[here, :], ow_ref[...])
        act, slope = gelu_parts(pre_ref[here, :])
        branch_low_ref[here, :] = (product_grad * get_tiles(states_ref, here, width) * slope).astype(bf16)
        put_tiles(adj, here, product_grad * act)

    for s in range(sequences):
        one(s)
        yield
    seq_scan(decay_ref, adj, sequences, length, True)
    yield

    def two(s):
        here = pl.ds(s * length, length)
        adjoint = get_tiles(adj, here, width)
        recur = recur_ref[here, :]
        inject = inject_ref[here, :]
        decay = get_tiles(decay_ref, here, width)
        values = values_ref[here, :]
        values_f = values.astype(f32)
        masks = label_masks(label_ref, here, length, width, taps, lines)
        inside = masks[0] > 0.5
        rate = bias_ref[3:4, :]
        log_decay = -decay_scale * rate * recur
        scale = jnp.where(inside, jnp.sqrt(minus_expm1(2.0 * log_decay)), 1.0)
        pad[0:8, :] = jnp.zeros((8, width), f32)
        pad[8 : 8 + length, :] = get_tiles(states_ref, here, width)
        previous = pad[7 : 7 + length, :]
        driven = adjoint * inject * values_f
        log_grad = jnp.where(inside, adjoint * previous * decay - driven * decay * decay / scale, 0.0)
        recur_low = (log_grad * (-decay_scale * rate) * recur * (1.0 - recur)).astype(bf16)
        inject_low = (driven * scale * (1.0 - inject)).astype(bf16)
        sums_ref[1:2, :] += jnp.sum(recur_low.astype(f32), axis=0, keepdims=True)
        sums_ref[2:3, :] += jnp.sum(inject_low.astype(f32), axis=0, keepdims=True)
        sums_ref[3:4, :] += jnp.sum(log_grad * recur, axis=0, keepdims=True)
        dr[...] += dot_tn(values, recur_low)
        di[...] += dot_tn(values, inject_low)
        grad = adjoint * scale * inject
        grad = grad + dot_nt(recur_low, rbig[...].astype(bf16)) + dot_nt(inject_low, ibig[...].astype(bf16))
        sums_ref[0:1, :] += jnp.sum(grad, axis=0, keepdims=True)
        pad[8 : 8 + length, :] = conv_in_ref[here, :].astype(f32)
        dconv_ref[0:1, :] += jnp.sum(grad * pad[8 : 8 + length, :], axis=0, keepdims=True)
        masked = []
        for k in range(1, taps):
            part = grad * masks[k - 1]
            masked.append(part)
            dconv_ref[k : k + 1, :] += jnp.sum(part * pad[8 - k : 8 - k + length, :], axis=0, keepdims=True)
        total = grad * conv_ref[0:1, :]
        pad[length : length + 8, :] = jnp.zeros((8, width), f32)
        for k in range(1, taps):
            pad[0:length, :] = masked[k - 1] * conv_ref[k : k + 1, :]
            total = total + pad[k : k + length, :]
        conv_low = total.astype(bf16)
        conv_low_ref[here, :] = conv_low
        partial[here, :] = (dot_nt(branch_low_ref[here, :], whole_weight(w_ref, 0)) + dot_nt(conv_low, whole_weight(w_ref, 1))).astype(bf16)

    for s in range(sequences):
        two(s)
        yield
    size = drw_ref.shape[1]
    for h in range(drw_ref.shape[0]):
        cut = slice(h * size, (h + 1) * size)
        drw_ref[h] = dr[cut, cut]
        diw_ref[h] = di[cut, cut]
    ends = [(partial, partial_out), (branch_low_ref, branch_low_out), (conv_low_ref, conv_low_out)]
    for k, pair in enumerate(ends):
        saves.append(pltpu.make_async_copy(*pair, save_sem.at[2 + k]))
        saves[-1].start()
    yield
    for save in saves:
        save.wait()


def end_steps(
    partial_hbm, grad_ref, x_ref, middle_ref, hidden_hbm, down_hbm, tokens_ref, block_ref, *rest,
):
    near, far, acc = rest[:3]
    scatter_sems = rest[3:7]
    more_sems = rest[7:11]
    near_two, far_two, partial, partial_two, hidden, down, load_sem = rest[11:]
    rows = x_ref.shape[0]
    loads = [
        pltpu.make_async_copy(source, target, load_sem.at[k])
        for k, (source, target) in enumerate(((partial_hbm, partial), (hidden_hbm, hidden), (down_hbm, down)))
    ]
    for load in loads:
        load.start()
    loads[0].wait()
    scatter = scatter_steps(rows, partial, near, far, acc, scatter_sems)
    next(scatter)
    yield
    loads[1].wait()
    loads[2].wait()
    pieces_of = 4
    height = hidden.shape[0] // pieces_of
    for k in range(pieces_of):
        here = pl.ds(k * height, height)
        partial_two[here, :] = dot_nn(hidden[here, :], down[...]).astype(bf16)
        yield
    waits = next(scatter)

    def norm(here, i):
        value = x_ref[here, :].astype(f32)
        inverse = root_mean(value)
        grad = grad_ref[here, :] + norm_backward(acc[here, :], value * inverse, inverse)
        tokens_ref[here, :] = grad.astype(bf16)

    by_tiles(rows, norm)
    yield
    scatter = scatter_steps(rows, partial_two, near_two, far_two, acc, more_sems)
    next(scatter)
    yield
    waits = waits + next(scatter)

    def out(here, i):
        block_ref[here, :] = (middle_ref[here, :] + acc[here, :]).astype(bf16)

    by_tiles(rows, out)
    yield
    for wait in waits:
        wait()


def mlp_kernel(
    two_hbm, low_hbm, pair_hbm, down_hbm, hidden_out, partial_out, down_out, pair_out,
    two, low_rows, pair_w, down_w, hidden, pair_low, partial, down_grad, pair_grad, load_sem, save_sem, pair_sem,
):
    total, depth = two.shape
    ff = down_w.shape[0]
    tile = 256 if ff % 256 == 0 else 128
    height = 256
    steps = total // height

    def rows_of(hbm, ref, r, which):
        here = pl.ds(r * height, height)
        return pltpu.make_async_copy(hbm.at[here, :], ref.at[here, :], load_sem.at[which, r])

    weights = [
        pltpu.make_async_copy(pair_hbm, pair_w, load_sem.at[2, 0]),
        pltpu.make_async_copy(down_hbm, down_w, load_sem.at[2, 1]),
    ]
    rows_of(two_hbm, two, 0, 0).start()
    weights[0].start()
    rows_of(low_hbm, low_rows, 0, 1).start()
    weights[1].start()
    for r in range(1, steps):
        rows_of(two_hbm, two, r, 0).start()
        rows_of(low_hbm, low_rows, r, 1).start()
    weights[0].wait()
    weights[1].wait()

    def row_step(r, _):
        here = pl.ds(pl.multiple_of(r * height, height), height)
        pltpu.make_async_copy(two_hbm.at[here, :], two.at[here, :], load_sem.at[0, r]).wait()
        pltpu.make_async_copy(low_hbm.at[here, :], low_rows.at[here, :], load_sem.at[1, r]).wait()
        for f in range(ff // tile):
            cut = slice(f * tile, (f + 1) * tile)
            more = slice(ff + f * tile, ff + (f + 1) * tile)
            gate = dot_nn(two[here, :], pair_w[:, cut])
            up = dot_nn(two[here, :], pair_w[:, more])
            grad = dot_nt(low_rows[here, :], down_w[cut, :])
            act, slope = gelu_parts(gate)
            hidden[here, cut] = (act * up).astype(bf16)
            pair_low[here, cut] = (grad * up * slope).astype(bf16)
            pair_low[here, more] = (grad * act).astype(bf16)
        for d in range(0, depth, 512):
            partial[here, d : d + 512] = dot_nt(pair_low[here, :], pair_w[d : d + 512, :]).astype(bf16)
        return 0

    lax.fori_loop(0, steps, row_step, 0)
    saves = [
        pltpu.make_async_copy(partial, partial_out, save_sem.at[0]),
        pltpu.make_async_copy(hidden, hidden_out, save_sem.at[1]),
    ]
    for save in saves:
        save.start()
    for f in range(ff // tile):
        cut = slice(f * tile, (f + 1) * tile)
        down_grad[cut, :] = dot_tn(hidden[:, cut], low_rows[...]).astype(bf16)
    saves.append(pltpu.make_async_copy(down_grad, down_out, save_sem.at[2]))
    saves[-1].start()

    def column_step(d, _):
        here = pl.ds(pl.multiple_of(d * height, height), height)
        pair_grad[here, :] = dot_tn(two[:, here], pair_low[...]).astype(bf16)
        pltpu.make_async_copy(pair_grad.at[here, :], pair_out.at[here, :], pair_sem.at[d]).start()
        return 0

    lax.fori_loop(0, depth // height, column_step, 0)
    for d in range(depth // height):
        here = pl.ds(d * height, height)
        pltpu.make_async_copy(pair_grad.at[here, :], pair_out.at[here, :], pair_sem.at[d]).wait()
    for save in saves:
        save.wait()


def mlp(unit_two, out_low, pair_w, down_w):
    total, depth = unit_two.shape
    ff = down_w.shape[0]
    kept = [((total, ff), bf16), ((total, depth), bf16), ((ff, depth), bf16), ((depth, 2 * ff), bf16)]
    vm, dma = pltpu.VMEM, pltpu.SemaphoreType.DMA
    return pl.pallas_call(
        mlp_kernel,
        out_shape=tuple(jax.ShapeDtypeStruct(*item) for item in kept),
        in_specs=[ANY] * 4,
        out_specs=[ANY] * 4,
        scratch_shapes=[vm(item.shape, bf16) for item in (unit_two, out_low, pair_w, down_w)]
        + [vm((total, ff), bf16), vm((total, 2 * ff), bf16)]
        + [vm(*item) for item in kept[1:]]
        + [dma((3, total // 256)), dma((3,)), dma((depth // 256,))],
        compiler_params=pltpu.CompilerParams(vmem_limit_bytes=60 * 2**20),
        cost_estimate=pl.CostEstimate(
            flops=2 * total * depth * ff * 8, bytes_accessed=36 * 2**20, transcendentals=total * ff
        ),
    )(unit_two, out_low, pair_w, down_w)


def pieces(rows, most):
    count = -(-rows // most)
    while rows % count or (rows // count) % 16:
        count += 1
    return count


def line_kernel(n, kinds, cuts, beside, turns, extra, *refs):
    ins = len(cuts)
    made = ins + kinds.count("pair")
    extra_ins, extra_outs, extra_scratch = extra
    refs = list(refs)

    def take(count):
        taken = refs[:count]
        del refs[:count]
        return taken

    own_hbm, side_in = take(ins), take(extra_ins)
    outs, side_out = take(made), take(extra_outs)
    side_scratch = take(extra_scratch)
    from_out, from_in = take(ins), take(ins)
    slots, whole_sem, slot_sem, sent_in, sent_out, got_out, got_in, sent_x, got_x = refs
    depth = slots.shape[0]
    me = lax.axis_index("replica")
    y, s = lax.axis_index("seq"), lax.axis_index("shard")
    shards = lax.axis_size("shard")
    owners = shards * lax.axis_size("seq")
    left = me < n // 2
    inward = jnp.where(left, me + 1, me - 1)
    outward = jnp.where(left, me - 1, me + 1)
    has_out = jnp.logical_and(me > 0, me < n - 1)
    at_end = jnp.logical_not(has_out)
    middle = jnp.logical_or(me == n // 2 - 1, me == n // 2)

    def peer(i):
        return {"seq": jnp.bitwise_xor(y, i // shards), "shard": jnp.bitwise_xor(s, i % shards)}

    def place(i):
        return jnp.bitwise_xor(y, i // shards) * shards + jnp.bitwise_xor(s, i % shards)

    chunks = []
    for k, (lead, count, rows) in enumerate(cuts):
        for step in range(lead):
            for i in range(count):
                chunks.append((k, step if kinds[k] == "row" else (step + 1) % lead, i * rows, rows))
    total = len(chunks)

    def view(group, c):
        k, i, start, rows = chunks[c]
        return group[k].at[0 if kinds[k] == "row" else place(i), pl.ds(start, rows), :]

    def slot(c):
        k, i, start, rows = chunks[c]
        return slots.at[c % depth, pl.ds(0, rows), pl.ds(0, from_in[k].shape[2])]

    def load(c):
        return pltpu.make_async_copy(view(own_hbm, c), slot(c), slot_sem.at[c % depth])

    wholes = [pltpu.make_async_copy(own_hbm[k], from_out[k], whole_sem.at[k]) for k in range(ins)]

    @pl.when(at_end)
    def _():
        for item in wholes:
            item.start()

    @pl.when(has_out)
    def _():
        for c in range(min(depth - 1, total)):
            load(c).start()

    barrier = pltpu.get_barrier_semaphore()
    for i in range(1, owners):
        pl.semaphore_signal(barrier, inc=1, device_id=peer(i), device_id_type=MESH)
    pl.semaphore_signal(barrier, inc=1, device_id={"replica": inward}, device_id_type=MESH)

    @pl.when(has_out)
    def _():
        pl.semaphore_signal(barrier, inc=1, device_id={"replica": outward}, device_id_type=MESH)
        pl.semaphore_wait(barrier, owners + 1)

    @pl.when(at_end)
    def _():
        pl.semaphore_wait(barrier, owners)

    def push(group, target, c, sent, got, device):
        return remote(view(group, c), view(target, c), sent.at[c], got.at[c], {"replica": device})

    def add(target, other, c):
        k, i, start, rows = chunks[c]
        into, more = view(target, c), slot(c) if other is None else view(other, c)

        def tile(t, _):
            here = pl.ds(pl.multiple_of(t * 16, 16), 16)
            into[here, :] = (into[here, :].astype(f32) + more[here, :].astype(f32)).astype(bf16)
            return 0

        lax.fori_loop(0, rows // 16, tile, 0)

    def pass_in(c):
        @pl.when(middle)
        def _():
            push(from_out, from_in, c, sent_in, got_in, inward).start()

        @pl.when(jnp.logical_not(middle))
        def _():
            push(from_out, from_out, c, sent_in, got_out, inward).start()

    def gather_in(c):
        @pl.when(has_out)
        def _():
            load(c).wait()
            push(from_out, from_out, c, sent_in, got_out, inward).wait_recv()
            add(from_out, None, c)
            pass_in(c)
            if c + depth - 1 < total:
                load(c + depth - 1).start()

    @pl.when(at_end)
    def _():
        for c in range(total):
            if c == 0 or chunks[c][0] != chunks[c - 1][0]:
                wholes[chunks[c][0]].wait()
            pass_in(c)

    work = beside(*side_in, *side_out, *side_scratch)
    next(work)

    def deliveries(c):
        k, i, start, rows = chunks[c]
        here = pl.ds(start, rows)
        first = k + kinds[:k].count("pair")
        source = view(from_in, c)
        if kinds[k] == "row":
            ends = [(source, outs[first].at[here, :])]
        elif kinds[k] == "side":
            ends = [(source, outs[first].at[place(0), here, :])]
        else:
            half = source.shape[1] // 2
            there = pl.ds(pl.multiple_of(place(0) * half, half), half)
            ends = [
                (source.at[:, pl.ds(part * half, half)], outs[first + part].at[here, there]) for part in range(2)
            ]
        if kinds[k] == "row" or i == 0:
            return [pltpu.make_async_copy(*pair, sent_x.at[c, p]) for p, pair in enumerate(ends)], False
        return [remote(*pair, sent_x.at[c, p], got_x.at[c, p], peer(i)) for p, pair in enumerate(ends)], True

    def give_back(c):
        push(from_out, from_in, c, sent_out, got_in, inward).wait_recv()

        @pl.when(middle)
        def _():
            add(from_in, from_out, c)

        @pl.when(has_out)
        def _():
            push(from_in, from_in, c, sent_out, got_in, outward).start()

        for copy in deliveries(c)[0]:
            copy.start()

    lag = 1
    for c in range(total + lag):
        for _ in range(turns.count(c)):
            next(work)
        if c < total:
            gather_in(c)
        if c >= lag:
            give_back(c - lag)
    for _ in work:
        pass
    for c in range(total):
        copies, away = deliveries(c)
        for copy in copies:
            if away:
                copy.wait_recv()
                copy.wait_send()
            else:
                copy.wait()
        push(from_out, from_in, c, sent_in, got_in, inward).wait_send()

        @pl.when(has_out)
        def _():
            push(from_in, from_in, c, sent_out, got_in, outward).wait_send()


def replica_sum(arrays, kinds, identity, beside, turns, inputs, results, side_scratch):
    cuts, outs = [], []
    tall = broad = 0
    for item, kind in zip(arrays, kinds):
        lead, height, columns = item.shape
        count = pieces(height, max(16, (105 * 1024) // columns // 16 * 16))
        cuts.append((lead, count, height // count))
        tall, broad = max(tall, height // count), max(broad, columns)
        if kind == "pair":
            outs += [jax.ShapeDtypeStruct((height, lead * columns // 2), bf16)] * 2
        elif kind == "side":
            outs.append(jax.ShapeDtypeStruct(item.shape, bf16))
        else:
            outs.append(jax.ShapeDtypeStruct((height, columns), bf16))
    count = sum(lead * cut for lead, cut, _ in cuts)
    buffers = [pltpu.VMEM(item.shape, bf16) for item in arrays]
    dma = pltpu.SemaphoreType.DMA
    return pl.pallas_call(
        functools.partial(
            line_kernel, lax.axis_size("replica"), tuple(kinds), tuple(cuts), beside, turns,
            (len(inputs), len(results), len(side_scratch)),
        ),
        out_shape=tuple(outs) + tuple(jax.ShapeDtypeStruct(shape, kind) for shape, kind, _ in results),
        in_specs=[ANY] * len(arrays) + [spec for _, spec in inputs],
        out_specs=[ANY] * len(outs) + [spec for _, _, spec in results],
        scratch_shapes=list(side_scratch)
        + buffers * 2
        + [pltpu.VMEM((4, tall, broad), bf16), dma((len(arrays),)), dma((4,))]
        + [dma((count,))] * 4
        + [dma((count, 2))] * 2,
        compiler_params=pltpu.CompilerParams(
            collective_id=identity, has_side_effects=True, vmem_limit_bytes=61 * 2**20
        ),
        cost_estimate=pl.CostEstimate(flops=10**6, bytes_accessed=200 * 2**20, transcendentals=0),
    )(*arrays, *[item for item, _ in inputs])


def finish_pair_kernel(gain_ref, a_ref, b_ref, wa_ref, wb_ref, outa_ref, outb_ref, grad_ref):
    grad = jnp.zeros(gain_ref.shape, f32)
    for sum_ref, weight_ref, out_ref in ((a_ref, wa_ref, outa_ref), (b_ref, wb_ref, outb_ref)):
        total = sum_ref[...].astype(f32)
        out_ref[...] = total * gain_ref[...]
        grad = grad + jnp.sum(total * low(weight_ref[...]), axis=1, keepdims=True)
    grad_ref[...] = grad


def finish_pair(gain, a, b, wa, wb):
    rows, columns = wa.shape
    cut = min(rows, 32)
    wide = pl.BlockSpec((cut, columns), lambda i: (i, 0))
    thin = pl.BlockSpec((cut, 1), lambda i: (i, 0))
    out = jax.ShapeDtypeStruct((rows, columns), f32)
    return pl.pallas_call(
        finish_pair_kernel,
        grid=(rows // cut,),
        out_shape=(out, out, jax.ShapeDtypeStruct((rows, 1), f32)),
        in_specs=[thin, wide, wide, wide, wide],
        out_specs=[wide, wide, thin],
        compiler_params=pltpu.CompilerParams(vmem_limit_bytes=61 * 2**20),
        cost_estimate=pl.CostEstimate(flops=6 * rows * columns, bytes_accessed=20 * rows * columns, transcendentals=0),
    )(gain, a, b, wa, wb)


def finish_rest_kernel(gain_ref, mix_ref, wa_ref, wb_ref, out_sum_ref, down_sum_ref, outa_ref, outb_ref, grad_ref, out_ref, down_ref):
    owners = mix_ref.shape[0]
    width = wa_ref.shape[1] // owners
    grad = jnp.zeros(gain_ref.shape, f32)
    for part, (weight_ref, target_ref) in enumerate(((wa_ref, outa_ref), (wb_ref, outb_ref))):
        total = jnp.concatenate(
            [mix_ref[j, :, part * width : (part + 1) * width].astype(f32) for j in range(owners)], axis=1
        )
        target_ref[...] = total * gain_ref[...]
        grad = grad + jnp.sum(total * low(weight_ref[...]), axis=1, keepdims=True)
    grad_ref[...] = grad
    out_ref[...] = out_sum_ref[...].astype(f32)
    down_ref[...] = down_sum_ref[...].astype(f32)


def finish_rest(gain, mix, wa, wb, out_sum, down_sum):
    rows, columns = wa.shape
    steps = 4
    while out_sum.shape[0] % (16 * steps) or down_sum.shape[0] % (16 * steps) or rows % (16 * steps):
        steps //= 2

    def tall(item):
        return pl.BlockSpec((item.shape[0] // steps, item.shape[1]), lambda i: (i, 0))

    owners, _, both = mix.shape
    wide, thin = tall(wa), tall(gain)
    return pl.pallas_call(
        finish_rest_kernel,
        grid=(steps,),
        out_shape=(
            jax.ShapeDtypeStruct(wa.shape, f32),
            jax.ShapeDtypeStruct(wa.shape, f32),
            jax.ShapeDtypeStruct((rows, 1), f32),
            jax.ShapeDtypeStruct(out_sum.shape, f32),
            jax.ShapeDtypeStruct(down_sum.shape, f32),
        ),
        in_specs=[
            thin,
            pl.BlockSpec((owners, rows // steps, both), lambda i: (0, i, 0)),
            wide,
            wide,
            tall(out_sum),
            tall(down_sum),
        ],
        out_specs=[wide, wide, thin, tall(out_sum), tall(down_sum)],
        compiler_params=pltpu.CompilerParams(vmem_limit_bytes=61 * 2**20),
        cost_estimate=pl.CostEstimate(flops=10**7, bytes_accessed=40 * 2**20, transcendentals=0),
    )(gain, mix, wa, wb, out_sum, down_sum)


def body(
    tokens,
    segments,
    cotangent,
    norm_gain,
    branch_weight,
    input_weight,
    conv_weight,
    conv_bias,
    recur_gate_weight,
    recur_gate_bias,
    input_gate_weight,
    input_gate_bias,
    decay_param,
    output_weight,
    mlp_norm_gain,
    gate_weight,
    up_weight,
    down_weight,
):
    x, cot = tokens[0], cotangent[0]
    rows, depth = x.shape
    members = lax.axis_size(GROUP)
    sequences = lax.axis_size("shard")
    total = members * rows
    gain, mlp_gain = low(norm_gain)[:, None], low(mlp_norm_gain)[:, None]
    own_labels = jnp.broadcast_to(segments[0].astype(bf16)[:, None], (rows, 128))
    width = branch_weight.shape[1] // members
    conv_f = low(conv_weight)
    decay_f = low(decay_param)
    bias = jnp.stack([low(conv_bias), low(recur_gate_bias), low(input_gate_bias), jax.nn.softplus(-decay_f)])
    (
        unit_all, labels, out_low, product, *mixed, mix_w, output_w, unit_two, middle, pair_w,
    ) = front(
        sequences, x, own_labels, cot, low(jnp.stack([norm_gain, mlp_norm_gain], 1)), conv_f, bias,
        recur_gate_weight, input_gate_weight, branch_weight, input_weight, gate_weight, up_weight, output_weight,
    )
    pair_w = pair_w.reshape(depth, -1)
    down_w = down_weight.astype(bf16)
    whole = ((total, depth), bf16)
    hidden, partial, down_partial, pair_partial = mlp(unit_two, out_low, pair_w, down_w)
    down_partial = down_partial[None]
    pair_partial = pair_partial.reshape(members, -1, pair_w.shape[1])
    kept = (output_w, mix_w, *mixed)
    narrow = ((total, width), bf16)
    vm, dma = pltpu.VMEM, pltpu.SemaphoreType.DMA
    length = total // sequences
    back = replica_sum(
        [down_partial, pair_partial], ["row", "pair"], 3,
        functools.partial(turn_steps, sequences, length),
        (6, 9, 12) + tuple(range(14, 14 + 2 * sequences + 2)),
        [(partial, ANY)] + [(item, VM) for item in (middle, cot, labels, conv_f, bias, recur_gate_weight, input_gate_weight)]
        + [(item, ANY) for item in kept],
        [whole + (ANY,), ((rows, depth), f32, ANY), whole + (ANY,), narrow + (ANY,), narrow + (ANY,)]
        + [(conv_f.shape, f32, VM), ((4, width), f32, VM), (recur_gate_weight.shape, f32, VM), (input_gate_weight.shape, f32, VM)],
        plane_scratch(rows, depth, 1, 1)
        + [vm(item.shape, item.dtype) for item in kept]
        + [vm(*whole), vm(*whole), vm((rows, depth), f32), vm(*narrow), vm(*narrow), vm(mixed[-1].shape, f32)]
        + [vm((8 + length, width), f32), vm((8 + length, 128), f32)]
        + [vm((width, width), f32)] * 4
        + [dma((10,)), dma((5,))],
    )
    down_sum, gate_sum, up_sum, mid_low, middle_grad, partial, branch_low, conv_low = back[:8]
    conv_weight_grad, sums, recur_weight_grad, inject_weight_grad = back[8:]
    gate_grad, up_grad, mlp_gain_grad = finish_pair(mlp_gain, gate_sum, up_sum, gate_weight, up_weight)
    output_partial = mm_tn(product, mid_low).astype(bf16)[None]
    mix_low = jnp.concatenate([branch_low, conv_low], 1)
    mix_low = jnp.pad(mix_low, ((0, 0), (0, -2 * width % 128)))
    mix_partial = mm_tn(unit_all, mix_low).astype(bf16).reshape(members, -1, mix_low.shape[1])
    size = recur_gate_weight.shape[1]
    gates = jnp.concatenate([recur_weight_grad, inject_weight_grad], 2).reshape(width, 2 * size)
    lanes = -(-max(width, 2 * size) // 128) * 128
    lines = jnp.concatenate([conv_weight_grad, sums], 0)
    packed = jnp.concatenate(
        [
            jnp.pad(gates, ((0, 0), (0, lanes - 2 * size))),
            jnp.pad(lines, ((0, 16 - lines.shape[0]), (0, lanes - width))),
        ],
        0,
    ).astype(bf16)[None]
    again = plane_scratch(rows, depth, 1, 1)
    output_sum, mix_sum, packed, tokens_grad, block_out = replica_sum(
        [output_partial, mix_partial, packed], ["row", "side", "row"], 4, end_steps, (1, 2, 3, 4, 6, 7, 14),
        [(partial, ANY), (middle_grad, VM), (x, VM), (middle, VM), (hidden, ANY), (down_w, ANY)],
        [((rows, depth), bf16, VM), ((rows, depth), bf16, VM)],
        again + again[:2] + [vm(*whole), vm(*whole), vm(hidden.shape, bf16), vm(down_w.shape, bf16), dma((3,))],
    )
    packed = packed.astype(f32)
    branch_grad, input_grad, gain_grad, output_grad, down_grad = finish_rest(
        gain, mix_sum, branch_weight, input_weight, output_sum, down_sum
    )
    recur_weight_grad = packed[:width, :size].reshape(-1, size, size)
    inject_weight_grad = packed[:width, size : 2 * size].reshape(-1, size, size)
    conv_weight_grad = packed[width : width + conv_weight.shape[0], :width]
    conv_bias_grad, recur_bias_grad, inject_bias_grad, rate_grad = [packed[width + conv_weight.shape[0] + i, :width] for i in range(4)]
    decay_param_grad = rate_grad * decay_scale * jax.nn.sigmoid(-decay_f)
    return (
        block_out[None],
        tokens_grad[None],
        gain_grad[:, 0],
        branch_grad,
        input_grad,
        conv_weight_grad,
        conv_bias_grad,
        recur_weight_grad,
        recur_bias_grad,
        inject_weight_grad,
        inject_bias_grad,
        decay_param_grad,
        output_grad,
        mlp_gain_grad[:, 0],
        gate_grad,
        up_grad,
        down_grad,
    )


def solution(mesh):
    row3 = P(("shard", "replica"), "seq", None)
    vec = P(("seq", "shard"))
    mat = P(("seq", "shard"), None)
    cube = P(("seq", "shard"), None, None)
    taps = P(None, ("seq", "shard"))
    params = (vec, mat, mat, taps, vec, cube, vec, cube, vec, vec, mat, vec, mat, mat, mat)
    in_specs = (row3, P(("shard", "replica"), "seq"), row3) + params
    out_specs = (row3, row3) + params
    return jax.shard_map(body, mesh=mesh, in_specs=in_specs, out_specs=out_specs, check_vma=False)
```

```python
import functools

import jax
import jax.numpy as jnp
from jax import lax
from jax.experimental import pallas as pl
from jax.experimental.pallas import tpu as pltpu
from jax.sharding import PartitionSpec as P

epsilon = 1e-06
decay_scale = 8.0
GROUP = ("seq", "shard")
ROWS = ("shard", "seq")
f32 = jnp.float32
bf16 = jnp.bfloat16
VM = pl.BlockSpec(memory_space=pltpu.VMEM)
ANY = pl.BlockSpec(memory_space=pl.ANY)
MESH = pl.DeviceIdType.MESH


def mm(left, right):
    return jnp.dot(left, right, preferred_element_type=f32)


def mm_nt(left, right):
    return lax.dot_general(left, right, (((1,), (1,)), ((), ())), preferred_element_type=f32)


def mm_tn(left, right):
    return lax.dot_general(left, right, (((0,), (0,)), ((), ())), preferred_element_type=f32)


def low(item):
    return item.astype(bf16).astype(f32)


def by_owner(weight, gain):
    owners = lax.axis_size(GROUP)
    scaled = (low(weight) * gain).astype(bf16)
    return jnp.swapaxes(scaled.reshape(weight.shape[0], owners, -1), 0, 1)


def swap(cut):
    return lax.all_to_all(cut, GROUP, split_axis=0, concat_axis=0, tiled=True)


def gelu_parts(x):
    inner = 0.7978845608028654 * (x + 0.044715 * x * x * x)
    t = jnp.tanh(inner)
    value = 0.5 * x * (1.0 + t)
    slope = 0.5 * (1.0 + t) + 0.5 * x * (1.0 - t * t) * 0.7978845608028654 * (
        1.0 + 3.0 * 0.044715 * x * x
    )
    return value, slope


def minus_expm1(y):
    poly = 1.0 + y * (1.0 / 8.0)
    for order in (7.0, 6.0, 5.0, 4.0, 3.0, 2.0):
        poly = 1.0 + y * (1.0 / order) * poly
    return jnp.where(y > -0.5, -y * poly, 1.0 - jnp.exp(y))


def dot_nn(a, b):
    return lax.dot_general(a, b, (((1,), (0,)), ((), ())), preferred_element_type=f32)


def dot_nt(a, b):
    return lax.dot_general(a, b, (((1,), (1,)), ((), ())), preferred_element_type=f32)


def dot_tn(a, b):
    return lax.dot_general(a, b, (((0,), (0,)), ((), ())), preferred_element_type=f32)


def whole_weight(ref, part):
    owners, _, rows, width = ref.shape
    return ref[:, part].reshape(owners * rows, width)


def fill_blocks(target, source):
    target[...] = jnp.zeros_like(target)
    count, size = source.shape[0], source.shape[1]
    for h in range(count):
        target[h * size : (h + 1) * size, h * size : (h + 1) * size] = source[h].astype(bf16).astype(f32)


def put_tiles(ref, here, value):
    width = value.shape[1]
    for tile in range(ref.shape[0]):
        lanes = min(128, width - 128 * tile)
        ref[tile, here, 0:lanes] = value[:, 128 * tile : 128 * tile + lanes]


def get_tiles(ref, here, width):
    parts = [ref[tile, here, 0 : min(128, width - 128 * tile)] for tile in range(ref.shape[0])]
    return jnp.concatenate(parts, axis=1)


def clear_tail(ref, width):
    tail = ref.shape[0] * 128 - width
    if tail:
        ref[ref.shape[0] - 1, :, 128 - tail :] = jnp.zeros((ref.shape[1], tail), f32)


def fill_small(conv, bias, raw_conv, raw_a, raw_b, raw_c, rate):
    conv[0 : raw_conv.shape[0], :] = low(raw_conv[...])
    for row, ref in enumerate((raw_a, raw_b, raw_c)):
        bias[row : row + 1, :] = low(ref[...])
    bias[3:4, :] = rate[...]


def label_masks(label_ref, here, length, width, taps, lines):
    own = label_ref[here, :].astype(f32)
    lines[0:8, :] = jnp.full((8, 128), -1.0, f32)
    lines[8 : 8 + length, :] = own
    masks = []
    for k in range(1, taps):
        same = jnp.where(lines[8 - k : 8 - k + length, :] == own, 1.0, 0.0)
        masks.append(jnp.concatenate([same] * -(-width // 128), axis=1)[:, :width])
    return masks


def seq_scan(decay_ref, value_ref, sequences, length, reverse):
    tiles = decay_ref.shape[0]
    unroll = 8

    def step(i, states):
        states = list(states)
        for j in range(unroll):
            at = i * unroll + j
            if reverse:
                at = length - 1 - at
            here = pl.ds(at, sequences, stride=length)
            for tile in range(tiles):
                value = value_ref[tile, here, :]
                decay = decay_ref[tile, here, :]
                if reverse:
                    new = value + states[tile]
                    value_ref[tile, here, :] = new
                    states[tile] = decay * new
                else:
                    states[tile] = value + decay * states[tile]
                    value_ref[tile, here, :] = states[tile]
        return tuple(states)

    lax.fori_loop(0, length // unroll, step, (jnp.zeros((sequences, 128), f32),) * tiles)


def plane():
    halves, shards = lax.axis_size("seq"), lax.axis_size("shard")
    y, s = lax.axis_index("seq"), lax.axis_index("shard")
    offsets = [(dy, ds) for ds in range(0, shards, 2) for dy in range(halves)]

    def at(dy, ds):
        return {"seq": jnp.bitwise_xor(y, dy), "shard": jnp.bitwise_xor(s, ds)}

    def block(dy, ds):
        return jnp.bitwise_xor(s, ds) * halves + jnp.bitwise_xor(y, dy)

    return offsets, at, block


def remote(src, dst, sent, got, device):
    return pltpu.make_async_remote_copy(
        src_ref=src, dst_ref=dst, send_sem=sent, recv_sem=got, device_id=device, device_id_type=MESH
    )


def row_block(ref, index, rows):
    return ref.at[pl.ds(pl.multiple_of(index * rows, rows), rows), :]


def scatter_steps(rows, partial, near, far, acc, sems):
    offsets, at, block = plane()
    near_sent, near_got, far_sent, far_got = sems
    count = len(offsets)
    order = list(range(count - 1, -1, -1))
    firsts = {}
    for q in order:
        dy, ds = offsets[q]
        firsts[q] = remote(
            row_block(partial, block(dy, ds ^ 1), rows), near.at[q], near_sent.at[q], near_got.at[q], at(0, 1)
        )
        firsts[q].start()
    seconds = {}
    for q in order:
        dy, ds = offsets[q]
        firsts[q].wait_recv()
        base = block(dy, ds) * rows

        def tile(i, _):
            step = pl.multiple_of(i * 16, 16)
            here = pl.ds(step, 16)
            total = partial[pl.ds(pl.multiple_of(base + step, 16), 16), :].astype(f32) + near[q, here, :].astype(f32)
            if q:
                near[q, here, :] = total.astype(bf16)
            else:
                acc[here, :] = total
            return 0

        lax.fori_loop(0, rows // 16, tile, 0)
        if q:
            seconds[q] = remote(near.at[q], far.at[q - 1], far_sent.at[q - 1], far_got.at[q - 1], at(dy, ds))
            seconds[q].start()
    yield None
    for q in order[:-1]:
        seconds[q].wait_recv()

        def more(i, _):
            here = pl.ds(pl.multiple_of(i * 16, 16), 16)
            acc[here, :] += far[q - 1, here, :].astype(f32)
            return 0

        lax.fori_loop(0, rows // 16, more, 0)
    yield [firsts[q].wait_send for q in order] + [seconds[q].wait_send for q in order[:-1]]


def gather_steps(rows, whole, sems):
    offsets, at, block = plane()
    near_sent, near_got, far_sent, far_got = sems
    count = len(offsets)
    half = rows // 2

    def piece(q, part):
        start = pl.multiple_of(block(*offsets[q]) * rows + part * half, 16)
        return whole.at[pl.ds(start, half), :]

    own = row_block(whole, block(0, 0), rows)
    straight = [q for q in range(1, count) if offsets[q][0] == 0 or offsets[q][1] == 0]
    across = [q for q in range(1, count) if q not in straight]
    upright = [q for q in straight if offsets[q][0]]
    sends, arrivals = [], []
    outs = {}
    for q in straight:
        outs[q] = remote(own, own, far_sent.at[q], far_got.at[q], at(*offsets[q]))
        outs[q].start()
        sends.append(outs[q].wait_send)

    def hand(q, part=None):
        source = row_block(whole, block(*offsets[q]), rows) if part is None else piece(q, part)
        place = q if part is None or part == 0 else count + q
        copy = remote(source, source, near_sent.at[place], near_got.at[place], at(0, 1))
        copy.start()
        sends.append(copy.wait_send)
        arrivals.append(copy.wait_recv)

    hand(0)
    yield None
    onward = {}
    for q in straight:
        outs[q].wait_recv()
        if q in upright:
            targets = [(1, t) for t in straight if t not in upright]
        else:
            targets = [(0, t) for t in upright]
        for part, t in targets:
            dy, ds = offsets[q][0] | offsets[t][0], offsets[q][1] | offsets[t][1]
            a = offsets.index((dy, ds))
            source = piece(q, part)
            onward[a, part] = remote(source, source, far_sent.at[part * count + a], far_got.at[part * count + a], at(*offsets[t]))
            onward[a, part].start()
            sends.append(onward[a, part].wait_send)
        hand(q)
    yield None
    for a in across:
        for part in range(2):
            onward[a, part].wait_recv()
            hand(a, part)
    yield arrivals + sends


def root_mean(rows):
    return lax.rsqrt(jnp.mean(rows * rows, axis=-1, keepdims=True) + epsilon)


def norm_backward(grad_unit, unit, inverse):
    return inverse * (grad_unit - unit * jnp.mean(grad_unit * unit, axis=-1, keepdims=True))


def by_tiles(rows, work):
    def tile(i, _):
        work(pl.ds(pl.multiple_of(i * 16, 16), 16), i)
        return 0

    lax.fori_loop(0, rows // 16, tile, 0)


def plane_scratch(rows, depth, gathers, scatters):
    count = lax.axis_size("seq") * lax.axis_size("shard") // 2
    block = (rows, depth)
    scratch = []
    if scatters:
        scratch = [
            pltpu.VMEM((count,) + block, bf16),
            pltpu.VMEM((count - 1,) + block, bf16),
            pltpu.VMEM(block, f32),
        ]
    dma = pltpu.SemaphoreType.DMA
    for _ in range(scatters):
        scratch += [dma((count,))] * 2 + [dma((count - 1,))] * 2
    for _ in range(gathers):
        scratch += [dma((2 * count,))] * 4
    return scratch


def cut_columns(weight_ref, gain, target, start, lanes):
    owners = weight_ref.shape[1] // lanes

    def tile(i, _):
        step = pl.multiple_of(i * 16, 16)
        here = pl.ds(step, 16)
        scaled = low(weight_ref[here, :]) * gain(step)
        for j in range(owners):
            target(j)[here, start : start + lanes] = scaled[:, j * lanes : (j + 1) * lanes].astype(bf16)
        return 0

    lax.fori_loop(0, weight_ref.shape[0] // 16, tile, 0)


def quarter_steps(n, part, whole, sems):
    me = lax.axis_index("replica")
    right_sent, right_got, left_sent, left_got = sems

    def rows(q):
        return whole.at[:, pl.ds(pl.multiple_of(q * part, 16), part), :]

    def to_right(hop):
        block = rows(me - hop)
        return remote(block, block, right_sent.at[hop], right_got.at[hop], {"replica": me + 1})

    def to_left(hop):
        block = rows(me + hop)
        return remote(block, block, left_sent.at[hop], left_got.at[hop], {"replica": me - 1})

    def from_left(hop):
        block = rows(me - hop - 1)
        return remote(block, block, right_sent.at[hop], right_got.at[hop], {"replica": me + 1})

    def from_right(hop):
        block = rows(me + hop + 1)
        return remote(block, block, left_sent.at[hop], left_got.at[hop], {"replica": me - 1})

    for hop in range(n - 1):
        if hop:

            @pl.when(me >= hop)
            def _():
                from_left(hop - 1).wait_recv()

            @pl.when(me + hop < n)
            def _():
                from_right(hop - 1).wait_recv()

        @pl.when(jnp.logical_and(me >= hop, me < n - 1))
        def _():
            to_right(hop).start()

        @pl.when(jnp.logical_and(me + hop < n, me > 0))
        def _():
            to_left(hop).start()

        yield

    @pl.when(me >= n - 1)
    def _():
        from_left(n - 2).wait_recv()

    @pl.when(me + n - 1 < n)
    def _():
        from_right(n - 2).wait_recv()

    for hop in range(n - 1):

        @pl.when(jnp.logical_and(me >= hop, me < n - 1))
        def _():
            to_right(hop).wait_send()

        @pl.when(jnp.logical_and(me + hop < n, me > 0))
        def _():
            to_left(hop).wait_send()

    yield


def front_kernel(
    n, sequences, length,
    x_ref, label_ref, cot_ref, gains_ref, raw_conv, raw_a, raw_b, raw_c, rate_ref, rw_ref, iw_ref,
    branch_hbm, input_hbm, gate_hbm, up_hbm, ow_hbm, down_hbm,
    unit_out, labels_out, low_out, product_out, pre_out, conv_in_out, values_out, recur_out, inject_out, decay_out,
    states_out, mix_out, ow_out, two_out, middle_out, pair_out, down_out,
    unit_ref, labels_ref, product_ref, pre_ref, conv_in_ref, values_ref, recur_ref, inject_ref, decay_ref,
    states_ref, mix_ref, ow_ref, two_ref, middle_ref,
    wide, tall, ow_f, mix_cut, pair_cut, pad, lines, rbig, ibig, partial, conv_ref, bias_ref, down_f, down_low,
    near, far, acc, *sems,
):
    rows = x_ref.shape[0]
    scatter_sems, sems = sems[:4], sems[4:]
    unit_sems, label_sems, low_sems, two_sems, sems = sems[:4], sems[4:8], sems[8:12], sems[12:16], sems[16:]
    load_sem, save_sem, mix_sent, mix_got, pair_sent, pair_got, down_sem = sems[:7]
    line_sems = sems[7:]
    offsets, at, block = plane()
    z = lax.axis_index("replica")
    y, s = lax.axis_index("seq"), lax.axis_index("shard")
    shards = lax.axis_size("shard")
    owners = shards * lax.axis_size("seq")
    part = gate_hbm.shape[0] // n
    width = pad.shape[1]
    ff = gate_hbm.shape[1] // owners

    def peer(i):
        return {"seq": jnp.bitwise_xor(y, i // shards), "shard": jnp.bitwise_xor(s, i % shards)}

    def place(i):
        return jnp.bitwise_xor(y, i // shards) * shards + jnp.bitwise_xor(s, i % shards)

    own_rows = pl.ds(pl.multiple_of(z * part, 16), part)
    loads = [
        pltpu.make_async_copy(gate_hbm.at[own_rows, :], tall.at[0], load_sem.at[0]),
        pltpu.make_async_copy(up_hbm.at[own_rows, :], tall.at[1], load_sem.at[1]),
        pltpu.make_async_copy(branch_hbm, wide.at[0], load_sem.at[2]),
        pltpu.make_async_copy(input_hbm, wide.at[1], load_sem.at[3]),
        pltpu.make_async_copy(ow_hbm, ow_f, load_sem.at[4]),
    ]
    for load in loads:
        load.start()
    saves = []

    def save(source, target):
        copy = pltpu.make_async_copy(source, target, save_sem.at[len(saves)])
        copy.start()
        saves.append(copy)

    low_own = pltpu.make_async_copy(cot_ref, row_block(low_out, block(0, 0), rows), load_sem.at[5])
    low_own.start()
    barrier = pltpu.get_barrier_semaphore()
    for i in range(1, owners):
        pl.semaphore_signal(barrier, inc=1, device_id=peer(i), device_id_type=MESH)

    @pl.when(z > 0)
    def _():
        pl.semaphore_signal(barrier, inc=1, device_id={"replica": z - 1}, device_id_type=MESH)

    @pl.when(z < n - 1)
    def _():
        pl.semaphore_signal(barrier, inc=1, device_id={"replica": z + 1}, device_id_type=MESH)

    for side in range(2):
        loads[side].wait()

        cut_columns(
            tall.at[side],
            lambda step: gains_ref[pl.ds(pl.multiple_of(z * part + step, 16), 16), 1:2],
            lambda j: pair_cut.at[j],
            side * ff,
            ff,
        )

    inside_line = jnp.logical_and(z > 0, z < n - 1)

    @pl.when(inside_line)
    def _():
        pl.semaphore_wait(barrier, owners + 1)

    @pl.when(jnp.logical_not(inside_line))
    def _():
        pl.semaphore_wait(barrier, owners)

    me = place(0)
    pair_there = pair_out.at[me, own_rows, :]
    pair_moves = [
        remote(pair_cut.at[place(i)], pair_there, pair_sent.at[i], pair_got.at[i], peer(i)) for i in range(1, owners)
    ]
    for move in pair_moves:
        move.start()
    pair_own = pltpu.make_async_copy(pair_cut.at[me], pair_there, pair_sent.at[0])
    pair_own.start()

    base = block(0, 0) * rows

    def unit(here, i):
        value = x_ref[here, :].astype(f32)
        there = pl.ds(pl.multiple_of(base + i * 16, 16), 16)
        unit_ref[there, :] = (value * root_mean(value)).astype(bf16)
        labels_ref[there, :] = label_ref[here, :]

    by_tiles(rows, unit)
    label_gather = gather_steps(rows, labels_ref, label_sems)
    unit_gather = gather_steps(rows, unit_ref, unit_sems)
    next(label_gather)
    next(unit_gather)

    for side in range(2):
        loads[2 + side].wait()
        cut_columns(
            wide.at[side], lambda step: gains_ref[pl.ds(step, 16), 0:1], lambda j: mix_cut.at[j, side], 0, width
        )
    mix_moves = [
        remote(mix_cut.at[place(i)], mix_ref.at[me], mix_sent.at[i], mix_got.at[i], peer(i)) for i in range(1, owners)
    ]
    for move in mix_moves:
        move.start()
    mix_own = pltpu.make_async_copy(mix_cut.at[me], mix_ref.at[me], mix_sent.at[0])
    mix_own.start()
    loads[4].wait()
    ow_ref[...] = ow_f[...].astype(bf16)
    save(ow_ref, ow_out)
    fill_small(conv_ref, bias_ref, raw_conv, raw_a, raw_b, raw_c, rate_ref)
    fill_blocks(rbig, rw_ref)
    fill_blocks(ibig, iw_ref)
    pad[0:8, :] = jnp.zeros((8, width), f32)
    taps = raw_conv.shape[0]
    clear_tail(decay_ref, width)
    clear_tail(states_ref, width)

    cuts = down_hbm.shape[0] // down_low.shape[1]
    height = down_low.shape[1]

    def down_load(k):
        return pltpu.make_async_copy(down_hbm.at[pl.ds(k * height, height), :], down_f.at[k % 2], down_sem.at[k % 2])

    def down_save(k):
        return pltpu.make_async_copy(down_low.at[k % 2], down_out.at[pl.ds(k * height, height), :], down_sem.at[2 + k % 2])

    def down_cast(k):
        down_load(k).wait()
        if k >= 2:
            down_save(k - 2).wait()
        down_low[k % 2] = down_f[k % 2].astype(bf16)
        down_save(k).start()
        if k + 2 < cuts:
            down_load(k + 2).start()

    for k in range(2):
        down_load(k).start()
    pair_own.wait()
    for move in pair_moves:
        move.wait_recv()
    line = quarter_steps(n, part, pair_out, line_sems)
    next(line)
    next(label_gather)
    next(unit_gather)
    waits = next(label_gather) + next(unit_gather)
    for wait in waits:
        wait()
    mix_own.wait()
    for k in range(cuts):
        down_cast(k)
    for k in range(cuts - 2, cuts):
        down_save(k).wait()
    for move in mix_moves:
        move.wait_recv()
    save(unit_ref, unit_out)
    save(labels_ref, labels_out)
    save(mix_ref, mix_out)

    low_own.wait()
    low_gather = gather_steps(rows, low_out, low_sems)
    next(low_gather)
    next(line)

    def one(q, _):
        here = pl.ds(pl.multiple_of(q * length, length), length)
        sequence = unit_ref[here, :]
        masks = label_masks(labels_ref, here, length, width, taps, lines)
        pre_ref[here, :] = dot_nn(sequence, whole_weight(mix_ref, 0))
        conv_in = dot_nn(sequence, whole_weight(mix_ref, 1)).astype(bf16)
        conv_in_ref[here, :] = conv_in
        pad[8 : 8 + length, :] = conv_in.astype(f32)
        total = bias_ref[0:1, :] + conv_ref[0:1, :] * pad[8 : 8 + length, :]
        for k in range(1, taps):
            total = total + conv_ref[k : k + 1, :] * pad[8 - k : 8 - k + length, :] * masks[k - 1]
        values = total.astype(bf16)
        values_ref[here, :] = values
        recur = jax.nn.sigmoid(dot_nn(values, rbig[...].astype(bf16)) + bias_ref[1:2, :])
        inject = jax.nn.sigmoid(dot_nn(values, ibig[...].astype(bf16)) + bias_ref[2:3, :])
        recur_ref[here, :] = recur
        inject_ref[here, :] = inject
        log_decay = -decay_scale * bias_ref[3:4, :] * recur
        inside = masks[0] > 0.5
        put_tiles(decay_ref, here, jnp.where(inside, jnp.exp(log_decay), 0.0))
        scale = jnp.where(inside, jnp.sqrt(minus_expm1(2.0 * log_decay)), 1.0)
        put_tiles(states_ref, here, scale * inject * values.astype(f32))
        return 0

    lax.fori_loop(0, sequences, one, 0)
    seq_scan(decay_ref, states_ref, sequences, length, False)

    def two(q, _):
        here = pl.ds(pl.multiple_of(q * length, length), length)
        act, _unused = gelu_parts(pre_ref[here, :])
        product = (act * get_tiles(states_ref, here, width)).astype(bf16)
        product_ref[here, :] = product
        partial[here, :] = dot_nn(product, ow_ref[...]).astype(bf16)
        return 0

    lax.fori_loop(0, sequences, two, 0)
    scatter = scatter_steps(rows, partial, near, far, acc, scatter_sems)
    next(scatter)
    for source, target in (
        (product_ref, product_out), (pre_ref, pre_out), (conv_in_ref, conv_in_out), (values_ref, values_out),
        (recur_ref, recur_out), (inject_ref, inject_out), (decay_ref, decay_out), (states_ref, states_out),
    ):
        save(source, target)
    next(line)
    next(low_gather)
    waits = next(low_gather) + next(scatter)

    def norm(here, i):
        middle = x_ref[here, :].astype(f32) + acc[here, :]
        middle_ref[here, :] = middle
        there = pl.ds(pl.multiple_of(base + i * 16, 16), 16)
        two_ref[there, :] = (middle * root_mean(middle)).astype(bf16)

    by_tiles(rows, norm)
    two_gather = gather_steps(rows, two_ref, two_sems)
    next(two_gather)
    save(middle_ref, middle_out)
    for _ in range(n - 4):
        next(line)
    for wait in waits:
        wait()
    next(two_gather)
    for wait in next(two_gather):
        wait()
    save(two_ref, two_out)
    for _ in line:
        pass
    for move in pair_moves + mix_moves:
        move.wait_send()
    for copy in saves:
        copy.wait()


def front(sequences, x, label, cot, gains, small, rw, iw, branch_w, input_w, gate_w, up_w, output_w, down_w):
    rows, depth = x.shape
    own, n = branch_w.shape[0], lax.axis_size("replica")
    owners = lax.axis_size(GROUP)
    total, width, ff = owners * rows, branch_w.shape[1] // owners, gate_w.shape[1] // owners
    part = own // n
    length = total // sequences
    tiles = -(-width // 128)
    kept = [
        ((total, depth), bf16), ((total, 128), bf16), ((total, depth), bf16), ((total, width), bf16),
        ((total, width), f32), ((total, width), bf16), ((total, width), bf16), ((total, width), f32),
        ((total, width), f32), ((tiles, total, 128), f32), ((tiles, total, 128), f32), ((owners, 2, own, width), bf16),
        ((width, depth), bf16), ((total, depth), bf16), ((rows, depth), f32),
    ]
    vm = pltpu.VMEM
    dma = pltpu.SemaphoreType.DMA
    scratch = [vm(*item) for k, item in enumerate(kept) if k != 2] + [
        vm((2,) + branch_w.shape, f32),
        vm((2, part, gate_w.shape[1]), f32),
        vm(output_w.shape, f32),
        vm((owners, 2, own, width), bf16),
        vm((owners, part, 2 * ff), bf16),
        vm((8 + length, width), f32),
        vm((8 + length, 128), f32),
        vm((width, width), f32),
        vm((width, width), f32),
        vm((total, depth), bf16),
        vm((8, width), f32),
        vm((8, width), f32),
        vm((2, down_w.shape[0] // 8, depth), f32),
        vm((2, down_w.shape[0] // 8, depth), bf16),
    ]
    scratch += plane_scratch(rows, depth, 4, 1)
    scratch += [dma((6,)), dma((len(kept),))] + [dma((owners,))] * 4 + [dma((4,))] + [dma((n - 1,))] * 4
    outs = kept + [((owners, own, 2 * ff), bf16), (down_w.shape, bf16)]
    return pl.pallas_call(
        functools.partial(front_kernel, n, sequences, length),
        out_shape=tuple(jax.ShapeDtypeStruct(*item) for item in outs),
        in_specs=[VM] * 11 + [ANY] * 6,
        out_specs=[ANY] * len(outs),
        scratch_shapes=scratch,
        compiler_params=pltpu.CompilerParams(
            collective_id=1, has_side_effects=True, vmem_limit_bytes=62 * 2**20
        ),
        cost_estimate=pl.CostEstimate(flops=10**6, bytes_accessed=200 * 2**20, transcendentals=0),
    )(x, label, cot, gains, *small, rw, iw, branch_w, input_w, gate_w, up_w, output_w, down_w)


def turn_steps(
    sequences, length,
    partial_hbm, middle_ref, cot_ref, label_ref, raw_conv, raw_a, raw_b, raw_c, rate_ref, rw_ref, iw_ref, *rest,
):
    kept_hbm, rest = rest[:9], rest[9:]
    low_out, grad_out, partial_out, branch_low_out, conv_low_out, dconv_ref, sums_ref, drw_ref, diw_ref = rest[:9]
    scatter_sems, gather_sems = rest[9 + 3 : 9 + 7], rest[9 + 7 : 9 + 11]
    near, far, acc = rest[9:12]
    rest = rest[20:]
    kept, rest = rest[:9], rest[9:]
    ow_ref, w_ref, pre_ref, conv_in_ref, values_ref, recur_ref, inject_ref, decay_ref, states_ref = kept
    partial, low_ref, grad_ref, branch_low_ref, conv_low_ref, adj, pad, lines, rbig, ibig, dr, di, conv_ref, bias_ref, load_sem, save_sem = rest
    rows = middle_ref.shape[0]
    offsets, at, block = plane()
    first = pltpu.make_async_copy(partial_hbm, partial, load_sem.at[9])
    first.start()
    loads = [pltpu.make_async_copy(kept_hbm[k], kept[k], load_sem.at[k]) for k in range(9)]
    for load in loads:
        load.start()
    first.wait()
    scatter = scatter_steps(rows, partial, near, far, acc, scatter_sems)
    next(scatter)
    yield
    waits = next(scatter)
    base = block(0, 0) * rows

    def norm(here, i):
        middle = middle_ref[here, :]
        inverse = root_mean(middle)
        grad = cot_ref[here, :].astype(f32) + norm_backward(acc[here, :], middle * inverse, inverse)
        grad_ref[here, :] = grad
        there = pl.ds(pl.multiple_of(base + i * 16, 16), 16)
        low_ref[there, :] = grad.astype(bf16)

    by_tiles(rows, norm)
    gather = gather_steps(rows, low_ref, gather_sems)
    next(gather)
    yield
    next(gather)
    yield
    waits = waits + next(gather)
    yield
    for wait in waits:
        wait()
    for load in loads:
        load.wait()
    saves = [pltpu.make_async_copy(low_ref, low_out, save_sem.at[0]), pltpu.make_async_copy(grad_ref, grad_out, save_sem.at[1])]
    for save in saves:
        save.start()
    fill_blocks(rbig, rw_ref)
    fill_blocks(ibig, iw_ref)
    dr[...] = jnp.zeros_like(dr)
    di[...] = jnp.zeros_like(di)
    sums_ref[...] = jnp.zeros_like(sums_ref)
    dconv_ref[...] = jnp.zeros_like(dconv_ref)
    taps = raw_conv.shape[0]
    fill_small(conv_ref, bias_ref, raw_conv, raw_a, raw_b, raw_c, rate_ref)
    width = pad.shape[1]
    clear_tail(adj, width)

    def one(s):
        here = pl.ds(s * length, length)
        product_grad = dot_nt(low_ref[here, :], ow_ref[...])
        act, slope = gelu_parts(pre_ref[here, :])
        branch_low_ref[here, :] = (product_grad * get_tiles(states_ref, here, width) * slope).astype(bf16)
        put_tiles(adj, here, product_grad * act)

    for s in range(sequences):
        one(s)
        yield
    seq_scan(decay_ref, adj, sequences, length, True)
    yield

    def two(s):
        here = pl.ds(s * length, length)
        adjoint = get_tiles(adj, here, width)
        recur = recur_ref[here, :]
        inject = inject_ref[here, :]
        decay = get_tiles(decay_ref, here, width)
        values = values_ref[here, :]
        values_f = values.astype(f32)
        masks = label_masks(label_ref, here, length, width, taps, lines)
        inside = masks[0] > 0.5
        rate = bias_ref[3:4, :]
        log_decay = -decay_scale * rate * recur
        scale = jnp.where(inside, jnp.sqrt(minus_expm1(2.0 * log_decay)), 1.0)
        pad[0:8, :] = jnp.zeros((8, width), f32)
        pad[8 : 8 + length, :] = get_tiles(states_ref, here, width)
        previous = pad[7 : 7 + length, :]
        driven = adjoint * inject * values_f
        log_grad = jnp.where(inside, adjoint * previous * decay - driven * decay * decay / scale, 0.0)
        recur_low = (log_grad * (-decay_scale * rate) * recur * (1.0 - recur)).astype(bf16)
        inject_low = (driven * scale * (1.0 - inject)).astype(bf16)
        sums_ref[1:2, :] += jnp.sum(recur_low.astype(f32), axis=0, keepdims=True)
        sums_ref[2:3, :] += jnp.sum(inject_low.astype(f32), axis=0, keepdims=True)
        sums_ref[3:4, :] += jnp.sum(log_grad * recur, axis=0, keepdims=True)
        dr[...] += dot_tn(values, recur_low)
        di[...] += dot_tn(values, inject_low)
        grad = adjoint * scale * inject
        grad = grad + dot_nt(recur_low, rbig[...].astype(bf16)) + dot_nt(inject_low, ibig[...].astype(bf16))
        sums_ref[0:1, :] += jnp.sum(grad, axis=0, keepdims=True)
        pad[8 : 8 + length, :] = conv_in_ref[here, :].astype(f32)
        dconv_ref[0:1, :] += jnp.sum(grad * pad[8 : 8 + length, :], axis=0, keepdims=True)
        masked = []
        for k in range(1, taps):
            part = grad * masks[k - 1]
            masked.append(part)
            dconv_ref[k : k + 1, :] += jnp.sum(part * pad[8 - k : 8 - k + length, :], axis=0, keepdims=True)
        total = grad * conv_ref[0:1, :]
        pad[length : length + 8, :] = jnp.zeros((8, width), f32)
        for k in range(1, taps):
            pad[0:length, :] = masked[k - 1] * conv_ref[k : k + 1, :]
            total = total + pad[k : k + length, :]
        conv_low = total.astype(bf16)
        conv_low_ref[here, :] = conv_low
        partial[here, :] = (dot_nt(branch_low_ref[here, :], whole_weight(w_ref, 0)) + dot_nt(conv_low, whole_weight(w_ref, 1))).astype(bf16)

    for s in range(sequences):
        two(s)
        yield
    size = drw_ref.shape[1]
    for h in range(drw_ref.shape[0]):
        cut = slice(h * size, (h + 1) * size)
        drw_ref[h] = dr[cut, cut]
        diw_ref[h] = di[cut, cut]
    ends = [(partial, partial_out), (branch_low_ref, branch_low_out), (conv_low_ref, conv_low_out)]
    for k, pair in enumerate(ends):
        saves.append(pltpu.make_async_copy(*pair, save_sem.at[2 + k]))
        saves[-1].start()
    yield
    for save in saves:
        save.wait()


def end_steps(
    outputs_at, mixes_at,
    partial_hbm, grad_ref, x_ref, middle_ref, hidden_hbm, down_hbm, product_hbm, mid_hbm, unit_hbm, branch_hbm, conv_hbm,
    tokens_ref, block_ref, *rest,
):
    near, far, acc = rest[:3]
    scatter_sems, more_sems = rest[3:7], rest[7:11]
    near_two, far_two, partial, hidden, down, product, tokens_wide, branch_low, conv_low, mix_low, load_sem = rest[11:22]
    output_made, mix_made = rest[22:]
    rows = x_ref.shape[0]
    depth = down.shape[1]

    def load(k, source, target):
        copy = pltpu.make_async_copy(source, target, load_sem.at[k])
        copy.start()
        return copy

    first = load(0, mid_hbm, tokens_wide), load(1, product_hbm, product)
    loads = [
        load(2, partial_hbm, partial), load(3, branch_hbm, branch_low), load(4, conv_hbm, conv_low),
        load(5, hidden_hbm, hidden), load(6, down_hbm, down),
    ]
    for copy in first:
        copy.wait()
    for d in range(0, depth, 512):
        output_made[0, :, d : d + 512] = dot_tn(product[...], tokens_wide[:, d : d + 512]).astype(bf16)
    again = load(7, unit_hbm, tokens_wide)
    yield outputs_at
    loads[0].wait()
    scatter = scatter_steps(rows, partial, near, far, acc, scatter_sems)
    next(scatter)
    yield None
    loads[1].wait()
    loads[2].wait()
    width = branch_low.shape[1]
    if mix_low.shape[1] > 2 * width:
        mix_low[...] = jnp.zeros_like(mix_low)

    def pack(here, i):
        mix_low[here, 0 : 2 * width] = jnp.concatenate([branch_low[here, :], conv_low[here, :]], axis=1)

    by_tiles(mix_low.shape[0], pack)
    again.wait()
    owners, own = mix_made.shape[:2]
    for part in range(4):
        for j in range(part * owners // 4, (part + 1) * owners // 4):
            mix_made[j] = dot_tn(tokens_wide[:, j * own : (j + 1) * own], mix_low[...]).astype(bf16)
        yield mixes_at if part == 3 else None
    waits = next(scatter)

    def norm(here, i):
        value = x_ref[here, :].astype(f32)
        inverse = root_mean(value)
        grad = grad_ref[here, :] + norm_backward(acc[here, :], value * inverse, inverse)
        tokens_ref[here, :] = grad.astype(bf16)

    by_tiles(rows, norm)
    for wait in waits:
        wait()
    yield None
    loads[3].wait()
    loads[4].wait()
    pieces_of = 4
    height = hidden.shape[0] // pieces_of
    for k in range(pieces_of):
        here = pl.ds(k * height, height)
        partial[here, :] = dot_nn(hidden[here, :], down[...]).astype(bf16)
        yield None
    scatter = scatter_steps(rows, partial, near_two, far_two, acc, more_sems)
    next(scatter)
    yield None
    waits = next(scatter)

    def out(here, i):
        block_ref[here, :] = (middle_ref[here, :] + acc[here, :]).astype(bf16)

    by_tiles(rows, out)
    yield None
    for wait in waits:
        wait()


def mlp_kernel(
    two_hbm, low_hbm, pair_hbm, down_hbm, hidden_out, partial_out, down_out, pair_out,
    two, low_rows, pair_w, down_w, hidden, pair_low, partial, down_grad, pair_grad, load_sem, save_sem, pair_sem,
):
    total, depth = two.shape
    ff = down_w.shape[0]
    tile = 256 if ff % 256 == 0 else 128
    height = 256
    steps = total // height

    def rows_of(hbm, ref, r, which):
        here = pl.ds(r * height, height)
        return pltpu.make_async_copy(hbm.at[here, :], ref.at[here, :], load_sem.at[which, r])

    weights = [
        pltpu.make_async_copy(pair_hbm, pair_w, load_sem.at[2, 0]),
        pltpu.make_async_copy(down_hbm, down_w, load_sem.at[2, 1]),
    ]
    rows_of(two_hbm, two, 0, 0).start()
    weights[0].start()
    rows_of(low_hbm, low_rows, 0, 1).start()
    weights[1].start()
    for r in range(1, steps):
        rows_of(two_hbm, two, r, 0).start()
        rows_of(low_hbm, low_rows, r, 1).start()
    weights[0].wait()
    weights[1].wait()

    def row_step(r, _):
        here = pl.ds(pl.multiple_of(r * height, height), height)
        pltpu.make_async_copy(two_hbm.at[here, :], two.at[here, :], load_sem.at[0, r]).wait()
        pltpu.make_async_copy(low_hbm.at[here, :], low_rows.at[here, :], load_sem.at[1, r]).wait()
        for f in range(ff // tile):
            cut = slice(f * tile, (f + 1) * tile)
            more = slice(ff + f * tile, ff + (f + 1) * tile)
            gate = dot_nn(two[here, :], pair_w[:, cut])
            up = dot_nn(two[here, :], pair_w[:, more])
            grad = dot_nt(low_rows[here, :], down_w[cut, :])
            act, slope = gelu_parts(gate)
            hidden[here, cut] = (act * up).astype(bf16)
            pair_low[here, cut] = (grad * up * slope).astype(bf16)
            pair_low[here, more] = (grad * act).astype(bf16)
        for d in range(0, depth, 512):
            partial[here, d : d + 512] = dot_nt(pair_low[here, :], pair_w[d : d + 512, :]).astype(bf16)
        return 0

    lax.fori_loop(0, steps, row_step, 0)
    saves = [
        pltpu.make_async_copy(partial, partial_out, save_sem.at[0]),
        pltpu.make_async_copy(hidden, hidden_out, save_sem.at[1]),
    ]
    for save in saves:
        save.start()
    for f in range(ff // tile):
        cut = slice(f * tile, (f + 1) * tile)
        down_grad[cut, :] = dot_tn(hidden[:, cut], low_rows[...]).astype(bf16)
    saves.append(pltpu.make_async_copy(down_grad, down_out, save_sem.at[2]))
    saves[-1].start()

    def column_step(d, _):
        here = pl.ds(pl.multiple_of(d * height, height), height)
        pair_grad[here, :] = dot_tn(two[:, here], pair_low[...]).astype(bf16)
        pltpu.make_async_copy(pair_grad.at[here, :], pair_out.at[here, :], pair_sem.at[d]).start()
        return 0

    lax.fori_loop(0, depth // height, column_step, 0)
    for d in range(depth // height):
        here = pl.ds(d * height, height)
        pltpu.make_async_copy(pair_grad.at[here, :], pair_out.at[here, :], pair_sem.at[d]).wait()
    for save in saves:
        save.wait()


def mlp(unit_two, out_low, pair_w, down_w):
    total, depth = unit_two.shape
    ff = down_w.shape[0]
    kept = [((total, ff), bf16), ((total, depth), bf16), ((ff, depth), bf16), ((depth, 2 * ff), bf16)]
    vm, dma = pltpu.VMEM, pltpu.SemaphoreType.DMA
    return pl.pallas_call(
        mlp_kernel,
        out_shape=tuple(jax.ShapeDtypeStruct(*item) for item in kept),
        in_specs=[ANY] * 4,
        out_specs=[ANY] * 4,
        scratch_shapes=[vm(item.shape, bf16) for item in (unit_two, out_low, pair_w, down_w)]
        + [vm((total, ff), bf16), vm((total, 2 * ff), bf16)]
        + [vm(*item) for item in kept[1:]]
        + [dma((3, total // 256)), dma((3,)), dma((depth // 256,))],
        compiler_params=pltpu.CompilerParams(vmem_limit_bytes=60 * 2**20),
        cost_estimate=pl.CostEstimate(
            flops=2 * total * depth * ff * 8, bytes_accessed=36 * 2**20, transcendentals=total * ff
        ),
    )(unit_two, out_low, pair_w, down_w)


def pieces(rows, most):
    count = -(-rows // most)
    while rows % count or (rows // count) % 16:
        count += 1
    return count


def line_kernel(n, kinds, cuts, made_here, beside, turns, extra, *refs):
    ins = len(cuts)
    made = ins + kinds.count("pair")
    extra_ins, extra_outs, extra_scratch = extra
    refs = list(refs)

    def take(count):
        taken = refs[:count]
        del refs[:count]
        return taken

    given = [k for k in range(ins) if k not in made_here]
    own_hbm, side_in = dict(zip(given, take(len(given)))), take(extra_ins)
    outs, side_out = take(made), take(extra_outs)
    side_scratch = take(extra_scratch)
    from_out, from_in = take(ins), take(ins)
    own_made = dict(zip(made_here, take(len(made_here))))
    slots, whole_sem, slot_sem, sent_in, sent_out, got_out, got_in, sent_x, got_x = refs
    depth = slots.shape[0]
    me = lax.axis_index("replica")
    y, s = lax.axis_index("seq"), lax.axis_index("shard")
    shards = lax.axis_size("shard")
    owners = shards * lax.axis_size("seq")
    left = me < n // 2
    inward = jnp.where(left, me + 1, me - 1)
    outward = jnp.where(left, me - 1, me + 1)
    has_out = jnp.logical_and(me > 0, me < n - 1)
    at_end = jnp.logical_not(has_out)
    middle = jnp.logical_or(me == n // 2 - 1, me == n // 2)

    def peer(i):
        return {"seq": jnp.bitwise_xor(y, i // shards), "shard": jnp.bitwise_xor(s, i % shards)}

    def place(i):
        return jnp.bitwise_xor(y, i // shards) * shards + jnp.bitwise_xor(s, i % shards)

    chunks = []
    for k, (lead, count, rows) in enumerate(cuts):
        for step in range(lead):
            for i in range(count):
                chunks.append((k, step if kinds[k] == "row" else (step + 1) % lead, i * rows, rows))
    total = len(chunks)

    def view(group, c):
        k, i, start, rows = chunks[c]
        return group[k].at[0 if kinds[k] == "row" else place(i), pl.ds(start, rows), :]

    def slot(c):
        k, i, start, rows = chunks[c]
        return slots.at[c % depth, pl.ds(0, rows), pl.ds(0, from_in[k].shape[2])]

    def load(c):
        return pltpu.make_async_copy(view(own_hbm, c), slot(c), slot_sem.at[c % depth])

    wholes = {k: pltpu.make_async_copy(own_hbm[k], from_out[k], whole_sem.at[k]) for k in given}
    loaded = [c for c in range(total) if chunks[c][0] in given]

    @pl.when(at_end)
    def _():
        for k in given:
            wholes[k].start()

    @pl.when(has_out)
    def _():
        for c in loaded[: depth - 1]:
            load(c).start()

    barrier = pltpu.get_barrier_semaphore()
    for i in range(1, owners):
        pl.semaphore_signal(barrier, inc=1, device_id=peer(i), device_id_type=MESH)
    pl.semaphore_signal(barrier, inc=1, device_id={"replica": inward}, device_id_type=MESH)

    @pl.when(has_out)
    def _():
        pl.semaphore_signal(barrier, inc=1, device_id={"replica": outward}, device_id_type=MESH)
        pl.semaphore_wait(barrier, owners + 1)

    @pl.when(at_end)
    def _():
        pl.semaphore_wait(barrier, owners)

    def push(group, target, c, sent, got, device):
        return remote(view(group, c), view(target, c), sent.at[c], got.at[c], {"replica": device})

    def add(target, other, c):
        k, i, start, rows = chunks[c]
        if other is None:
            more = view(own_made, c) if k in made_here else slot(c)
        else:
            more = view(other, c)
        into = view(target, c)

        def tile(t, _):
            here = pl.ds(pl.multiple_of(t * 16, 16), 16)
            into[here, :] = (into[here, :].astype(f32) + more[here, :].astype(f32)).astype(bf16)
            return 0

        lax.fori_loop(0, rows // 16, tile, 0)

    def pass_in(c, source):
        @pl.when(middle)
        def _():
            push(source, from_in, c, sent_in, got_in, inward).start()

        @pl.when(jnp.logical_not(middle))
        def _():
            push(source, from_out, c, sent_in, got_out, inward).start()

    def gather_in(c):
        @pl.when(has_out)
        def _():
            if c in loaded:
                load(c).wait()
            push(from_out, from_out, c, sent_in, got_out, inward).wait_recv()
            add(from_out, None, c)
            pass_in(c, from_out)
            if c + depth - 1 in loaded:
                load(c + depth - 1).start()

    @pl.when(at_end)
    def _():
        for c in loaded:
            if c == 0 or chunks[c][0] != chunks[c - 1][0]:
                wholes[chunks[c][0]].wait()
            pass_in(c, from_out)

    def advance():
        k = next(work)
        if k is not None:

            @pl.when(at_end)
            def _():
                for c in range(total):
                    if chunks[c][0] == k:
                        pass_in(c, own_made)

    work = beside(*side_in, *side_out, *side_scratch, *[own_made[k] for k in made_here])
    advance()

    def deliveries(c):
        k, i, start, rows = chunks[c]
        here = pl.ds(start, rows)
        first = k + kinds[:k].count("pair")
        source = view(from_in, c)
        if kinds[k] == "row":
            ends = [(source, outs[first].at[here, :])]
        elif kinds[k] == "side":
            ends = [(source, outs[first].at[place(0), here, :])]
        else:
            half = source.shape[1] // 2
            there = pl.ds(pl.multiple_of(place(0) * half, half), half)
            ends = [
                (source.at[:, pl.ds(part * half, half)], outs[first + part].at[here, there]) for part in range(2)
            ]
        if kinds[k] == "row" or i == 0:
            return [pltpu.make_async_copy(*pair, sent_x.at[c, p]) for p, pair in enumerate(ends)], False
        return [remote(*pair, sent_x.at[c, p], got_x.at[c, p], peer(i)) for p, pair in enumerate(ends)], True

    def give_back(c):
        push(from_out, from_in, c, sent_out, got_in, inward).wait_recv()

        @pl.when(middle)
        def _():
            add(from_in, from_out, c)

        @pl.when(has_out)
        def _():
            push(from_in, from_in, c, sent_out, got_in, outward).start()

        for copy in deliveries(c)[0]:
            copy.start()

    lag = 1
    for c in range(total + lag):
        for _ in range(turns.count(c)):
            advance()
        if c < total:
            gather_in(c)
        if c >= lag:
            give_back(c - lag)
    for _ in work:
        pass
    for c in range(total):
        copies, away = deliveries(c)
        for copy in copies:
            if away:
                copy.wait_recv()
                copy.wait_send()
            else:
                copy.wait()
        push(from_out, from_in, c, sent_in, got_in, inward).wait_send()

        @pl.when(has_out)
        def _():
            push(from_in, from_in, c, sent_out, got_in, outward).wait_send()


def replica_sum(arrays, kinds, made_here, identity, beside, turns, inputs, results, side_scratch):
    cuts, outs = [], []
    tall = broad = 0
    for item, kind in zip(arrays, kinds):
        lead, height, columns = item.shape
        count = pieces(height, max(16, (105 * 1024) // columns // 16 * 16))
        cuts.append((lead, count, height // count))
        tall, broad = max(tall, height // count), max(broad, columns)
        if kind == "pair":
            outs += [jax.ShapeDtypeStruct((height, lead * columns // 2), bf16)] * 2
        elif kind == "side":
            outs.append(jax.ShapeDtypeStruct(item.shape, bf16))
        else:
            outs.append(jax.ShapeDtypeStruct((height, columns), bf16))
    count = sum(lead * cut for lead, cut, _ in cuts)
    buffers = [pltpu.VMEM(item.shape, bf16) for item in arrays]
    dma = pltpu.SemaphoreType.DMA
    return pl.pallas_call(
        functools.partial(
            line_kernel, lax.axis_size("replica"), tuple(kinds), tuple(cuts), tuple(made_here), beside, turns,
            (len(inputs), len(results), len(side_scratch)),
        ),
        out_shape=tuple(outs) + tuple(jax.ShapeDtypeStruct(shape, kind) for shape, kind, _ in results),
        in_specs=[ANY] * (len(arrays) - len(made_here)) + [spec for _, spec in inputs],
        out_specs=[ANY] * len(outs) + [spec for _, _, spec in results],
        scratch_shapes=list(side_scratch)
        + buffers * 2
        + [buffers[k] for k in made_here]
        + [pltpu.VMEM((4, tall, broad), bf16), dma((len(arrays),)), dma((4,))]
        + [dma((count,))] * 4
        + [dma((count, 2))] * 2,
        compiler_params=pltpu.CompilerParams(
            collective_id=identity, has_side_effects=True, vmem_limit_bytes=62 * 2**20
        ),
        cost_estimate=pl.CostEstimate(flops=10**6, bytes_accessed=200 * 2**20, transcendentals=0),
    )(*[item for k, item in enumerate(arrays) if k not in made_here], *[item for item, _ in inputs])


def finish_pair_kernel(gain_ref, a_ref, b_ref, wa_ref, wb_ref, outa_ref, outb_ref, grad_ref):
    grad = jnp.zeros(gain_ref.shape, f32)
    for sum_ref, weight_ref, out_ref in ((a_ref, wa_ref, outa_ref), (b_ref, wb_ref, outb_ref)):
        total = sum_ref[...].astype(f32)
        out_ref[...] = total * gain_ref[...]
        grad = grad + jnp.sum(total * low(weight_ref[...]), axis=1, keepdims=True)
    grad_ref[...] = grad


def finish_pair(gain, a, b, wa, wb):
    rows, columns = wa.shape
    cut = min(rows, 32)
    wide = pl.BlockSpec((cut, columns), lambda i: (i, 0))
    thin = pl.BlockSpec((cut, 1), lambda i: (i, 0))
    out = jax.ShapeDtypeStruct((rows, columns), f32)
    return pl.pallas_call(
        finish_pair_kernel,
        grid=(rows // cut,),
        out_shape=(out, out, jax.ShapeDtypeStruct((rows, 1), f32)),
        in_specs=[thin, wide, wide, wide, wide],
        out_specs=[wide, wide, thin],
        compiler_params=pltpu.CompilerParams(vmem_limit_bytes=62 * 2**20),
        cost_estimate=pl.CostEstimate(flops=6 * rows * columns, bytes_accessed=20 * rows * columns, transcendentals=0),
    )(gain, a, b, wa, wb)


def finish_rest_kernel(gain_ref, mix_ref, wa_ref, wb_ref, out_sum_ref, down_sum_ref, outa_ref, outb_ref, grad_ref, out_ref, down_ref):
    owners = mix_ref.shape[0]
    width = wa_ref.shape[1] // owners
    grad = jnp.zeros(gain_ref.shape, f32)
    for part, (weight_ref, target_ref) in enumerate(((wa_ref, outa_ref), (wb_ref, outb_ref))):
        total = jnp.concatenate(
            [mix_ref[j, :, part * width : (part + 1) * width].astype(f32) for j in range(owners)], axis=1
        )
        target_ref[...] = total * gain_ref[...]
        grad = grad + jnp.sum(total * low(weight_ref[...]), axis=1, keepdims=True)
    grad_ref[...] = grad
    out_ref[...] = out_sum_ref[...].astype(f32)
    down_ref[...] = down_sum_ref[...].astype(f32)


def finish_rest(gain, mix, wa, wb, out_sum, down_sum):
    rows, columns = wa.shape
    steps = 4
    while out_sum.shape[0] % (16 * steps) or down_sum.shape[0] % (16 * steps) or rows % (16 * steps):
        steps //= 2

    def tall(item):
        return pl.BlockSpec((item.shape[0] // steps, item.shape[1]), lambda i: (i, 0))

    owners, _, both = mix.shape
    wide, thin = tall(wa), tall(gain)
    return pl.pallas_call(
        finish_rest_kernel,
        grid=(steps,),
        out_shape=(
            jax.ShapeDtypeStruct(wa.shape, f32),
            jax.ShapeDtypeStruct(wa.shape, f32),
            jax.ShapeDtypeStruct((rows, 1), f32),
            jax.ShapeDtypeStruct(out_sum.shape, f32),
            jax.ShapeDtypeStruct(down_sum.shape, f32),
        ),
        in_specs=[
            thin,
            pl.BlockSpec((owners, rows // steps, both), lambda i: (0, i, 0)),
            wide,
            wide,
            tall(out_sum),
            tall(down_sum),
        ],
        out_specs=[wide, wide, thin, tall(out_sum), tall(down_sum)],
        compiler_params=pltpu.CompilerParams(vmem_limit_bytes=62 * 2**20),
        cost_estimate=pl.CostEstimate(flops=10**7, bytes_accessed=40 * 2**20, transcendentals=0),
    )(gain, mix, wa, wb, out_sum, down_sum)


def body(
    tokens,
    segments,
    cotangent,
    norm_gain,
    branch_weight,
    input_weight,
    conv_weight,
    conv_bias,
    recur_gate_weight,
    recur_gate_bias,
    input_gate_weight,
    input_gate_bias,
    decay_param,
    output_weight,
    mlp_norm_gain,
    gate_weight,
    up_weight,
    down_weight,
):
    x, cot = tokens[0], cotangent[0]
    rows, depth = x.shape
    members = lax.axis_size(GROUP)
    sequences = lax.axis_size("shard")
    total = members * rows
    gain, mlp_gain = low(norm_gain)[:, None], low(mlp_norm_gain)[:, None]
    own_labels = jnp.broadcast_to(segments[0].astype(bf16)[:, None], (rows, 128))
    width = branch_weight.shape[1] // members
    decay_f = low(decay_param)
    small = (
        conv_weight, conv_bias[None], recur_gate_bias[None], input_gate_bias[None], jax.nn.softplus(-decay_f)[None],
    )
    (
        unit_all, labels, out_low, product, *mixed, mix_w, output_w, unit_two, middle, pair_w, down_w,
    ) = front(
        sequences, x, own_labels, cot, low(jnp.stack([norm_gain, mlp_norm_gain], 1)), small,
        recur_gate_weight, input_gate_weight, branch_weight, input_weight, gate_weight, up_weight, output_weight,
        down_weight,
    )
    pair_w = pair_w.reshape(depth, -1)
    whole = ((total, depth), bf16)
    hidden, partial, down_partial, pair_partial = mlp(unit_two, out_low, pair_w, down_w)
    down_partial = down_partial[None]
    pair_partial = pair_partial.reshape(members, -1, pair_w.shape[1])
    kept = (output_w, mix_w, *mixed)
    narrow = ((total, width), bf16)
    vm, dma = pltpu.VMEM, pltpu.SemaphoreType.DMA
    length = total // sequences
    back = replica_sum(
        [down_partial, pair_partial], ["row", "pair"], (), 3,
        functools.partial(turn_steps, sequences, length),
        (6, 9, 12) + tuple(range(14, 14 + 2 * sequences + 2)),
        [(partial, ANY)] + [(item, VM) for item in (middle, cot, labels, *small, recur_gate_weight, input_gate_weight)]
        + [(item, ANY) for item in kept],
        [whole + (ANY,), ((rows, depth), f32, ANY), whole + (ANY,), narrow + (ANY,), narrow + (ANY,)]
        + [(conv_weight.shape, f32, VM), ((4, width), f32, VM), (recur_gate_weight.shape, f32, VM), (input_gate_weight.shape, f32, VM)],
        plane_scratch(rows, depth, 1, 1)
        + [vm(item.shape, item.dtype) for item in kept]
        + [vm(*whole), vm(*whole), vm((rows, depth), f32), vm(*narrow), vm(*narrow), vm(mixed[-1].shape, f32)]
        + [vm((8 + length, width), f32), vm((8 + length, 128), f32)]
        + [vm((width, width), f32)] * 4
        + [vm((8, width), f32)] * 2
        + [dma((10,)), dma((5,))],
    )
    down_sum, gate_sum, up_sum, mid_low, middle_grad, partial, branch_low, conv_low = back[:8]
    conv_weight_grad, sums, recur_weight_grad, inject_weight_grad = back[8:]
    gate_grad, up_grad, mlp_gain_grad = finish_pair(mlp_gain, gate_sum, up_sum, gate_weight, up_weight)
    size = recur_gate_weight.shape[1]
    gates = jnp.concatenate([recur_weight_grad, inject_weight_grad], 2).reshape(width, 2 * size)
    lanes = -(-max(width, 2 * size) // 128) * 128
    lines = jnp.concatenate([conv_weight_grad, sums], 0)
    packed = jnp.concatenate(
        [
            jnp.pad(gates, ((0, 0), (0, lanes - 2 * size))),
            jnp.pad(lines, ((0, 16 - lines.shape[0]), (0, lanes - width))),
        ],
        0,
    ).astype(bf16)[None]
    both = -(-2 * width // 128) * 128
    mix_shape = jax.ShapeDtypeStruct((members, depth // members, both), bf16)
    output_shape = jax.ShapeDtypeStruct((1,) + output_w.shape, bf16)
    again = plane_scratch(rows, depth, 0, 1)
    packed, output_sum, mix_sum, tokens_grad, block_out = replica_sum(
        [packed, output_shape, mix_shape], ["row", "row", "side"], (1, 2), 4, functools.partial(end_steps, 1, 2),
        (0, 1, 2, 3, 4, 7, 8, 9, 10, 11, 12, 19),
        [(partial, ANY), (middle_grad, VM), (x, VM), (middle, VM)]
        + [(item, ANY) for item in (hidden, down_w, product, mid_low, unit_all, branch_low, conv_low)],
        [((rows, depth), bf16, VM), ((rows, depth), bf16, VM)],
        again + again[3:] + again[:2] + [vm(*whole), vm(hidden.shape, bf16), vm(down_w.shape, bf16)]
        + [vm(*narrow), vm(*whole), vm(*narrow), vm(*narrow), vm((total, both), bf16), dma((8,))],
    )
    packed = packed.astype(f32)
    branch_grad, input_grad, gain_grad, output_grad, down_grad = finish_rest(
        gain, mix_sum, branch_weight, input_weight, output_sum, down_sum
    )
    recur_weight_grad = packed[:width, :size].reshape(-1, size, size)
    inject_weight_grad = packed[:width, size : 2 * size].reshape(-1, size, size)
    conv_weight_grad = packed[width : width + conv_weight.shape[0], :width]
    conv_bias_grad, recur_bias_grad, inject_bias_grad, rate_grad = [packed[width + conv_weight.shape[0] + i, :width] for i in range(4)]
    decay_param_grad = rate_grad * decay_scale * jax.nn.sigmoid(-decay_f)
    return (
        block_out[None],
        tokens_grad[None],
        gain_grad[:, 0],
        branch_grad,
        input_grad,
        conv_weight_grad,
        conv_bias_grad,
        recur_weight_grad,
        recur_bias_grad,
        inject_weight_grad,
        inject_bias_grad,
        decay_param_grad,
        output_grad,
        mlp_gain_grad[:, 0],
        gate_grad,
        up_grad,
        down_grad,
    )


def solution(mesh):
    row3 = P(("shard", "replica"), "seq", None)
    vec = P(("seq", "shard"))
    mat = P(("seq", "shard"), None)
    cube = P(("seq", "shard"), None, None)
    taps = P(None, ("seq", "shard"))
    params = (vec, mat, mat, taps, vec, cube, vec, cube, vec, vec, mat, vec, mat, mat, mat)
    in_specs = (row3, P(("shard", "replica"), "seq"), row3) + params
    out_specs = (row3, row3) + params
    return jax.shard_map(body, mesh=mesh, in_specs=in_specs, out_specs=out_specs, check_vma=False)
```

```python
import functools

import jax
import jax.numpy as jnp
from jax import lax
from jax.experimental import pallas as pl
from jax.experimental.pallas import tpu as pltpu
from jax.sharding import PartitionSpec as P

epsilon = 1e-06
decay_scale = 8.0
GROUP = ("seq", "shard")
ROWS = ("shard", "seq")
f32 = jnp.float32
bf16 = jnp.bfloat16
VM = pl.BlockSpec(memory_space=pltpu.VMEM)
ANY = pl.BlockSpec(memory_space=pl.ANY)
MESH = pl.DeviceIdType.MESH


def mm(left, right):
    return jnp.dot(left, right, preferred_element_type=f32)


def mm_nt(left, right):
    return lax.dot_general(left, right, (((1,), (1,)), ((), ())), preferred_element_type=f32)


def mm_tn(left, right):
    return lax.dot_general(left, right, (((0,), (0,)), ((), ())), preferred_element_type=f32)


def low(item):
    return item.astype(bf16).astype(f32)


def by_owner(weight, gain):
    owners = lax.axis_size(GROUP)
    scaled = (low(weight) * gain).astype(bf16)
    return jnp.swapaxes(scaled.reshape(weight.shape[0], owners, -1), 0, 1)


def swap(cut):
    return lax.all_to_all(cut, GROUP, split_axis=0, concat_axis=0, tiled=True)


def gelu_parts(x):
    inner = 0.7978845608028654 * (x + 0.044715 * x * x * x)
    t = jnp.tanh(inner)
    value = 0.5 * x * (1.0 + t)
    slope = 0.5 * (1.0 + t) + 0.5 * x * (1.0 - t * t) * 0.7978845608028654 * (
        1.0 + 3.0 * 0.044715 * x * x
    )
    return value, slope


def minus_expm1(y):
    poly = 1.0 + y * (1.0 / 8.0)
    for order in (7.0, 6.0, 5.0, 4.0, 3.0, 2.0):
        poly = 1.0 + y * (1.0 / order) * poly
    return jnp.where(y > -0.5, -y * poly, 1.0 - jnp.exp(y))


def dot_nn(a, b):
    return lax.dot_general(a, b, (((1,), (0,)), ((), ())), preferred_element_type=f32)


def dot_nt(a, b):
    return lax.dot_general(a, b, (((1,), (1,)), ((), ())), preferred_element_type=f32)


def dot_tn(a, b):
    return lax.dot_general(a, b, (((0,), (0,)), ((), ())), preferred_element_type=f32)


def whole_weight(ref, part):
    owners, _, rows, width = ref.shape
    return ref[:, part].reshape(owners * rows, width)


def fill_blocks(target, source):
    target[...] = jnp.zeros_like(target)
    count, size = source.shape[0], source.shape[1]
    for h in range(count):
        target[h * size : (h + 1) * size, h * size : (h + 1) * size] = source[h].astype(bf16).astype(f32)


def put_tiles(ref, here, value):
    width = value.shape[1]
    for tile in range(ref.shape[0]):
        lanes = min(128, width - 128 * tile)
        ref[tile, here, 0:lanes] = value[:, 128 * tile : 128 * tile + lanes]


def get_tiles(ref, here, width):
    parts = [ref[tile, here, 0 : min(128, width - 128 * tile)] for tile in range(ref.shape[0])]
    return jnp.concatenate(parts, axis=1)


def clear_tail(ref, width):
    tail = ref.shape[0] * 128 - width
    if tail:
        ref[ref.shape[0] - 1, :, 128 - tail :] = jnp.zeros((ref.shape[1], tail), f32)


def fill_small(conv, bias, raw_conv, raw_a, raw_b, raw_c, rate):
    conv[0 : raw_conv.shape[0], :] = low(raw_conv[...])
    for row, ref in enumerate((raw_a, raw_b, raw_c)):
        bias[row : row + 1, :] = low(ref[...])[None, :]
    bias[3:4, :] = rate[...][None, :]


def label_masks(label_ref, here, length, width, taps, lines):
    own = label_ref[here, :].astype(f32)
    lines[0:8, :] = jnp.full((8, 128), -1.0, f32)
    lines[8 : 8 + length, :] = own
    masks = []
    for k in range(1, taps):
        same = jnp.where(lines[8 - k : 8 - k + length, :] == own, 1.0, 0.0)
        masks.append(jnp.concatenate([same] * -(-width // 128), axis=1)[:, :width])
    return masks


def seq_scan(decay_ref, value_ref, sequences, length, reverse):
    tiles = decay_ref.shape[0]
    unroll = 8

    def step(i, states):
        states = list(states)
        for j in range(unroll):
            at = i * unroll + j
            if reverse:
                at = length - 1 - at
            here = pl.ds(at, sequences, stride=length)
            for tile in range(tiles):
                value = value_ref[tile, here, :]
                decay = decay_ref[tile, here, :]
                if reverse:
                    new = value + states[tile]
                    value_ref[tile, here, :] = new
                    states[tile] = decay * new
                else:
                    states[tile] = value + decay * states[tile]
                    value_ref[tile, here, :] = states[tile]
        return tuple(states)

    lax.fori_loop(0, length // unroll, step, (jnp.zeros((sequences, 128), f32),) * tiles)


def plane():
    halves, shards = lax.axis_size("seq"), lax.axis_size("shard")
    y, s = lax.axis_index("seq"), lax.axis_index("shard")
    offsets = [(dy, ds) for ds in range(0, shards, 2) for dy in range(halves)]

    def at(dy, ds):
        return {"seq": jnp.bitwise_xor(y, dy), "shard": jnp.bitwise_xor(s, ds)}

    def block(dy, ds):
        return jnp.bitwise_xor(s, ds) * halves + jnp.bitwise_xor(y, dy)

    return offsets, at, block


def remote(src, dst, sent, got, device):
    return pltpu.make_async_remote_copy(
        src_ref=src, dst_ref=dst, send_sem=sent, recv_sem=got, device_id=device, device_id_type=MESH
    )


def row_block(ref, index, rows):
    return ref.at[pl.ds(pl.multiple_of(index * rows, rows), rows), :]


def scatter_steps(rows, partial, near, far, acc, sems):
    offsets, at, block = plane()
    near_sent, near_got, far_sent, far_got = sems
    count = len(offsets)
    order = list(range(count - 1, -1, -1))
    firsts = {}
    for q in order:
        dy, ds = offsets[q]
        firsts[q] = remote(
            row_block(partial, block(dy, ds ^ 1), rows), near.at[q], near_sent.at[q], near_got.at[q], at(0, 1)
        )
        firsts[q].start()
    seconds = {}
    for q in order:
        dy, ds = offsets[q]
        firsts[q].wait_recv()
        base = block(dy, ds) * rows

        def tile(i, _):
            step = pl.multiple_of(i * 16, 16)
            here = pl.ds(step, 16)
            total = partial[pl.ds(pl.multiple_of(base + step, 16), 16), :].astype(f32) + near[q, here, :].astype(f32)
            if q:
                near[q, here, :] = total.astype(bf16)
            else:
                acc[here, :] = total
            return 0

        lax.fori_loop(0, rows // 16, tile, 0)
        if q:
            seconds[q] = remote(near.at[q], far.at[q - 1], far_sent.at[q - 1], far_got.at[q - 1], at(dy, ds))
            seconds[q].start()
    yield None
    for q in order[:-1]:
        seconds[q].wait_recv()

        def more(i, _):
            here = pl.ds(pl.multiple_of(i * 16, 16), 16)
            acc[here, :] += far[q - 1, here, :].astype(f32)
            return 0

        lax.fori_loop(0, rows // 16, more, 0)
    yield [firsts[q].wait_send for q in order] + [seconds[q].wait_send for q in order[:-1]]


def gather_steps(rows, whole, sems):
    offsets, at, block = plane()
    near_sent, near_got, far_sent, far_got = sems
    count = len(offsets)
    half = rows // 2

    def piece(q, part):
        start = pl.multiple_of(block(*offsets[q]) * rows + part * half, 16)
        return whole.at[pl.ds(start, half), :]

    own = row_block(whole, block(0, 0), rows)
    straight = [q for q in range(1, count) if offsets[q][0] == 0 or offsets[q][1] == 0]
    across = [q for q in range(1, count) if q not in straight]
    upright = [q for q in straight if offsets[q][0]]
    sends, arrivals = [], []
    outs = {}
    for q in straight:
        outs[q] = remote(own, own, far_sent.at[q], far_got.at[q], at(*offsets[q]))
        outs[q].start()
        sends.append(outs[q].wait_send)

    def hand(q, part=None):
        source = row_block(whole, block(*offsets[q]), rows) if part is None else piece(q, part)
        place = q if part is None or part == 0 else count + q
        copy = remote(source, source, near_sent.at[place], near_got.at[place], at(0, 1))
        copy.start()
        sends.append(copy.wait_send)
        arrivals.append(copy.wait_recv)

    hand(0)
    yield None
    onward = {}
    for q in straight:
        outs[q].wait_recv()
        if q in upright:
            targets = [(1, t) for t in straight if t not in upright]
        else:
            targets = [(0, t) for t in upright]
        for part, t in targets:
            dy, ds = offsets[q][0] | offsets[t][0], offsets[q][1] | offsets[t][1]
            a = offsets.index((dy, ds))
            source = piece(q, part)
            onward[a, part] = remote(source, source, far_sent.at[part * count + a], far_got.at[part * count + a], at(*offsets[t]))
            onward[a, part].start()
            sends.append(onward[a, part].wait_send)
        hand(q)
    yield None
    for a in across:
        for part in range(2):
            onward[a, part].wait_recv()
            hand(a, part)
    yield arrivals + sends


def root_mean(rows):
    return lax.rsqrt(jnp.mean(rows * rows, axis=-1, keepdims=True) + epsilon)


def norm_backward(grad_unit, unit, inverse):
    return inverse * (grad_unit - unit * jnp.mean(grad_unit * unit, axis=-1, keepdims=True))


def by_tiles(rows, work):
    def tile(i, _):
        work(pl.ds(pl.multiple_of(i * 16, 16), 16), i)
        return 0

    lax.fori_loop(0, rows // 16, tile, 0)


def plane_scratch(rows, depth, gathers, scatters):
    count = lax.axis_size("seq") * lax.axis_size("shard") // 2
    block = (rows, depth)
    scratch = []
    if scatters:
        scratch = [
            pltpu.VMEM((count,) + block, bf16),
            pltpu.VMEM((count - 1,) + block, bf16),
            pltpu.VMEM(block, f32),
        ]
    dma = pltpu.SemaphoreType.DMA
    for _ in range(scatters):
        scratch += [dma((count,))] * 2 + [dma((count - 1,))] * 2
    for _ in range(gathers):
        scratch += [dma((2 * count,))] * 4
    return scratch


def cut_columns(weight_ref, gain, target, start, lanes):
    owners = weight_ref.shape[1] // lanes

    def tile(i, _):
        step = pl.multiple_of(i * 16, 16)
        here = pl.ds(step, 16)
        scaled = low(weight_ref[here, :]) * gain(step)
        for j in range(owners):
            target(j)[here, start : start + lanes] = scaled[:, j * lanes : (j + 1) * lanes].astype(bf16)
        return 0

    lax.fori_loop(0, weight_ref.shape[0] // 16, tile, 0)


def quarter_steps(n, part, whole, sems):
    me = lax.axis_index("replica")
    right_sent, right_got, left_sent, left_got = sems

    def rows(q):
        return whole.at[:, pl.ds(pl.multiple_of(q * part, 16), part), :]

    def to_right(hop):
        block = rows(me - hop)
        return remote(block, block, right_sent.at[hop], right_got.at[hop], {"replica": me + 1})

    def to_left(hop):
        block = rows(me + hop)
        return remote(block, block, left_sent.at[hop], left_got.at[hop], {"replica": me - 1})

    def from_left(hop):
        block = rows(me - hop - 1)
        return remote(block, block, right_sent.at[hop], right_got.at[hop], {"replica": me + 1})

    def from_right(hop):
        block = rows(me + hop + 1)
        return remote(block, block, left_sent.at[hop], left_got.at[hop], {"replica": me - 1})

    for hop in range(n - 1):
        if hop:

            @pl.when(me >= hop)
            def _():
                from_left(hop - 1).wait_recv()

            @pl.when(me + hop < n)
            def _():
                from_right(hop - 1).wait_recv()

        @pl.when(jnp.logical_and(me >= hop, me < n - 1))
        def _():
            to_right(hop).start()

        @pl.when(jnp.logical_and(me + hop < n, me > 0))
        def _():
            to_left(hop).start()

        yield

    @pl.when(me >= n - 1)
    def _():
        from_left(n - 2).wait_recv()

    @pl.when(me + n - 1 < n)
    def _():
        from_right(n - 2).wait_recv()

    for hop in range(n - 1):

        @pl.when(jnp.logical_and(me >= hop, me < n - 1))
        def _():
            to_right(hop).wait_send()

        @pl.when(jnp.logical_and(me + hop < n, me > 0))
        def _():
            to_left(hop).wait_send()

    yield


def front_kernel(
    n, sequences, length,
    x_ref, label_ref, cot_ref, gains_ref, raw_conv, raw_a, raw_b, raw_c, rate_ref, rw_ref, iw_ref,
    branch_hbm, input_hbm, gate_hbm, up_hbm, ow_hbm, down_hbm,
    unit_out, labels_out, low_out, product_out, pre_out, conv_in_out, values_out, recur_out, inject_out, decay_out,
    states_out, mix_out, ow_out, two_out, middle_out, pair_out, down_out,
    unit_ref, labels_ref, product_ref, pre_ref, conv_in_ref, values_ref, recur_ref, inject_ref, decay_ref,
    states_ref, mix_ref, ow_ref, two_ref, middle_ref,
    wide, tall, ow_f, mix_cut, pair_cut, pad, lines, rbig, ibig, partial, conv_ref, bias_ref, down_f, down_low,
    near, far, acc, *sems,
):
    rows = x_ref.shape[0]
    scatter_sems, sems = sems[:4], sems[4:]
    unit_sems, label_sems, low_sems, two_sems, sems = sems[:4], sems[4:8], sems[8:12], sems[12:16], sems[16:]
    load_sem, save_sem, mix_sent, mix_got, pair_sent, pair_got, down_sem = sems[:7]
    line_sems = sems[7:]
    offsets, at, block = plane()
    z = lax.axis_index("replica")
    y, s = lax.axis_index("seq"), lax.axis_index("shard")
    shards = lax.axis_size("shard")
    owners = shards * lax.axis_size("seq")
    part = gate_hbm.shape[0] // n
    width = pad.shape[1]
    ff = gate_hbm.shape[1] // owners

    def peer(i):
        return {"seq": jnp.bitwise_xor(y, i // shards), "shard": jnp.bitwise_xor(s, i % shards)}

    def place(i):
        return jnp.bitwise_xor(y, i // shards) * shards + jnp.bitwise_xor(s, i % shards)

    own_rows = pl.ds(pl.multiple_of(z * part, 16), part)
    loads = [
        pltpu.make_async_copy(gate_hbm.at[own_rows, :], tall.at[0], load_sem.at[0]),
        pltpu.make_async_copy(up_hbm.at[own_rows, :], tall.at[1], load_sem.at[1]),
        pltpu.make_async_copy(branch_hbm, wide.at[0], load_sem.at[2]),
        pltpu.make_async_copy(input_hbm, wide.at[1], load_sem.at[3]),
        pltpu.make_async_copy(ow_hbm, ow_f, load_sem.at[4]),
    ]
    for load in loads:
        load.start()
    saves = []

    def save(source, target):
        copy = pltpu.make_async_copy(source, target, save_sem.at[len(saves)])
        copy.start()
        saves.append(copy)

    low_own = pltpu.make_async_copy(cot_ref, row_block(low_out, block(0, 0), rows), load_sem.at[5])
    low_own.start()
    barrier = pltpu.get_barrier_semaphore()
    for i in range(1, owners):
        pl.semaphore_signal(barrier, inc=1, device_id=peer(i), device_id_type=MESH)

    @pl.when(z > 0)
    def _():
        pl.semaphore_signal(barrier, inc=1, device_id={"replica": z - 1}, device_id_type=MESH)

    @pl.when(z < n - 1)
    def _():
        pl.semaphore_signal(barrier, inc=1, device_id={"replica": z + 1}, device_id_type=MESH)

    for side in range(2):
        loads[side].wait()

        cut_columns(
            tall.at[side],
            lambda step: low(gains_ref[pl.ds(pl.multiple_of(z * part + step, 16), 16), 1:2]),
            lambda j: pair_cut.at[j],
            side * ff,
            ff,
        )

    inside_line = jnp.logical_and(z > 0, z < n - 1)

    @pl.when(inside_line)
    def _():
        pl.semaphore_wait(barrier, owners + 1)

    @pl.when(jnp.logical_not(inside_line))
    def _():
        pl.semaphore_wait(barrier, owners)

    me = place(0)
    pair_there = pair_out.at[me, own_rows, :]
    pair_moves = [
        remote(pair_cut.at[place(i)], pair_there, pair_sent.at[i], pair_got.at[i], peer(i)) for i in range(1, owners)
    ]
    for move in pair_moves:
        move.start()
    pair_own = pltpu.make_async_copy(pair_cut.at[me], pair_there, pair_sent.at[0])
    pair_own.start()

    base = block(0, 0) * rows

    def unit(here, i):
        value = x_ref[here, :].astype(f32)
        there = pl.ds(pl.multiple_of(base + i * 16, 16), 16)
        unit_ref[there, :] = (value * root_mean(value)).astype(bf16)
        labels_ref[there, :] = label_ref[here, :]

    by_tiles(rows, unit)
    label_gather = gather_steps(rows, labels_ref, label_sems)
    unit_gather = gather_steps(rows, unit_ref, unit_sems)
    next(label_gather)
    next(unit_gather)

    for side in range(2):
        loads[2 + side].wait()
        cut_columns(
            wide.at[side], lambda step: low(gains_ref[pl.ds(step, 16), 0:1]), lambda j: mix_cut.at[j, side], 0, width
        )
    mix_moves = [
        remote(mix_cut.at[place(i)], mix_ref.at[me], mix_sent.at[i], mix_got.at[i], peer(i)) for i in range(1, owners)
    ]
    for move in mix_moves:
        move.start()
    mix_own = pltpu.make_async_copy(mix_cut.at[me], mix_ref.at[me], mix_sent.at[0])
    mix_own.start()
    loads[4].wait()
    ow_ref[...] = ow_f[...].astype(bf16)
    save(ow_ref, ow_out)
    fill_small(conv_ref, bias_ref, raw_conv, raw_a, raw_b, raw_c, rate_ref)
    fill_blocks(rbig, rw_ref)
    fill_blocks(ibig, iw_ref)
    pad[0:8, :] = jnp.zeros((8, width), f32)
    taps = raw_conv.shape[0]
    clear_tail(decay_ref, width)
    clear_tail(states_ref, width)

    cuts = down_hbm.shape[0] // down_low.shape[1]
    height = down_low.shape[1]

    def down_load(k):
        return pltpu.make_async_copy(down_hbm.at[pl.ds(k * height, height), :], down_f.at[k % 2], down_sem.at[k % 2])

    def down_save(k):
        return pltpu.make_async_copy(down_low.at[k % 2], down_out.at[pl.ds(k * height, height), :], down_sem.at[2 + k % 2])

    def down_cast(k):
        down_load(k).wait()
        if k >= 2:
            down_save(k - 2).wait()
        down_low[k % 2] = down_f[k % 2].astype(bf16)
        down_save(k).start()
        if k + 2 < cuts:
            down_load(k + 2).start()

    pair_own.wait()
    for move in pair_moves:
        move.wait_recv()
    line = quarter_steps(n, part, pair_out, line_sems)
    next(line)
    next(label_gather)
    next(unit_gather)
    waits = next(label_gather) + next(unit_gather)
    for wait in waits:
        wait()
    mix_own.wait()
    for move in mix_moves:
        move.wait_recv()
    save(unit_ref, unit_out)
    save(labels_ref, labels_out)
    save(mix_ref, mix_out)

    low_own.wait()
    low_gather = gather_steps(rows, low_out, low_sems)
    next(low_gather)
    next(line)

    def one(q, _):
        here = pl.ds(pl.multiple_of(q * length, length), length)
        sequence = unit_ref[here, :]
        masks = label_masks(labels_ref, here, length, width, taps, lines)
        pre_ref[here, :] = dot_nn(sequence, whole_weight(mix_ref, 0))
        conv_in = dot_nn(sequence, whole_weight(mix_ref, 1)).astype(bf16)
        conv_in_ref[here, :] = conv_in
        pad[8 : 8 + length, :] = conv_in.astype(f32)
        total = bias_ref[0:1, :] + conv_ref[0:1, :] * pad[8 : 8 + length, :]
        for k in range(1, taps):
            total = total + conv_ref[k : k + 1, :] * pad[8 - k : 8 - k + length, :] * masks[k - 1]
        values = total.astype(bf16)
        values_ref[here, :] = values
        recur = jax.nn.sigmoid(dot_nn(values, rbig[...].astype(bf16)) + bias_ref[1:2, :])
        inject = jax.nn.sigmoid(dot_nn(values, ibig[...].astype(bf16)) + bias_ref[2:3, :])
        recur_ref[here, :] = recur
        inject_ref[here, :] = inject
        log_decay = -decay_scale * bias_ref[3:4, :] * recur
        inside = masks[0] > 0.5
        put_tiles(decay_ref, here, jnp.where(inside, jnp.exp(log_decay), 0.0))
        scale = jnp.where(inside, jnp.sqrt(minus_expm1(2.0 * log_decay)), 1.0)
        put_tiles(states_ref, here, scale * inject * values.astype(f32))
        return 0

    lax.fori_loop(0, sequences, one, 0)
    seq_scan(decay_ref, states_ref, sequences, length, False)

    def two(q, _):
        here = pl.ds(pl.multiple_of(q * length, length), length)
        act, _unused = gelu_parts(pre_ref[here, :])
        product = (act * get_tiles(states_ref, here, width)).astype(bf16)
        product_ref[here, :] = product
        partial[here, :] = dot_nn(product, ow_ref[...]).astype(bf16)
        return 0

    for k in range(2):
        down_load(k).start()
    lax.fori_loop(0, sequences, two, 0)
    scatter = scatter_steps(rows, partial, near, far, acc, scatter_sems)
    next(scatter)
    for source, target in (
        (product_ref, product_out), (pre_ref, pre_out), (conv_in_ref, conv_in_out), (values_ref, values_out),
        (recur_ref, recur_out), (inject_ref, inject_out), (decay_ref, decay_out), (states_ref, states_out),
    ):
        save(source, target)
    next(line)
    for k in range(cuts):
        down_cast(k)
    for k in range(cuts - 2, cuts):
        down_save(k).wait()
    next(low_gather)
    waits = next(low_gather) + next(scatter)

    def norm(here, i):
        middle = x_ref[here, :].astype(f32) + acc[here, :]
        middle_ref[here, :] = middle
        there = pl.ds(pl.multiple_of(base + i * 16, 16), 16)
        two_ref[there, :] = (middle * root_mean(middle)).astype(bf16)

    by_tiles(rows, norm)
    two_gather = gather_steps(rows, two_ref, two_sems)
    next(two_gather)
    save(middle_ref, middle_out)
    for _ in range(n - 4):
        next(line)
    for wait in waits:
        wait()
    next(two_gather)
    for wait in next(two_gather):
        wait()
    save(two_ref, two_out)
    for _ in line:
        pass
    for move in pair_moves + mix_moves:
        move.wait_send()
    for copy in saves:
        copy.wait()


def front(sequences, x, label, cot, gains, small, rw, iw, branch_w, input_w, gate_w, up_w, output_w, down_w):
    rows, depth = x.shape
    own, n = branch_w.shape[0], lax.axis_size("replica")
    owners = lax.axis_size(GROUP)
    total, width, ff = owners * rows, branch_w.shape[1] // owners, gate_w.shape[1] // owners
    part = own // n
    length = total // sequences
    tiles = -(-width // 128)
    kept = [
        ((total, depth), bf16), ((total, 128), bf16), ((total, depth), bf16), ((total, width), bf16),
        ((total, width), f32), ((total, width), bf16), ((total, width), bf16), ((total, width), f32),
        ((total, width), f32), ((tiles, total, 128), f32), ((tiles, total, 128), f32), ((owners, 2, own, width), bf16),
        ((width, depth), bf16), ((total, depth), bf16), ((rows, depth), f32),
    ]
    vm = pltpu.VMEM
    dma = pltpu.SemaphoreType.DMA
    scratch = [vm(*item) for k, item in enumerate(kept) if k != 2] + [
        vm((2,) + branch_w.shape, f32),
        vm((2, part, gate_w.shape[1]), f32),
        vm(output_w.shape, f32),
        vm((owners, 2, own, width), bf16),
        vm((owners, part, 2 * ff), bf16),
        vm((8 + length, width), f32),
        vm((8 + length, 128), f32),
        vm((width, width), f32),
        vm((width, width), f32),
        vm((total, depth), bf16),
        vm((8, width), f32),
        vm((8, width), f32),
        vm((2, down_w.shape[0] // 8, depth), f32),
        vm((2, down_w.shape[0] // 8, depth), bf16),
    ]
    scratch += plane_scratch(rows, depth, 4, 1)
    scratch += [dma((6,)), dma((len(kept),))] + [dma((owners,))] * 4 + [dma((4,))] + [dma((n - 1,))] * 4
    outs = kept + [((owners, own, 2 * ff), bf16), (down_w.shape, bf16)]
    return pl.pallas_call(
        functools.partial(front_kernel, n, sequences, length),
        out_shape=tuple(jax.ShapeDtypeStruct(*item) for item in outs),
        in_specs=[VM] * 11 + [ANY] * 6,
        out_specs=[ANY] * len(outs),
        scratch_shapes=scratch,
        compiler_params=pltpu.CompilerParams(
            collective_id=1, has_side_effects=True, vmem_limit_bytes=62 * 2**20
        ),
        cost_estimate=pl.CostEstimate(flops=10**6, bytes_accessed=200 * 2**20, transcendentals=0),
    )(x, label, cot, gains, *small, rw, iw, branch_w, input_w, gate_w, up_w, output_w, down_w)


def turn_steps(
    sequences, length,
    partial_hbm, middle_ref, cot_ref, label_ref, raw_conv, raw_a, raw_b, raw_c, rate_ref, rw_ref, iw_ref, *rest,
):
    kept_hbm, rest = rest[:9], rest[9:]
    low_out, grad_out, partial_out, branch_low_out, conv_low_out, dconv_ref, sums_ref, drw_ref, diw_ref = rest[:9]
    scatter_sems, gather_sems = rest[9 + 3 : 9 + 7], rest[9 + 7 : 9 + 11]
    near, far, acc = rest[9:12]
    rest = rest[20:]
    kept, rest = rest[:9], rest[9:]
    ow_ref, w_ref, pre_ref, conv_in_ref, values_ref, recur_ref, inject_ref, decay_ref, states_ref = kept
    partial, low_ref, grad_ref, branch_low_ref, conv_low_ref, adj, pad, lines, rbig, ibig, dr, di, conv_ref, bias_ref, load_sem, save_sem = rest
    rows = middle_ref.shape[0]
    offsets, at, block = plane()
    first = pltpu.make_async_copy(partial_hbm, partial, load_sem.at[9])
    first.start()
    loads = [pltpu.make_async_copy(kept_hbm[k], kept[k], load_sem.at[k]) for k in range(9)]
    for load in loads:
        load.start()
    first.wait()
    scatter = scatter_steps(rows, partial, near, far, acc, scatter_sems)
    next(scatter)
    yield
    waits = next(scatter)
    base = block(0, 0) * rows

    def norm(here, i):
        middle = middle_ref[here, :]
        inverse = root_mean(middle)
        grad = cot_ref[here, :].astype(f32) + norm_backward(acc[here, :], middle * inverse, inverse)
        grad_ref[here, :] = grad
        there = pl.ds(pl.multiple_of(base + i * 16, 16), 16)
        low_ref[there, :] = grad.astype(bf16)

    by_tiles(rows, norm)
    gather = gather_steps(rows, low_ref, gather_sems)
    next(gather)
    yield
    next(gather)
    yield
    waits = waits + next(gather)
    yield
    for wait in waits:
        wait()
    for load in loads:
        load.wait()
    saves = [pltpu.make_async_copy(low_ref, low_out, save_sem.at[0]), pltpu.make_async_copy(grad_ref, grad_out, save_sem.at[1])]
    for save in saves:
        save.start()
    fill_blocks(rbig, rw_ref)
    fill_blocks(ibig, iw_ref)
    dr[...] = jnp.zeros_like(dr)
    di[...] = jnp.zeros_like(di)
    sums_ref[...] = jnp.zeros_like(sums_ref)
    dconv_ref[...] = jnp.zeros_like(dconv_ref)
    taps = raw_conv.shape[0]
    fill_small(conv_ref, bias_ref, raw_conv, raw_a, raw_b, raw_c, rate_ref)
    width = pad.shape[1]
    clear_tail(adj, width)

    def one(s):
        here = pl.ds(s * length, length)
        product_grad = dot_nt(low_ref[here, :], ow_ref[...])
        act, slope = gelu_parts(pre_ref[here, :])
        branch_low_ref[here, :] = (product_grad * get_tiles(states_ref, here, width) * slope).astype(bf16)
        put_tiles(adj, here, product_grad * act)

    for s in range(sequences):
        one(s)
        yield
    seq_scan(decay_ref, adj, sequences, length, True)
    yield

    def two(s):
        here = pl.ds(s * length, length)
        adjoint = get_tiles(adj, here, width)
        recur = recur_ref[here, :]
        inject = inject_ref[here, :]
        decay = get_tiles(decay_ref, here, width)
        values = values_ref[here, :]
        values_f = values.astype(f32)
        masks = label_masks(label_ref, here, length, width, taps, lines)
        inside = masks[0] > 0.5
        rate = bias_ref[3:4, :]
        log_decay = -decay_scale * rate * recur
        scale = jnp.where(inside, jnp.sqrt(minus_expm1(2.0 * log_decay)), 1.0)
        pad[0:8, :] = jnp.zeros((8, width), f32)
        pad[8 : 8 + length, :] = get_tiles(states_ref, here, width)
        previous = pad[7 : 7 + length, :]
        driven = adjoint * inject * values_f
        log_grad = jnp.where(inside, adjoint * previous * decay - driven * decay * decay / scale, 0.0)
        recur_low = (log_grad * (-decay_scale * rate) * recur * (1.0 - recur)).astype(bf16)
        inject_low = (driven * scale * (1.0 - inject)).astype(bf16)
        sums_ref[1:2, :] += jnp.sum(recur_low.astype(f32), axis=0, keepdims=True)
        sums_ref[2:3, :] += jnp.sum(inject_low.astype(f32), axis=0, keepdims=True)
        sums_ref[3:4, :] += jnp.sum(log_grad * recur, axis=0, keepdims=True)
        dr[...] += dot_tn(values, recur_low)
        di[...] += dot_tn(values, inject_low)
        grad = adjoint * scale * inject
        grad = grad + dot_nt(recur_low, rbig[...].astype(bf16)) + dot_nt(inject_low, ibig[...].astype(bf16))
        sums_ref[0:1, :] += jnp.sum(grad, axis=0, keepdims=True)
        pad[8 : 8 + length, :] = conv_in_ref[here, :].astype(f32)
        dconv_ref[0:1, :] += jnp.sum(grad * pad[8 : 8 + length, :], axis=0, keepdims=True)
        masked = []
        for k in range(1, taps):
            part = grad * masks[k - 1]
            masked.append(part)
            dconv_ref[k : k + 1, :] += jnp.sum(part * pad[8 - k : 8 - k + length, :], axis=0, keepdims=True)
        total = grad * conv_ref[0:1, :]
        pad[length : length + 8, :] = jnp.zeros((8, width), f32)
        for k in range(1, taps):
            pad[0:length, :] = masked[k - 1] * conv_ref[k : k + 1, :]
            total = total + pad[k : k + length, :]
        conv_low = total.astype(bf16)
        conv_low_ref[here, :] = conv_low
        partial[here, :] = (dot_nt(branch_low_ref[here, :], whole_weight(w_ref, 0)) + dot_nt(conv_low, whole_weight(w_ref, 1))).astype(bf16)

    for s in range(sequences):
        two(s)
        yield
    size = drw_ref.shape[1]
    for h in range(drw_ref.shape[0]):
        cut = slice(h * size, (h + 1) * size)
        drw_ref[h] = dr[cut, cut]
        diw_ref[h] = di[cut, cut]
    ends = [(partial, partial_out), (branch_low_ref, branch_low_out), (conv_low_ref, conv_low_out)]
    for k, pair in enumerate(ends):
        saves.append(pltpu.make_async_copy(*pair, save_sem.at[2 + k]))
        saves[-1].start()
    yield
    for save in saves:
        save.wait()


def end_steps(
    outputs_at, mixes_at,
    partial_hbm, grad_ref, x_ref, middle_ref, hidden_hbm, down_hbm, product_hbm, mid_hbm, unit_hbm, branch_hbm, conv_hbm,
    tokens_ref, block_ref, *rest,
):
    near, far, acc = rest[:3]
    scatter_sems, more_sems = rest[3:7], rest[7:11]
    near_two, far_two, partial, hidden, down, product, tokens_wide, branch_low, conv_low, mix_low, load_sem = rest[11:22]
    output_made, mix_made = rest[22:]
    rows = x_ref.shape[0]
    depth = down.shape[1]

    def load(k, source, target):
        copy = pltpu.make_async_copy(source, target, load_sem.at[k])
        copy.start()
        return copy

    first = load(0, mid_hbm, tokens_wide), load(1, product_hbm, product)
    loads = [
        load(2, partial_hbm, partial), load(3, branch_hbm, branch_low), load(4, conv_hbm, conv_low),
        load(5, hidden_hbm, hidden), load(6, down_hbm, down),
    ]
    for copy in first:
        copy.wait()
    for d in range(0, depth, 512):
        output_made[0, :, d : d + 512] = dot_tn(product[...], tokens_wide[:, d : d + 512]).astype(bf16)
    again = load(7, unit_hbm, tokens_wide)
    yield outputs_at
    loads[0].wait()
    scatter = scatter_steps(rows, partial, near, far, acc, scatter_sems)
    next(scatter)
    yield None
    loads[1].wait()
    loads[2].wait()
    width = branch_low.shape[1]
    if mix_low.shape[1] > 2 * width:
        mix_low[...] = jnp.zeros_like(mix_low)

    def pack(here, i):
        mix_low[here, 0 : 2 * width] = jnp.concatenate([branch_low[here, :], conv_low[here, :]], axis=1)

    by_tiles(mix_low.shape[0], pack)
    again.wait()
    owners, own = mix_made.shape[:2]
    for part in range(4):
        for j in range(part * owners // 4, (part + 1) * owners // 4):
            mix_made[j] = dot_tn(tokens_wide[:, j * own : (j + 1) * own], mix_low[...]).astype(bf16)
        yield mixes_at if part == 3 else None
    waits = next(scatter)

    def norm(here, i):
        value = x_ref[here, :].astype(f32)
        inverse = root_mean(value)
        grad = grad_ref[here, :] + norm_backward(acc[here, :], value * inverse, inverse)
        tokens_ref[here, :] = grad.astype(bf16)

    by_tiles(rows, norm)
    for wait in waits:
        wait()
    yield None
    loads[3].wait()
    loads[4].wait()
    pieces_of = 4
    height = hidden.shape[0] // pieces_of
    for k in range(pieces_of):
        here = pl.ds(k * height, height)
        partial[here, :] = dot_nn(hidden[here, :], down[...]).astype(bf16)
        yield None
    scatter = scatter_steps(rows, partial, near_two, far_two, acc, more_sems)
    next(scatter)
    yield None
    waits = next(scatter)

    def out(here, i):
        block_ref[here, :] = (middle_ref[here, :] + acc[here, :]).astype(bf16)

    by_tiles(rows, out)
    yield None
    for wait in waits:
        wait()


def mlp_kernel(
    two_hbm, low_hbm, pair_hbm, down_hbm, hidden_out, partial_out, down_out, pair_out,
    two, low_rows, pair_w, down_w, hidden, pair_low, partial, down_grad, pair_grad, load_sem, save_sem, pair_sem,
):
    total, depth = two.shape
    ff = down_w.shape[0]
    tile = 256 if ff % 256 == 0 else 128
    height = 512
    steps = total // height

    def rows_of(hbm, ref, r, which):
        here = pl.ds(r * height, height)
        return pltpu.make_async_copy(hbm.at[here, :], ref.at[here, :], load_sem.at[which, r])

    weights = [
        pltpu.make_async_copy(pair_hbm, pair_w, load_sem.at[2, 0]),
        pltpu.make_async_copy(down_hbm, down_w, load_sem.at[2, 1]),
    ]
    rows_of(two_hbm, two, 0, 0).start()
    weights[0].start()
    rows_of(low_hbm, low_rows, 0, 1).start()
    weights[1].start()
    for r in range(1, steps):
        rows_of(two_hbm, two, r, 0).start()
        rows_of(low_hbm, low_rows, r, 1).start()
    weights[0].wait()
    weights[1].wait()

    def row_step(r, _):
        here = pl.ds(pl.multiple_of(r * height, height), height)
        pltpu.make_async_copy(two_hbm.at[here, :], two.at[here, :], load_sem.at[0, r]).wait()
        pltpu.make_async_copy(low_hbm.at[here, :], low_rows.at[here, :], load_sem.at[1, r]).wait()
        for f in range(ff // tile):
            cut = slice(f * tile, (f + 1) * tile)
            more = slice(ff + f * tile, ff + (f + 1) * tile)
            gate = dot_nn(two[here, :], pair_w[:, cut])
            up = dot_nn(two[here, :], pair_w[:, more])
            grad = dot_nt(low_rows[here, :], down_w[cut, :])
            act, slope = gelu_parts(gate)
            hidden[here, cut] = (act * up).astype(bf16)
            pair_low[here, cut] = (grad * up * slope).astype(bf16)
            pair_low[here, more] = (grad * act).astype(bf16)
        for d in range(0, depth, 512):
            partial[here, d : d + 512] = dot_nt(pair_low[here, :], pair_w[d : d + 512, :]).astype(bf16)
        return 0

    lax.fori_loop(0, steps, row_step, 0)
    saves = [
        pltpu.make_async_copy(partial, partial_out, save_sem.at[0]),
        pltpu.make_async_copy(hidden, hidden_out, save_sem.at[1]),
    ]
    for save in saves:
        save.start()
    for f in range(ff // tile):
        cut = slice(f * tile, (f + 1) * tile)
        down_grad[cut, :] = dot_tn(hidden[:, cut], low_rows[...]).astype(bf16)
    saves.append(pltpu.make_async_copy(down_grad, down_out, save_sem.at[2]))
    saves[-1].start()

    height = 256

    def column_step(d, _):
        here = pl.ds(pl.multiple_of(d * height, height), height)
        pair_grad[here, :] = dot_tn(two[:, here], pair_low[...]).astype(bf16)
        pltpu.make_async_copy(pair_grad.at[here, :], pair_out.at[here, :], pair_sem.at[d]).start()
        return 0

    lax.fori_loop(0, depth // height, column_step, 0)
    for d in range(depth // height):
        here = pl.ds(d * height, height)
        pltpu.make_async_copy(pair_grad.at[here, :], pair_out.at[here, :], pair_sem.at[d]).wait()
    for save in saves:
        save.wait()


def mlp(unit_two, out_low, pair_w, down_w):
    total, depth = unit_two.shape
    ff = down_w.shape[0]
    kept = [((total, ff), bf16), ((total, depth), bf16), ((ff, depth), bf16), ((depth, 2 * ff), bf16)]
    vm, dma = pltpu.VMEM, pltpu.SemaphoreType.DMA
    return pl.pallas_call(
        mlp_kernel,
        out_shape=tuple(jax.ShapeDtypeStruct(*item) for item in kept),
        in_specs=[ANY] * 4,
        out_specs=[ANY] * 4,
        scratch_shapes=[vm(item.shape, bf16) for item in (unit_two, out_low, pair_w, down_w)]
        + [vm((total, ff), bf16), vm((total, 2 * ff), bf16)]
        + [vm(*item) for item in kept[1:]]
        + [dma((3, total // 512)), dma((3,)), dma((depth // 256,))],
        compiler_params=pltpu.CompilerParams(vmem_limit_bytes=60 * 2**20),
        cost_estimate=pl.CostEstimate(
            flops=2 * total * depth * ff * 8, bytes_accessed=36 * 2**20, transcendentals=total * ff
        ),
    )(unit_two, out_low, pair_w, down_w)


def pieces(rows, most):
    count = -(-rows // most)
    while rows % count or (rows // count) % 16:
        count += 1
    return count


def line_kernel(n, kinds, cuts, made_here, beside, turns, extra, *refs):
    ins = len(cuts)
    made = ins + kinds.count("pair")
    extra_ins, extra_outs, extra_scratch = extra
    refs = list(refs)

    def take(count):
        taken = refs[:count]
        del refs[:count]
        return taken

    given = [k for k in range(ins) if k not in made_here]
    own_hbm, side_in = dict(zip(given, take(len(given)))), take(extra_ins)
    outs, side_out = take(made), take(extra_outs)
    side_scratch = take(extra_scratch)
    from_out, from_in = take(ins), take(ins)
    own_made = dict(zip(made_here, take(len(made_here))))
    slots, whole_sem, slot_sem, sent_in, sent_out, got_out, got_in, sent_x, got_x = refs
    depth = slots.shape[0]
    me = lax.axis_index("replica")
    y, s = lax.axis_index("seq"), lax.axis_index("shard")
    shards = lax.axis_size("shard")
    owners = shards * lax.axis_size("seq")
    left = me < n // 2
    inward = jnp.where(left, me + 1, me - 1)
    outward = jnp.where(left, me - 1, me + 1)
    has_out = jnp.logical_and(me > 0, me < n - 1)
    at_end = jnp.logical_not(has_out)
    middle = jnp.logical_or(me == n // 2 - 1, me == n // 2)

    def peer(i):
        return {"seq": jnp.bitwise_xor(y, i // shards), "shard": jnp.bitwise_xor(s, i % shards)}

    def place(i):
        return jnp.bitwise_xor(y, i // shards) * shards + jnp.bitwise_xor(s, i % shards)

    chunks = []
    for k, (lead, count, rows) in enumerate(cuts):
        for step in range(lead):
            for i in range(count):
                chunks.append((k, step if kinds[k] == "row" else (step + 1) % lead, i * rows, rows))
    total = len(chunks)

    def view(group, c):
        k, i, start, rows = chunks[c]
        return group[k].at[0 if kinds[k] == "row" else place(i), pl.ds(start, rows), :]

    def slot(c):
        k, i, start, rows = chunks[c]
        return slots.at[c % depth, pl.ds(0, rows), pl.ds(0, from_in[k].shape[2])]

    def load(c):
        return pltpu.make_async_copy(view(own_hbm, c), slot(c), slot_sem.at[c % depth])

    wholes = {k: pltpu.make_async_copy(own_hbm[k], from_out[k], whole_sem.at[k]) for k in given}
    loaded = [c for c in range(total) if chunks[c][0] in given]

    @pl.when(at_end)
    def _():
        for k in given:
            wholes[k].start()

    @pl.when(has_out)
    def _():
        for c in loaded[: depth - 1]:
            load(c).start()

    barrier = pltpu.get_barrier_semaphore()
    for i in range(1, owners):
        pl.semaphore_signal(barrier, inc=1, device_id=peer(i), device_id_type=MESH)
    pl.semaphore_signal(barrier, inc=1, device_id={"replica": inward}, device_id_type=MESH)

    @pl.when(has_out)
    def _():
        pl.semaphore_signal(barrier, inc=1, device_id={"replica": outward}, device_id_type=MESH)
        pl.semaphore_wait(barrier, owners + 1)

    @pl.when(at_end)
    def _():
        pl.semaphore_wait(barrier, owners)

    def push(group, target, c, sent, got, device):
        return remote(view(group, c), view(target, c), sent.at[c], got.at[c], {"replica": device})

    def add(target, other, c):
        k, i, start, rows = chunks[c]
        if other is None:
            more = view(own_made, c) if k in made_here else slot(c)
        else:
            more = view(other, c)
        into = view(target, c)

        def tile(t, _):
            here = pl.ds(pl.multiple_of(t * 16, 16), 16)
            into[here, :] = (into[here, :].astype(f32) + more[here, :].astype(f32)).astype(bf16)
            return 0

        lax.fori_loop(0, rows // 16, tile, 0)

    def pass_in(c, source):
        @pl.when(middle)
        def _():
            push(source, from_in, c, sent_in, got_in, inward).start()

        @pl.when(jnp.logical_not(middle))
        def _():
            push(source, from_out, c, sent_in, got_out, inward).start()

    def gather_in(c):
        @pl.when(has_out)
        def _():
            if c in loaded:
                load(c).wait()
            push(from_out, from_out, c, sent_in, got_out, inward).wait_recv()
            add(from_out, None, c)
            pass_in(c, from_out)
            if c + depth - 1 in loaded:
                load(c + depth - 1).start()

    @pl.when(at_end)
    def _():
        for c in loaded:
            if c == 0 or chunks[c][0] != chunks[c - 1][0]:
                wholes[chunks[c][0]].wait()
            pass_in(c, from_out)

    def advance():
        k = next(work)
        if k is not None:

            @pl.when(at_end)
            def _():
                for c in range(total):
                    if chunks[c][0] == k:
                        pass_in(c, own_made)

    work = beside(*side_in, *side_out, *side_scratch, *[own_made[k] for k in made_here])
    advance()

    def deliveries(c):
        k, i, start, rows = chunks[c]
        here = pl.ds(start, rows)
        first = k + kinds[:k].count("pair")
        source = view(from_in, c)
        if kinds[k] == "row":
            ends = [(source, outs[first].at[here, :])]
        elif kinds[k] == "side":
            ends = [(source, outs[first].at[place(0), here, :])]
        else:
            half = source.shape[1] // 2
            there = pl.ds(pl.multiple_of(place(0) * half, half), half)
            ends = [
                (source.at[:, pl.ds(part * half, half)], outs[first + part].at[here, there]) for part in range(2)
            ]
        if kinds[k] == "row" or i == 0:
            return [pltpu.make_async_copy(*pair, sent_x.at[c, p]) for p, pair in enumerate(ends)], False
        return [remote(*pair, sent_x.at[c, p], got_x.at[c, p], peer(i)) for p, pair in enumerate(ends)], True

    def give_back(c):
        push(from_out, from_in, c, sent_out, got_in, inward).wait_recv()

        @pl.when(middle)
        def _():
            add(from_in, from_out, c)

        @pl.when(has_out)
        def _():
            push(from_in, from_in, c, sent_out, got_in, outward).start()

        for copy in deliveries(c)[0]:
            copy.start()

    lag = 1
    for c in range(total + lag):
        for _ in range(turns.count(c)):
            advance()
        if c < total:
            gather_in(c)
        if c >= lag:
            give_back(c - lag)
    for _ in work:
        pass
    for c in range(total):
        copies, away = deliveries(c)
        for copy in copies:
            if away:
                copy.wait_recv()
                copy.wait_send()
            else:
                copy.wait()
        push(from_out, from_in, c, sent_in, got_in, inward).wait_send()

        @pl.when(has_out)
        def _():
            push(from_in, from_in, c, sent_out, got_in, outward).wait_send()


def replica_sum(arrays, kinds, made_here, identity, beside, turns, inputs, results, side_scratch):
    cuts, outs = [], []
    tall = broad = 0
    for item, kind in zip(arrays, kinds):
        lead, height, columns = item.shape
        count = pieces(height, max(16, (105 * 1024) // columns // 16 * 16))
        cuts.append((lead, count, height // count))
        tall, broad = max(tall, height // count), max(broad, columns)
        if kind == "pair":
            outs += [jax.ShapeDtypeStruct((height, lead * columns // 2), bf16)] * 2
        elif kind == "side":
            outs.append(jax.ShapeDtypeStruct(item.shape, bf16))
        else:
            outs.append(jax.ShapeDtypeStruct((height, columns), bf16))
    count = sum(lead * cut for lead, cut, _ in cuts)
    buffers = [pltpu.VMEM(item.shape, bf16) for item in arrays]
    dma = pltpu.SemaphoreType.DMA
    return pl.pallas_call(
        functools.partial(
            line_kernel, lax.axis_size("replica"), tuple(kinds), tuple(cuts), tuple(made_here), beside, turns,
            (len(inputs), len(results), len(side_scratch)),
        ),
        out_shape=tuple(outs) + tuple(jax.ShapeDtypeStruct(shape, kind) for shape, kind, _ in results),
        in_specs=[ANY] * (len(arrays) - len(made_here)) + [spec for _, spec in inputs],
        out_specs=[ANY] * len(outs) + [spec for _, _, spec in results],
        scratch_shapes=list(side_scratch)
        + buffers * 2
        + [buffers[k] for k in made_here]
        + [pltpu.VMEM((4, tall, broad), bf16), dma((len(arrays),)), dma((4,))]
        + [dma((count,))] * 4
        + [dma((count, 2))] * 2,
        compiler_params=pltpu.CompilerParams(
            collective_id=identity, has_side_effects=True, vmem_limit_bytes=62 * 2**20
        ),
        cost_estimate=pl.CostEstimate(flops=10**6, bytes_accessed=200 * 2**20, transcendentals=0),
    )(*[item for k, item in enumerate(arrays) if k not in made_here], *[item for item, _ in inputs])


def finish_pair_kernel(gain_ref, a_ref, b_ref, wa_ref, wb_ref, outa_ref, outb_ref, grad_ref):
    gain = low(gain_ref[:, 1:2])
    grad = jnp.zeros(gain.shape, f32)
    for sum_ref, weight_ref, out_ref in ((a_ref, wa_ref, outa_ref), (b_ref, wb_ref, outb_ref)):
        total = sum_ref[...].astype(f32)
        out_ref[...] = total * gain
        grad = grad + jnp.sum(total * low(weight_ref[...]), axis=1, keepdims=True)
    grad_ref[...] = grad


def finish_pair(gain, a, b, wa, wb):
    rows, columns = wa.shape
    cut = min(rows, 64)
    wide = pl.BlockSpec((cut, columns), lambda i: (i, 0))
    thin = pl.BlockSpec((cut, 1), lambda i: (i, 0))
    out = jax.ShapeDtypeStruct((rows, columns), f32)
    return pl.pallas_call(
        finish_pair_kernel,
        grid=(rows // cut,),
        out_shape=(out, out, jax.ShapeDtypeStruct((rows, 1), f32)),
        in_specs=[pl.BlockSpec((cut, 2), lambda i: (i, 0)), wide, wide, wide, wide],
        out_specs=[wide, wide, thin],
        compiler_params=pltpu.CompilerParams(vmem_limit_bytes=62 * 2**20),
        cost_estimate=pl.CostEstimate(flops=6 * rows * columns, bytes_accessed=20 * rows * columns, transcendentals=0),
    )(gain, a, b, wa, wb)


def finish_rest_kernel(gain_ref, mix_ref, wa_ref, wb_ref, out_sum_ref, down_sum_ref, outa_ref, outb_ref, grad_ref, out_ref, down_ref):
    owners = mix_ref.shape[0]
    width = wa_ref.shape[1] // owners
    gain = low(gain_ref[:, 0:1])
    grad = jnp.zeros(gain.shape, f32)
    for part, (weight_ref, target_ref) in enumerate(((wa_ref, outa_ref), (wb_ref, outb_ref))):
        total = jnp.concatenate(
            [mix_ref[j, :, part * width : (part + 1) * width].astype(f32) for j in range(owners)], axis=1
        )
        target_ref[...] = total * gain
        grad = grad + jnp.sum(total * low(weight_ref[...]), axis=1, keepdims=True)
    grad_ref[...] = grad
    out_ref[...] = out_sum_ref[...].astype(f32)
    down_ref[...] = down_sum_ref[...].astype(f32)


def finish_rest(gain, mix, wa, wb, out_sum, down_sum):
    rows, columns = wa.shape
    steps = 4
    while out_sum.shape[0] % (16 * steps) or down_sum.shape[0] % (16 * steps) or rows % (16 * steps):
        steps //= 2

    def tall(item):
        return pl.BlockSpec((item.shape[0] // steps, item.shape[1]), lambda i: (i, 0))

    owners, _, both = mix.shape
    wide, thin = tall(wa), pl.BlockSpec((rows // steps, 1), lambda i: (i, 0))
    return pl.pallas_call(
        finish_rest_kernel,
        grid=(steps,),
        out_shape=(
            jax.ShapeDtypeStruct(wa.shape, f32),
            jax.ShapeDtypeStruct(wa.shape, f32),
            jax.ShapeDtypeStruct((rows, 1), f32),
            jax.ShapeDtypeStruct(out_sum.shape, f32),
            jax.ShapeDtypeStruct(down_sum.shape, f32),
        ),
        in_specs=[
            tall(gain),
            pl.BlockSpec((owners, rows // steps, both), lambda i: (0, i, 0)),
            wide,
            wide,
            tall(out_sum),
            tall(down_sum),
        ],
        out_specs=[wide, wide, thin, tall(out_sum), tall(down_sum)],
        compiler_params=pltpu.CompilerParams(vmem_limit_bytes=62 * 2**20),
        cost_estimate=pl.CostEstimate(flops=10**7, bytes_accessed=40 * 2**20, transcendentals=0),
    )(gain, mix, wa, wb, out_sum, down_sum)


def body(
    tokens,
    segments,
    cotangent,
    norm_gain,
    branch_weight,
    input_weight,
    conv_weight,
    conv_bias,
    recur_gate_weight,
    recur_gate_bias,
    input_gate_weight,
    input_gate_bias,
    decay_param,
    output_weight,
    mlp_norm_gain,
    gate_weight,
    up_weight,
    down_weight,
):
    x, cot = tokens[0], cotangent[0]
    rows, depth = x.shape
    members = lax.axis_size(GROUP)
    sequences = lax.axis_size("shard")
    total = members * rows
    gains = jnp.stack([norm_gain, mlp_norm_gain], 1)
    own_labels = jnp.broadcast_to(segments[0].astype(bf16)[:, None], (rows, 128))
    width = branch_weight.shape[1] // members
    decay_f = low(decay_param)
    small = (
        conv_weight, conv_bias, recur_gate_bias, input_gate_bias, jax.nn.softplus(-decay_f),
    )
    (
        unit_all, labels, out_low, product, *mixed, mix_w, output_w, unit_two, middle, pair_w, down_w,
    ) = front(
        sequences, x, own_labels, cot, gains, small,
        recur_gate_weight, input_gate_weight, branch_weight, input_weight, gate_weight, up_weight, output_weight,
        down_weight,
    )
    pair_w = pair_w.reshape(depth, -1)
    whole = ((total, depth), bf16)
    hidden, partial, down_partial, pair_partial = mlp(unit_two, out_low, pair_w, down_w)
    down_partial = down_partial[None]
    pair_partial = pair_partial.reshape(members, -1, pair_w.shape[1])
    kept = (output_w, mix_w, *mixed)
    narrow = ((total, width), bf16)
    vm, dma = pltpu.VMEM, pltpu.SemaphoreType.DMA
    length = total // sequences
    back = replica_sum(
        [down_partial, pair_partial], ["row", "pair"], (), 3,
        functools.partial(turn_steps, sequences, length),
        (6, 9, 12) + tuple(range(14, 14 + 2 * sequences + 2)),
        [(partial, ANY)] + [(item, VM) for item in (middle, cot, labels, *small, recur_gate_weight, input_gate_weight)]
        + [(item, ANY) for item in kept],
        [whole + (ANY,), ((rows, depth), f32, ANY), whole + (ANY,), narrow + (ANY,), narrow + (ANY,)]
        + [(conv_weight.shape, f32, VM), ((4, width), f32, VM), (recur_gate_weight.shape, f32, VM), (input_gate_weight.shape, f32, VM)],
        plane_scratch(rows, depth, 1, 1)
        + [vm(item.shape, item.dtype) for item in kept]
        + [vm(*whole), vm(*whole), vm((rows, depth), f32), vm(*narrow), vm(*narrow), vm(mixed[-1].shape, f32)]
        + [vm((8 + length, width), f32), vm((8 + length, 128), f32)]
        + [vm((width, width), f32)] * 4
        + [vm((8, width), f32)] * 2
        + [dma((10,)), dma((5,))],
    )
    down_sum, gate_sum, up_sum, mid_low, middle_grad, partial, branch_low, conv_low = back[:8]
    conv_weight_grad, sums, recur_weight_grad, inject_weight_grad = back[8:]
    gate_grad, up_grad, mlp_gain_grad = finish_pair(gains, gate_sum, up_sum, gate_weight, up_weight)
    size = recur_gate_weight.shape[1]
    gates = jnp.concatenate([recur_weight_grad, inject_weight_grad], 2).reshape(width, 2 * size)
    lanes = -(-max(width, 2 * size) // 128) * 128
    lines = jnp.concatenate([conv_weight_grad, sums], 0)
    packed = jnp.concatenate(
        [
            jnp.pad(gates, ((0, 0), (0, lanes - 2 * size))),
            jnp.pad(lines, ((0, 16 - lines.shape[0]), (0, lanes - width))),
        ],
        0,
    ).astype(bf16)[None]
    both = -(-2 * width // 128) * 128
    mix_shape = jax.ShapeDtypeStruct((members, depth // members, both), bf16)
    output_shape = jax.ShapeDtypeStruct((1,) + output_w.shape, bf16)
    again = plane_scratch(rows, depth, 0, 1)
    packed, output_sum, mix_sum, tokens_grad, block_out = replica_sum(
        [packed, output_shape, mix_shape], ["row", "row", "side"], (1, 2), 4, functools.partial(end_steps, 1, 2),
        (0, 1, 2, 3, 4, 7, 8, 9, 10, 11, 12, 19),
        [(partial, ANY), (middle_grad, VM), (x, VM), (middle, VM)]
        + [(item, ANY) for item in (hidden, down_w, product, mid_low, unit_all, branch_low, conv_low)],
        [((rows, depth), bf16, VM), ((rows, depth), bf16, VM)],
        again + again[3:] + again[:2] + [vm(*whole), vm(hidden.shape, bf16), vm(down_w.shape, bf16)]
        + [vm(*narrow), vm(*whole), vm(*narrow), vm(*narrow), vm((total, both), bf16), dma((8,))],
    )
    packed = packed.astype(f32)
    branch_grad, input_grad, gain_grad, output_grad, down_grad = finish_rest(
        gains, mix_sum, branch_weight, input_weight, output_sum, down_sum
    )
    recur_weight_grad = packed[:width, :size].reshape(-1, size, size)
    inject_weight_grad = packed[:width, size : 2 * size].reshape(-1, size, size)
    conv_weight_grad = packed[width : width + conv_weight.shape[0], :width]
    conv_bias_grad, recur_bias_grad, inject_bias_grad, rate_grad = [packed[width + conv_weight.shape[0] + i, :width] for i in range(4)]
    decay_param_grad = rate_grad * decay_scale * jax.nn.sigmoid(-decay_f)
    return (
        block_out[None],
        tokens_grad[None],
        gain_grad[:, 0],
        branch_grad,
        input_grad,
        conv_weight_grad,
        conv_bias_grad,
        recur_weight_grad,
        recur_bias_grad,
        inject_weight_grad,
        inject_bias_grad,
        decay_param_grad,
        output_grad,
        mlp_gain_grad[:, 0],
        gate_grad,
        up_grad,
        down_grad,
    )


def solution(mesh):
    row3 = P(("shard", "replica"), "seq", None)
    vec = P(("seq", "shard"))
    mat = P(("seq", "shard"), None)
    cube = P(("seq", "shard"), None, None)
    taps = P(None, ("seq", "shard"))
    params = (vec, mat, mat, taps, vec, cube, vec, cube, vec, vec, mat, vec, mat, mat, mat)
    in_specs = (row3, P(("shard", "replica"), "seq"), row3) + params
    out_specs = (row3, row3) + params
    return jax.shard_map(body, mesh=mesh, in_specs=in_specs, out_specs=out_specs, check_vma=False)
```

```python
import functools

import jax
import jax.numpy as jnp
from jax import lax
from jax.experimental import pallas as pl
from jax.experimental.pallas import tpu as pltpu
from jax.sharding import PartitionSpec as P

epsilon = 1e-06
decay_scale = 8.0
GROUP = ("seq", "shard")
ROWS = ("shard", "seq")
f32 = jnp.float32
bf16 = jnp.bfloat16
VM = pl.BlockSpec(memory_space=pltpu.VMEM)
ANY = pl.BlockSpec(memory_space=pl.ANY)
MESH = pl.DeviceIdType.MESH


def mm(left, right):
    return jnp.dot(left, right, preferred_element_type=f32)


def mm_nt(left, right):
    return lax.dot_general(left, right, (((1,), (1,)), ((), ())), preferred_element_type=f32)


def mm_tn(left, right):
    return lax.dot_general(left, right, (((0,), (0,)), ((), ())), preferred_element_type=f32)


def low(item):
    return item.astype(bf16).astype(f32)


def by_owner(weight, gain):
    owners = lax.axis_size(GROUP)
    scaled = (low(weight) * gain).astype(bf16)
    return jnp.swapaxes(scaled.reshape(weight.shape[0], owners, -1), 0, 1)


def swap(cut):
    return lax.all_to_all(cut, GROUP, split_axis=0, concat_axis=0, tiled=True)


def gelu_parts(x):
    inner = 0.7978845608028654 * (x + 0.044715 * x * x * x)
    t = jnp.tanh(inner)
    value = 0.5 * x * (1.0 + t)
    slope = 0.5 * (1.0 + t) + 0.5 * x * (1.0 - t * t) * 0.7978845608028654 * (
        1.0 + 3.0 * 0.044715 * x * x
    )
    return value, slope


def minus_expm1(y):
    poly = 1.0 + y * (1.0 / 8.0)
    for order in (7.0, 6.0, 5.0, 4.0, 3.0, 2.0):
        poly = 1.0 + y * (1.0 / order) * poly
    return jnp.where(y > -0.5, -y * poly, 1.0 - jnp.exp(y))


def dot_nn(a, b):
    return lax.dot_general(a, b, (((1,), (0,)), ((), ())), preferred_element_type=f32)


def dot_nt(a, b):
    return lax.dot_general(a, b, (((1,), (1,)), ((), ())), preferred_element_type=f32)


def dot_tn(a, b):
    return lax.dot_general(a, b, (((0,), (0,)), ((), ())), preferred_element_type=f32)


def whole_weight(ref, part):
    owners, _, rows, width = ref.shape
    return ref[:, part].reshape(owners * rows, width)


def fill_blocks(target, source):
    target[...] = jnp.zeros_like(target)
    count, size = source.shape[0], source.shape[1]
    for h in range(count):
        target[h * size : (h + 1) * size, h * size : (h + 1) * size] = source[h].astype(bf16).astype(f32)


def put_tiles(ref, here, value):
    width = value.shape[1]
    for tile in range(ref.shape[0]):
        lanes = min(128, width - 128 * tile)
        ref[tile, here, 0:lanes] = value[:, 128 * tile : 128 * tile + lanes]


def get_tiles(ref, here, width):
    parts = [ref[tile, here, 0 : min(128, width - 128 * tile)] for tile in range(ref.shape[0])]
    return jnp.concatenate(parts, axis=1)


def clear_tail(ref, width):
    tail = ref.shape[0] * 128 - width
    if tail:
        ref[ref.shape[0] - 1, :, 128 - tail :] = jnp.zeros((ref.shape[1], tail), f32)


def fill_small(conv, bias, raw_conv, raw_a, raw_b, raw_c, rate):
    conv[0 : raw_conv.shape[0], :] = low(raw_conv[...])
    for row, ref in enumerate((raw_a, raw_b, raw_c)):
        bias[row : row + 1, :] = low(ref[...])[None, :]
    bias[3:4, :] = rate[...][None, :]


def label_masks(label_ref, here, length, width, taps, lines):
    own = label_ref[here, :].astype(f32)
    lines[0:8, :] = jnp.full((8, 128), -1.0, f32)
    lines[8 : 8 + length, :] = own
    masks = []
    for k in range(1, taps):
        same = jnp.where(lines[8 - k : 8 - k + length, :] == own, 1.0, 0.0)
        masks.append(jnp.concatenate([same] * -(-width // 128), axis=1)[:, :width])
    return masks


def seq_scan(decay_ref, value_ref, sequences, length, reverse):
    tiles = decay_ref.shape[0]
    unroll = 8

    def step(i, states):
        states = list(states)
        for j in range(unroll):
            at = i * unroll + j
            if reverse:
                at = length - 1 - at
            here = pl.ds(at, sequences, stride=length)
            for tile in range(tiles):
                value = value_ref[tile, here, :]
                decay = decay_ref[tile, here, :]
                if reverse:
                    new = value + states[tile]
                    value_ref[tile, here, :] = new
                    states[tile] = decay * new
                else:
                    states[tile] = value + decay * states[tile]
                    value_ref[tile, here, :] = states[tile]
        return tuple(states)

    lax.fori_loop(0, length // unroll, step, (jnp.zeros((sequences, 128), f32),) * tiles)


def plane():
    halves, shards = lax.axis_size("seq"), lax.axis_size("shard")
    y, s = lax.axis_index("seq"), lax.axis_index("shard")
    offsets = [(dy, ds) for ds in range(0, shards, 2) for dy in range(halves)]

    def at(dy, ds):
        return {"seq": jnp.bitwise_xor(y, dy), "shard": jnp.bitwise_xor(s, ds)}

    def block(dy, ds):
        return jnp.bitwise_xor(s, ds) * halves + jnp.bitwise_xor(y, dy)

    return offsets, at, block


def remote(src, dst, sent, got, device):
    return pltpu.make_async_remote_copy(
        src_ref=src, dst_ref=dst, send_sem=sent, recv_sem=got, device_id=device, device_id_type=MESH
    )


def row_block(ref, index, rows):
    return ref.at[pl.ds(pl.multiple_of(index * rows, rows), rows), :]


def scatter_steps(rows, partial, near, far, acc, sems):
    offsets, at, block = plane()
    near_sent, near_got, far_sent, far_got = sems
    count = len(offsets)
    order = list(range(count - 1, -1, -1))
    firsts = {}
    for q in order:
        dy, ds = offsets[q]
        firsts[q] = remote(
            row_block(partial, block(dy, ds ^ 1), rows), near.at[q], near_sent.at[q], near_got.at[q], at(0, 1)
        )
        firsts[q].start()
    seconds = {}
    for q in order:
        dy, ds = offsets[q]
        firsts[q].wait_recv()
        base = block(dy, ds) * rows

        def tile(i, _):
            step = pl.multiple_of(i * 16, 16)
            here = pl.ds(step, 16)
            total = partial[pl.ds(pl.multiple_of(base + step, 16), 16), :].astype(f32) + near[q, here, :].astype(f32)
            if q:
                near[q, here, :] = total.astype(bf16)
            else:
                acc[here, :] = total
            return 0

        lax.fori_loop(0, rows // 16, tile, 0)
        if q:
            seconds[q] = remote(near.at[q], far.at[q - 1], far_sent.at[q - 1], far_got.at[q - 1], at(dy, ds))
            seconds[q].start()
    yield None
    for q in order[:-1]:
        seconds[q].wait_recv()

        def more(i, _):
            here = pl.ds(pl.multiple_of(i * 16, 16), 16)
            acc[here, :] += far[q - 1, here, :].astype(f32)
            return 0

        lax.fori_loop(0, rows // 16, more, 0)
    yield [firsts[q].wait_send for q in order] + [seconds[q].wait_send for q in order[:-1]]


def gather_steps(rows, whole, sems):
    offsets, at, block = plane()
    near_sent, near_got, far_sent, far_got = sems
    count = len(offsets)
    half = rows // 2

    def piece(q, part):
        start = pl.multiple_of(block(*offsets[q]) * rows + part * half, 16)
        return whole.at[pl.ds(start, half), :]

    own = row_block(whole, block(0, 0), rows)
    straight = [q for q in range(1, count) if offsets[q][0] == 0 or offsets[q][1] == 0]
    across = [q for q in range(1, count) if q not in straight]
    upright = [q for q in straight if offsets[q][0]]
    sends, arrivals = [], []
    outs = {}
    for q in straight:
        outs[q] = remote(own, own, far_sent.at[q], far_got.at[q], at(*offsets[q]))
        outs[q].start()
        sends.append(outs[q].wait_send)

    def hand(q, part=None):
        source = row_block(whole, block(*offsets[q]), rows) if part is None else piece(q, part)
        place = q if part is None or part == 0 else count + q
        copy = remote(source, source, near_sent.at[place], near_got.at[place], at(0, 1))
        copy.start()
        sends.append(copy.wait_send)
        arrivals.append(copy.wait_recv)

    hand(0)
    yield None
    onward = {}
    for q in straight:
        outs[q].wait_recv()
        if q in upright:
            targets = [(1, t) for t in straight if t not in upright]
        else:
            targets = [(0, t) for t in upright]
        for part, t in targets:
            dy, ds = offsets[q][0] | offsets[t][0], offsets[q][1] | offsets[t][1]
            a = offsets.index((dy, ds))
            source = piece(q, part)
            onward[a, part] = remote(source, source, far_sent.at[part * count + a], far_got.at[part * count + a], at(*offsets[t]))
            onward[a, part].start()
            sends.append(onward[a, part].wait_send)
        hand(q)
    yield None
    for a in across:
        for part in range(2):
            onward[a, part].wait_recv()
            hand(a, part)
    yield arrivals + sends


def root_mean(rows):
    return lax.rsqrt(jnp.mean(rows * rows, axis=-1, keepdims=True) + epsilon)


def norm_backward(grad_unit, unit, inverse):
    return inverse * (grad_unit - unit * jnp.mean(grad_unit * unit, axis=-1, keepdims=True))


def by_tiles(rows, work):
    def tile(i, _):
        work(pl.ds(pl.multiple_of(i * 16, 16), 16), i)
        return 0

    lax.fori_loop(0, rows // 16, tile, 0)


def plane_scratch(rows, depth, gathers, scatters):
    count = lax.axis_size("seq") * lax.axis_size("shard") // 2
    block = (rows, depth)
    scratch = []
    if scatters:
        scratch = [
            pltpu.VMEM((count,) + block, bf16),
            pltpu.VMEM((count - 1,) + block, bf16),
            pltpu.VMEM(block, f32),
        ]
    dma = pltpu.SemaphoreType.DMA
    for _ in range(scatters):
        scratch += [dma((count,))] * 2 + [dma((count - 1,))] * 2
    for _ in range(gathers):
        scratch += [dma((2 * count,))] * 4
    return scratch


def cut_columns(weight_ref, gain, target, start, lanes):
    owners = weight_ref.shape[1] // lanes

    def tile(i, _):
        step = pl.multiple_of(i * 16, 16)
        here = pl.ds(step, 16)
        scaled = low(weight_ref[here, :]) * gain(step)
        for j in range(owners):
            target(j)[here, start : start + lanes] = scaled[:, j * lanes : (j + 1) * lanes].astype(bf16)
        return 0

    lax.fori_loop(0, weight_ref.shape[0] // 16, tile, 0)


def quarter_steps(n, part, whole, sems):
    me = lax.axis_index("replica")
    right_sent, right_got, left_sent, left_got = sems

    def rows(q):
        return whole.at[:, pl.ds(pl.multiple_of(q * part, 16), part), :]

    def to_right(hop):
        block = rows(me - hop)
        return remote(block, block, right_sent.at[hop], right_got.at[hop], {"replica": me + 1})

    def to_left(hop):
        block = rows(me + hop)
        return remote(block, block, left_sent.at[hop], left_got.at[hop], {"replica": me - 1})

    def from_left(hop):
        block = rows(me - hop - 1)
        return remote(block, block, right_sent.at[hop], right_got.at[hop], {"replica": me + 1})

    def from_right(hop):
        block = rows(me + hop + 1)
        return remote(block, block, left_sent.at[hop], left_got.at[hop], {"replica": me - 1})

    for hop in range(n - 1):
        if hop:

            @pl.when(me >= hop)
            def _():
                from_left(hop - 1).wait_recv()

            @pl.when(me + hop < n)
            def _():
                from_right(hop - 1).wait_recv()

        @pl.when(jnp.logical_and(me >= hop, me < n - 1))
        def _():
            to_right(hop).start()

        @pl.when(jnp.logical_and(me + hop < n, me > 0))
        def _():
            to_left(hop).start()

        yield

    @pl.when(me >= n - 1)
    def _():
        from_left(n - 2).wait_recv()

    @pl.when(me + n - 1 < n)
    def _():
        from_right(n - 2).wait_recv()

    for hop in range(n - 1):

        @pl.when(jnp.logical_and(me >= hop, me < n - 1))
        def _():
            to_right(hop).wait_send()

        @pl.when(jnp.logical_and(me + hop < n, me > 0))
        def _():
            to_left(hop).wait_send()

    yield


def front_kernel(
    n, sequences, length,
    x_ref, label_ref, cot_ref, gains_ref, raw_conv, raw_a, raw_b, raw_c, rate_ref, rw_ref, iw_ref,
    branch_hbm, input_hbm, gate_hbm, up_hbm, ow_hbm, down_hbm,
    unit_out, labels_out, low_out, product_out, pre_out, conv_in_out, values_out, recur_out, inject_out, decay_out,
    states_out, mix_out, ow_out, two_out, middle_out, pair_out, down_out,
    unit_ref, labels_ref, product_ref, pre_ref, conv_in_ref, values_ref, recur_ref, inject_ref, decay_ref,
    states_ref, mix_ref, ow_ref, two_ref, middle_ref,
    wide, tall, ow_f, mix_cut, pair_cut, pad, lines, rbig, ibig, partial, conv_ref, bias_ref, down_f, down_low,
    near, far, acc, *sems,
):
    rows = x_ref.shape[0]
    scatter_sems, sems = sems[:4], sems[4:]
    unit_sems, label_sems, low_sems, two_sems, sems = sems[:4], sems[4:8], sems[8:12], sems[12:16], sems[16:]
    load_sem, save_sem, mix_sent, mix_got, pair_sent, pair_got, down_sem = sems[:7]
    line_sems = sems[7:]
    offsets, at, block = plane()
    z = lax.axis_index("replica")
    y, s = lax.axis_index("seq"), lax.axis_index("shard")
    shards = lax.axis_size("shard")
    owners = shards * lax.axis_size("seq")
    part = gate_hbm.shape[0] // n
    width = pad.shape[1]
    ff = gate_hbm.shape[1] // owners

    def peer(i):
        return {"seq": jnp.bitwise_xor(y, i // shards), "shard": jnp.bitwise_xor(s, i % shards)}

    def place(i):
        return jnp.bitwise_xor(y, i // shards) * shards + jnp.bitwise_xor(s, i % shards)

    own_rows = pl.ds(pl.multiple_of(z * part, 16), part)
    loads = [
        pltpu.make_async_copy(gate_hbm.at[own_rows, :], tall.at[0], load_sem.at[0]),
        pltpu.make_async_copy(up_hbm.at[own_rows, :], tall.at[1], load_sem.at[1]),
        pltpu.make_async_copy(branch_hbm, wide.at[0], load_sem.at[2]),
        pltpu.make_async_copy(input_hbm, wide.at[1], load_sem.at[3]),
        pltpu.make_async_copy(ow_hbm, ow_f, load_sem.at[4]),
    ]
    for load in loads:
        load.start()
    saves = []

    def save(source, target):
        copy = pltpu.make_async_copy(source, target, save_sem.at[len(saves)])
        copy.start()
        saves.append(copy)

    low_own = pltpu.make_async_copy(cot_ref, row_block(low_out, block(0, 0), rows), load_sem.at[5])
    low_own.start()
    barrier = pltpu.get_barrier_semaphore()
    for i in range(1, owners):
        pl.semaphore_signal(barrier, inc=1, device_id=peer(i), device_id_type=MESH)

    @pl.when(z > 0)
    def _():
        pl.semaphore_signal(barrier, inc=1, device_id={"replica": z - 1}, device_id_type=MESH)

    @pl.when(z < n - 1)
    def _():
        pl.semaphore_signal(barrier, inc=1, device_id={"replica": z + 1}, device_id_type=MESH)

    for side in range(2):
        loads[side].wait()

        cut_columns(
            tall.at[side],
            lambda step: low(gains_ref[pl.ds(pl.multiple_of(z * part + step, 16), 16), 1:2]),
            lambda j: pair_cut.at[j],
            side * ff,
            ff,
        )

    inside_line = jnp.logical_and(z > 0, z < n - 1)

    @pl.when(inside_line)
    def _():
        pl.semaphore_wait(barrier, owners + 1)

    @pl.when(jnp.logical_not(inside_line))
    def _():
        pl.semaphore_wait(barrier, owners)

    me = place(0)
    pair_there = pair_out.at[me, own_rows, :]
    pair_moves = [
        remote(pair_cut.at[place(i)], pair_there, pair_sent.at[i], pair_got.at[i], peer(i)) for i in range(1, owners)
    ]
    for move in pair_moves:
        move.start()
    pair_own = pltpu.make_async_copy(pair_cut.at[me], pair_there, pair_sent.at[0])
    pair_own.start()

    base = block(0, 0) * rows

    def unit(here, i):
        value = x_ref[here, :].astype(f32)
        there = pl.ds(pl.multiple_of(base + i * 16, 16), 16)
        unit_ref[there, :] = (value * root_mean(value)).astype(bf16)
        labels_ref[there, :] = label_ref[here, :]

    by_tiles(rows, unit)
    label_gather = gather_steps(rows, labels_ref, label_sems)
    unit_gather = gather_steps(rows, unit_ref, unit_sems)
    next(label_gather)
    next(unit_gather)

    for side in range(2):
        loads[2 + side].wait()
        cut_columns(
            wide.at[side], lambda step: low(gains_ref[pl.ds(step, 16), 0:1]), lambda j: mix_cut.at[j, side], 0, width
        )
    mix_moves = [
        remote(mix_cut.at[place(i)], mix_ref.at[me], mix_sent.at[i], mix_got.at[i], peer(i)) for i in range(1, owners)
    ]
    for move in mix_moves:
        move.start()
    mix_own = pltpu.make_async_copy(mix_cut.at[me], mix_ref.at[me], mix_sent.at[0])
    mix_own.start()
    loads[4].wait()
    ow_ref[...] = ow_f[...].astype(bf16)
    save(ow_ref, ow_out)
    fill_small(conv_ref, bias_ref, raw_conv, raw_a, raw_b, raw_c, rate_ref)
    fill_blocks(rbig, rw_ref)
    fill_blocks(ibig, iw_ref)
    pad[0:8, :] = jnp.zeros((8, width), f32)
    taps = raw_conv.shape[0]
    clear_tail(decay_ref, width)
    clear_tail(states_ref, width)

    cuts = down_hbm.shape[0] // down_low.shape[1]
    height = down_low.shape[1]

    def down_load(k):
        return pltpu.make_async_copy(down_hbm.at[pl.ds(k * height, height), :], down_f.at[k % 2], down_sem.at[k % 2])

    def down_save(k):
        return pltpu.make_async_copy(down_low.at[k % 2], down_out.at[pl.ds(k * height, height), :], down_sem.at[2 + k % 2])

    def down_cast(k):
        down_load(k).wait()
        if k >= 2:
            down_save(k - 2).wait()
        down_low[k % 2] = down_f[k % 2].astype(bf16)
        down_save(k).start()
        if k + 2 < cuts:
            down_load(k + 2).start()

    pair_own.wait()
    for move in pair_moves:
        move.wait_recv()
    line = quarter_steps(n, part, pair_out, line_sems)
    next(line)
    next(label_gather)
    next(unit_gather)
    waits = next(label_gather) + next(unit_gather)
    for wait in waits:
        wait()
    mix_own.wait()
    for move in mix_moves:
        move.wait_recv()
    save(unit_ref, unit_out)
    save(labels_ref, labels_out)
    save(mix_ref, mix_out)

    low_own.wait()
    low_gather = gather_steps(rows, low_out, low_sems)
    next(low_gather)
    next(line)

    def one(q, _):
        here = pl.ds(pl.multiple_of(q * length, length), length)
        sequence = unit_ref[here, :]
        masks = label_masks(labels_ref, here, length, width, taps, lines)
        pre_ref[here, :] = dot_nn(sequence, whole_weight(mix_ref, 0))
        conv_in = dot_nn(sequence, whole_weight(mix_ref, 1)).astype(bf16)
        conv_in_ref[here, :] = conv_in
        pad[8 : 8 + length, :] = conv_in.astype(f32)
        total = bias_ref[0:1, :] + conv_ref[0:1, :] * pad[8 : 8 + length, :]
        for k in range(1, taps):
            total = total + conv_ref[k : k + 1, :] * pad[8 - k : 8 - k + length, :] * masks[k - 1]
        values = total.astype(bf16)
        values_ref[here, :] = values
        recur = jax.nn.sigmoid(dot_nn(values, rbig[...].astype(bf16)) + bias_ref[1:2, :])
        inject = jax.nn.sigmoid(dot_nn(values, ibig[...].astype(bf16)) + bias_ref[2:3, :])
        recur_ref[here, :] = recur
        inject_ref[here, :] = inject
        log_decay = -decay_scale * bias_ref[3:4, :] * recur
        inside = masks[0] > 0.5
        put_tiles(decay_ref, here, jnp.where(inside, jnp.exp(log_decay), 0.0))
        scale = jnp.where(inside, jnp.sqrt(minus_expm1(2.0 * log_decay)), 1.0)
        put_tiles(states_ref, here, scale * inject * values.astype(f32))
        return 0

    lax.fori_loop(0, sequences, one, 0)
    seq_scan(decay_ref, states_ref, sequences, length, False)

    def two(q, _):
        here = pl.ds(pl.multiple_of(q * length, length), length)
        act, _unused = gelu_parts(pre_ref[here, :])
        product = (act * get_tiles(states_ref, here, width)).astype(bf16)
        product_ref[here, :] = product
        partial[here, :] = dot_nn(product, ow_ref[...]).astype(bf16)
        return 0

    for k in range(2):
        down_load(k).start()
    lax.fori_loop(0, sequences, two, 0)
    scatter = scatter_steps(rows, partial, near, far, acc, scatter_sems)
    next(scatter)
    for source, target in (
        (product_ref, product_out), (pre_ref, pre_out), (conv_in_ref, conv_in_out), (values_ref, values_out),
        (recur_ref, recur_out), (inject_ref, inject_out), (decay_ref, decay_out), (states_ref, states_out),
    ):
        save(source, target)
    next(line)
    for k in range(cuts):
        down_cast(k)
    for k in range(cuts - 2, cuts):
        down_save(k).wait()
    next(low_gather)
    waits = next(low_gather) + next(scatter)

    def norm(here, i):
        middle = x_ref[here, :].astype(f32) + acc[here, :]
        middle_ref[here, :] = middle
        there = pl.ds(pl.multiple_of(base + i * 16, 16), 16)
        two_ref[there, :] = (middle * root_mean(middle)).astype(bf16)

    by_tiles(rows, norm)
    two_gather = gather_steps(rows, two_ref, two_sems)
    next(two_gather)
    save(middle_ref, middle_out)
    for _ in range(n - 4):
        next(line)
    for wait in waits:
        wait()
    next(two_gather)
    for wait in next(two_gather):
        wait()
    save(two_ref, two_out)
    for _ in line:
        pass
    for move in pair_moves + mix_moves:
        move.wait_send()
    for copy in saves:
        copy.wait()


def front(sequences, x, label, cot, gains, small, rw, iw, branch_w, input_w, gate_w, up_w, output_w, down_w):
    rows, depth = x.shape
    own, n = branch_w.shape[0], lax.axis_size("replica")
    owners = lax.axis_size(GROUP)
    total, width, ff = owners * rows, branch_w.shape[1] // owners, gate_w.shape[1] // owners
    part = own // n
    length = total // sequences
    tiles = -(-width // 128)
    kept = [
        ((total, depth), bf16), ((total, 128), bf16), ((total, depth), bf16), ((total, width), bf16),
        ((total, width), f32), ((total, width), bf16), ((total, width), bf16), ((total, width), f32),
        ((total, width), f32), ((tiles, total, 128), f32), ((tiles, total, 128), f32), ((owners, 2, own, width), bf16),
        ((width, depth), bf16), ((total, depth), bf16), ((rows, depth), f32),
    ]
    vm = pltpu.VMEM
    dma = pltpu.SemaphoreType.DMA
    scratch = [vm(*item) for k, item in enumerate(kept) if k != 2] + [
        vm((2,) + branch_w.shape, f32),
        vm((2, part, gate_w.shape[1]), f32),
        vm(output_w.shape, f32),
        vm((owners, 2, own, width), bf16),
        vm((owners, part, 2 * ff), bf16),
        vm((8 + length, width), f32),
        vm((8 + length, 128), f32),
        vm((width, width), f32),
        vm((width, width), f32),
        vm((total, depth), bf16),
        vm((8, width), f32),
        vm((8, width), f32),
        vm((2, down_w.shape[0] // 8, depth), f32),
        vm((2, down_w.shape[0] // 8, depth), bf16),
    ]
    scratch += plane_scratch(rows, depth, 4, 1)
    scratch += [dma((6,)), dma((len(kept),))] + [dma((owners,))] * 4 + [dma((4,))] + [dma((n - 1,))] * 4
    outs = kept + [((owners, own, 2 * ff), bf16), (down_w.shape, bf16)]
    return pl.pallas_call(
        functools.partial(front_kernel, n, sequences, length),
        out_shape=tuple(jax.ShapeDtypeStruct(*item) for item in outs),
        in_specs=[VM] * 11 + [ANY] * 6,
        out_specs=[ANY] * len(outs),
        scratch_shapes=scratch,
        compiler_params=pltpu.CompilerParams(
            collective_id=1, has_side_effects=True, vmem_limit_bytes=62 * 2**20
        ),
        cost_estimate=pl.CostEstimate(flops=10**6, bytes_accessed=200 * 2**20, transcendentals=0),
    )(x, label, cot, gains, *small, rw, iw, branch_w, input_w, gate_w, up_w, output_w, down_w)


def turn_steps(
    sequences, length,
    partial_hbm, middle_ref, cot_ref, label_ref, raw_conv, raw_a, raw_b, raw_c, rate_ref, rw_ref, iw_ref, *rest,
):
    kept_hbm, rest = rest[:9], rest[9:]
    low_out, grad_out, partial_out, branch_low_out, conv_low_out, packed_ref = rest[:6]
    scatter_sems, gather_sems = rest[6 + 3 : 6 + 7], rest[6 + 7 : 6 + 11]
    near, far, acc = rest[6:9]
    rest = rest[17:]
    kept, rest = rest[:9], rest[9:]
    ow_ref, w_ref, pre_ref, conv_in_ref, values_ref, recur_ref, inject_ref, decay_ref, states_ref = kept
    partial, low_ref, grad_ref, branch_low_ref, conv_low_ref, adj, pad, lines, rbig, ibig, dr, di, conv_ref, bias_ref, dconv_ref, sums_ref, load_sem, save_sem = rest
    rows = middle_ref.shape[0]
    offsets, at, block = plane()
    first = pltpu.make_async_copy(partial_hbm, partial, load_sem.at[9])
    first.start()
    loads = [pltpu.make_async_copy(kept_hbm[k], kept[k], load_sem.at[k]) for k in range(9)]
    for load in loads:
        load.start()
    first.wait()
    scatter = scatter_steps(rows, partial, near, far, acc, scatter_sems)
    next(scatter)
    yield
    waits = next(scatter)
    base = block(0, 0) * rows

    def norm(here, i):
        middle = middle_ref[here, :]
        inverse = root_mean(middle)
        grad = cot_ref[here, :].astype(f32) + norm_backward(acc[here, :], middle * inverse, inverse)
        grad_ref[here, :] = grad
        there = pl.ds(pl.multiple_of(base + i * 16, 16), 16)
        low_ref[there, :] = grad.astype(bf16)

    by_tiles(rows, norm)
    gather = gather_steps(rows, low_ref, gather_sems)
    next(gather)
    yield
    next(gather)
    yield
    waits = waits + next(gather)
    yield
    for wait in waits:
        wait()
    for load in loads:
        load.wait()
    saves = [pltpu.make_async_copy(low_ref, low_out, save_sem.at[0]), pltpu.make_async_copy(grad_ref, grad_out, save_sem.at[1])]
    for save in saves:
        save.start()
    fill_blocks(rbig, rw_ref)
    fill_blocks(ibig, iw_ref)
    dr[...] = jnp.zeros_like(dr)
    di[...] = jnp.zeros_like(di)
    sums_ref[...] = jnp.zeros_like(sums_ref)
    dconv_ref[...] = jnp.zeros_like(dconv_ref)
    taps = raw_conv.shape[0]
    fill_small(conv_ref, bias_ref, raw_conv, raw_a, raw_b, raw_c, rate_ref)
    width = pad.shape[1]
    clear_tail(adj, width)

    def one(s):
        here = pl.ds(s * length, length)
        product_grad = dot_nt(low_ref[here, :], ow_ref[...])
        act, slope = gelu_parts(pre_ref[here, :])
        branch_low_ref[here, :] = (product_grad * get_tiles(states_ref, here, width) * slope).astype(bf16)
        put_tiles(adj, here, product_grad * act)

    for s in range(sequences):
        one(s)
        yield
    seq_scan(decay_ref, adj, sequences, length, True)
    yield

    def two(s):
        here = pl.ds(s * length, length)
        adjoint = get_tiles(adj, here, width)
        recur = recur_ref[here, :]
        inject = inject_ref[here, :]
        decay = get_tiles(decay_ref, here, width)
        values = values_ref[here, :]
        values_f = values.astype(f32)
        masks = label_masks(label_ref, here, length, width, taps, lines)
        inside = masks[0] > 0.5
        rate = bias_ref[3:4, :]
        log_decay = -decay_scale * rate * recur
        scale = jnp.where(inside, jnp.sqrt(minus_expm1(2.0 * log_decay)), 1.0)
        pad[0:8, :] = jnp.zeros((8, width), f32)
        pad[8 : 8 + length, :] = get_tiles(states_ref, here, width)
        previous = pad[7 : 7 + length, :]
        driven = adjoint * inject * values_f
        log_grad = jnp.where(inside, adjoint * previous * decay - driven * decay * decay / scale, 0.0)
        recur_low = (log_grad * (-decay_scale * rate) * recur * (1.0 - recur)).astype(bf16)
        inject_low = (driven * scale * (1.0 - inject)).astype(bf16)
        sums_ref[1:2, :] += jnp.sum(recur_low.astype(f32), axis=0, keepdims=True)
        sums_ref[2:3, :] += jnp.sum(inject_low.astype(f32), axis=0, keepdims=True)
        sums_ref[3:4, :] += jnp.sum(log_grad * recur, axis=0, keepdims=True)
        dr[...] += dot_tn(values, recur_low)
        di[...] += dot_tn(values, inject_low)
        grad = adjoint * scale * inject
        grad = grad + dot_nt(recur_low, rbig[...].astype(bf16)) + dot_nt(inject_low, ibig[...].astype(bf16))
        sums_ref[0:1, :] += jnp.sum(grad, axis=0, keepdims=True)
        pad[8 : 8 + length, :] = conv_in_ref[here, :].astype(f32)
        dconv_ref[0:1, :] += jnp.sum(grad * pad[8 : 8 + length, :], axis=0, keepdims=True)
        masked = []
        for k in range(1, taps):
            part = grad * masks[k - 1]
            masked.append(part)
            dconv_ref[k : k + 1, :] += jnp.sum(part * pad[8 - k : 8 - k + length, :], axis=0, keepdims=True)
        total = grad * conv_ref[0:1, :]
        pad[length : length + 8, :] = jnp.zeros((8, width), f32)
        for k in range(1, taps):
            pad[0:length, :] = masked[k - 1] * conv_ref[k : k + 1, :]
            total = total + pad[k : k + length, :]
        conv_low = total.astype(bf16)
        conv_low_ref[here, :] = conv_low
        partial[here, :] = (dot_nt(branch_low_ref[here, :], whole_weight(w_ref, 0)) + dot_nt(conv_low, whole_weight(w_ref, 1))).astype(bf16)

    for s in range(sequences):
        two(s)
        yield
    size = rw_ref.shape[1]
    packed_ref[...] = jnp.zeros_like(packed_ref)
    for h in range(rw_ref.shape[0]):
        cut = slice(h * size, (h + 1) * size)
        packed_ref[0, cut, 0 : 2 * size] = jnp.concatenate([dr[cut, cut], di[cut, cut]], axis=1).astype(bf16)
    packed_ref[0, width : width + 16, 0:width] = jnp.concatenate([dconv_ref[...], sums_ref[...]], axis=0).astype(bf16)
    ends = [(partial, partial_out), (branch_low_ref, branch_low_out), (conv_low_ref, conv_low_out)]
    for k, pair in enumerate(ends):
        saves.append(pltpu.make_async_copy(*pair, save_sem.at[2 + k]))
        saves[-1].start()
    yield
    for save in saves:
        save.wait()


def end_steps(
    outputs_at, mixes_at,
    partial_hbm, grad_ref, x_ref, middle_ref, hidden_hbm, down_hbm, product_hbm, mid_hbm, unit_hbm, branch_hbm, conv_hbm,
    gate_sum, up_sum, gate_hbm, up_hbm, tokens_ref, block_ref, gain_ref, *rest,
):
    near, far, acc = rest[:3]
    scatter_sems, more_sems = rest[3:7], rest[7:11]
    near_two, far_two, partial, hidden, down, product, tokens_wide, branch_low, conv_low, mix_low, sums, weights = rest[11:23]
    load_sem, gain_sem, output_made, mix_made = rest[23:]
    rows = x_ref.shape[0]
    depth = down.shape[1]

    def load(k, source, target):
        copy = pltpu.make_async_copy(source, target, load_sem.at[k])
        copy.start()
        return copy

    first = load(0, mid_hbm, tokens_wide), load(1, product_hbm, product)
    loads = [
        load(2, partial_hbm, partial), load(3, branch_hbm, branch_low), load(4, conv_hbm, conv_low),
        load(5, hidden_hbm, hidden), load(6, down_hbm, down),
    ]
    for copy in first:
        copy.wait()
    for d in range(0, depth, 512):
        output_made[0, :, d : d + 512] = dot_tn(product[...], tokens_wide[:, d : d + 512]).astype(bf16)
    again = load(7, unit_hbm, tokens_wide)

    def gain_loads(r):
        here = pl.ds(r * 16, 16)
        slot = r % 2
        return [
            pltpu.make_async_copy(source.at[here, :], target.at[slot, side], gain_sem.at[slot, 2 * group + side])
            for group, (target, sources) in enumerate(((sums, (gate_sum, up_sum)), (weights, (gate_hbm, up_hbm))))
            for side, source in enumerate(sources)
        ]

    gain_steps = gain_ref.shape[0] // 16
    for r in range(2):
        for copy in gain_loads(r):
            copy.start()
    yield outputs_at
    loads[0].wait()
    scatter = scatter_steps(rows, partial, near, far, acc, scatter_sems)
    next(scatter)
    yield None
    loads[1].wait()
    loads[2].wait()
    width = branch_low.shape[1]
    if mix_low.shape[1] > 2 * width:
        mix_low[...] = jnp.zeros_like(mix_low)

    def pack(here, i):
        mix_low[here, 0 : 2 * width] = jnp.concatenate([branch_low[here, :], conv_low[here, :]], axis=1)

    by_tiles(mix_low.shape[0], pack)
    again.wait()
    owners, own = mix_made.shape[:2]
    for part in range(4):
        for j in range(part * owners // 4, (part + 1) * owners // 4):
            mix_made[j] = dot_tn(tokens_wide[:, j * own : (j + 1) * own], mix_low[...]).astype(bf16)
        yield mixes_at if part == 3 else None
    waits = next(scatter)

    def norm(here, i):
        value = x_ref[here, :].astype(f32)
        inverse = root_mean(value)
        grad = grad_ref[here, :] + norm_backward(acc[here, :], value * inverse, inverse)
        tokens_ref[here, :] = grad.astype(bf16)

    by_tiles(rows, norm)
    for wait in waits:
        wait()
    yield None
    loads[3].wait()
    loads[4].wait()
    pieces_of = 4
    height = hidden.shape[0] // pieces_of
    for k in range(pieces_of):
        here = pl.ds(k * height, height)
        partial[here, :] = dot_nn(hidden[here, :], down[...]).astype(bf16)
        yield None
    scatter = scatter_steps(rows, partial, near_two, far_two, acc, more_sems)
    next(scatter)
    yield None
    waits = next(scatter)

    def out(here, i):
        block_ref[here, :] = (middle_ref[here, :] + acc[here, :]).astype(bf16)

    by_tiles(rows, out)
    yield None
    for r in range(gain_steps):
        slot = r % 2
        for copy in gain_loads(r):
            copy.wait()
        both = jnp.zeros((16, 1), f32)
        for side in range(2):
            both = both + jnp.sum(
                sums[slot, side].astype(f32) * low(weights[slot, side]), axis=1, keepdims=True
            )
        gain_ref[r * 16 : (r + 1) * 16, :] = both
        if r + 2 < gain_steps:
            for copy in gain_loads(r + 2):
                copy.start()
        yield None
    for wait in waits:
        wait()


def mlp_kernel(
    two_hbm, low_hbm, pair_hbm, down_hbm, hidden_out, partial_out, down_out, pair_out,
    two, low_rows, pair_w, down_w, hidden, pair_low, partial, down_grad, pair_grad, load_sem, save_sem, pair_sem,
):
    total, depth = two.shape
    ff = down_w.shape[0]
    tile = 256 if ff % 256 == 0 else 128
    height = 512
    steps = total // height

    def rows_of(hbm, ref, r, which):
        here = pl.ds(r * height, height)
        return pltpu.make_async_copy(hbm.at[here, :], ref.at[here, :], load_sem.at[which, r])

    weights = [
        pltpu.make_async_copy(pair_hbm, pair_w, load_sem.at[2, 0]),
        pltpu.make_async_copy(down_hbm, down_w, load_sem.at[2, 1]),
    ]
    rows_of(two_hbm, two, 0, 0).start()
    weights[0].start()
    rows_of(low_hbm, low_rows, 0, 1).start()
    weights[1].start()
    for r in range(1, steps):
        rows_of(two_hbm, two, r, 0).start()
        rows_of(low_hbm, low_rows, r, 1).start()
    weights[0].wait()
    weights[1].wait()

    def row_step(r, _):
        here = pl.ds(pl.multiple_of(r * height, height), height)
        pltpu.make_async_copy(two_hbm.at[here, :], two.at[here, :], load_sem.at[0, r]).wait()
        pltpu.make_async_copy(low_hbm.at[here, :], low_rows.at[here, :], load_sem.at[1, r]).wait()
        for f in range(ff // tile):
            cut = slice(f * tile, (f + 1) * tile)
            more = slice(ff + f * tile, ff + (f + 1) * tile)
            gate = dot_nn(two[here, :], pair_w[:, cut])
            up = dot_nn(two[here, :], pair_w[:, more])
            grad = dot_nt(low_rows[here, :], down_w[cut, :])
            act, slope = gelu_parts(gate)
            hidden[here, cut] = (act * up).astype(bf16)
            pair_low[here, cut] = (grad * up * slope).astype(bf16)
            pair_low[here, more] = (grad * act).astype(bf16)
        for d in range(0, depth, 512):
            partial[here, d : d + 512] = dot_nt(pair_low[here, :], pair_w[d : d + 512, :]).astype(bf16)
        return 0

    lax.fori_loop(0, steps, row_step, 0)
    saves = [
        pltpu.make_async_copy(partial, partial_out, save_sem.at[0]),
        pltpu.make_async_copy(hidden, hidden_out, save_sem.at[1]),
    ]
    for save in saves:
        save.start()
    for f in range(ff // tile):
        cut = slice(f * tile, (f + 1) * tile)
        down_grad[cut, :] = dot_tn(hidden[:, cut], low_rows[...]).astype(bf16)
    saves.append(pltpu.make_async_copy(down_grad, down_out, save_sem.at[2]))
    saves[-1].start()

    height = 256

    def column_step(d, _):
        here = pl.ds(pl.multiple_of(d * height, height), height)
        pair_grad[here, :] = dot_tn(two[:, here], pair_low[...]).astype(bf16)
        pltpu.make_async_copy(pair_grad.at[here, :], pair_out.at[here, :], pair_sem.at[d]).start()
        return 0

    lax.fori_loop(0, depth // height, column_step, 0)
    for d in range(depth // height):
        here = pl.ds(d * height, height)
        pltpu.make_async_copy(pair_grad.at[here, :], pair_out.at[here, :], pair_sem.at[d]).wait()
    for save in saves:
        save.wait()


def mlp(unit_two, out_low, pair_w, down_w):
    total, depth = unit_two.shape
    ff = down_w.shape[0]
    kept = [((total, ff), bf16), ((total, depth), bf16), ((ff, depth), bf16), ((depth, 2 * ff), bf16)]
    vm, dma = pltpu.VMEM, pltpu.SemaphoreType.DMA
    return pl.pallas_call(
        mlp_kernel,
        out_shape=tuple(jax.ShapeDtypeStruct(*item) for item in kept),
        in_specs=[ANY] * 4,
        out_specs=[ANY] * 4,
        scratch_shapes=[vm(item.shape, bf16) for item in (unit_two, out_low, pair_w, down_w)]
        + [vm((total, ff), bf16), vm((total, 2 * ff), bf16)]
        + [vm(*item) for item in kept[1:]]
        + [dma((3, total // 512)), dma((3,)), dma((depth // 256,))],
        compiler_params=pltpu.CompilerParams(vmem_limit_bytes=60 * 2**20),
        cost_estimate=pl.CostEstimate(
            flops=2 * total * depth * ff * 8, bytes_accessed=36 * 2**20, transcendentals=total * ff
        ),
    )(unit_two, out_low, pair_w, down_w)


def pieces(rows, most):
    count = -(-rows // most)
    while rows % count or (rows // count) % 16:
        count += 1
    return count


def line_kernel(n, kinds, cuts, made_here, beside, turns, extra, *refs):
    ins = len(cuts)
    made = ins + kinds.count("pair")
    extra_ins, extra_outs, extra_scratch = extra
    refs = list(refs)

    def take(count):
        taken = refs[:count]
        del refs[:count]
        return taken

    given = [k for k in range(ins) if k not in made_here]
    own_hbm, side_in = dict(zip(given, take(len(given)))), take(extra_ins)
    outs, side_out = take(made), take(extra_outs)
    side_scratch = take(extra_scratch)
    from_out, from_in = take(ins), take(ins)
    own_made = dict(zip(made_here, take(len(made_here))))
    slots, whole_sem, slot_sem, sent_in, sent_out, got_out, got_in, sent_x, got_x = refs
    depth = slots.shape[0]
    me = lax.axis_index("replica")
    y, s = lax.axis_index("seq"), lax.axis_index("shard")
    shards = lax.axis_size("shard")
    owners = shards * lax.axis_size("seq")
    left = me < n // 2
    inward = jnp.where(left, me + 1, me - 1)
    outward = jnp.where(left, me - 1, me + 1)
    has_out = jnp.logical_and(me > 0, me < n - 1)
    at_end = jnp.logical_not(has_out)
    middle = jnp.logical_or(me == n // 2 - 1, me == n // 2)

    def peer(i):
        return {"seq": jnp.bitwise_xor(y, i // shards), "shard": jnp.bitwise_xor(s, i % shards)}

    def place(i):
        return jnp.bitwise_xor(y, i // shards) * shards + jnp.bitwise_xor(s, i % shards)

    chunks = []
    for k, (lead, count, rows) in enumerate(cuts):
        for step in range(lead):
            for i in range(count):
                chunks.append((k, step if kinds[k] == "row" else (step + 1) % lead, i * rows, rows))
    total = len(chunks)

    def view(group, c):
        k, i, start, rows = chunks[c]
        return group[k].at[0 if kinds[k] == "row" else place(i), pl.ds(start, rows), :]

    def slot(c):
        k, i, start, rows = chunks[c]
        return slots.at[c % depth, pl.ds(0, rows), pl.ds(0, from_in[k].shape[2])]

    def load(c):
        return pltpu.make_async_copy(view(own_hbm, c), slot(c), slot_sem.at[c % depth])

    wholes = {k: pltpu.make_async_copy(own_hbm[k], from_out[k], whole_sem.at[k]) for k in given}
    loaded = [c for c in range(total) if chunks[c][0] in given]

    @pl.when(at_end)
    def _():
        for k in given:
            wholes[k].start()

    @pl.when(has_out)
    def _():
        for c in loaded[: depth - 1]:
            load(c).start()

    barrier = pltpu.get_barrier_semaphore()
    for i in range(1, owners):
        pl.semaphore_signal(barrier, inc=1, device_id=peer(i), device_id_type=MESH)
    pl.semaphore_signal(barrier, inc=1, device_id={"replica": inward}, device_id_type=MESH)

    @pl.when(has_out)
    def _():
        pl.semaphore_signal(barrier, inc=1, device_id={"replica": outward}, device_id_type=MESH)
        pl.semaphore_wait(barrier, owners + 1)

    @pl.when(at_end)
    def _():
        pl.semaphore_wait(barrier, owners)

    def push(group, target, c, sent, got, device):
        return remote(view(group, c), view(target, c), sent.at[c], got.at[c], {"replica": device})

    def add(target, other, c):
        k, i, start, rows = chunks[c]
        if other is None:
            more = view(own_made, c) if k in made_here else slot(c)
        else:
            more = view(other, c)
        into = view(target, c)

        def tile(t, _):
            here = pl.ds(pl.multiple_of(t * 16, 16), 16)
            into[here, :] = (into[here, :].astype(f32) + more[here, :].astype(f32)).astype(bf16)
            return 0

        lax.fori_loop(0, rows // 16, tile, 0)

    def pass_in(c, source):
        @pl.when(middle)
        def _():
            push(source, from_in, c, sent_in, got_in, inward).start()

        @pl.when(jnp.logical_not(middle))
        def _():
            push(source, from_out, c, sent_in, got_out, inward).start()

    def gather_in(c):
        @pl.when(has_out)
        def _():
            if c in loaded:
                load(c).wait()
            push(from_out, from_out, c, sent_in, got_out, inward).wait_recv()
            add(from_out, None, c)
            pass_in(c, from_out)
            if c + depth - 1 in loaded:
                load(c + depth - 1).start()

    @pl.when(at_end)
    def _():
        for c in loaded:
            if c == 0 or chunks[c][0] != chunks[c - 1][0]:
                wholes[chunks[c][0]].wait()
            pass_in(c, from_out)

    def advance():
        k = next(work)
        if k is not None:

            @pl.when(at_end)
            def _():
                for c in range(total):
                    if chunks[c][0] == k:
                        pass_in(c, own_made)

    work = beside(*side_in, *side_out, *side_scratch, *[own_made[k] for k in made_here])
    advance()

    def deliveries(c):
        k, i, start, rows = chunks[c]
        here = pl.ds(start, rows)
        first = k + kinds[:k].count("pair")
        source = view(from_in, c)
        if kinds[k] == "row":
            ends = [(source, outs[first].at[here, :])]
        elif kinds[k] == "side":
            ends = [(source, outs[first].at[place(0), here, :])]
        else:
            half = source.shape[1] // 2
            there = pl.ds(pl.multiple_of(place(0) * half, half), half)
            ends = [
                (source.at[:, pl.ds(part * half, half)], outs[first + part].at[here, there]) for part in range(2)
            ]
        if kinds[k] == "row" or i == 0:
            return [pltpu.make_async_copy(*pair, sent_x.at[c, p]) for p, pair in enumerate(ends)], False
        return [remote(*pair, sent_x.at[c, p], got_x.at[c, p], peer(i)) for p, pair in enumerate(ends)], True

    def give_back(c):
        push(from_out, from_in, c, sent_out, got_in, inward).wait_recv()

        @pl.when(middle)
        def _():
            add(from_in, from_out, c)

        @pl.when(has_out)
        def _():
            push(from_in, from_in, c, sent_out, got_in, outward).start()

        for copy in deliveries(c)[0]:
            copy.start()

    lag = 1
    for c in range(total + lag):
        for _ in range(turns.count(c)):
            advance()
        if c < total:
            gather_in(c)
        if c >= lag:
            give_back(c - lag)
    for _ in work:
        pass
    for c in range(total):
        copies, away = deliveries(c)
        for copy in copies:
            if away:
                copy.wait_recv()
                copy.wait_send()
            else:
                copy.wait()
        push(from_out, from_in, c, sent_in, got_in, inward).wait_send()

        @pl.when(has_out)
        def _():
            push(from_in, from_in, c, sent_out, got_in, outward).wait_send()


def replica_sum(arrays, kinds, made_here, identity, beside, turns, inputs, results, side_scratch):
    cuts, outs = [], []
    tall = broad = 0
    for item, kind in zip(arrays, kinds):
        lead, height, columns = item.shape
        count = pieces(height, max(16, (105 * 1024) // columns // 16 * 16))
        cuts.append((lead, count, height // count))
        tall, broad = max(tall, height // count), max(broad, columns)
        if kind == "pair":
            outs += [jax.ShapeDtypeStruct((height, lead * columns // 2), bf16)] * 2
        elif kind == "side":
            outs.append(jax.ShapeDtypeStruct(item.shape, bf16))
        else:
            outs.append(jax.ShapeDtypeStruct((height, columns), bf16))
    count = sum(lead * cut for lead, cut, _ in cuts)
    buffers = [pltpu.VMEM(item.shape, bf16) for item in arrays]
    dma = pltpu.SemaphoreType.DMA
    return pl.pallas_call(
        functools.partial(
            line_kernel, lax.axis_size("replica"), tuple(kinds), tuple(cuts), tuple(made_here), beside, turns,
            (len(inputs), len(results), len(side_scratch)),
        ),
        out_shape=tuple(outs) + tuple(jax.ShapeDtypeStruct(shape, kind) for shape, kind, _ in results),
        in_specs=[ANY] * (len(arrays) - len(made_here)) + [spec for _, spec in inputs],
        out_specs=[ANY] * len(outs) + [spec for _, _, spec in results],
        scratch_shapes=list(side_scratch)
        + buffers * 2
        + [buffers[k] for k in made_here]
        + [pltpu.VMEM((4, tall, broad), bf16), dma((len(arrays),)), dma((4,))]
        + [dma((count,))] * 4
        + [dma((count, 2))] * 2,
        compiler_params=pltpu.CompilerParams(
            collective_id=identity, has_side_effects=True, vmem_limit_bytes=62 * 2**20
        ),
        cost_estimate=pl.CostEstimate(flops=10**6, bytes_accessed=200 * 2**20, transcendentals=0),
    )(*[item for k, item in enumerate(arrays) if k not in made_here], *[item for item, _ in inputs])


def finish_pair_kernel(gain_ref, a_ref, b_ref, outa_ref, outb_ref):
    gain = low(gain_ref[:, 1:2])
    outa_ref[...] = a_ref[...].astype(f32) * gain
    outb_ref[...] = b_ref[...].astype(f32) * gain


def finish_pair(gain, a, b):
    rows, columns = a.shape
    cut = min(rows, 64)
    wide = pl.BlockSpec((cut, columns), lambda i: (i, 0))
    out = jax.ShapeDtypeStruct((rows, columns), f32)
    return pl.pallas_call(
        finish_pair_kernel,
        grid=(rows // cut,),
        out_shape=(out, out),
        in_specs=[pl.BlockSpec((cut, 2), lambda i: (i, 0)), wide, wide],
        out_specs=[wide, wide],
        compiler_params=pltpu.CompilerParams(vmem_limit_bytes=62 * 2**20),
        cost_estimate=pl.CostEstimate(flops=2 * rows * columns, bytes_accessed=12 * rows * columns, transcendentals=0),
    )(gain, a, b)


def finish_rest_kernel(gain_ref, mix_ref, wa_ref, wb_ref, out_sum_ref, down_sum_ref, outa_ref, outb_ref, grad_ref, out_ref, down_ref):
    owners = mix_ref.shape[0]
    width = wa_ref.shape[1] // owners
    gain = low(gain_ref[:, 0:1])
    grad = jnp.zeros(gain.shape, f32)
    for part, (weight_ref, target_ref) in enumerate(((wa_ref, outa_ref), (wb_ref, outb_ref))):
        total = jnp.concatenate(
            [mix_ref[j, :, part * width : (part + 1) * width].astype(f32) for j in range(owners)], axis=1
        )
        target_ref[...] = total * gain
        grad = grad + jnp.sum(total * low(weight_ref[...]), axis=1, keepdims=True)
    grad_ref[...] = grad
    out_ref[...] = out_sum_ref[...].astype(f32)
    down_ref[...] = down_sum_ref[...].astype(f32)


def finish_rest(gain, mix, wa, wb, out_sum, down_sum):
    rows, columns = wa.shape
    steps = 4
    while out_sum.shape[0] % (16 * steps) or down_sum.shape[0] % (16 * steps) or rows % (16 * steps):
        steps //= 2

    def tall(item):
        return pl.BlockSpec((item.shape[0] // steps, item.shape[1]), lambda i: (i, 0))

    owners, _, both = mix.shape
    wide, thin = tall(wa), pl.BlockSpec((rows // steps, 1), lambda i: (i, 0))
    return pl.pallas_call(
        finish_rest_kernel,
        grid=(steps,),
        out_shape=(
            jax.ShapeDtypeStruct(wa.shape, f32),
            jax.ShapeDtypeStruct(wa.shape, f32),
            jax.ShapeDtypeStruct((rows, 1), f32),
            jax.ShapeDtypeStruct(out_sum.shape, f32),
            jax.ShapeDtypeStruct(down_sum.shape, f32),
        ),
        in_specs=[
            tall(gain),
            pl.BlockSpec((owners, rows // steps, both), lambda i: (0, i, 0)),
            wide,
            wide,
            tall(out_sum),
            tall(down_sum),
        ],
        out_specs=[wide, wide, thin, tall(out_sum), tall(down_sum)],
        compiler_params=pltpu.CompilerParams(vmem_limit_bytes=62 * 2**20),
        cost_estimate=pl.CostEstimate(flops=10**7, bytes_accessed=40 * 2**20, transcendentals=0),
    )(gain, mix, wa, wb, out_sum, down_sum)


def body(
    tokens,
    segments,
    cotangent,
    norm_gain,
    branch_weight,
    input_weight,
    conv_weight,
    conv_bias,
    recur_gate_weight,
    recur_gate_bias,
    input_gate_weight,
    input_gate_bias,
    decay_param,
    output_weight,
    mlp_norm_gain,
    gate_weight,
    up_weight,
    down_weight,
):
    x, cot = tokens[0], cotangent[0]
    rows, depth = x.shape
    members = lax.axis_size(GROUP)
    sequences = lax.axis_size("shard")
    total = members * rows
    gains = jnp.stack([norm_gain, mlp_norm_gain], 1)
    own_labels = jnp.broadcast_to(segments[0].astype(bf16)[:, None], (rows, 128))
    width = branch_weight.shape[1] // members
    decay_f = low(decay_param)
    small = (
        conv_weight, conv_bias, recur_gate_bias, input_gate_bias, jax.nn.softplus(-decay_f),
    )
    (
        unit_all, labels, out_low, product, *mixed, mix_w, output_w, unit_two, middle, pair_w, down_w,
    ) = front(
        sequences, x, own_labels, cot, gains, small,
        recur_gate_weight, input_gate_weight, branch_weight, input_weight, gate_weight, up_weight, output_weight,
        down_weight,
    )
    pair_w = pair_w.reshape(depth, -1)
    whole = ((total, depth), bf16)
    hidden, partial, down_partial, pair_partial = mlp(unit_two, out_low, pair_w, down_w)
    down_partial = down_partial[None]
    pair_partial = pair_partial.reshape(members, -1, pair_w.shape[1])
    kept = (output_w, mix_w, *mixed)
    narrow = ((total, width), bf16)
    vm, dma = pltpu.VMEM, pltpu.SemaphoreType.DMA
    length = total // sequences
    size = recur_gate_weight.shape[1]
    lanes = -(-max(width, 2 * size) // 128) * 128
    back = replica_sum(
        [down_partial, pair_partial], ["row", "pair"], (), 3,
        functools.partial(turn_steps, sequences, length),
        (6, 9, 12) + tuple(range(14, 14 + 2 * sequences + 2)),
        [(partial, ANY)] + [(item, VM) for item in (middle, cot, labels, *small, recur_gate_weight, input_gate_weight)]
        + [(item, ANY) for item in kept],
        [whole + (ANY,), ((rows, depth), f32, ANY), whole + (ANY,), narrow + (ANY,), narrow + (ANY,)]
        + [((1, width + 16, lanes), bf16, VM)],
        plane_scratch(rows, depth, 1, 1)
        + [vm(item.shape, item.dtype) for item in kept]
        + [vm(*whole), vm(*whole), vm((rows, depth), f32), vm(*narrow), vm(*narrow), vm(mixed[-1].shape, f32)]
        + [vm((8 + length, width), f32), vm((8 + length, 128), f32)]
        + [vm((width, width), f32)] * 4
        + [vm((8, width), f32)] * 2
        + [vm((8, width), f32), vm((8, width), f32)]
        + [dma((10,)), dma((5,))],
    )
    down_sum, gate_sum, up_sum, mid_low, middle_grad, partial, branch_low, conv_low = back[:8]
    packed = back[8]
    both = -(-2 * width // 128) * 128
    mix_shape = jax.ShapeDtypeStruct((members, depth // members, both), bf16)
    output_shape = jax.ShapeDtypeStruct((1,) + output_w.shape, bf16)
    again = plane_scratch(rows, depth, 0, 1)
    packed, output_sum, mix_sum, tokens_grad, block_out, mlp_gain_grad = replica_sum(
        [packed, output_shape, mix_shape], ["row", "row", "side"], (1, 2), 4, functools.partial(end_steps, 1, 2),
        (0, 1, 2, 3, 4, 7, 8, 9, 10, 11, 12, 19) + tuple(19 + i // 2 for i in range(gate_weight.shape[0] // 16)),
        [(partial, ANY), (middle_grad, VM), (x, VM), (middle, VM)]
        + [(item, ANY) for item in (hidden, down_w, product, mid_low, unit_all, branch_low, conv_low, gate_sum, up_sum, gate_weight, up_weight)],
        [((rows, depth), bf16, VM), ((rows, depth), bf16, VM), ((gate_weight.shape[0], 1), f32, VM)],
        again + again[3:] + again[:2] + [vm(*whole), vm(hidden.shape, bf16), vm(down_w.shape, bf16)]
        + [vm(*narrow), vm(*whole), vm(*narrow), vm(*narrow), vm((total, both), bf16)]
        + [vm((2, 2, 16, gate_weight.shape[1]), bf16), vm((2, 2, 16, gate_weight.shape[1]), f32), dma((8,)), dma((2, 4))],
    )
    packed = packed.astype(f32)
    gate_grad, up_grad = finish_pair(gains, gate_sum, up_sum)
    branch_grad, input_grad, gain_grad, output_grad, down_grad = finish_rest(
        gains, mix_sum, branch_weight, input_weight, output_sum, down_sum
    )
    recur_weight_grad = packed[:width, :size].reshape(-1, size, size)
    inject_weight_grad = packed[:width, size : 2 * size].reshape(-1, size, size)
    conv_weight_grad = packed[width : width + conv_weight.shape[0], :width]
    conv_bias_grad, recur_bias_grad, inject_bias_grad, rate_grad = [packed[width + 8 + i, :width] for i in range(4)]
    decay_param_grad = rate_grad * decay_scale * jax.nn.sigmoid(-decay_f)
    return (
        block_out[None],
        tokens_grad[None],
        gain_grad[:, 0],
        branch_grad,
        input_grad,
        conv_weight_grad,
        conv_bias_grad,
        recur_weight_grad,
        recur_bias_grad,
        inject_weight_grad,
        inject_bias_grad,
        decay_param_grad,
        output_grad,
        mlp_gain_grad[:, 0],
        gate_grad,
        up_grad,
        down_grad,
    )


def solution(mesh):
    row3 = P(("shard", "replica"), "seq", None)
    vec = P(("seq", "shard"))
    mat = P(("seq", "shard"), None)
    cube = P(("seq", "shard"), None, None)
    taps = P(None, ("seq", "shard"))
    params = (vec, mat, mat, taps, vec, cube, vec, cube, vec, vec, mat, vec, mat, mat, mat)
    in_specs = (row3, P(("shard", "replica"), "seq"), row3) + params
    out_specs = (row3, row3) + params
    return jax.shard_map(body, mesh=mesh, in_specs=in_specs, out_specs=out_specs, check_vma=False)
```

```python
import functools

import jax
import jax.numpy as jnp
from jax import lax
from jax.experimental import pallas as pl
from jax.experimental.pallas import tpu as pltpu
from jax.sharding import PartitionSpec as P

epsilon = 1e-06
decay_scale = 8.0
GROUP = ("seq", "shard")
ROWS = ("shard", "seq")
f32 = jnp.float32
bf16 = jnp.bfloat16
VM = pl.BlockSpec(memory_space=pltpu.VMEM)
ANY = pl.BlockSpec(memory_space=pl.ANY)
MESH = pl.DeviceIdType.MESH


def mm(left, right):
    return jnp.dot(left, right, preferred_element_type=f32)


def mm_nt(left, right):
    return lax.dot_general(left, right, (((1,), (1,)), ((), ())), preferred_element_type=f32)


def mm_tn(left, right):
    return lax.dot_general(left, right, (((0,), (0,)), ((), ())), preferred_element_type=f32)


def low(item):
    return item.astype(bf16).astype(f32)


def by_owner(weight, gain):
    owners = lax.axis_size(GROUP)
    scaled = (low(weight) * gain).astype(bf16)
    return jnp.swapaxes(scaled.reshape(weight.shape[0], owners, -1), 0, 1)


def swap(cut):
    return lax.all_to_all(cut, GROUP, split_axis=0, concat_axis=0, tiled=True)


def gelu_parts(x):
    inner = 0.7978845608028654 * (x + 0.044715 * x * x * x)
    t = jnp.tanh(inner)
    value = 0.5 * x * (1.0 + t)
    slope = 0.5 * (1.0 + t) + 0.5 * x * (1.0 - t * t) * 0.7978845608028654 * (
        1.0 + 3.0 * 0.044715 * x * x
    )
    return value, slope


def minus_expm1(y):
    poly = 1.0 + y * (1.0 / 8.0)
    for order in (7.0, 6.0, 5.0, 4.0, 3.0, 2.0):
        poly = 1.0 + y * (1.0 / order) * poly
    return jnp.where(y > -0.5, -y * poly, 1.0 - jnp.exp(y))


def dot_nn(a, b):
    return lax.dot_general(a, b, (((1,), (0,)), ((), ())), preferred_element_type=f32)


def dot_nt(a, b):
    return lax.dot_general(a, b, (((1,), (1,)), ((), ())), preferred_element_type=f32)


def dot_tn(a, b):
    return lax.dot_general(a, b, (((0,), (0,)), ((), ())), preferred_element_type=f32)


def whole_weight(ref, part):
    owners, _, rows, width = ref.shape
    return ref[:, part].reshape(owners * rows, width)


def fill_blocks(target, source):
    target[...] = jnp.zeros_like(target)
    count, size = source.shape[0], source.shape[1]
    for h in range(count):
        target[h * size : (h + 1) * size, h * size : (h + 1) * size] = source[h].astype(bf16).astype(f32)


def put_tiles(ref, here, value):
    width = value.shape[1]
    for tile in range(ref.shape[0]):
        lanes = min(128, width - 128 * tile)
        ref[tile, here, 0:lanes] = value[:, 128 * tile : 128 * tile + lanes]


def get_tiles(ref, here, width):
    parts = [ref[tile, here, 0 : min(128, width - 128 * tile)] for tile in range(ref.shape[0])]
    return jnp.concatenate(parts, axis=1)


def clear_tail(ref, width):
    tail = ref.shape[0] * 128 - width
    if tail:
        ref[ref.shape[0] - 1, :, 128 - tail :] = jnp.zeros((ref.shape[1], tail), f32)


def fill_small(conv, bias, raw_conv, raw_a, raw_b, raw_c, rate):
    conv[0 : raw_conv.shape[0], :] = low(raw_conv[...])
    for row, ref in enumerate((raw_a, raw_b, raw_c)):
        bias[row : row + 1, :] = low(ref[...])[None, :]
    bias[3:4, :] = rate[...][None, :]


def label_masks(label_ref, here, length, width, taps, lines):
    own = label_ref[here, :].astype(f32)
    lines[0:8, :] = jnp.full((8, 128), -1.0, f32)
    lines[8 : 8 + length, :] = own
    masks = []
    for k in range(1, taps):
        same = jnp.where(lines[8 - k : 8 - k + length, :] == own, 1.0, 0.0)
        masks.append(jnp.concatenate([same] * -(-width // 128), axis=1)[:, :width])
    return masks


def seq_scan(decay_ref, value_ref, sequences, length, reverse):
    tiles = decay_ref.shape[0]
    unroll = 8

    def step(i, states):
        states = list(states)
        for j in range(unroll):
            at = i * unroll + j
            if reverse:
                at = length - 1 - at
            here = pl.ds(at, sequences, stride=length)
            for tile in range(tiles):
                value = value_ref[tile, here, :]
                decay = decay_ref[tile, here, :]
                if reverse:
                    new = value + states[tile]
                    value_ref[tile, here, :] = new
                    states[tile] = decay * new
                else:
                    states[tile] = value + decay * states[tile]
                    value_ref[tile, here, :] = states[tile]
        return tuple(states)

    lax.fori_loop(0, length // unroll, step, (jnp.zeros((sequences, 128), f32),) * tiles)


def plane():
    halves, shards = lax.axis_size("seq"), lax.axis_size("shard")
    y, s = lax.axis_index("seq"), lax.axis_index("shard")
    offsets = [(dy, ds) for ds in range(0, shards, 2) for dy in range(halves)]

    def at(dy, ds):
        return {"seq": jnp.bitwise_xor(y, dy), "shard": jnp.bitwise_xor(s, ds)}

    def block(dy, ds):
        return jnp.bitwise_xor(s, ds) * halves + jnp.bitwise_xor(y, dy)

    return offsets, at, block


def remote(src, dst, sent, got, device):
    return pltpu.make_async_remote_copy(
        src_ref=src, dst_ref=dst, send_sem=sent, recv_sem=got, device_id=device, device_id_type=MESH
    )


def row_block(ref, index, rows):
    return ref.at[pl.ds(pl.multiple_of(index * rows, rows), rows), :]


def scatter_steps(rows, partial, near, far, acc, sems):
    offsets, at, block = plane()
    near_sent, near_got, far_sent, far_got = sems
    count = len(offsets)
    order = list(range(count - 1, -1, -1))
    firsts = {}
    for q in order:
        dy, ds = offsets[q]
        firsts[q] = remote(
            row_block(partial, block(dy, ds ^ 1), rows), near.at[q], near_sent.at[q], near_got.at[q], at(0, 1)
        )
        firsts[q].start()
    seconds = {}
    for q in order:
        dy, ds = offsets[q]
        firsts[q].wait_recv()
        base = block(dy, ds) * rows

        def tile(i, _):
            step = pl.multiple_of(i * 16, 16)
            here = pl.ds(step, 16)
            total = partial[pl.ds(pl.multiple_of(base + step, 16), 16), :].astype(f32) + near[q, here, :].astype(f32)
            if q:
                near[q, here, :] = total.astype(bf16)
            else:
                acc[here, :] = total
            return 0

        lax.fori_loop(0, rows // 16, tile, 0)
        if q:
            seconds[q] = remote(near.at[q], far.at[q - 1], far_sent.at[q - 1], far_got.at[q - 1], at(dy, ds))
            seconds[q].start()
    yield None
    for q in order[:-1]:
        seconds[q].wait_recv()

        def more(i, _):
            here = pl.ds(pl.multiple_of(i * 16, 16), 16)
            acc[here, :] += far[q - 1, here, :].astype(f32)
            return 0

        lax.fori_loop(0, rows // 16, more, 0)
    yield [firsts[q].wait_send for q in order] + [seconds[q].wait_send for q in order[:-1]]


def gather_steps(rows, whole, sems):
    offsets, at, block = plane()
    near_sent, near_got, far_sent, far_got = sems
    count = len(offsets)
    half = rows // 2

    def piece(q, part):
        start = pl.multiple_of(block(*offsets[q]) * rows + part * half, 16)
        return whole.at[pl.ds(start, half), :]

    own = row_block(whole, block(0, 0), rows)
    straight = [q for q in range(1, count) if offsets[q][0] == 0 or offsets[q][1] == 0]
    across = [q for q in range(1, count) if q not in straight]
    upright = [q for q in straight if offsets[q][0]]
    sends, arrivals = [], []
    outs = {}
    for q in straight:
        outs[q] = remote(own, own, far_sent.at[q], far_got.at[q], at(*offsets[q]))
        outs[q].start()
        sends.append(outs[q].wait_send)

    def hand(q, part=None):
        source = row_block(whole, block(*offsets[q]), rows) if part is None else piece(q, part)
        place = q if part is None or part == 0 else count + q
        copy = remote(source, source, near_sent.at[place], near_got.at[place], at(0, 1))
        copy.start()
        sends.append(copy.wait_send)
        arrivals.append(copy.wait_recv)

    hand(0)
    yield None
    onward = {}
    for q in straight:
        outs[q].wait_recv()
        if q in upright:
            targets = [(1, t) for t in straight if t not in upright]
        else:
            targets = [(0, t) for t in upright]
        for part, t in targets:
            dy, ds = offsets[q][0] | offsets[t][0], offsets[q][1] | offsets[t][1]
            a = offsets.index((dy, ds))
            source = piece(q, part)
            onward[a, part] = remote(source, source, far_sent.at[part * count + a], far_got.at[part * count + a], at(*offsets[t]))
            onward[a, part].start()
            sends.append(onward[a, part].wait_send)
        hand(q)
    yield None
    for a in across:
        for part in range(2):
            onward[a, part].wait_recv()
            hand(a, part)
    yield arrivals + sends


def root_mean(rows):
    return lax.rsqrt(jnp.mean(rows * rows, axis=-1, keepdims=True) + epsilon)


def norm_backward(grad_unit, unit, inverse):
    return inverse * (grad_unit - unit * jnp.mean(grad_unit * unit, axis=-1, keepdims=True))


def by_tiles(rows, work):
    def tile(i, _):
        work(pl.ds(pl.multiple_of(i * 16, 16), 16), i)
        return 0

    lax.fori_loop(0, rows // 16, tile, 0)


def plane_scratch(rows, depth, gathers, scatters):
    count = lax.axis_size("seq") * lax.axis_size("shard") // 2
    block = (rows, depth)
    scratch = []
    if scatters:
        scratch = [
            pltpu.VMEM((count,) + block, bf16),
            pltpu.VMEM((count - 1,) + block, bf16),
            pltpu.VMEM(block, f32),
        ]
    dma = pltpu.SemaphoreType.DMA
    for _ in range(scatters):
        scratch += [dma((count,))] * 2 + [dma((count - 1,))] * 2
    for _ in range(gathers):
        scratch += [dma((2 * count,))] * 4
    return scratch


def cut_columns(weight_ref, gain, target, start, lanes):
    owners = weight_ref.shape[1] // lanes

    def tile(i, _):
        step = pl.multiple_of(i * 16, 16)
        here = pl.ds(step, 16)
        scaled = low(weight_ref[here, :]) * gain(step)
        for j in range(owners):
            target(j)[here, start : start + lanes] = scaled[:, j * lanes : (j + 1) * lanes].astype(bf16)
        return 0

    lax.fori_loop(0, weight_ref.shape[0] // 16, tile, 0)


def quarter_steps(n, part, whole, sems):
    me = lax.axis_index("replica")
    right_sent, right_got, left_sent, left_got = sems

    def rows(q):
        return whole.at[:, pl.ds(pl.multiple_of(q * part, 16), part), :]

    def to_right(hop):
        block = rows(me - hop)
        return remote(block, block, right_sent.at[hop], right_got.at[hop], {"replica": me + 1})

    def to_left(hop):
        block = rows(me + hop)
        return remote(block, block, left_sent.at[hop], left_got.at[hop], {"replica": me - 1})

    def from_left(hop):
        block = rows(me - hop - 1)
        return remote(block, block, right_sent.at[hop], right_got.at[hop], {"replica": me + 1})

    def from_right(hop):
        block = rows(me + hop + 1)
        return remote(block, block, left_sent.at[hop], left_got.at[hop], {"replica": me - 1})

    for hop in range(n - 1):
        if hop:

            @pl.when(me >= hop)
            def _():
                from_left(hop - 1).wait_recv()

            @pl.when(me + hop < n)
            def _():
                from_right(hop - 1).wait_recv()

        @pl.when(jnp.logical_and(me >= hop, me < n - 1))
        def _():
            to_right(hop).start()

        @pl.when(jnp.logical_and(me + hop < n, me > 0))
        def _():
            to_left(hop).start()

        yield

    @pl.when(me >= n - 1)
    def _():
        from_left(n - 2).wait_recv()

    @pl.when(me + n - 1 < n)
    def _():
        from_right(n - 2).wait_recv()

    for hop in range(n - 1):

        @pl.when(jnp.logical_and(me >= hop, me < n - 1))
        def _():
            to_right(hop).wait_send()

        @pl.when(jnp.logical_and(me + hop < n, me > 0))
        def _():
            to_left(hop).wait_send()

    yield


def front_kernel(
    n, sequences, length,
    x_ref, label_ref, cot_ref, gains_ref, raw_conv, raw_a, raw_b, raw_c, rate_ref, rw_ref, iw_ref,
    branch_hbm, input_hbm, gate_hbm, up_hbm, ow_hbm, down_hbm,
    unit_out, labels_out, low_out, product_out, pre_out, conv_in_out, values_out, recur_out, inject_out, decay_out,
    states_out, mix_out, ow_out, two_out, middle_out, pair_out, down_out,
    unit_ref, labels_ref, product_ref, pre_ref, conv_in_ref, values_ref, recur_ref, inject_ref, decay_ref,
    states_ref, mix_ref, ow_ref, two_ref, middle_ref,
    wide, tall, ow_f, mix_cut, pair_cut, pad, lines, rbig, ibig, partial, conv_ref, bias_ref, down_f, down_low,
    near, far, acc, *sems,
):
    rows = x_ref.shape[0]
    scatter_sems, sems = sems[:4], sems[4:]
    unit_sems, label_sems, low_sems, two_sems, sems = sems[:4], sems[4:8], sems[8:12], sems[12:16], sems[16:]
    load_sem, save_sem, mix_sent, mix_got, pair_sent, pair_got, down_sem = sems[:7]
    line_sems = sems[7:]
    offsets, at, block = plane()
    z = lax.axis_index("replica")
    y, s = lax.axis_index("seq"), lax.axis_index("shard")
    shards = lax.axis_size("shard")
    owners = shards * lax.axis_size("seq")
    part = gate_hbm.shape[0] // n
    width = pad.shape[1]
    ff = gate_hbm.shape[1] // owners

    def peer(i):
        return {"seq": jnp.bitwise_xor(y, i // shards), "shard": jnp.bitwise_xor(s, i % shards)}

    def place(i):
        return jnp.bitwise_xor(y, i // shards) * shards + jnp.bitwise_xor(s, i % shards)

    own_rows = pl.ds(pl.multiple_of(z * part, 16), part)
    loads = [
        pltpu.make_async_copy(gate_hbm.at[own_rows, :], tall.at[0], load_sem.at[0]),
        pltpu.make_async_copy(up_hbm.at[own_rows, :], tall.at[1], load_sem.at[1]),
        pltpu.make_async_copy(branch_hbm, wide.at[0], load_sem.at[2]),
        pltpu.make_async_copy(input_hbm, wide.at[1], load_sem.at[3]),
        pltpu.make_async_copy(ow_hbm, ow_f, load_sem.at[4]),
    ]
    for load in loads:
        load.start()
    saves = []

    def save(source, target):
        copy = pltpu.make_async_copy(source, target, save_sem.at[len(saves)])
        copy.start()
        saves.append(copy)

    low_own = pltpu.make_async_copy(cot_ref, row_block(low_out, block(0, 0), rows), load_sem.at[5])
    low_own.start()
    barrier = pltpu.get_barrier_semaphore()
    for i in range(1, owners):
        pl.semaphore_signal(barrier, inc=1, device_id=peer(i), device_id_type=MESH)

    @pl.when(z > 0)
    def _():
        pl.semaphore_signal(barrier, inc=1, device_id={"replica": z - 1}, device_id_type=MESH)

    @pl.when(z < n - 1)
    def _():
        pl.semaphore_signal(barrier, inc=1, device_id={"replica": z + 1}, device_id_type=MESH)

    for side in range(2):
        loads[side].wait()

        cut_columns(
            tall.at[side],
            lambda step: low(gains_ref[pl.ds(pl.multiple_of(z * part + step, 16), 16), 1:2]),
            lambda j: pair_cut.at[j],
            side * ff,
            ff,
        )

    inside_line = jnp.logical_and(z > 0, z < n - 1)

    @pl.when(inside_line)
    def _():
        pl.semaphore_wait(barrier, owners + 1)

    @pl.when(jnp.logical_not(inside_line))
    def _():
        pl.semaphore_wait(barrier, owners)

    me = place(0)
    pair_there = pair_out.at[me, own_rows, :]
    pair_moves = [
        remote(pair_cut.at[place(i)], pair_there, pair_sent.at[i], pair_got.at[i], peer(i)) for i in range(1, owners)
    ]
    for move in pair_moves:
        move.start()
    pair_own = pltpu.make_async_copy(pair_cut.at[me], pair_there, pair_sent.at[0])
    pair_own.start()

    base = block(0, 0) * rows

    def unit(here, i):
        value = x_ref[here, :].astype(f32)
        there = pl.ds(pl.multiple_of(base + i * 16, 16), 16)
        unit_ref[there, :] = (value * root_mean(value)).astype(bf16)
        labels_ref[there, :] = label_ref[here, :]

    by_tiles(rows, unit)
    label_gather = gather_steps(rows, labels_ref, label_sems)
    unit_gather = gather_steps(rows, unit_ref, unit_sems)
    next(label_gather)
    next(unit_gather)

    for side in range(2):
        loads[2 + side].wait()
        cut_columns(
            wide.at[side], lambda step: low(gains_ref[pl.ds(step, 16), 0:1]), lambda j: mix_cut.at[j, side], 0, width
        )
    mix_moves = [
        remote(mix_cut.at[place(i)], mix_ref.at[me], mix_sent.at[i], mix_got.at[i], peer(i)) for i in range(1, owners)
    ]
    for move in mix_moves:
        move.start()
    mix_own = pltpu.make_async_copy(mix_cut.at[me], mix_ref.at[me], mix_sent.at[0])
    mix_own.start()
    loads[4].wait()
    ow_ref[...] = ow_f[...].astype(bf16)
    save(ow_ref, ow_out)
    fill_small(conv_ref, bias_ref, raw_conv, raw_a, raw_b, raw_c, rate_ref)
    fill_blocks(rbig, rw_ref)
    fill_blocks(ibig, iw_ref)
    pad[0:8, :] = jnp.zeros((8, width), f32)
    taps = raw_conv.shape[0]
    clear_tail(decay_ref, width)
    clear_tail(states_ref, width)

    cuts = down_hbm.shape[0] // down_low.shape[1]
    height = down_low.shape[1]

    def down_load(k):
        return pltpu.make_async_copy(down_hbm.at[pl.ds(k * height, height), :], down_f.at[k % 2], down_sem.at[k % 2])

    def down_save(k):
        return pltpu.make_async_copy(down_low.at[k % 2], down_out.at[pl.ds(k * height, height), :], down_sem.at[2 + k % 2])

    def down_cast(k):
        down_load(k).wait()
        if k >= 2:
            down_save(k - 2).wait()
        down_low[k % 2] = down_f[k % 2].astype(bf16)
        down_save(k).start()
        if k + 2 < cuts:
            down_load(k + 2).start()

    pair_own.wait()
    for move in pair_moves:
        move.wait_recv()
    line = quarter_steps(n, part, pair_out, line_sems)
    next(line)
    next(label_gather)
    next(unit_gather)
    waits = next(label_gather) + next(unit_gather)
    for wait in waits:
        wait()
    mix_own.wait()
    for move in mix_moves:
        move.wait_recv()
    save(unit_ref, unit_out)
    save(labels_ref, labels_out)
    save(mix_ref, mix_out)

    low_own.wait()
    low_gather = gather_steps(rows, low_out, low_sems)
    next(low_gather)
    next(line)

    def one(q, _):
        here = pl.ds(pl.multiple_of(q * length, length), length)
        sequence = unit_ref[here, :]
        masks = label_masks(labels_ref, here, length, width, taps, lines)
        pre_ref[here, :] = dot_nn(sequence, whole_weight(mix_ref, 0))
        conv_in = dot_nn(sequence, whole_weight(mix_ref, 1)).astype(bf16)
        conv_in_ref[here, :] = conv_in
        pad[8 : 8 + length, :] = conv_in.astype(f32)
        total = bias_ref[0:1, :] + conv_ref[0:1, :] * pad[8 : 8 + length, :]
        for k in range(1, taps):
            total = total + conv_ref[k : k + 1, :] * pad[8 - k : 8 - k + length, :] * masks[k - 1]
        values = total.astype(bf16)
        values_ref[here, :] = values
        recur = jax.nn.sigmoid(dot_nn(values, rbig[...].astype(bf16)) + bias_ref[1:2, :])
        inject = jax.nn.sigmoid(dot_nn(values, ibig[...].astype(bf16)) + bias_ref[2:3, :])
        recur_ref[here, :] = recur
        inject_ref[here, :] = inject
        log_decay = -decay_scale * bias_ref[3:4, :] * recur
        inside = masks[0] > 0.5
        put_tiles(decay_ref, here, jnp.where(inside, jnp.exp(log_decay), 0.0))
        scale = jnp.where(inside, jnp.sqrt(minus_expm1(2.0 * log_decay)), 1.0)
        put_tiles(states_ref, here, scale * inject * values.astype(f32))
        return 0

    lax.fori_loop(0, sequences, one, 0)
    seq_scan(decay_ref, states_ref, sequences, length, False)

    def two(q, _):
        here = pl.ds(pl.multiple_of(q * length, length), length)
        act, _unused = gelu_parts(pre_ref[here, :])
        product = (act * get_tiles(states_ref, here, width)).astype(bf16)
        product_ref[here, :] = product
        partial[here, :] = dot_nn(product, ow_ref[...]).astype(bf16)
        return 0

    for k in range(2):
        down_load(k).start()
    lax.fori_loop(0, sequences, two, 0)
    scatter = scatter_steps(rows, partial, near, far, acc, scatter_sems)
    next(scatter)
    for source, target in (
        (product_ref, product_out), (pre_ref, pre_out), (conv_in_ref, conv_in_out), (values_ref, values_out),
        (recur_ref, recur_out), (inject_ref, inject_out), (decay_ref, decay_out), (states_ref, states_out),
    ):
        save(source, target)
    next(line)
    for k in range(cuts):
        down_cast(k)
    for k in range(cuts - 2, cuts):
        down_save(k).wait()
    next(low_gather)
    waits = next(low_gather) + next(scatter)

    def norm(here, i):
        middle = x_ref[here, :].astype(f32) + acc[here, :]
        middle_ref[here, :] = middle
        there = pl.ds(pl.multiple_of(base + i * 16, 16), 16)
        two_ref[there, :] = (middle * root_mean(middle)).astype(bf16)

    by_tiles(rows, norm)
    two_gather = gather_steps(rows, two_ref, two_sems)
    next(two_gather)
    save(middle_ref, middle_out)
    for _ in range(n - 4):
        next(line)
    for wait in waits:
        wait()
    next(two_gather)
    for wait in next(two_gather):
        wait()
    save(two_ref, two_out)
    for _ in line:
        pass
    for move in pair_moves + mix_moves:
        move.wait_send()
    for copy in saves:
        copy.wait()


def front(sequences, x, label, cot, gains, small, rw, iw, branch_w, input_w, gate_w, up_w, output_w, down_w):
    rows, depth = x.shape
    own, n = branch_w.shape[0], lax.axis_size("replica")
    owners = lax.axis_size(GROUP)
    total, width, ff = owners * rows, branch_w.shape[1] // owners, gate_w.shape[1] // owners
    part = own // n
    length = total // sequences
    tiles = -(-width // 128)
    kept = [
        ((total, depth), bf16), ((total, 128), bf16), ((total, depth), bf16), ((total, width), bf16),
        ((total, width), f32), ((total, width), bf16), ((total, width), bf16), ((total, width), f32),
        ((total, width), f32), ((tiles, total, 128), f32), ((tiles, total, 128), f32), ((owners, 2, own, width), bf16),
        ((width, depth), bf16), ((total, depth), bf16), ((rows, depth), f32),
    ]
    vm = pltpu.VMEM
    dma = pltpu.SemaphoreType.DMA
    scratch = [vm(*item) for k, item in enumerate(kept) if k != 2] + [
        vm((2,) + branch_w.shape, f32),
        vm((2, part, gate_w.shape[1]), f32),
        vm(output_w.shape, f32),
        vm((owners, 2, own, width), bf16),
        vm((owners, part, 2 * ff), bf16),
        vm((8 + length, width), f32),
        vm((8 + length, 128), f32),
        vm((width, width), f32),
        vm((width, width), f32),
        vm((total, depth), bf16),
        vm((8, width), f32),
        vm((8, width), f32),
        vm((2, down_w.shape[0] // 8, depth), f32),
        vm((2, down_w.shape[0] // 8, depth), bf16),
    ]
    scratch += plane_scratch(rows, depth, 4, 1)
    scratch += [dma((6,)), dma((len(kept),))] + [dma((owners,))] * 4 + [dma((4,))] + [dma((n - 1,))] * 4
    outs = kept + [((owners, own, 2 * ff), bf16), (down_w.shape, bf16)]
    return pl.pallas_call(
        functools.partial(front_kernel, n, sequences, length),
        out_shape=tuple(jax.ShapeDtypeStruct(*item) for item in outs),
        in_specs=[VM] * 11 + [ANY] * 6,
        out_specs=[ANY] * len(outs),
        scratch_shapes=scratch,
        compiler_params=pltpu.CompilerParams(
            collective_id=1, has_side_effects=True, vmem_limit_bytes=62 * 2**20
        ),
        cost_estimate=pl.CostEstimate(flops=10**6, bytes_accessed=200 * 2**20, transcendentals=0),
    )(x, label, cot, gains, *small, rw, iw, branch_w, input_w, gate_w, up_w, output_w, down_w)


def turn_steps(
    sequences, length,
    partial_hbm, middle_ref, cot_ref, label_ref, raw_conv, raw_a, raw_b, raw_c, rate_ref, rw_ref, iw_ref, *rest,
):
    kept_hbm, rest = rest[:9], rest[9:]
    low_out, grad_out, partial_out, branch_low_out, conv_low_out, packed_ref = rest[:6]
    scatter_sems, gather_sems = rest[6 + 3 : 6 + 7], rest[6 + 7 : 6 + 11]
    near, far, acc = rest[6:9]
    rest = rest[17:]
    kept, rest = rest[:9], rest[9:]
    ow_ref, w_ref, pre_ref, conv_in_ref, values_ref, recur_ref, inject_ref, decay_ref, states_ref = kept
    partial, low_ref, grad_ref, branch_low_ref, conv_low_ref, adj, pad, lines, rbig, ibig, dr, di, conv_ref, bias_ref, dconv_ref, sums_ref, load_sem, save_sem = rest
    rows = middle_ref.shape[0]
    offsets, at, block = plane()
    first = pltpu.make_async_copy(partial_hbm, partial, load_sem.at[9])
    first.start()
    loads = [pltpu.make_async_copy(kept_hbm[k], kept[k], load_sem.at[k]) for k in range(9)]
    for load in loads:
        load.start()
    first.wait()
    scatter = scatter_steps(rows, partial, near, far, acc, scatter_sems)
    next(scatter)
    yield
    waits = next(scatter)
    base = block(0, 0) * rows

    def norm(here, i):
        middle = middle_ref[here, :]
        inverse = root_mean(middle)
        grad = cot_ref[here, :].astype(f32) + norm_backward(acc[here, :], middle * inverse, inverse)
        grad_ref[here, :] = grad
        there = pl.ds(pl.multiple_of(base + i * 16, 16), 16)
        low_ref[there, :] = grad.astype(bf16)

    by_tiles(rows, norm)
    gather = gather_steps(rows, low_ref, gather_sems)
    next(gather)
    yield
    next(gather)
    yield
    waits = waits + next(gather)
    yield
    for wait in waits:
        wait()
    for load in loads:
        load.wait()
    saves = [pltpu.make_async_copy(low_ref, low_out, save_sem.at[0]), pltpu.make_async_copy(grad_ref, grad_out, save_sem.at[1])]
    for save in saves:
        save.start()
    fill_blocks(rbig, rw_ref)
    fill_blocks(ibig, iw_ref)
    dr[...] = jnp.zeros_like(dr)
    di[...] = jnp.zeros_like(di)
    sums_ref[...] = jnp.zeros_like(sums_ref)
    dconv_ref[...] = jnp.zeros_like(dconv_ref)
    taps = raw_conv.shape[0]
    fill_small(conv_ref, bias_ref, raw_conv, raw_a, raw_b, raw_c, rate_ref)
    width = pad.shape[1]
    clear_tail(adj, width)

    def one(s):
        here = pl.ds(s * length, length)
        product_grad = dot_nt(low_ref[here, :], ow_ref[...])
        act, slope = gelu_parts(pre_ref[here, :])
        branch_low_ref[here, :] = (product_grad * get_tiles(states_ref, here, width) * slope).astype(bf16)
        put_tiles(adj, here, product_grad * act)

    for s in range(sequences):
        one(s)
        yield
    seq_scan(decay_ref, adj, sequences, length, True)
    yield

    def two(s):
        here = pl.ds(s * length, length)
        adjoint = get_tiles(adj, here, width)
        recur = recur_ref[here, :]
        inject = inject_ref[here, :]
        decay = get_tiles(decay_ref, here, width)
        values = values_ref[here, :]
        values_f = values.astype(f32)
        masks = label_masks(label_ref, here, length, width, taps, lines)
        inside = masks[0] > 0.5
        rate = bias_ref[3:4, :]
        log_decay = -decay_scale * rate * recur
        scale = jnp.where(inside, jnp.sqrt(minus_expm1(2.0 * log_decay)), 1.0)
        pad[0:8, :] = jnp.zeros((8, width), f32)
        pad[8 : 8 + length, :] = get_tiles(states_ref, here, width)
        previous = pad[7 : 7 + length, :]
        driven = adjoint * inject * values_f
        log_grad = jnp.where(inside, adjoint * previous * decay - driven * decay * decay / scale, 0.0)
        recur_low = (log_grad * (-decay_scale * rate) * recur * (1.0 - recur)).astype(bf16)
        inject_low = (driven * scale * (1.0 - inject)).astype(bf16)
        sums_ref[1:2, :] += jnp.sum(recur_low.astype(f32), axis=0, keepdims=True)
        sums_ref[2:3, :] += jnp.sum(inject_low.astype(f32), axis=0, keepdims=True)
        sums_ref[3:4, :] += jnp.sum(log_grad * recur, axis=0, keepdims=True)
        dr[...] += dot_tn(values, recur_low)
        di[...] += dot_tn(values, inject_low)
        grad = adjoint * scale * inject
        grad = grad + dot_nt(recur_low, rbig[...].astype(bf16)) + dot_nt(inject_low, ibig[...].astype(bf16))
        sums_ref[0:1, :] += jnp.sum(grad, axis=0, keepdims=True)
        pad[8 : 8 + length, :] = conv_in_ref[here, :].astype(f32)
        dconv_ref[0:1, :] += jnp.sum(grad * pad[8 : 8 + length, :], axis=0, keepdims=True)
        masked = []
        for k in range(1, taps):
            part = grad * masks[k - 1]
            masked.append(part)
            dconv_ref[k : k + 1, :] += jnp.sum(part * pad[8 - k : 8 - k + length, :], axis=0, keepdims=True)
        total = grad * conv_ref[0:1, :]
        pad[length : length + 8, :] = jnp.zeros((8, width), f32)
        for k in range(1, taps):
            pad[0:length, :] = masked[k - 1] * conv_ref[k : k + 1, :]
            total = total + pad[k : k + length, :]
        conv_low = total.astype(bf16)
        conv_low_ref[here, :] = conv_low
        partial[here, :] = (dot_nt(branch_low_ref[here, :], whole_weight(w_ref, 0)) + dot_nt(conv_low, whole_weight(w_ref, 1))).astype(bf16)

    for s in range(sequences):
        two(s)
        yield
    size = rw_ref.shape[1]
    packed_ref[...] = jnp.zeros_like(packed_ref)
    for h in range(rw_ref.shape[0]):
        cut = slice(h * size, (h + 1) * size)
        packed_ref[0, cut, 0 : 2 * size] = jnp.concatenate([dr[cut, cut], di[cut, cut]], axis=1).astype(bf16)
    packed_ref[0, width : width + 16, 0:width] = jnp.concatenate([dconv_ref[...], sums_ref[...]], axis=0).astype(bf16)
    ends = [(partial, partial_out), (branch_low_ref, branch_low_out), (conv_low_ref, conv_low_out)]
    for k, pair in enumerate(ends):
        saves.append(pltpu.make_async_copy(*pair, save_sem.at[2 + k]))
        saves[-1].start()
    yield
    for save in saves:
        save.wait()


def end_steps(
    outputs_at, mixes_at,
    partial_hbm, grad_ref, x_ref, middle_ref, hidden_hbm, down_hbm, product_hbm, mid_hbm, unit_hbm, branch_hbm, conv_hbm,
    gate_sum, up_sum, gate_hbm, up_hbm, tokens_ref, block_ref, gain_ref, *rest,
):
    near, far, acc = rest[:3]
    scatter_sems, more_sems = rest[3:7], rest[7:11]
    near_two, far_two, partial, hidden, down, product, tokens_wide, branch_low, conv_low, mix_low, sums, weights = rest[11:23]
    load_sem, gain_sem, output_made, mix_made = rest[23:]
    rows = x_ref.shape[0]
    depth = down.shape[1]

    def load(k, source, target):
        copy = pltpu.make_async_copy(source, target, load_sem.at[k])
        copy.start()
        return copy

    first = load(0, mid_hbm, tokens_wide), load(1, product_hbm, product)
    loads = [
        load(2, partial_hbm, partial), load(3, branch_hbm, branch_low), load(4, conv_hbm, conv_low),
        load(5, hidden_hbm, hidden), load(6, down_hbm, down),
    ]
    for copy in first:
        copy.wait()
    for d in range(0, depth, 512):
        output_made[0, :, d : d + 512] = dot_tn(product[...], tokens_wide[:, d : d + 512]).astype(bf16)
    again = load(7, unit_hbm, tokens_wide)

    def gain_loads(r):
        here = pl.ds(r * 16, 16)
        slot = r % 2
        return [
            pltpu.make_async_copy(source.at[here, :], target.at[slot, side], gain_sem.at[slot, 2 * group + side])
            for group, (target, sources) in enumerate(((sums, (gate_sum, up_sum)), (weights, (gate_hbm, up_hbm))))
            for side, source in enumerate(sources)
        ]

    gain_steps = gain_ref.shape[0] // 16
    for r in range(2):
        for copy in gain_loads(r):
            copy.start()
    yield outputs_at
    loads[1].wait()
    loads[2].wait()
    width = branch_low.shape[1]
    if mix_low.shape[1] > 2 * width:
        mix_low[...] = jnp.zeros_like(mix_low)

    def pack(here, i):
        mix_low[here, 0 : 2 * width] = jnp.concatenate([branch_low[here, :], conv_low[here, :]], axis=1)

    by_tiles(mix_low.shape[0], pack)
    again.wait()
    owners, own = mix_made.shape[:2]
    for part in range(4):
        for j in range(part * owners // 4, (part + 1) * owners // 4):
            mix_made[j] = dot_tn(tokens_wide[:, j * own : (j + 1) * own], mix_low[...]).astype(bf16)
        yield mixes_at if part == 3 else None
    loads[0].wait()
    scatter = scatter_steps(rows, partial, near, far, acc, scatter_sems)
    next(scatter)
    yield None
    for r in range(gain_steps):
        slot = r % 2
        for copy in gain_loads(r):
            copy.wait()
        both = jnp.zeros((16, 1), f32)
        for side in range(2):
            both = both + jnp.sum(
                sums[slot, side].astype(f32) * low(weights[slot, side]), axis=1, keepdims=True
            )
        gain_ref[r * 16 : (r + 1) * 16, :] = both
        if r + 2 < gain_steps:
            for copy in gain_loads(r + 2):
                copy.start()
        yield None
    waits = next(scatter)

    def norm(here, i):
        value = x_ref[here, :].astype(f32)
        inverse = root_mean(value)
        grad = grad_ref[here, :] + norm_backward(acc[here, :], value * inverse, inverse)
        tokens_ref[here, :] = grad.astype(bf16)

    by_tiles(rows, norm)
    for wait in waits:
        wait()
    yield None
    loads[3].wait()
    loads[4].wait()
    pieces_of = 4
    height = hidden.shape[0] // pieces_of
    for k in range(pieces_of):
        here = pl.ds(k * height, height)
        partial[here, :] = dot_nn(hidden[here, :], down[...]).astype(bf16)
        yield None
    scatter = scatter_steps(rows, partial, near_two, far_two, acc, more_sems)
    next(scatter)
    yield None
    waits = next(scatter)

    def out(here, i):
        block_ref[here, :] = (middle_ref[here, :] + acc[here, :]).astype(bf16)

    by_tiles(rows, out)
    yield None
    for wait in waits:
        wait()


def mlp_kernel(
    two_hbm, low_hbm, pair_hbm, down_hbm, hidden_out, partial_out, down_out, pair_out,
    two, low_rows, pair_w, down_w, hidden, pair_low, partial, down_grad, pair_grad, load_sem, save_sem, pair_sem,
):
    total, depth = two.shape
    ff = down_w.shape[0]
    tile = 256 if ff % 256 == 0 else 128
    height = 512
    steps = total // height

    def rows_of(hbm, ref, r, which):
        here = pl.ds(r * height, height)
        return pltpu.make_async_copy(hbm.at[here, :], ref.at[here, :], load_sem.at[which, r])

    weights = [
        pltpu.make_async_copy(pair_hbm, pair_w, load_sem.at[2, 0]),
        pltpu.make_async_copy(down_hbm, down_w, load_sem.at[2, 1]),
    ]
    rows_of(two_hbm, two, 0, 0).start()
    weights[0].start()
    rows_of(low_hbm, low_rows, 0, 1).start()
    weights[1].start()
    for r in range(1, steps):
        rows_of(two_hbm, two, r, 0).start()
        rows_of(low_hbm, low_rows, r, 1).start()
    weights[0].wait()
    weights[1].wait()

    def row_step(r, _):
        here = pl.ds(pl.multiple_of(r * height, height), height)
        pltpu.make_async_copy(two_hbm.at[here, :], two.at[here, :], load_sem.at[0, r]).wait()
        pltpu.make_async_copy(low_hbm.at[here, :], low_rows.at[here, :], load_sem.at[1, r]).wait()
        for f in range(ff // tile):
            cut = slice(f * tile, (f + 1) * tile)
            more = slice(ff + f * tile, ff + (f + 1) * tile)
            gate = dot_nn(two[here, :], pair_w[:, cut])
            up = dot_nn(two[here, :], pair_w[:, more])
            grad = dot_nt(low_rows[here, :], down_w[cut, :])
            act, slope = gelu_parts(gate)
            hidden[here, cut] = (act * up).astype(bf16)
            pair_low[here, cut] = (grad * up * slope).astype(bf16)
            pair_low[here, more] = (grad * act).astype(bf16)
        for d in range(0, depth, 512):
            partial[here, d : d + 512] = dot_nt(pair_low[here, :], pair_w[d : d + 512, :]).astype(bf16)
        return 0

    lax.fori_loop(0, steps, row_step, 0)
    saves = [
        pltpu.make_async_copy(partial, partial_out, save_sem.at[0]),
        pltpu.make_async_copy(hidden, hidden_out, save_sem.at[1]),
    ]
    for save in saves:
        save.start()
    for f in range(ff // tile):
        cut = slice(f * tile, (f + 1) * tile)
        down_grad[cut, :] = dot_tn(hidden[:, cut], low_rows[...]).astype(bf16)
    saves.append(pltpu.make_async_copy(down_grad, down_out, save_sem.at[2]))
    saves[-1].start()

    height = 256

    def column_step(d, _):
        here = pl.ds(pl.multiple_of(d * height, height), height)
        pair_grad[here, :] = dot_tn(two[:, here], pair_low[...]).astype(bf16)
        pltpu.make_async_copy(pair_grad.at[here, :], pair_out.at[here, :], pair_sem.at[d]).start()
        return 0

    lax.fori_loop(0, depth // height, column_step, 0)
    for d in range(depth // height):
        here = pl.ds(d * height, height)
        pltpu.make_async_copy(pair_grad.at[here, :], pair_out.at[here, :], pair_sem.at[d]).wait()
    for save in saves:
        save.wait()


def mlp(unit_two, out_low, pair_w, down_w):
    total, depth = unit_two.shape
    ff = down_w.shape[0]
    kept = [((total, ff), bf16), ((total, depth), bf16), ((ff, depth), bf16), ((depth, 2 * ff), bf16)]
    vm, dma = pltpu.VMEM, pltpu.SemaphoreType.DMA
    return pl.pallas_call(
        mlp_kernel,
        out_shape=tuple(jax.ShapeDtypeStruct(*item) for item in kept),
        in_specs=[ANY] * 4,
        out_specs=[ANY] * 4,
        scratch_shapes=[vm(item.shape, bf16) for item in (unit_two, out_low, pair_w, down_w)]
        + [vm((total, ff), bf16), vm((total, 2 * ff), bf16)]
        + [vm(*item) for item in kept[1:]]
        + [dma((3, total // 512)), dma((3,)), dma((depth // 256,))],
        compiler_params=pltpu.CompilerParams(vmem_limit_bytes=60 * 2**20),
        cost_estimate=pl.CostEstimate(
            flops=2 * total * depth * ff * 8, bytes_accessed=36 * 2**20, transcendentals=total * ff
        ),
    )(unit_two, out_low, pair_w, down_w)


def pieces(rows, most):
    count = -(-rows // most)
    while rows % count or (rows // count) % 16:
        count += 1
    return count


def chunk_count(height, columns):
    return pieces(height, max(16, (105 * 1024) // columns // 16 * 16))


def line_kernel(n, kinds, cuts, made_here, beside, turns, extra, *refs):
    ins = len(cuts)
    made = ins + kinds.count("pair")
    extra_ins, extra_outs, extra_scratch = extra
    refs = list(refs)

    def take(count):
        taken = refs[:count]
        del refs[:count]
        return taken

    given = [k for k in range(ins) if k not in made_here]
    own_hbm, side_in = dict(zip(given, take(len(given)))), take(extra_ins)
    outs, side_out = take(made), take(extra_outs)
    side_scratch = take(extra_scratch)
    from_out, from_in = take(ins), take(ins)
    own_made = dict(zip(made_here, take(len(made_here))))
    slots, whole_sem, slot_sem, sent_in, sent_out, got_out, got_in, sent_x, got_x = refs
    depth = slots.shape[0]
    me = lax.axis_index("replica")
    y, s = lax.axis_index("seq"), lax.axis_index("shard")
    shards = lax.axis_size("shard")
    owners = shards * lax.axis_size("seq")
    left = me < n // 2
    inward = jnp.where(left, me + 1, me - 1)
    outward = jnp.where(left, me - 1, me + 1)
    has_out = jnp.logical_and(me > 0, me < n - 1)
    at_end = jnp.logical_not(has_out)
    middle = jnp.logical_or(me == n // 2 - 1, me == n // 2)

    def peer(i):
        return {"seq": jnp.bitwise_xor(y, i // shards), "shard": jnp.bitwise_xor(s, i % shards)}

    def place(i):
        return jnp.bitwise_xor(y, i // shards) * shards + jnp.bitwise_xor(s, i % shards)

    chunks = []
    for k, (lead, count, rows) in enumerate(cuts):
        for step in range(lead):
            for i in range(count):
                chunks.append((k, step if kinds[k] == "row" else (step + 1) % lead, i * rows, rows))
    total = len(chunks)

    def view(group, c):
        k, i, start, rows = chunks[c]
        return group[k].at[0 if kinds[k] == "row" else place(i), pl.ds(start, rows), :]

    def slot(c):
        k, i, start, rows = chunks[c]
        return slots.at[c % depth, pl.ds(0, rows), pl.ds(0, from_in[k].shape[2])]

    def load(c):
        return pltpu.make_async_copy(view(own_hbm, c), slot(c), slot_sem.at[c % depth])

    wholes = {k: pltpu.make_async_copy(own_hbm[k], from_out[k], whole_sem.at[k]) for k in given}
    loaded = [c for c in range(total) if chunks[c][0] in given]

    @pl.when(at_end)
    def _():
        for k in given:
            wholes[k].start()

    @pl.when(has_out)
    def _():
        for c in loaded[: depth - 1]:
            load(c).start()

    barrier = pltpu.get_barrier_semaphore()
    for i in range(1, owners):
        pl.semaphore_signal(barrier, inc=1, device_id=peer(i), device_id_type=MESH)
    pl.semaphore_signal(barrier, inc=1, device_id={"replica": inward}, device_id_type=MESH)

    @pl.when(has_out)
    def _():
        pl.semaphore_signal(barrier, inc=1, device_id={"replica": outward}, device_id_type=MESH)
        pl.semaphore_wait(barrier, owners + 1)

    @pl.when(at_end)
    def _():
        pl.semaphore_wait(barrier, owners)

    def push(group, target, c, sent, got, device):
        return remote(view(group, c), view(target, c), sent.at[c], got.at[c], {"replica": device})

    def add(target, other, c):
        k, i, start, rows = chunks[c]
        if other is None:
            more = view(own_made, c) if k in made_here else slot(c)
        else:
            more = view(other, c)
        into = view(target, c)

        def tile(t, _):
            here = pl.ds(pl.multiple_of(t * 16, 16), 16)
            into[here, :] = (into[here, :].astype(f32) + more[here, :].astype(f32)).astype(bf16)
            return 0

        lax.fori_loop(0, rows // 16, tile, 0)

    def pass_in(c, source):
        @pl.when(middle)
        def _():
            push(source, from_in, c, sent_in, got_in, inward).start()

        @pl.when(jnp.logical_not(middle))
        def _():
            push(source, from_out, c, sent_in, got_out, inward).start()

    def gather_in(c):
        @pl.when(has_out)
        def _():
            if c in loaded:
                load(c).wait()
            push(from_out, from_out, c, sent_in, got_out, inward).wait_recv()
            add(from_out, None, c)
            pass_in(c, from_out)
            if c + depth - 1 in loaded:
                load(c + depth - 1).start()

    @pl.when(at_end)
    def _():
        for c in loaded:
            if c == 0 or chunks[c][0] != chunks[c - 1][0]:
                wholes[chunks[c][0]].wait()
            pass_in(c, from_out)

    def advance():
        k = next(work)
        if k is not None:

            @pl.when(at_end)
            def _():
                for c in range(total):
                    if chunks[c][0] == k:
                        pass_in(c, own_made)

    work = beside(*side_in, *side_out, *side_scratch, *[own_made[k] for k in made_here])
    advance()

    def deliveries(c):
        k, i, start, rows = chunks[c]
        here = pl.ds(start, rows)
        first = k + kinds[:k].count("pair")
        source = view(from_in, c)
        if kinds[k] == "row":
            ends = [(source, outs[first].at[here, :])]
        elif kinds[k] == "side":
            ends = [(source, outs[first].at[place(0), here, :])]
        else:
            half = source.shape[1] // 2
            there = pl.ds(pl.multiple_of(place(0) * half, half), half)
            ends = [
                (source.at[:, pl.ds(part * half, half)], outs[first + part].at[here, there]) for part in range(2)
            ]
        if kinds[k] == "row" or i == 0:
            return [pltpu.make_async_copy(*pair, sent_x.at[c, p]) for p, pair in enumerate(ends)], False
        return [remote(*pair, sent_x.at[c, p], got_x.at[c, p], peer(i)) for p, pair in enumerate(ends)], True

    def give_back(c):
        push(from_out, from_in, c, sent_out, got_in, inward).wait_recv()

        @pl.when(middle)
        def _():
            add(from_in, from_out, c)

        @pl.when(has_out)
        def _():
            push(from_in, from_in, c, sent_out, got_in, outward).start()

        for copy in deliveries(c)[0]:
            copy.start()

    lag = 1
    for c in range(total + lag):
        for _ in range(turns.count(c)):
            advance()
        if c < total:
            gather_in(c)
        if c >= lag:
            give_back(c - lag)
    for _ in work:
        pass
    for c in range(total):
        copies, away = deliveries(c)
        for copy in copies:
            if away:
                copy.wait_recv()
                copy.wait_send()
            else:
                copy.wait()
        push(from_out, from_in, c, sent_in, got_in, inward).wait_send()

        @pl.when(has_out)
        def _():
            push(from_in, from_in, c, sent_out, got_in, outward).wait_send()


def replica_sum(arrays, kinds, made_here, identity, beside, turns, inputs, results, side_scratch):
    cuts, outs = [], []
    tall = broad = 0
    for item, kind in zip(arrays, kinds):
        lead, height, columns = item.shape
        count = chunk_count(height, columns)
        cuts.append((lead, count, height // count))
        tall, broad = max(tall, height // count), max(broad, columns)
        if kind == "pair":
            outs += [jax.ShapeDtypeStruct((height, lead * columns // 2), bf16)] * 2
        elif kind == "side":
            outs.append(jax.ShapeDtypeStruct(item.shape, bf16))
        else:
            outs.append(jax.ShapeDtypeStruct((height, columns), bf16))
    count = sum(lead * cut for lead, cut, _ in cuts)
    buffers = [pltpu.VMEM(item.shape, bf16) for item in arrays]
    dma = pltpu.SemaphoreType.DMA
    return pl.pallas_call(
        functools.partial(
            line_kernel, lax.axis_size("replica"), tuple(kinds), tuple(cuts), tuple(made_here), beside, turns,
            (len(inputs), len(results), len(side_scratch)),
        ),
        out_shape=tuple(outs) + tuple(jax.ShapeDtypeStruct(shape, kind) for shape, kind, _ in results),
        in_specs=[ANY] * (len(arrays) - len(made_here)) + [spec for _, spec in inputs],
        out_specs=[ANY] * len(outs) + [spec for _, _, spec in results],
        scratch_shapes=list(side_scratch)
        + buffers * 2
        + [buffers[k] for k in made_here]
        + [pltpu.VMEM((4, tall, broad), bf16), dma((len(arrays),)), dma((4,))]
        + [dma((count,))] * 4
        + [dma((count, 2))] * 2,
        compiler_params=pltpu.CompilerParams(
            collective_id=identity, has_side_effects=True, vmem_limit_bytes=62 * 2**20
        ),
        cost_estimate=pl.CostEstimate(flops=10**6, bytes_accessed=200 * 2**20, transcendentals=0),
    )(*[item for k, item in enumerate(arrays) if k not in made_here], *[item for item, _ in inputs])


def finish_pair_kernel(gain_ref, a_ref, b_ref, outa_ref, outb_ref):
    gain = low(gain_ref[:, 1:2])
    outa_ref[...] = a_ref[...].astype(f32) * gain
    outb_ref[...] = b_ref[...].astype(f32) * gain


def finish_pair(gain, a, b):
    rows, columns = a.shape
    cut = min(rows, 64)
    wide = pl.BlockSpec((cut, columns), lambda i: (i, 0))
    out = jax.ShapeDtypeStruct((rows, columns), f32)
    return pl.pallas_call(
        finish_pair_kernel,
        grid=(rows // cut,),
        out_shape=(out, out),
        in_specs=[pl.BlockSpec((cut, 2), lambda i: (i, 0)), wide, wide],
        out_specs=[wide, wide],
        compiler_params=pltpu.CompilerParams(vmem_limit_bytes=62 * 2**20),
        cost_estimate=pl.CostEstimate(flops=2 * rows * columns, bytes_accessed=12 * rows * columns, transcendentals=0),
    )(gain, a, b)


def finish_rest_kernel(gain_ref, mix_ref, wa_ref, wb_ref, out_sum_ref, down_sum_ref, outa_ref, outb_ref, grad_ref, out_ref, down_ref):
    owners = mix_ref.shape[0]
    width = wa_ref.shape[1] // owners
    gain = low(gain_ref[:, 0:1])
    grad = jnp.zeros(gain.shape, f32)
    for part, (weight_ref, target_ref) in enumerate(((wa_ref, outa_ref), (wb_ref, outb_ref))):
        total = jnp.concatenate(
            [mix_ref[j, :, part * width : (part + 1) * width].astype(f32) for j in range(owners)], axis=1
        )
        target_ref[...] = total * gain
        grad = grad + jnp.sum(total * low(weight_ref[...]), axis=1, keepdims=True)
    grad_ref[...] = grad
    out_ref[...] = out_sum_ref[...].astype(f32)
    down_ref[...] = down_sum_ref[...].astype(f32)


def finish_rest(gain, mix, wa, wb, out_sum, down_sum):
    rows, columns = wa.shape
    steps = 4
    while out_sum.shape[0] % (16 * steps) or down_sum.shape[0] % (16 * steps) or rows % (16 * steps):
        steps //= 2

    def tall(item):
        return pl.BlockSpec((item.shape[0] // steps, item.shape[1]), lambda i: (i, 0))

    owners, _, both = mix.shape
    wide, thin = tall(wa), pl.BlockSpec((rows // steps, 1), lambda i: (i, 0))
    return pl.pallas_call(
        finish_rest_kernel,
        grid=(steps,),
        out_shape=(
            jax.ShapeDtypeStruct(wa.shape, f32),
            jax.ShapeDtypeStruct(wa.shape, f32),
            jax.ShapeDtypeStruct((rows, 1), f32),
            jax.ShapeDtypeStruct(out_sum.shape, f32),
            jax.ShapeDtypeStruct(down_sum.shape, f32),
        ),
        in_specs=[
            tall(gain),
            pl.BlockSpec((owners, rows // steps, both), lambda i: (0, i, 0)),
            wide,
            wide,
            tall(out_sum),
            tall(down_sum),
        ],
        out_specs=[wide, wide, thin, tall(out_sum), tall(down_sum)],
        compiler_params=pltpu.CompilerParams(vmem_limit_bytes=62 * 2**20),
        cost_estimate=pl.CostEstimate(flops=10**7, bytes_accessed=40 * 2**20, transcendentals=0),
    )(gain, mix, wa, wb, out_sum, down_sum)


def body(
    tokens,
    segments,
    cotangent,
    norm_gain,
    branch_weight,
    input_weight,
    conv_weight,
    conv_bias,
    recur_gate_weight,
    recur_gate_bias,
    input_gate_weight,
    input_gate_bias,
    decay_param,
    output_weight,
    mlp_norm_gain,
    gate_weight,
    up_weight,
    down_weight,
):
    x, cot = tokens[0], cotangent[0]
    rows, depth = x.shape
    members = lax.axis_size(GROUP)
    sequences = lax.axis_size("shard")
    total = members * rows
    gains = jnp.stack([norm_gain, mlp_norm_gain], 1)
    own_labels = jnp.broadcast_to(segments[0].astype(bf16)[:, None], (rows, 128))
    width = branch_weight.shape[1] // members
    decay_f = low(decay_param)
    small = (
        conv_weight, conv_bias, recur_gate_bias, input_gate_bias, jax.nn.softplus(-decay_f),
    )
    (
        unit_all, labels, out_low, product, *mixed, mix_w, output_w, unit_two, middle, pair_w, down_w,
    ) = front(
        sequences, x, own_labels, cot, gains, small,
        recur_gate_weight, input_gate_weight, branch_weight, input_weight, gate_weight, up_weight, output_weight,
        down_weight,
    )
    pair_w = pair_w.reshape(depth, -1)
    whole = ((total, depth), bf16)
    hidden, partial, down_partial, pair_partial = mlp(unit_two, out_low, pair_w, down_w)
    down_partial = down_partial[None]
    pair_partial = pair_partial.reshape(members, -1, pair_w.shape[1])
    kept = (output_w, mix_w, *mixed)
    narrow = ((total, width), bf16)
    vm, dma = pltpu.VMEM, pltpu.SemaphoreType.DMA
    length = total // sequences
    size = recur_gate_weight.shape[1]
    lanes = -(-max(width, 2 * size) // 128) * 128
    back = replica_sum(
        [down_partial, pair_partial], ["row", "pair"], (), 3,
        functools.partial(turn_steps, sequences, length),
        (6, 9, 12) + tuple(range(14, 14 + 2 * sequences + 2)),
        [(partial, ANY)] + [(item, VM) for item in (middle, cot, labels, *small, recur_gate_weight, input_gate_weight)]
        + [(item, ANY) for item in kept],
        [whole + (ANY,), ((rows, depth), f32, ANY), whole + (ANY,), narrow + (ANY,), narrow + (ANY,)]
        + [((1, width + 16, lanes), bf16, VM)],
        plane_scratch(rows, depth, 1, 1)
        + [vm(item.shape, item.dtype) for item in kept]
        + [vm(*whole), vm(*whole), vm((rows, depth), f32), vm(*narrow), vm(*narrow), vm(mixed[-1].shape, f32)]
        + [vm((8 + length, width), f32), vm((8 + length, 128), f32)]
        + [vm((width, width), f32)] * 4
        + [vm((8, width), f32)] * 2
        + [vm((8, width), f32), vm((8, width), f32)]
        + [dma((10,)), dma((5,))],
    )
    down_sum, gate_sum, up_sum, mid_low, middle_grad, partial, branch_low, conv_low = back[:8]
    packed = back[8]
    both = -(-2 * width // 128) * 128
    mix_shape = jax.ShapeDtypeStruct((members, depth // members, both), bf16)
    output_shape = jax.ShapeDtypeStruct((1,) + output_w.shape, bf16)
    ahead = sum(chunk_count(*item.shape[1:]) for item in (packed, output_shape))
    made_by = tuple(min(2 * k, ahead) for k in (1, 2, 3, 4))
    again = plane_scratch(rows, depth, 0, 1)
    packed, output_sum, mix_sum, tokens_grad, block_out, mlp_gain_grad = replica_sum(
        [packed, output_shape, mix_shape], ["row", "row", "side"], (1, 2), 4, functools.partial(end_steps, 1, 2),
        made_by + (10, 19, 20, 21, 22, 23, 24, 30) + tuple(11 + i // 2 for i in range(gate_weight.shape[0] // 16)),
        [(partial, ANY), (middle_grad, VM), (x, VM), (middle, VM)]
        + [(item, ANY) for item in (hidden, down_w, product, mid_low, unit_all, branch_low, conv_low, gate_sum, up_sum, gate_weight, up_weight)],
        [((rows, depth), bf16, VM), ((rows, depth), bf16, VM), ((gate_weight.shape[0], 1), f32, VM)],
        again + again[3:] + again[:2] + [vm(*whole), vm(hidden.shape, bf16), vm(down_w.shape, bf16)]
        + [vm(*narrow), vm(*whole), vm(*narrow), vm(*narrow), vm((total, both), bf16)]
        + [vm((2, 2, 16, gate_weight.shape[1]), bf16), vm((2, 2, 16, gate_weight.shape[1]), f32), dma((8,)), dma((2, 4))],
    )
    packed = packed.astype(f32)
    gate_grad, up_grad = finish_pair(gains, gate_sum, up_sum)
    branch_grad, input_grad, gain_grad, output_grad, down_grad = finish_rest(
        gains, mix_sum, branch_weight, input_weight, output_sum, down_sum
    )
    recur_weight_grad = packed[:width, :size].reshape(-1, size, size)
    inject_weight_grad = packed[:width, size : 2 * size].reshape(-1, size, size)
    conv_weight_grad = packed[width : width + conv_weight.shape[0], :width]
    conv_bias_grad, recur_bias_grad, inject_bias_grad, rate_grad = [packed[width + 8 + i, :width] for i in range(4)]
    decay_param_grad = rate_grad * decay_scale * jax.nn.sigmoid(-decay_f)
    return (
        block_out[None],
        tokens_grad[None],
        gain_grad[:, 0],
        branch_grad,
        input_grad,
        conv_weight_grad,
        conv_bias_grad,
        recur_weight_grad,
        recur_bias_grad,
        inject_weight_grad,
        inject_bias_grad,
        decay_param_grad,
        output_grad,
        mlp_gain_grad[:, 0],
        gate_grad,
        up_grad,
        down_grad,
    )


def solution(mesh):
    row3 = P(("shard", "replica"), "seq", None)
    vec = P(("seq", "shard"))
    mat = P(("seq", "shard"), None)
    cube = P(("seq", "shard"), None, None)
    taps = P(None, ("seq", "shard"))
    params = (vec, mat, mat, taps, vec, cube, vec, cube, vec, vec, mat, vec, mat, mat, mat)
    in_specs = (row3, P(("shard", "replica"), "seq"), row3) + params
    out_specs = (row3, row3) + params
    return jax.shard_map(body, mesh=mesh, in_specs=in_specs, out_specs=out_specs, check_vma=False)
```

```python
import functools

import jax
import jax.numpy as jnp
from jax import lax
from jax.experimental import pallas as pl
from jax.experimental.pallas import tpu as pltpu
from jax.sharding import PartitionSpec as P

epsilon = 1e-06
decay_scale = 8.0
GROUP = ("seq", "shard")
ROWS = ("shard", "seq")
f32 = jnp.float32
bf16 = jnp.bfloat16
VM = pl.BlockSpec(memory_space=pltpu.VMEM)
ANY = pl.BlockSpec(memory_space=pl.ANY)
MESH = pl.DeviceIdType.MESH


def mm(left, right):
    return jnp.dot(left, right, preferred_element_type=f32)


def mm_nt(left, right):
    return lax.dot_general(left, right, (((1,), (1,)), ((), ())), preferred_element_type=f32)


def mm_tn(left, right):
    return lax.dot_general(left, right, (((0,), (0,)), ((), ())), preferred_element_type=f32)


def low(item):
    return item.astype(bf16).astype(f32)


def by_owner(weight, gain):
    owners = lax.axis_size(GROUP)
    scaled = (low(weight) * gain).astype(bf16)
    return jnp.swapaxes(scaled.reshape(weight.shape[0], owners, -1), 0, 1)


def swap(cut):
    return lax.all_to_all(cut, GROUP, split_axis=0, concat_axis=0, tiled=True)


def gelu_parts(x):
    inner = 0.7978845608028654 * (x + 0.044715 * x * x * x)
    t = jnp.tanh(inner)
    value = 0.5 * x * (1.0 + t)
    slope = 0.5 * (1.0 + t) + 0.5 * x * (1.0 - t * t) * 0.7978845608028654 * (
        1.0 + 3.0 * 0.044715 * x * x
    )
    return value, slope


def minus_expm1(y):
    poly = 1.0 + y * (1.0 / 8.0)
    for order in (7.0, 6.0, 5.0, 4.0, 3.0, 2.0):
        poly = 1.0 + y * (1.0 / order) * poly
    return jnp.where(y > -0.5, -y * poly, 1.0 - jnp.exp(y))


def dot_nn(a, b):
    return lax.dot_general(a, b, (((1,), (0,)), ((), ())), preferred_element_type=f32)


def dot_nt(a, b):
    return lax.dot_general(a, b, (((1,), (1,)), ((), ())), preferred_element_type=f32)


def dot_tn(a, b):
    return lax.dot_general(a, b, (((0,), (0,)), ((), ())), preferred_element_type=f32)


def whole_weight(ref, part):
    owners, _, rows, width = ref.shape
    return ref[:, part].reshape(owners * rows, width)


def fill_blocks(target, source):
    target[...] = jnp.zeros_like(target)
    count, size = source.shape[0], source.shape[1]
    for h in range(count):
        target[h * size : (h + 1) * size, h * size : (h + 1) * size] = source[h].astype(bf16).astype(f32)


def put_tiles(ref, here, value):
    width = value.shape[1]
    for tile in range(ref.shape[0]):
        lanes = min(128, width - 128 * tile)
        ref[tile, here, 0:lanes] = value[:, 128 * tile : 128 * tile + lanes]


def get_tiles(ref, here, width):
    parts = [ref[tile, here, 0 : min(128, width - 128 * tile)] for tile in range(ref.shape[0])]
    return jnp.concatenate(parts, axis=1)


def clear_tail(ref, width):
    tail = ref.shape[0] * 128 - width
    if tail:
        ref[ref.shape[0] - 1, :, 128 - tail :] = jnp.zeros((ref.shape[1], tail), f32)


def fill_small(conv, bias, raw_conv, raw_a, raw_b, raw_c, rate):
    conv[0 : raw_conv.shape[0], :] = low(raw_conv[...])
    for row, ref in enumerate((raw_a, raw_b, raw_c)):
        bias[row : row + 1, :] = low(ref[...])[None, :]
    bias[3:4, :] = rate[...][None, :]


def label_masks(label_ref, here, length, width, taps, lines):
    own = label_ref[here, :].astype(f32)
    lines[0:8, :] = jnp.full((8, 128), -1.0, f32)
    lines[8 : 8 + length, :] = own
    masks = []
    for k in range(1, taps):
        same = jnp.where(lines[8 - k : 8 - k + length, :] == own, 1.0, 0.0)
        masks.append(jnp.concatenate([same] * -(-width // 128), axis=1)[:, :width])
    return masks


def seq_scan(decay_ref, value_ref, sequences, length, reverse):
    tiles = decay_ref.shape[0]
    unroll = 8

    def step(i, states):
        states = list(states)
        for j in range(unroll):
            at = i * unroll + j
            if reverse:
                at = length - 1 - at
            here = pl.ds(at, sequences, stride=length)
            for tile in range(tiles):
                value = value_ref[tile, here, :]
                decay = decay_ref[tile, here, :]
                if reverse:
                    new = value + states[tile]
                    value_ref[tile, here, :] = new
                    states[tile] = decay * new
                else:
                    states[tile] = value + decay * states[tile]
                    value_ref[tile, here, :] = states[tile]
        return tuple(states)

    lax.fori_loop(0, length // unroll, step, (jnp.zeros((sequences, 128), f32),) * tiles)


def plane():
    halves, shards = lax.axis_size("seq"), lax.axis_size("shard")
    y, s = lax.axis_index("seq"), lax.axis_index("shard")
    offsets = [(dy, ds) for ds in range(0, shards, 2) for dy in range(halves)]

    def at(dy, ds):
        return {"seq": jnp.bitwise_xor(y, dy), "shard": jnp.bitwise_xor(s, ds)}

    def block(dy, ds):
        return jnp.bitwise_xor(s, ds) * halves + jnp.bitwise_xor(y, dy)

    return offsets, at, block


def remote(src, dst, sent, got, device):
    return pltpu.make_async_remote_copy(
        src_ref=src, dst_ref=dst, send_sem=sent, recv_sem=got, device_id=device, device_id_type=MESH
    )


def row_block(ref, index, rows):
    return ref.at[pl.ds(pl.multiple_of(index * rows, rows), rows), :]


def scatter_steps(rows, partial, near, far, acc, sems):
    offsets, at, block = plane()
    near_sent, near_got, far_sent, far_got = sems
    count = len(offsets)
    order = list(range(count - 1, -1, -1))
    firsts = {}
    for q in order:
        dy, ds = offsets[q]
        firsts[q] = remote(
            row_block(partial, block(dy, ds ^ 1), rows), near.at[q], near_sent.at[q], near_got.at[q], at(0, 1)
        )
        firsts[q].start()
    seconds = {}
    for q in order:
        dy, ds = offsets[q]
        firsts[q].wait_recv()
        base = block(dy, ds) * rows

        def tile(i, _):
            step = pl.multiple_of(i * 16, 16)
            here = pl.ds(step, 16)
            total = partial[pl.ds(pl.multiple_of(base + step, 16), 16), :].astype(f32) + near[q, here, :].astype(f32)
            if q:
                near[q, here, :] = total.astype(bf16)
            else:
                acc[here, :] = total
            return 0

        lax.fori_loop(0, rows // 16, tile, 0)
        if q:
            seconds[q] = remote(near.at[q], far.at[q - 1], far_sent.at[q - 1], far_got.at[q - 1], at(dy, ds))
            seconds[q].start()
    yield None
    for q in order[:-1]:
        seconds[q].wait_recv()

        def more(i, _):
            here = pl.ds(pl.multiple_of(i * 16, 16), 16)
            acc[here, :] += far[q - 1, here, :].astype(f32)
            return 0

        lax.fori_loop(0, rows // 16, more, 0)
    yield [firsts[q].wait_send for q in order] + [seconds[q].wait_send for q in order[:-1]]


def gather_steps(rows, whole, sems):
    offsets, at, block = plane()
    near_sent, near_got, far_sent, far_got = sems
    count = len(offsets)
    half = rows // 2

    def piece(q, part):
        start = pl.multiple_of(block(*offsets[q]) * rows + part * half, 16)
        return whole.at[pl.ds(start, half), :]

    own = row_block(whole, block(0, 0), rows)
    straight = [q for q in range(1, count) if offsets[q][0] == 0 or offsets[q][1] == 0]
    across = [q for q in range(1, count) if q not in straight]
    upright = [q for q in straight if offsets[q][0]]
    sends, arrivals = [], []
    outs = {}
    for q in straight:
        outs[q] = remote(own, own, far_sent.at[q], far_got.at[q], at(*offsets[q]))
        outs[q].start()
        sends.append(outs[q].wait_send)

    def hand(q, part=None):
        source = row_block(whole, block(*offsets[q]), rows) if part is None else piece(q, part)
        place = q if part is None or part == 0 else count + q
        copy = remote(source, source, near_sent.at[place], near_got.at[place], at(0, 1))
        copy.start()
        sends.append(copy.wait_send)
        arrivals.append(copy.wait_recv)

    hand(0)
    yield None
    onward = {}
    for q in straight:
        outs[q].wait_recv()
        if q in upright:
            targets = [(1, t) for t in straight if t not in upright]
        else:
            targets = [(0, t) for t in upright]
        for part, t in targets:
            dy, ds = offsets[q][0] | offsets[t][0], offsets[q][1] | offsets[t][1]
            a = offsets.index((dy, ds))
            source = piece(q, part)
            onward[a, part] = remote(source, source, far_sent.at[part * count + a], far_got.at[part * count + a], at(*offsets[t]))
            onward[a, part].start()
            sends.append(onward[a, part].wait_send)
        hand(q)
    yield None
    for a in across:
        for part in range(2):
            onward[a, part].wait_recv()
            hand(a, part)
    yield arrivals + sends


def root_mean(rows):
    return lax.rsqrt(jnp.mean(rows * rows, axis=-1, keepdims=True) + epsilon)


def norm_backward(grad_unit, unit, inverse):
    return inverse * (grad_unit - unit * jnp.mean(grad_unit * unit, axis=-1, keepdims=True))


def by_tiles(rows, work):
    def tile(i, _):
        work(pl.ds(pl.multiple_of(i * 16, 16), 16), i)
        return 0

    lax.fori_loop(0, rows // 16, tile, 0)


def plane_scratch(rows, depth, gathers, scatters):
    count = lax.axis_size("seq") * lax.axis_size("shard") // 2
    block = (rows, depth)
    scratch = []
    if scatters:
        scratch = [
            pltpu.VMEM((count,) + block, bf16),
            pltpu.VMEM((count - 1,) + block, bf16),
            pltpu.VMEM(block, f32),
        ]
    dma = pltpu.SemaphoreType.DMA
    for _ in range(scatters):
        scratch += [dma((count,))] * 2 + [dma((count - 1,))] * 2
    for _ in range(gathers):
        scratch += [dma((2 * count,))] * 4
    return scratch


def cut_columns(weight_ref, gain, target, start, lanes):
    owners = weight_ref.shape[1] // lanes

    def tile(i, _):
        step = pl.multiple_of(i * 16, 16)
        here = pl.ds(step, 16)
        scaled = low(weight_ref[here, :]) * gain(step)
        for j in range(owners):
            target(j)[here, start : start + lanes] = scaled[:, j * lanes : (j + 1) * lanes].astype(bf16)
        return 0

    lax.fori_loop(0, weight_ref.shape[0] // 16, tile, 0)


def quarter_steps(n, part, whole, sems):
    me = lax.axis_index("replica")
    right_sent, right_got, left_sent, left_got = sems

    def rows(q):
        return whole.at[:, pl.ds(pl.multiple_of(q * part, 16), part), :]

    def to_right(hop):
        block = rows(me - hop)
        return remote(block, block, right_sent.at[hop], right_got.at[hop], {"replica": me + 1})

    def to_left(hop):
        block = rows(me + hop)
        return remote(block, block, left_sent.at[hop], left_got.at[hop], {"replica": me - 1})

    def from_left(hop):
        block = rows(me - hop - 1)
        return remote(block, block, right_sent.at[hop], right_got.at[hop], {"replica": me + 1})

    def from_right(hop):
        block = rows(me + hop + 1)
        return remote(block, block, left_sent.at[hop], left_got.at[hop], {"replica": me - 1})

    for hop in range(n - 1):
        if hop:

            @pl.when(me >= hop)
            def _():
                from_left(hop - 1).wait_recv()

            @pl.when(me + hop < n)
            def _():
                from_right(hop - 1).wait_recv()

        @pl.when(jnp.logical_and(me >= hop, me < n - 1))
        def _():
            to_right(hop).start()

        @pl.when(jnp.logical_and(me + hop < n, me > 0))
        def _():
            to_left(hop).start()

        yield

    @pl.when(me >= n - 1)
    def _():
        from_left(n - 2).wait_recv()

    @pl.when(me + n - 1 < n)
    def _():
        from_right(n - 2).wait_recv()

    for hop in range(n - 1):

        @pl.when(jnp.logical_and(me >= hop, me < n - 1))
        def _():
            to_right(hop).wait_send()

        @pl.when(jnp.logical_and(me + hop < n, me > 0))
        def _():
            to_left(hop).wait_send()

    yield


def front_kernel(
    n, sequences, length,
    x_ref, label_ref, cot_ref, gains_ref, raw_conv, raw_a, raw_b, raw_c, rate_ref, rw_ref, iw_ref,
    branch_hbm, input_hbm, gate_hbm, up_hbm, ow_hbm, down_hbm,
    unit_out, labels_out, low_out, product_out, pre_out, conv_in_out, values_out, recur_out, inject_out, decay_out,
    states_out, mix_out, ow_out, two_out, middle_out, pair_out, down_out,
    unit_ref, labels_ref, product_ref, pre_ref, conv_in_ref, values_ref, recur_ref, inject_ref, decay_ref,
    states_ref, mix_ref, ow_ref, two_ref, middle_ref,
    wide, tall, ow_f, mix_cut, pair_cut, pad, lines, rbig, ibig, partial, conv_ref, bias_ref, down_f, down_low,
    near, far, acc, *sems,
):
    rows = x_ref.shape[0]
    scatter_sems, sems = sems[:4], sems[4:]
    unit_sems, label_sems, low_sems, two_sems, sems = sems[:4], sems[4:8], sems[8:12], sems[12:16], sems[16:]
    load_sem, save_sem, mix_sent, mix_got, pair_sent, pair_got, down_sem = sems[:7]
    line_sems = sems[7:]
    offsets, at, block = plane()
    z = lax.axis_index("replica")
    y, s = lax.axis_index("seq"), lax.axis_index("shard")
    shards = lax.axis_size("shard")
    owners = shards * lax.axis_size("seq")
    part = gate_hbm.shape[0] // n
    width = pad.shape[1]
    ff = gate_hbm.shape[1] // owners

    def peer(i):
        return {"seq": jnp.bitwise_xor(y, i // shards), "shard": jnp.bitwise_xor(s, i % shards)}

    def place(i):
        return jnp.bitwise_xor(y, i // shards) * shards + jnp.bitwise_xor(s, i % shards)

    own_rows = pl.ds(pl.multiple_of(z * part, 16), part)
    loads = [
        pltpu.make_async_copy(gate_hbm.at[own_rows, :], tall.at[0], load_sem.at[0]),
        pltpu.make_async_copy(up_hbm.at[own_rows, :], tall.at[1], load_sem.at[1]),
        pltpu.make_async_copy(branch_hbm, wide.at[0], load_sem.at[2]),
        pltpu.make_async_copy(input_hbm, wide.at[1], load_sem.at[3]),
        pltpu.make_async_copy(ow_hbm, ow_f, load_sem.at[4]),
    ]
    for load in loads:
        load.start()
    saves = []

    def save(source, target):
        copy = pltpu.make_async_copy(source, target, save_sem.at[len(saves)])
        copy.start()
        saves.append(copy)

    low_own = pltpu.make_async_copy(cot_ref, row_block(low_out, block(0, 0), rows), load_sem.at[5])
    low_own.start()
    barrier = pltpu.get_barrier_semaphore()
    for i in range(1, owners):
        pl.semaphore_signal(barrier, inc=1, device_id=peer(i), device_id_type=MESH)

    @pl.when(z > 0)
    def _():
        pl.semaphore_signal(barrier, inc=1, device_id={"replica": z - 1}, device_id_type=MESH)

    @pl.when(z < n - 1)
    def _():
        pl.semaphore_signal(barrier, inc=1, device_id={"replica": z + 1}, device_id_type=MESH)

    for side in range(2):
        loads[side].wait()

        cut_columns(
            tall.at[side],
            lambda step: low(gains_ref[pl.ds(pl.multiple_of(z * part + step, 16), 16), 1:2]),
            lambda j: pair_cut.at[j],
            side * ff,
            ff,
        )

    inside_line = jnp.logical_and(z > 0, z < n - 1)

    @pl.when(inside_line)
    def _():
        pl.semaphore_wait(barrier, owners + 1)

    @pl.when(jnp.logical_not(inside_line))
    def _():
        pl.semaphore_wait(barrier, owners)

    me = place(0)
    pair_there = pair_out.at[me, own_rows, :]
    pair_moves = [
        remote(pair_cut.at[place(i)], pair_there, pair_sent.at[i], pair_got.at[i], peer(i)) for i in range(1, owners)
    ]
    for move in pair_moves:
        move.start()
    pair_own = pltpu.make_async_copy(pair_cut.at[me], pair_there, pair_sent.at[0])
    pair_own.start()

    base = block(0, 0) * rows

    def unit(here, i):
        value = x_ref[here, :].astype(f32)
        there = pl.ds(pl.multiple_of(base + i * 16, 16), 16)
        unit_ref[there, :] = (value * root_mean(value)).astype(bf16)
        labels_ref[there, :] = label_ref[here, :]

    by_tiles(rows, unit)
    label_gather = gather_steps(rows, labels_ref, label_sems)
    unit_gather = gather_steps(rows, unit_ref, unit_sems)
    next(label_gather)
    next(unit_gather)

    for side in range(2):
        loads[2 + side].wait()
        cut_columns(
            wide.at[side], lambda step: low(gains_ref[pl.ds(step, 16), 0:1]), lambda j: mix_cut.at[j, side], 0, width
        )
    mix_moves = [
        remote(mix_cut.at[place(i)], mix_ref.at[me], mix_sent.at[i], mix_got.at[i], peer(i)) for i in range(1, owners)
    ]
    for move in mix_moves:
        move.start()
    mix_own = pltpu.make_async_copy(mix_cut.at[me], mix_ref.at[me], mix_sent.at[0])
    mix_own.start()
    loads[4].wait()
    ow_ref[...] = ow_f[...].astype(bf16)
    save(ow_ref, ow_out)
    fill_small(conv_ref, bias_ref, raw_conv, raw_a, raw_b, raw_c, rate_ref)
    fill_blocks(rbig, rw_ref)
    fill_blocks(ibig, iw_ref)
    pad[0:8, :] = jnp.zeros((8, width), f32)
    taps = raw_conv.shape[0]
    clear_tail(decay_ref, width)
    clear_tail(states_ref, width)

    cuts = down_hbm.shape[0] // down_low.shape[1]
    height = down_low.shape[1]

    def down_load(k):
        return pltpu.make_async_copy(down_hbm.at[pl.ds(k * height, height), :], down_f.at[k % 2], down_sem.at[k % 2])

    def down_save(k):
        return pltpu.make_async_copy(down_low.at[k % 2], down_out.at[pl.ds(k * height, height), :], down_sem.at[2 + k % 2])

    def down_cast(k):
        down_load(k).wait()
        if k >= 2:
            down_save(k - 2).wait()
        down_low[k % 2] = down_f[k % 2].astype(bf16)
        down_save(k).start()
        if k + 2 < cuts:
            down_load(k + 2).start()

    pair_own.wait()
    for move in pair_moves:
        move.wait_recv()
    line = quarter_steps(n, part, pair_out, line_sems)
    next(line)
    next(label_gather)
    next(unit_gather)
    waits = next(label_gather) + next(unit_gather)
    for wait in waits:
        wait()
    mix_own.wait()
    for move in mix_moves:
        move.wait_recv()
    save(unit_ref, unit_out)
    save(labels_ref, labels_out)
    save(mix_ref, mix_out)

    low_own.wait()
    low_gather = gather_steps(rows, low_out, low_sems)
    next(low_gather)
    next(line)

    def one(q, _):
        here = pl.ds(pl.multiple_of(q * length, length), length)
        sequence = unit_ref[here, :]
        masks = label_masks(labels_ref, here, length, width, taps, lines)
        pre_ref[here, :] = dot_nn(sequence, whole_weight(mix_ref, 0))
        conv_in = dot_nn(sequence, whole_weight(mix_ref, 1)).astype(bf16)
        conv_in_ref[here, :] = conv_in
        pad[8 : 8 + length, :] = conv_in.astype(f32)
        total = bias_ref[0:1, :] + conv_ref[0:1, :] * pad[8 : 8 + length, :]
        for k in range(1, taps):
            total = total + conv_ref[k : k + 1, :] * pad[8 - k : 8 - k + length, :] * masks[k - 1]
        values = total.astype(bf16)
        values_ref[here, :] = values
        recur = jax.nn.sigmoid(dot_nn(values, rbig[...].astype(bf16)) + bias_ref[1:2, :])
        inject = jax.nn.sigmoid(dot_nn(values, ibig[...].astype(bf16)) + bias_ref[2:3, :])
        recur_ref[here, :] = recur
        inject_ref[here, :] = inject
        log_decay = -decay_scale * bias_ref[3:4, :] * recur
        inside = masks[0] > 0.5
        put_tiles(decay_ref, here, jnp.where(inside, jnp.exp(log_decay), 0.0))
        scale = jnp.where(inside, jnp.sqrt(minus_expm1(2.0 * log_decay)), 1.0)
        put_tiles(states_ref, here, scale * inject * values.astype(f32))
        return 0

    lax.fori_loop(0, sequences, one, 0)
    seq_scan(decay_ref, states_ref, sequences, length, False)

    def two(q, _):
        here = pl.ds(pl.multiple_of(q * length, length), length)
        act, _unused = gelu_parts(pre_ref[here, :])
        product = (act * get_tiles(states_ref, here, width)).astype(bf16)
        product_ref[here, :] = product
        partial[here, :] = dot_nn(product, ow_ref[...]).astype(bf16)
        return 0

    for k in range(2):
        down_load(k).start()
    lax.fori_loop(0, sequences, two, 0)
    scatter = scatter_steps(rows, partial, near, far, acc, scatter_sems)
    next(scatter)
    for source, target in (
        (product_ref, product_out), (pre_ref, pre_out), (conv_in_ref, conv_in_out), (values_ref, values_out),
        (recur_ref, recur_out), (inject_ref, inject_out), (decay_ref, decay_out), (states_ref, states_out),
    ):
        save(source, target)
    next(line)
    for k in range(cuts):
        down_cast(k)
    for k in range(cuts - 2, cuts):
        down_save(k).wait()
    next(low_gather)
    waits = next(low_gather) + next(scatter)

    def norm(here, i):
        middle = x_ref[here, :].astype(f32) + acc[here, :]
        middle_ref[here, :] = middle
        there = pl.ds(pl.multiple_of(base + i * 16, 16), 16)
        two_ref[there, :] = (middle * root_mean(middle)).astype(bf16)

    by_tiles(rows, norm)
    two_gather = gather_steps(rows, two_ref, two_sems)
    next(two_gather)
    save(middle_ref, middle_out)
    for _ in range(n - 4):
        next(line)
    for wait in waits:
        wait()
    next(two_gather)
    for wait in next(two_gather):
        wait()
    save(two_ref, two_out)
    for _ in line:
        pass
    for move in pair_moves + mix_moves:
        move.wait_send()
    for copy in saves:
        copy.wait()


def front(sequences, x, label, cot, gains, small, rw, iw, branch_w, input_w, gate_w, up_w, output_w, down_w):
    rows, depth = x.shape
    own, n = branch_w.shape[0], lax.axis_size("replica")
    owners = lax.axis_size(GROUP)
    total, width, ff = owners * rows, branch_w.shape[1] // owners, gate_w.shape[1] // owners
    part = own // n
    length = total // sequences
    tiles = -(-width // 128)
    kept = [
        ((total, depth), bf16), ((total, 128), bf16), ((total, depth), bf16), ((total, width), bf16),
        ((total, width), f32), ((total, width), bf16), ((total, width), bf16), ((total, width), f32),
        ((total, width), f32), ((tiles, total, 128), f32), ((tiles, total, 128), f32), ((owners, 2, own, width), bf16),
        ((width, depth), bf16), ((total, depth), bf16), ((rows, depth), f32),
    ]
    vm = pltpu.VMEM
    dma = pltpu.SemaphoreType.DMA
    scratch = [vm(*item) for k, item in enumerate(kept) if k != 2] + [
        vm((2,) + branch_w.shape, f32),
        vm((2, part, gate_w.shape[1]), f32),
        vm(output_w.shape, f32),
        vm((owners, 2, own, width), bf16),
        vm((owners, part, 2 * ff), bf16),
        vm((8 + length, width), f32),
        vm((8 + length, 128), f32),
        vm((width, width), f32),
        vm((width, width), f32),
        vm((total, depth), bf16),
        vm((8, width), f32),
        vm((8, width), f32),
        vm((2, down_w.shape[0] // 8, depth), f32),
        vm((2, down_w.shape[0] // 8, depth), bf16),
    ]
    scratch += plane_scratch(rows, depth, 4, 1)
    scratch += [dma((6,)), dma((len(kept),))] + [dma((owners,))] * 4 + [dma((4,))] + [dma((n - 1,))] * 4
    outs = kept + [((owners, own, 2 * ff), bf16), (down_w.shape, bf16)]
    return pl.pallas_call(
        functools.partial(front_kernel, n, sequences, length),
        out_shape=tuple(jax.ShapeDtypeStruct(*item) for item in outs),
        in_specs=[VM] * 11 + [ANY] * 6,
        out_specs=[ANY] * len(outs),
        scratch_shapes=scratch,
        compiler_params=pltpu.CompilerParams(
            collective_id=1, has_side_effects=True, vmem_limit_bytes=62 * 2**20
        ),
        cost_estimate=pl.CostEstimate(flops=10**6, bytes_accessed=200 * 2**20, transcendentals=0),
    )(x, label, cot, gains, *small, rw, iw, branch_w, input_w, gate_w, up_w, output_w, down_w)


def turn_steps(
    sequences, length,
    partial_hbm, middle_ref, cot_ref, label_ref, raw_conv, raw_a, raw_b, raw_c, rate_ref, rw_ref, iw_ref, *rest,
):
    kept_hbm, rest = rest[:9], rest[9:]
    low_out, grad_out, partial_out, branch_low_out, conv_low_out, packed_ref = rest[:6]
    scatter_sems, gather_sems = rest[6 + 3 : 6 + 7], rest[6 + 7 : 6 + 11]
    near, far, acc = rest[6:9]
    rest = rest[17:]
    kept, rest = rest[:9], rest[9:]
    ow_ref, w_ref, pre_ref, conv_in_ref, values_ref, recur_ref, inject_ref, decay_ref, states_ref = kept
    partial, low_ref, grad_ref, branch_low_ref, conv_low_ref, adj, pad, lines, rbig, ibig, dr, di, conv_ref, bias_ref, dconv_ref, sums_ref, load_sem, save_sem = rest
    rows = middle_ref.shape[0]
    offsets, at, block = plane()
    first = pltpu.make_async_copy(partial_hbm, partial, load_sem.at[9])
    first.start()
    loads = [pltpu.make_async_copy(kept_hbm[k], kept[k], load_sem.at[k]) for k in range(9)]
    for load in loads:
        load.start()
    first.wait()
    scatter = scatter_steps(rows, partial, near, far, acc, scatter_sems)
    next(scatter)
    yield
    waits = next(scatter)
    base = block(0, 0) * rows

    def norm(here, i):
        middle = middle_ref[here, :]
        inverse = root_mean(middle)
        grad = cot_ref[here, :].astype(f32) + norm_backward(acc[here, :], middle * inverse, inverse)
        grad_ref[here, :] = grad
        there = pl.ds(pl.multiple_of(base + i * 16, 16), 16)
        low_ref[there, :] = grad.astype(bf16)

    by_tiles(rows, norm)
    gather = gather_steps(rows, low_ref, gather_sems)
    next(gather)
    yield
    next(gather)
    yield
    waits = waits + next(gather)
    yield
    for wait in waits:
        wait()
    for load in loads:
        load.wait()
    saves = [pltpu.make_async_copy(low_ref, low_out, save_sem.at[0]), pltpu.make_async_copy(grad_ref, grad_out, save_sem.at[1])]
    for save in saves:
        save.start()
    fill_blocks(rbig, rw_ref)
    fill_blocks(ibig, iw_ref)
    dr[...] = jnp.zeros_like(dr)
    di[...] = jnp.zeros_like(di)
    sums_ref[...] = jnp.zeros_like(sums_ref)
    dconv_ref[...] = jnp.zeros_like(dconv_ref)
    taps = raw_conv.shape[0]
    fill_small(conv_ref, bias_ref, raw_conv, raw_a, raw_b, raw_c, rate_ref)
    width = pad.shape[1]
    clear_tail(adj, width)

    def one(s):
        here = pl.ds(s * length, length)
        product_grad = dot_nt(low_ref[here, :], ow_ref[...])
        act, slope = gelu_parts(pre_ref[here, :])
        branch_low_ref[here, :] = (product_grad * get_tiles(states_ref, here, width) * slope).astype(bf16)
        put_tiles(adj, here, product_grad * act)

    for s in range(sequences):
        one(s)
        yield
    seq_scan(decay_ref, adj, sequences, length, True)
    yield

    def two(s):
        here = pl.ds(s * length, length)
        adjoint = get_tiles(adj, here, width)
        recur = recur_ref[here, :]
        inject = inject_ref[here, :]
        decay = get_tiles(decay_ref, here, width)
        values = values_ref[here, :]
        values_f = values.astype(f32)
        masks = label_masks(label_ref, here, length, width, taps, lines)
        inside = masks[0] > 0.5
        rate = bias_ref[3:4, :]
        log_decay = -decay_scale * rate * recur
        scale = jnp.where(inside, jnp.sqrt(minus_expm1(2.0 * log_decay)), 1.0)
        pad[0:8, :] = jnp.zeros((8, width), f32)
        pad[8 : 8 + length, :] = get_tiles(states_ref, here, width)
        previous = pad[7 : 7 + length, :]
        driven = adjoint * inject * values_f
        log_grad = jnp.where(inside, adjoint * previous * decay - driven * decay * decay / scale, 0.0)
        recur_low = (log_grad * (-decay_scale * rate) * recur * (1.0 - recur)).astype(bf16)
        inject_low = (driven * scale * (1.0 - inject)).astype(bf16)
        sums_ref[1:2, :] += jnp.sum(recur_low.astype(f32), axis=0, keepdims=True)
        sums_ref[2:3, :] += jnp.sum(inject_low.astype(f32), axis=0, keepdims=True)
        sums_ref[3:4, :] += jnp.sum(log_grad * recur, axis=0, keepdims=True)
        dr[...] += dot_tn(values, recur_low)
        di[...] += dot_tn(values, inject_low)
        grad = adjoint * scale * inject
        grad = grad + dot_nt(recur_low, rbig[...].astype(bf16)) + dot_nt(inject_low, ibig[...].astype(bf16))
        sums_ref[0:1, :] += jnp.sum(grad, axis=0, keepdims=True)
        pad[8 : 8 + length, :] = conv_in_ref[here, :].astype(f32)
        dconv_ref[0:1, :] += jnp.sum(grad * pad[8 : 8 + length, :], axis=0, keepdims=True)
        masked = []
        for k in range(1, taps):
            part = grad * masks[k - 1]
            masked.append(part)
            dconv_ref[k : k + 1, :] += jnp.sum(part * pad[8 - k : 8 - k + length, :], axis=0, keepdims=True)
        total = grad * conv_ref[0:1, :]
        pad[length : length + 8, :] = jnp.zeros((8, width), f32)
        for k in range(1, taps):
            pad[0:length, :] = masked[k - 1] * conv_ref[k : k + 1, :]
            total = total + pad[k : k + length, :]
        conv_low = total.astype(bf16)
        conv_low_ref[here, :] = conv_low
        partial[here, :] = (dot_nt(branch_low_ref[here, :], whole_weight(w_ref, 0)) + dot_nt(conv_low, whole_weight(w_ref, 1))).astype(bf16)

    for s in range(sequences):
        two(s)
        yield
    size = rw_ref.shape[1]
    packed_ref[...] = jnp.zeros_like(packed_ref)
    for h in range(rw_ref.shape[0]):
        cut = slice(h * size, (h + 1) * size)
        packed_ref[0, cut, 0 : 2 * size] = jnp.concatenate([dr[cut, cut], di[cut, cut]], axis=1).astype(bf16)
    packed_ref[0, width : width + 16, 0:width] = jnp.concatenate([dconv_ref[...], sums_ref[...]], axis=0).astype(bf16)
    ends = [(partial, partial_out), (branch_low_ref, branch_low_out), (conv_low_ref, conv_low_out)]
    for k, pair in enumerate(ends):
        saves.append(pltpu.make_async_copy(*pair, save_sem.at[2 + k]))
        saves[-1].start()
    yield
    for save in saves:
        save.wait()


def end_steps(
    outputs_at, mixes_at,
    partial_hbm, grad_ref, x_ref, middle_ref, hidden_hbm, down_hbm, product_hbm, mid_hbm, unit_hbm, branch_hbm, conv_hbm,
    gate_sum, up_sum, gate_hbm, up_hbm, tokens_ref, block_ref, gain_ref, *rest,
):
    near, far, acc = rest[:3]
    scatter_sems, more_sems = rest[3:7], rest[7:11]
    near_two, far_two, partial, hidden, down, product, tokens_wide, branch_low, conv_low, mix_low, sums, weights = rest[11:23]
    load_sem, gain_sem, output_made, mix_made = rest[23:]
    rows = x_ref.shape[0]
    depth = down.shape[1]

    def load(k, source, target):
        copy = pltpu.make_async_copy(source, target, load_sem.at[k])
        copy.start()
        return copy

    first = load(0, mid_hbm, tokens_wide), load(1, product_hbm, product)
    loads = [
        load(2, partial_hbm, partial), load(3, branch_hbm, branch_low), load(4, conv_hbm, conv_low),
        load(5, hidden_hbm, hidden), load(6, down_hbm, down),
    ]
    for copy in first:
        copy.wait()
    for d in range(0, depth, 512):
        output_made[0, :, d : d + 512] = dot_tn(product[...], tokens_wide[:, d : d + 512]).astype(bf16)
    again = load(7, unit_hbm, tokens_wide)

    def gain_loads(r):
        here = pl.ds(r * 16, 16)
        slot = r % 2
        return [
            pltpu.make_async_copy(source.at[here, :], target.at[slot, side], gain_sem.at[slot, 2 * group + side])
            for group, (target, sources) in enumerate(((sums, (gate_sum, up_sum)), (weights, (gate_hbm, up_hbm))))
            for side, source in enumerate(sources)
        ]

    gain_steps = gain_ref.shape[0] // 16
    for r in range(2):
        for copy in gain_loads(r):
            copy.start()
    yield outputs_at
    loads[1].wait()
    loads[2].wait()
    width = branch_low.shape[1]
    if mix_low.shape[1] > 2 * width:
        mix_low[...] = jnp.zeros_like(mix_low)

    def pack(here, i):
        mix_low[here, 0 : 2 * width] = jnp.concatenate([branch_low[here, :], conv_low[here, :]], axis=1)

    by_tiles(mix_low.shape[0], pack)
    again.wait()
    owners, own = mix_made.shape[:2]
    for part in range(4):
        for j in range(part * owners // 4, (part + 1) * owners // 4):
            mix_made[j] = dot_tn(tokens_wide[:, j * own : (j + 1) * own], mix_low[...]).astype(bf16)
        yield mixes_at if part == 3 else None
    loads[0].wait()
    scatter = scatter_steps(rows, partial, near, far, acc, scatter_sems)
    next(scatter)
    yield None
    for r in range(gain_steps):
        slot = r % 2
        for copy in gain_loads(r):
            copy.wait()
        both = jnp.zeros((16, 1), f32)
        for side in range(2):
            both = both + jnp.sum(
                sums[slot, side].astype(f32) * low(weights[slot, side]), axis=1, keepdims=True
            )
        gain_ref[r * 16 : (r + 1) * 16, :] = both
        if r + 2 < gain_steps:
            for copy in gain_loads(r + 2):
                copy.start()
        yield None
    waits = next(scatter)

    def norm(here, i):
        value = x_ref[here, :].astype(f32)
        inverse = root_mean(value)
        grad = grad_ref[here, :] + norm_backward(acc[here, :], value * inverse, inverse)
        tokens_ref[here, :] = grad.astype(bf16)

    by_tiles(rows, norm)
    for wait in waits:
        wait()
    yield None
    loads[3].wait()
    loads[4].wait()
    pieces_of = 4
    height = hidden.shape[0] // pieces_of
    for k in range(pieces_of):
        here = pl.ds(k * height, height)
        partial[here, :] = dot_nn(hidden[here, :], down[...]).astype(bf16)
        yield None
    scatter = scatter_steps(rows, partial, near_two, far_two, acc, more_sems)
    next(scatter)
    yield None
    waits = next(scatter)

    def out(here, i):
        block_ref[here, :] = (middle_ref[here, :] + acc[here, :]).astype(bf16)

    by_tiles(rows, out)
    yield None
    for wait in waits:
        wait()


def mlp_kernel(
    two_hbm, low_hbm, pair_hbm, down_hbm, hidden_out, partial_out, down_out, pair_out,
    two, low_rows, pair_w, down_w, hidden, pair_low, partial, down_grad, pair_grad, load_sem, save_sem, pair_sem,
):
    total, depth = two.shape
    ff = down_w.shape[0]
    tile = 256 if ff % 256 == 0 else 128
    height = 512
    steps = total // height

    def rows_of(hbm, ref, r, which):
        here = pl.ds(r * height, height)
        return pltpu.make_async_copy(hbm.at[here, :], ref.at[here, :], load_sem.at[which, r])

    weights = [
        pltpu.make_async_copy(pair_hbm, pair_w, load_sem.at[2, 0]),
        pltpu.make_async_copy(down_hbm, down_w, load_sem.at[2, 1]),
    ]
    rows_of(two_hbm, two, 0, 0).start()
    weights[0].start()
    rows_of(low_hbm, low_rows, 0, 1).start()
    weights[1].start()
    for r in range(1, steps):
        rows_of(two_hbm, two, r, 0).start()
        rows_of(low_hbm, low_rows, r, 1).start()
    weights[0].wait()
    weights[1].wait()

    def row_step(r, _):
        here = pl.ds(pl.multiple_of(r * height, height), height)
        pltpu.make_async_copy(two_hbm.at[here, :], two.at[here, :], load_sem.at[0, r]).wait()
        pltpu.make_async_copy(low_hbm.at[here, :], low_rows.at[here, :], load_sem.at[1, r]).wait()
        for f in range(ff // tile):
            cut = slice(f * tile, (f + 1) * tile)
            more = slice(ff + f * tile, ff + (f + 1) * tile)
            gate = dot_nn(two[here, :], pair_w[:, cut])
            up = dot_nn(two[here, :], pair_w[:, more])
            grad = dot_nt(low_rows[here, :], down_w[cut, :])
            act, slope = gelu_parts(gate)
            hidden[here, cut] = (act * up).astype(bf16)
            pair_low[here, cut] = (grad * up * slope).astype(bf16)
            pair_low[here, more] = (grad * act).astype(bf16)
        for d in range(0, depth, 512):
            partial[here, d : d + 512] = dot_nt(pair_low[here, :], pair_w[d : d + 512, :]).astype(bf16)
        return 0

    lax.fori_loop(0, steps, row_step, 0)
    saves = [
        pltpu.make_async_copy(partial, partial_out, save_sem.at[0]),
        pltpu.make_async_copy(hidden, hidden_out, save_sem.at[1]),
    ]
    for save in saves:
        save.start()
    for f in range(ff // tile):
        cut = slice(f * tile, (f + 1) * tile)
        down_grad[cut, :] = dot_tn(hidden[:, cut], low_rows[...]).astype(bf16)
    saves.append(pltpu.make_async_copy(down_grad, down_out, save_sem.at[2]))
    saves[-1].start()

    height = 256

    def column_step(d, _):
        here = pl.ds(pl.multiple_of(d * height, height), height)
        pair_grad[here, :] = dot_tn(two[:, here], pair_low[...]).astype(bf16)
        pltpu.make_async_copy(pair_grad.at[here, :], pair_out.at[here, :], pair_sem.at[d]).start()
        return 0

    lax.fori_loop(0, depth // height, column_step, 0)
    for d in range(depth // height):
        here = pl.ds(d * height, height)
        pltpu.make_async_copy(pair_grad.at[here, :], pair_out.at[here, :], pair_sem.at[d]).wait()
    for save in saves:
        save.wait()


def mlp(unit_two, out_low, pair_w, down_w):
    total, depth = unit_two.shape
    ff = down_w.shape[0]
    kept = [((total, ff), bf16), ((total, depth), bf16), ((ff, depth), bf16), ((depth, 2 * ff), bf16)]
    vm, dma = pltpu.VMEM, pltpu.SemaphoreType.DMA
    return pl.pallas_call(
        mlp_kernel,
        out_shape=tuple(jax.ShapeDtypeStruct(*item) for item in kept),
        in_specs=[ANY] * 4,
        out_specs=[ANY] * 4,
        scratch_shapes=[vm(item.shape, bf16) for item in (unit_two, out_low, pair_w, down_w)]
        + [vm((total, ff), bf16), vm((total, 2 * ff), bf16)]
        + [vm(*item) for item in kept[1:]]
        + [dma((3, total // 512)), dma((3,)), dma((depth // 256,))],
        compiler_params=pltpu.CompilerParams(vmem_limit_bytes=60 * 2**20),
        cost_estimate=pl.CostEstimate(
            flops=2 * total * depth * ff * 8, bytes_accessed=36 * 2**20, transcendentals=total * ff
        ),
    )(unit_two, out_low, pair_w, down_w)


def pieces(rows, most):
    count = -(-rows // most)
    while rows % count or (rows // count) % 16:
        count += 1
    return count


def chunk_count(height, columns):
    return pieces(height, max(16, (105 * 1024) // columns // 16 * 16))


def line_kernel(n, kinds, cuts, made_here, beside, turns, extra, *refs):
    ins = len(cuts)
    made = ins + kinds.count("pair")
    extra_ins, extra_outs, extra_scratch = extra
    refs = list(refs)

    def take(count):
        taken = refs[:count]
        del refs[:count]
        return taken

    given = [k for k in range(ins) if k not in made_here]
    own_hbm, side_in = dict(zip(given, take(len(given)))), take(extra_ins)
    outs, side_out = take(made), take(extra_outs)
    side_scratch = take(extra_scratch)
    from_out, from_in = take(ins), take(ins)
    own_made = dict(zip(made_here, take(len(made_here))))
    slots, whole_sem, slot_sem, sent_in, sent_out, got_out, got_in, sent_x, got_x = refs
    depth = slots.shape[0]
    me = lax.axis_index("replica")
    y, s = lax.axis_index("seq"), lax.axis_index("shard")
    shards = lax.axis_size("shard")
    owners = shards * lax.axis_size("seq")
    left = me < n // 2
    inward = jnp.where(left, me + 1, me - 1)
    outward = jnp.where(left, me - 1, me + 1)
    has_out = jnp.logical_and(me > 0, me < n - 1)
    at_end = jnp.logical_not(has_out)
    middle = jnp.logical_or(me == n // 2 - 1, me == n // 2)

    def peer(i):
        return {"seq": jnp.bitwise_xor(y, i // shards), "shard": jnp.bitwise_xor(s, i % shards)}

    def place(i):
        return jnp.bitwise_xor(y, i // shards) * shards + jnp.bitwise_xor(s, i % shards)

    chunks = []
    for k, (lead, count, rows) in enumerate(cuts):
        for step in range(lead):
            for i in range(count):
                chunks.append((k, step if kinds[k] == "row" else (step + 1) % lead, i * rows, rows))
    total = len(chunks)

    def view(group, c):
        k, i, start, rows = chunks[c]
        return group[k].at[0 if kinds[k] == "row" else place(i), pl.ds(start, rows), :]

    def slot(c):
        k, i, start, rows = chunks[c]
        return slots.at[c % depth, pl.ds(0, rows), pl.ds(0, from_in[k].shape[2])]

    def load(c):
        return pltpu.make_async_copy(view(own_hbm, c), slot(c), slot_sem.at[c % depth])

    wholes = {k: pltpu.make_async_copy(own_hbm[k], from_out[k], whole_sem.at[k]) for k in given}
    loaded = [c for c in range(total) if chunks[c][0] in given]

    @pl.when(at_end)
    def _():
        for k in given:
            wholes[k].start()

    @pl.when(has_out)
    def _():
        for c in loaded[: depth - 1]:
            load(c).start()

    barrier = pltpu.get_barrier_semaphore()
    for i in range(1, owners):
        pl.semaphore_signal(barrier, inc=1, device_id=peer(i), device_id_type=MESH)
    pl.semaphore_signal(barrier, inc=1, device_id={"replica": inward}, device_id_type=MESH)

    @pl.when(has_out)
    def _():
        pl.semaphore_signal(barrier, inc=1, device_id={"replica": outward}, device_id_type=MESH)
        pl.semaphore_wait(barrier, owners + 1)

    @pl.when(at_end)
    def _():
        pl.semaphore_wait(barrier, owners)

    def push(group, target, c, sent, got, device):
        return remote(view(group, c), view(target, c), sent.at[c], got.at[c], {"replica": device})

    def add(target, other, c):
        k, i, start, rows = chunks[c]
        if other is None:
            more = view(own_made, c) if k in made_here else slot(c)
        else:
            more = view(other, c)
        into = view(target, c)

        def tile(t, _):
            here = pl.ds(pl.multiple_of(t * 16, 16), 16)
            into[here, :] = (into[here, :].astype(f32) + more[here, :].astype(f32)).astype(bf16)
            return 0

        lax.fori_loop(0, rows // 16, tile, 0)

    def pass_in(c, source):
        @pl.when(middle)
        def _():
            push(source, from_in, c, sent_in, got_in, inward).start()

        @pl.when(jnp.logical_not(middle))
        def _():
            push(source, from_out, c, sent_in, got_out, inward).start()

    def gather_in(c):
        @pl.when(has_out)
        def _():
            if c in loaded:
                load(c).wait()
            push(from_out, from_out, c, sent_in, got_out, inward).wait_recv()
            add(from_out, None, c)
            pass_in(c, from_out)
            if c + depth - 1 in loaded:
                load(c + depth - 1).start()

    @pl.when(at_end)
    def _():
        for c in loaded:
            if c == 0 or chunks[c][0] != chunks[c - 1][0]:
                wholes[chunks[c][0]].wait()
            pass_in(c, from_out)

    def advance():
        k = next(work)
        if k is not None:

            @pl.when(at_end)
            def _():
                for c in range(total):
                    if chunks[c][0] == k:
                        pass_in(c, own_made)

    work = beside(*side_in, *side_out, *side_scratch, *[own_made[k] for k in made_here])
    advance()

    def deliveries(c):
        k, i, start, rows = chunks[c]
        here = pl.ds(start, rows)
        first = k + kinds[:k].count("pair")
        source = view(from_in, c)
        if kinds[k] == "row":
            ends = [(source, outs[first].at[here, :])]
        elif kinds[k] == "side":
            ends = [(source, outs[first].at[place(0), here, :])]
        else:
            half = source.shape[1] // 2
            there = pl.ds(pl.multiple_of(place(0) * half, half), half)
            ends = [
                (source.at[:, pl.ds(part * half, half)], outs[first + part].at[here, there]) for part in range(2)
            ]
        if kinds[k] == "row" or i == 0:
            return [pltpu.make_async_copy(*pair, sent_x.at[c, p]) for p, pair in enumerate(ends)], False
        return [remote(*pair, sent_x.at[c, p], got_x.at[c, p], peer(i)) for p, pair in enumerate(ends)], True

    def give_back(c):
        push(from_out, from_in, c, sent_out, got_in, inward).wait_recv()

        @pl.when(middle)
        def _():
            add(from_in, from_out, c)

        @pl.when(has_out)
        def _():
            push(from_in, from_in, c, sent_out, got_in, outward).start()

        for copy in deliveries(c)[0]:
            copy.start()

    lag = 1
    for c in range(total + lag):
        for _ in range(turns.count(c)):
            advance()
        if c < total:
            gather_in(c)
        if c >= lag:
            give_back(c - lag)
    for _ in work:
        pass
    for c in range(total):
        copies, away = deliveries(c)
        for copy in copies:
            if away:
                copy.wait_recv()
                copy.wait_send()
            else:
                copy.wait()
        push(from_out, from_in, c, sent_in, got_in, inward).wait_send()

        @pl.when(has_out)
        def _():
            push(from_in, from_in, c, sent_out, got_in, outward).wait_send()


def replica_sum(arrays, kinds, made_here, identity, beside, turns, inputs, results, side_scratch):
    cuts, outs = [], []
    tall = broad = 0
    for item, kind in zip(arrays, kinds):
        lead, height, columns = item.shape
        count = chunk_count(height, columns)
        cuts.append((lead, count, height // count))
        tall, broad = max(tall, height // count), max(broad, columns)
        if kind == "pair":
            outs += [jax.ShapeDtypeStruct((height, lead * columns // 2), bf16)] * 2
        elif kind == "side":
            outs.append(jax.ShapeDtypeStruct(item.shape, bf16))
        else:
            outs.append(jax.ShapeDtypeStruct((height, columns), bf16))
    count = sum(lead * cut for lead, cut, _ in cuts)
    buffers = [pltpu.VMEM(item.shape, bf16) for item in arrays]
    dma = pltpu.SemaphoreType.DMA
    return pl.pallas_call(
        functools.partial(
            line_kernel, lax.axis_size("replica"), tuple(kinds), tuple(cuts), tuple(made_here), beside, turns,
            (len(inputs), len(results), len(side_scratch)),
        ),
        out_shape=tuple(outs) + tuple(jax.ShapeDtypeStruct(shape, kind) for shape, kind, _ in results),
        in_specs=[ANY] * (len(arrays) - len(made_here)) + [spec for _, spec in inputs],
        out_specs=[ANY] * len(outs) + [spec for _, _, spec in results],
        scratch_shapes=list(side_scratch)
        + buffers * 2
        + [buffers[k] for k in made_here]
        + [pltpu.VMEM((4, tall, broad), bf16), dma((len(arrays),)), dma((4,))]
        + [dma((count,))] * 4
        + [dma((count, 2))] * 2,
        compiler_params=pltpu.CompilerParams(
            collective_id=identity, has_side_effects=True, vmem_limit_bytes=62 * 2**20
        ),
        cost_estimate=pl.CostEstimate(flops=10**6, bytes_accessed=200 * 2**20, transcendentals=0),
    )(*[item for k, item in enumerate(arrays) if k not in made_here], *[item for item, _ in inputs])


def finish_pair_kernel(gain_ref, a_ref, b_ref, outa_ref, outb_ref):
    gain = low(gain_ref[:, 1:2])
    outa_ref[...] = a_ref[...].astype(f32) * gain
    outb_ref[...] = b_ref[...].astype(f32) * gain


def finish_pair(gain, a, b):
    rows, columns = a.shape
    cut = min(rows, 64)
    wide = pl.BlockSpec((cut, columns), lambda i: (i, 0))
    out = jax.ShapeDtypeStruct((rows, columns), f32)
    return pl.pallas_call(
        finish_pair_kernel,
        grid=(rows // cut,),
        out_shape=(out, out),
        in_specs=[pl.BlockSpec((cut, 2), lambda i: (i, 0)), wide, wide],
        out_specs=[wide, wide],
        compiler_params=pltpu.CompilerParams(vmem_limit_bytes=62 * 2**20),
        cost_estimate=pl.CostEstimate(flops=2 * rows * columns, bytes_accessed=12 * rows * columns, transcendentals=0),
    )(gain, a, b)


def finish_rest_kernel(gain_ref, mix_ref, wa_ref, wb_ref, out_sum_ref, down_sum_ref, outa_ref, outb_ref, grad_ref, out_ref, down_ref):
    owners = mix_ref.shape[0]
    width = wa_ref.shape[1] // owners
    gain = low(gain_ref[:, 0:1])
    grad = jnp.zeros(gain.shape, f32)
    for part, (weight_ref, target_ref) in enumerate(((wa_ref, outa_ref), (wb_ref, outb_ref))):
        total = jnp.concatenate(
            [mix_ref[j, :, part * width : (part + 1) * width].astype(f32) for j in range(owners)], axis=1
        )
        target_ref[...] = total * gain
        grad = grad + jnp.sum(total * low(weight_ref[...]), axis=1, keepdims=True)
    grad_ref[...] = grad
    out_ref[...] = out_sum_ref[...].astype(f32)
    down_ref[...] = down_sum_ref[...].astype(f32)


def finish_rest(gain, mix, wa, wb, out_sum, down_sum):
    rows, columns = wa.shape
    steps = 4
    while out_sum.shape[0] % (16 * steps) or down_sum.shape[0] % (16 * steps) or rows % (16 * steps):
        steps //= 2

    def tall(item):
        return pl.BlockSpec((item.shape[0] // steps, item.shape[1]), lambda i: (i, 0))

    owners, _, both = mix.shape
    wide, thin = tall(wa), pl.BlockSpec((rows // steps, 1), lambda i: (i, 0))
    return pl.pallas_call(
        finish_rest_kernel,
        grid=(steps,),
        out_shape=(
            jax.ShapeDtypeStruct(wa.shape, f32),
            jax.ShapeDtypeStruct(wa.shape, f32),
            jax.ShapeDtypeStruct((rows, 1), f32),
            jax.ShapeDtypeStruct(out_sum.shape, f32),
            jax.ShapeDtypeStruct(down_sum.shape, f32),
        ),
        in_specs=[
            tall(gain),
            pl.BlockSpec((owners, rows // steps, both), lambda i: (0, i, 0)),
            wide,
            wide,
            tall(out_sum),
            tall(down_sum),
        ],
        out_specs=[wide, wide, thin, tall(out_sum), tall(down_sum)],
        compiler_params=pltpu.CompilerParams(vmem_limit_bytes=62 * 2**20),
        cost_estimate=pl.CostEstimate(flops=10**7, bytes_accessed=40 * 2**20, transcendentals=0),
    )(gain, mix, wa, wb, out_sum, down_sum)


def body(
    tokens,
    segments,
    cotangent,
    norm_gain,
    branch_weight,
    input_weight,
    conv_weight,
    conv_bias,
    recur_gate_weight,
    recur_gate_bias,
    input_gate_weight,
    input_gate_bias,
    decay_param,
    output_weight,
    mlp_norm_gain,
    gate_weight,
    up_weight,
    down_weight,
):
    x, cot = tokens[0], cotangent[0]
    rows, depth = x.shape
    members = lax.axis_size(GROUP)
    sequences = lax.axis_size("shard")
    total = members * rows
    gains = jnp.stack([norm_gain, mlp_norm_gain], 1)
    own_labels = jnp.broadcast_to(segments[0].astype(bf16)[:, None], (rows, 128))
    width = branch_weight.shape[1] // members
    decay_f = low(decay_param)
    small = (
        conv_weight, conv_bias, recur_gate_bias, input_gate_bias, jax.nn.softplus(-decay_f),
    )
    (
        unit_all, labels, out_low, product, *mixed, mix_w, output_w, unit_two, middle, pair_w, down_w,
    ) = front(
        sequences, x, own_labels, cot, gains, small,
        recur_gate_weight, input_gate_weight, branch_weight, input_weight, gate_weight, up_weight, output_weight,
        down_weight,
    )
    pair_w = pair_w.reshape(depth, -1)
    whole = ((total, depth), bf16)
    hidden, partial, down_partial, pair_partial = mlp(unit_two, out_low, pair_w, down_w)
    down_partial = down_partial[None]
    pair_partial = pair_partial.reshape(members, -1, pair_w.shape[1])
    kept = (output_w, mix_w, *mixed)
    narrow = ((total, width), bf16)
    vm, dma = pltpu.VMEM, pltpu.SemaphoreType.DMA
    length = total // sequences
    size = recur_gate_weight.shape[1]
    lanes = -(-max(width, 2 * size) // 128) * 128
    back = replica_sum(
        [down_partial, pair_partial], ["row", "pair"], (), 3,
        functools.partial(turn_steps, sequences, length),
        (6, 9, 12) + tuple(range(14, 14 + 2 * sequences + 2)),
        [(partial, ANY)] + [(item, VM) for item in (middle, cot, labels, *small, recur_gate_weight, input_gate_weight)]
        + [(item, ANY) for item in kept],
        [whole + (ANY,), ((rows, depth), f32, ANY), whole + (ANY,), narrow + (ANY,), narrow + (ANY,)]
        + [((1, width + 16, lanes), bf16, VM)],
        plane_scratch(rows, depth, 1, 1)
        + [vm(item.shape, item.dtype) for item in kept]
        + [vm(*whole), vm(*whole), vm((rows, depth), f32), vm(*narrow), vm(*narrow), vm(mixed[-1].shape, f32)]
        + [vm((8 + length, width), f32), vm((8 + length, 128), f32)]
        + [vm((width, width), f32)] * 4
        + [vm((8, width), f32)] * 2
        + [vm((8, width), f32), vm((8, width), f32)]
        + [dma((10,)), dma((5,))],
    )
    down_sum, gate_sum, up_sum, mid_low, middle_grad, partial, branch_low, conv_low = back[:8]
    packed = back[8]
    both = -(-2 * width // 128) * 128
    mix_shape = jax.ShapeDtypeStruct((members, depth // members, both), bf16)
    output_shape = jax.ShapeDtypeStruct((1,) + output_w.shape, bf16)
    ahead = sum(chunk_count(*item.shape[1:]) for item in (packed, output_shape))
    made_by = tuple(min(k, ahead) for k in (0, 0, 1, 2))
    again = plane_scratch(rows, depth, 0, 1)
    packed, output_sum, mix_sum, tokens_grad, block_out, mlp_gain_grad = replica_sum(
        [packed, output_shape, mix_shape], ["row", "row", "side"], (1, 2), 4, functools.partial(end_steps, 1, 2),
        made_by + (4, 10, 11, 12, 13, 14, 15, 22) + tuple(5 + i // 4 for i in range(gate_weight.shape[0] // 16)),
        [(partial, ANY), (middle_grad, VM), (x, VM), (middle, VM)]
        + [(item, ANY) for item in (hidden, down_w, product, mid_low, unit_all, branch_low, conv_low, gate_sum, up_sum, gate_weight, up_weight)],
        [((rows, depth), bf16, VM), ((rows, depth), bf16, VM), ((gate_weight.shape[0], 1), f32, VM)],
        again + again[3:] + again[:2] + [vm(*whole), vm(hidden.shape, bf16), vm(down_w.shape, bf16)]
        + [vm(*narrow), vm(*whole), vm(*narrow), vm(*narrow), vm((total, both), bf16)]
        + [vm((2, 2, 16, gate_weight.shape[1]), bf16), vm((2, 2, 16, gate_weight.shape[1]), f32), dma((8,)), dma((2, 4))],
    )
    packed = packed.astype(f32)
    gate_grad, up_grad = finish_pair(gains, gate_sum, up_sum)
    branch_grad, input_grad, gain_grad, output_grad, down_grad = finish_rest(
        gains, mix_sum, branch_weight, input_weight, output_sum, down_sum
    )
    recur_weight_grad = packed[:width, :size].reshape(-1, size, size)
    inject_weight_grad = packed[:width, size : 2 * size].reshape(-1, size, size)
    conv_weight_grad = packed[width : width + conv_weight.shape[0], :width]
    conv_bias_grad, recur_bias_grad, inject_bias_grad, rate_grad = [packed[width + 8 + i, :width] for i in range(4)]
    decay_param_grad = rate_grad * decay_scale * jax.nn.sigmoid(-decay_f)
    return (
        block_out[None],
        tokens_grad[None],
        gain_grad[:, 0],
        branch_grad,
        input_grad,
        conv_weight_grad,
        conv_bias_grad,
        recur_weight_grad,
        recur_bias_grad,
        inject_weight_grad,
        inject_bias_grad,
        decay_param_grad,
        output_grad,
        mlp_gain_grad[:, 0],
        gate_grad,
        up_grad,
        down_grad,
    )


def solution(mesh):
    row3 = P(("shard", "replica"), "seq", None)
    vec = P(("seq", "shard"))
    mat = P(("seq", "shard"), None)
    cube = P(("seq", "shard"), None, None)
    taps = P(None, ("seq", "shard"))
    params = (vec, mat, mat, taps, vec, cube, vec, cube, vec, vec, mat, vec, mat, mat, mat)
    in_specs = (row3, P(("shard", "replica"), "seq"), row3) + params
    out_specs = (row3, row3) + params
    return jax.shard_map(body, mesh=mesh, in_specs=in_specs, out_specs=out_specs, check_vma=False)
```
